128 devices in a mesh: noise: 8 (over y, core), dp: 16 (over x, z).
Axes of the slice: x: 4, y: 4, z: 4, core: 2. Of those that a mesh axis runs over, the one named last changes fastest.
Arguments:
- noise_latents: bfloat16 [16384, 2048], P('noise', 'dp')
- data_latents: bfloat16 [16384, 2048], P('dp', 'noise')
Outputs:
- targets: float32 [16384, 2048], P('noise', 'dp')
- potential_rows: float32 [16384], P('noise')
- potential_cols: float32 [16384], P('dp')
All inputs are finite; a program needn't handle non-finite values.
Results may differ from the reference program's by a relative error of at most 0.0023.
Values may be sent and summed in bfloat16 or wider, within the bound.
A program may use at most 128 MiB of HBM per device.

```python
import jax
import jax.numpy as jnp
from jax import lax

W = 2048
NR_DEV = 2048
MC_DEV = 1024
ITERS = 3
N = 16384
M = 16384


def data_field(key, spread):
    values = jax.random.normal(key, (M, W), jnp.float32)
    scales = jnp.exp(jax.random.uniform(jax.random.fold_in(key, 11), (M, 1), jnp.float32) * jnp.log(spread))
    return values * scales


def draw_data_latents(key, part):
    spread = 1.0
    return data_field(key, spread).astype(jnp.bfloat16)


def draw_noise_latents(key, part):
    spread = 1.0
    key = jax.random.fold_in(key, 3)
    fresh = jax.random.normal(key, (N, W), jnp.float32)
    scales = jnp.exp(jax.random.uniform(jax.random.fold_in(key, 5), (N, 1), jnp.float32) * jnp.log(spread))
    result = fresh * scales
    return result.astype(jnp.bfloat16)


def setup_inputs(seed: int = 0) -> dict:
    keys = jax.random.split(jax.random.key(seed), 3)
    return {
        "noise_latents": draw_noise_latents(jax.random.fold_in(keys[2], 71), 0),
        "data_latents": draw_data_latents(jax.random.fold_in(keys[2], 71), 0),
    }


EPSILON = 0.04


def logsum(scores, axis):
    top = jnp.max(scores, axis=axis)
    return top + jnp.log(jnp.sum(jnp.exp(scores - jnp.expand_dims(top, axis)), axis=axis))


def reference(noise_latents, data_latents):
    sqy = jnp.sum(jnp.square(data_latents.astype(jnp.float32)), axis=1)
    blocks = noise_latents.reshape(N // NR_DEV, NR_DEV, W)

    def block_cost(rows):
        dots = jnp.dot(rows, data_latents.T, preferred_element_type=jnp.float32)
        norms = jnp.sum(jnp.square(rows.astype(jnp.float32)), axis=1)
        return (norms[:, None] + sqy[None, :] - 2.0 * dots) / W

    cost = lax.map(block_cost, blocks).reshape(N, M)
    rows_pot = jnp.zeros((N,), jnp.float32)
    cols_pot = jnp.zeros((M,), jnp.float32)
    rowlse = jnp.zeros((N,), jnp.float32)
    for step in range(ITERS):
        cols_pot = -EPSILON * (jnp.log(jnp.float32(M)) + logsum((rows_pot[:, None] - cost) / EPSILON, 0))
        rowlse = logsum((cols_pot[None, :] - cost) / EPSILON, 1)
        rows_pot = -EPSILON * (jnp.log(jnp.float32(N)) + rowlse)
    scores = ((cols_pot[None, :] - cost) / EPSILON - rowlse[:, None]).reshape(N // NR_DEV, NR_DEV, M)
    col_blocks = M // MC_DEV

    def block_target(block):
        weights = jnp.exp(block).astype(jnp.bfloat16)

        def one_part(index):
            start = (index * MC_DEV).astype(jnp.int32)
            left = lax.dynamic_slice_in_dim(weights, start, MC_DEV, 1)
            right = lax.dynamic_slice_in_dim(data_latents, start, MC_DEV, 0)
            return jnp.dot(left, right, preferred_element_type=jnp.float32)

        partials = lax.map(one_part, jnp.arange(col_blocks, dtype=jnp.int32))
        return jnp.sum(partials, axis=0)

    targets = lax.map(block_target, scores).reshape(N, W)
    return targets, rows_pot, cols_pot
```

```python
import functools
import math

import jax
import jax.numpy as jnp
from jax import lax
from jax.experimental import pallas as pl
from jax.experimental.pallas import tpu as pltpu
from jax.sharding import PartitionSpec as P

ITERS = 3
EPSILON = 0.04
LOG2E = 1.0 / math.log(2.0)
MESH = pl.DeviceIdType.MESH
LANES = 128
TILE = 32


def wrap(index, size):
    return lax.rem(index, size)


def spread_lanes(ref, row):
    return jnp.broadcast_to(ref[pl.ds(row, 1), :], (LANES, LANES)).T


def exchange(buf, send, recv, step, parts, me, size, peer_id):
    copies = []
    for k in range(1, size):
        peer = wrap(me + k, size)
        copy = pltpu.make_async_remote_copy(
            src_ref=buf.at[step, me, pl.ds(0, parts)],
            dst_ref=buf.at[step, me, pl.ds(0, parts)],
            send_sem=send.at[step, k],
            recv_sem=recv.at[step, me],
            device_id=peer_id(peer),
            device_id_type=MESH,
        )
        copy.start()
        copies.append(copy)
    for k in range(1, size):
        peer = wrap(me + k, size)
        pltpu.make_async_remote_copy(
            src_ref=buf.at[step, peer, pl.ds(0, parts)],
            dst_ref=buf.at[step, peer, pl.ds(0, parts)],
            send_sem=send.at[step, k],
            recv_sem=recv.at[step, peer],
            device_id=peer_id(peer),
            device_id_type=MESH,
        ).wait_recv()
    for copy in copies:
        copy.wait_send()


def combine(buf, step, size):
    top = buf[step, 0, 0]
    for s in range(1, size):
        top = jnp.maximum(top, buf[step, s, 0])
    total = buf[step, 0, 1] * jnp.exp2(buf[step, 0, 0] - top)
    for s in range(1, size):
        total = total + buf[step, s, 1] * jnp.exp2(buf[step, s, 0] - top)
    return top, total


def add_slots(buf, step, size):
    total = buf[step, 0, 0]
    for s in range(1, size):
        total = total + buf[step, s, 0]
    return total


def kernel(
    nsize, dsize, shape,
    dots, sqx, sqy,
    weights, rows_out, cols_out,
    scores, shift, first, scale, part, colvec, rowpack, colpack,
    col_buf, row_buf, col_send, col_recv, row_send, row_recv,
):
    rows, cols, width = shape
    n = lax.axis_index("noise")
    d = lax.axis_index("dp")
    kappa = LOG2E / EPSILON
    log_rows = math.log2(rows * nsize)
    log_cols = math.log2(cols * dsize)
    col_peer = lambda p: (p, d)
    row_peer = lambda p: (n, p)
    chunks = cols // LANES
    row_blocks = rows // LANES
    tiles = rows // TILE

    barrier = pltpu.get_barrier_semaphore()
    for k in range(1, nsize):
        pl.semaphore_signal(barrier, inc=1, device_id=col_peer(wrap(n + k, nsize)), device_id_type=MESH)
    for k in range(1, dsize):
        pl.semaphore_signal(barrier, inc=1, device_id=row_peer(wrap(d + k, dsize)), device_id_type=MESH)
    pl.semaphore_wait(barrier, nsize + dsize - 2)

    def fold(block, op):
        out = block[0:8]
        for r in range(1, TILE // 8):
            out = op(out, block[8 * r:8 * r + 8])
        return out

    def lane(c):
        return slice(LANES * c, LANES * (c + 1))

    def spread_cols():
        for c in range(chunks):
            colvec[:, lane(c)] = jnp.broadcast_to(colpack[pl.ds(c, 1), :], (8, LANES))

    factor = 2.0 * kappa / width
    for b in range(row_blocks):
        shift[pl.ds(b * LANES, LANES), :] = spread_lanes(sqx, b) * (-kappa / width)

    zero = tuple(jnp.full((8, LANES), -jnp.inf, jnp.float32) for _ in range(chunks))

    def top_step(t, accs):
        at = pl.ds(pl.multiple_of(t * TILE, TILE), TILE)
        add = shift[at, :]
        out = []
        for c in range(chunks):
            value = dots[at, lane(c)] * factor
            scores[at, lane(c)] = value
            out.append(jnp.maximum(accs[c], fold(value + add, jnp.maximum)))
        return tuple(out)

    tops = lax.fori_loop(0, tiles, top_step, zero)
    tops = tuple(jnp.max(a, axis=0, keepdims=True) for a in tops)
    for c in range(chunks):
        col_buf[0, n, 0, pl.ds(c, 1), :] = tops[c]
        colvec[:, lane(c)] = jnp.broadcast_to(tops[c], (8, LANES))

    zeros = tuple(jnp.zeros((8, LANES), jnp.float32) for _ in range(chunks))

    def tall(ref, c):
        return jnp.concatenate([ref[:, lane(c)]] * (TILE // 8), axis=0)

    def exp_step(t, accs):
        at = pl.ds(pl.multiple_of(t * TILE, TILE), TILE)
        add = shift[at, :]
        return tuple(
            accs[c] + fold(jnp.exp2(scores[at, lane(c)] + add - tall(colvec, c)), jnp.add)
            for c in range(chunks)
        )

    sums = lax.fori_loop(0, tiles, exp_step, zeros)
    for c in range(chunks):
        col_buf[0, n, 1, pl.ds(c, 1), :] = jnp.sum(sums[c], axis=0, keepdims=True)
    exchange(col_buf, col_send, col_recv, 0, 2, n, nsize, col_peer)
    top, total = combine(col_buf, 0, nsize)
    col_pot = -log_cols - top - jnp.log(total) * LOG2E
    colpack[...] = col_pot
    spread_cols()

    def row_step(t, carry):
        at = pl.ds(pl.multiple_of(t * TILE, TILE), TILE)
        values = [scores[at, lane(c)] + tall(colvec, c) for c in range(chunks)]
        top = values[0]
        for c in range(1, chunks):
            top = jnp.maximum(top, values[c])
        top = jnp.broadcast_to(jnp.max(top, axis=1, keepdims=True), (TILE, LANES))
        first[at, :] = top
        total = None
        for c in range(chunks):
            value = jnp.exp2(values[c] - top)
            scores[at, lane(c)] = value
            total = value if total is None else total + value
        part[at, :] = total
        return carry

    lax.fori_loop(0, tiles, row_step, 0)
    for b in range(row_blocks):
        at = pl.ds(b * LANES, LANES)
        row_buf[0, d, 0, pl.ds(b, 1), :] = first[at, :].T[0:1]
        row_buf[0, d, 1, pl.ds(b, 1), :] = jnp.sum(part[at, :].T, axis=0, keepdims=True)
    local_top = row_buf[0, d, 0]
    exchange(row_buf, row_send, row_recv, 0, 2, d, dsize, row_peer)
    top, total = combine(row_buf, 0, dsize)
    row_lse = top + jnp.log(total) * LOG2E
    base = jnp.exp2(local_top - row_lse)

    def spread_rows(value):
        rowpack[...] = value
        for b in range(row_blocks):
            scale[pl.ds(b * LANES, LANES), :] = spread_lanes(rowpack, b)

    spread_rows(base)

    def col_step(t, accs):
        at = pl.ds(pl.multiple_of(t * TILE, TILE), TILE)
        mul = scale[at, :]
        return tuple(accs[c] + fold(scores[at, lane(c)] * mul, jnp.add) for c in range(chunks))

    def sum_step(t, carry):
        at = pl.ds(pl.multiple_of(t * TILE, TILE), TILE)
        total = scores[at, lane(0)] * tall(colvec, 0)
        for c in range(1, chunks):
            total = total + scores[at, lane(c)] * tall(colvec, c)
        part[at, :] = total
        return carry

    for step in range(1, ITERS):
        sums = lax.fori_loop(0, tiles, col_step, zeros)
        for c in range(chunks):
            col_buf[step, n, 0, pl.ds(c, 1), :] = jnp.sum(sums[c], axis=0, keepdims=True)
        exchange(col_buf, col_send, col_recv, step, 1, n, nsize, col_peer)
        ratio = 1.0 / add_slots(col_buf, step, nsize)
        colpack[...] = ratio
        spread_cols()
        lax.fori_loop(0, tiles, sum_step, 0)
        for b in range(row_blocks):
            at = pl.ds(b * LANES, LANES)
            row_buf[step, d, 0, pl.ds(b, 1), :] = jnp.sum(part[at, :].T, axis=0, keepdims=True)
        row_buf[step, d, 0] = row_buf[step, d, 0] * base
        exchange(row_buf, row_send, row_recv, step, 1, d, dsize, row_peer)
        total = add_slots(row_buf, step, dsize)
        spread_rows(base / total)

    rows_out[...] = -(log_rows + row_lse + jnp.log(total) * LOG2E) / kappa + sqx[...] / width
    cols_out[...] = (col_pot + jnp.log(ratio) * LOG2E + (log_rows - log_cols)) / kappa + sqy[...] / width

    def weight_step(t, carry):
        at = pl.ds(pl.multiple_of(t * TILE, TILE), TILE)
        mul = scale[at, :]
        for c in range(chunks):
            weights[at, lane(c)] = (scores[at, lane(c)] * tall(colvec, c) * mul).astype(jnp.bfloat16)
        return carry

    lax.fori_loop(0, tiles, weight_step, 0)


def couple(dots, sqx, sqy, nsize, dsize, width):
    rows, cols = dots.shape
    vmem = pl.BlockSpec(memory_space=pltpu.VMEM)
    f32 = jnp.float32
    weights, rows_pot, cols_pot = pl.pallas_call(
        functools.partial(kernel, nsize, dsize, (rows, cols, width)),
        out_shape=(
            jax.ShapeDtypeStruct((rows, cols), jnp.bfloat16),
            jax.ShapeDtypeStruct((rows // LANES, LANES), f32),
            jax.ShapeDtypeStruct((cols // LANES, LANES), f32),
        ),
        in_specs=[vmem] * 3,
        out_specs=(vmem,) * 3,
        scratch_shapes=[
            pltpu.VMEM((rows, cols), f32),
            pltpu.VMEM((rows, LANES), f32),
            pltpu.VMEM((rows, LANES), f32),
            pltpu.VMEM((rows, LANES), f32),
            pltpu.VMEM((rows, LANES), f32),
            pltpu.VMEM((8, cols), f32),
            pltpu.VMEM((rows // LANES, LANES), f32),
            pltpu.VMEM((cols // LANES, LANES), f32),
            pltpu.VMEM((ITERS, nsize, 2, cols // LANES, LANES), f32),
            pltpu.VMEM((ITERS, dsize, 2, rows // LANES, LANES), f32),
            pltpu.SemaphoreType.DMA((ITERS, nsize)),
            pltpu.SemaphoreType.DMA((ITERS, nsize)),
            pltpu.SemaphoreType.DMA((ITERS, dsize)),
            pltpu.SemaphoreType.DMA((ITERS, dsize)),
        ],
        compiler_params=pltpu.CompilerParams(
            collective_id=0, has_side_effects=True, vmem_limit_bytes=48 * 2**20
        ),
    )(dots, sqx.reshape(rows // LANES, LANES), sqy.reshape(cols // LANES, LANES))
    return weights, rows_pot.reshape(rows), cols_pot.reshape(cols)


def shards(noise_latents, data_latents):
    nsize = lax.axis_size("noise")
    dsize = lax.axis_size("dp")
    data_full = lax.all_gather(data_latents, "noise", axis=1, tiled=True)
    width = data_full.shape[1]
    sqy = jnp.sum(jnp.square(data_full.astype(jnp.float32)), axis=1)
    noise_full = lax.all_gather(noise_latents, "dp", axis=1, tiled=True)
    sqx = jnp.sum(jnp.square(noise_full.astype(jnp.float32)), axis=1)
    dots = lax.dot_general(
        noise_full, data_full, (((1,), (1,)), ((), ())), preferred_element_type=jnp.float32
    )
    weights, rows_pot, cols_pot = couple(dots, sqx, sqy, nsize, dsize, width)
    partial_sum = jnp.dot(weights, data_full, preferred_element_type=jnp.float32)
    targets = lax.psum_scatter(partial_sum, "dp", scatter_dimension=1, tiled=True)
    return (targets, rows_pot, cols_pot)


def solution(mesh):
    return jax.shard_map(
        shards,
        mesh=mesh,
        in_specs=(P("noise", "dp"), P("dp", "noise")),
        out_specs=(P("noise", "dp"), P("noise"), P("dp")),
        check_vma=False,
    )
```

```python
import functools
import math

import jax
import jax.numpy as jnp
from jax import lax
from jax.experimental import pallas as pl
from jax.experimental.pallas import tpu as pltpu
from jax.sharding import PartitionSpec as P

ITERS = 3
EPSILON = 0.04
LOG2E = 1.0 / math.log(2.0)
MESH = pl.DeviceIdType.MESH
LANES = 128
TILE = 32
SIDE = 4
STRIPS = 2


def wrap(index, size):
    return lax.rem(index, size)


def spread_lanes(ref, row):
    return jnp.broadcast_to(ref[pl.ds(row, 1), :], (LANES, LANES)).T


def exchange(buf, send, recv, step, parts, me, size, peer_id, started):
    for k in range(1, size):
        peer = wrap(me + k, size)
        copy = pltpu.make_async_remote_copy(
            src_ref=buf.at[step, me, pl.ds(0, parts)],
            dst_ref=buf.at[step, me, pl.ds(0, parts)],
            send_sem=send.at[step, k],
            recv_sem=recv.at[step, me],
            device_id=peer_id(peer),
            device_id_type=MESH,
        )
        copy.start()
        started.append(copy)
    for k in range(1, size):
        peer = wrap(me + k, size)
        pltpu.make_async_remote_copy(
            src_ref=buf.at[step, peer, pl.ds(0, parts)],
            dst_ref=buf.at[step, peer, pl.ds(0, parts)],
            send_sem=send.at[step, k],
            recv_sem=recv.at[step, peer],
            device_id=peer_id(peer),
            device_id_type=MESH,
        ).wait_recv()


def combine(buf, step, size):
    top = buf[step, 0, 0]
    for s in range(1, size):
        top = jnp.maximum(top, buf[step, s, 0])
    total = buf[step, 0, 1] * jnp.exp2(buf[step, 0, 0] - top)
    for s in range(1, size):
        total = total + buf[step, s, 1] * jnp.exp2(buf[step, s, 0] - top)
    return top, total


def add_slots(buf, step, size):
    total = buf[step, 0, 0]
    for s in range(1, size):
        total = total + buf[step, s, 0]
    return total


def kernel(
    nsize, dsize, width,
    noise_ref, data_ref,
    targets, rows_out, cols_out,
    noise_all, data_all, scores, weights,
    shift, first, scale, part, colvec, rowpack, colpack, sqx, sqy,
    col_buf, row_buf, out_buf, own_buf, far_buf, near_buf, far_sum, near_sum,
    col_send, col_recv, row_send, row_recv,
    noise_send, noise_recv, data_send, data_recv, sum_send, sum_recv,
):
    rows, cols = scores.shape
    half = rows // 2
    n = lax.axis_index("noise")
    d = lax.axis_index("dp")
    x, z = d // SIDE, lax.rem(d, SIDE)
    y, core = n // 2, lax.rem(n, 2)
    kappa = LOG2E / EPSILON
    log_rows = math.log2(rows * nsize)
    log_cols = math.log2(cols * dsize)
    col_peer = lambda p: (p, d)
    row_peer = lambda p: (n, p)
    chunks = cols // LANES
    row_blocks = rows // LANES
    tiles = rows // TILE
    started = []

    barrier = pltpu.get_barrier_semaphore()
    for k in range(1, nsize):
        pl.semaphore_signal(barrier, inc=1, device_id=col_peer(wrap(n + k, nsize)), device_id_type=MESH)
    for k in range(1, dsize):
        pl.semaphore_signal(barrier, inc=1, device_id=row_peer(wrap(d + k, dsize)), device_id_type=MESH)
    pl.semaphore_wait(barrier, nsize + dsize - 2)

    def remote(src, dst, send, recv, to):
        return pltpu.make_async_remote_copy(
            src_ref=src, dst_ref=dst, send_sem=send, recv_sem=recv, device_id=to, device_id_type=MESH
        )

    def begin(copy):
        copy.start()
        started.append(copy)

    def lane(c):
        return slice(LANES * c, LANES * (c + 1))

    def place(h, f, s):
        dx, dz = (f, s) if h == 0 else (s, f)
        return wrap(x + dx + SIDE, SIDE) * SIDE + wrap(z + dz + SIDE, SIDE)

    def device(h, f, s):
        return (n, place(h, f, s))

    HOP = (1, -1)
    STEPS = (0, -1, 1, 2)

    def noise_copy(h, k, t, forward, slot, own=False):
        lo, size = h * half, half
        if forward:
            size = half // 2
            lo = lo + t * size
        at = pl.ds(lo, size)
        src = noise_ref.at[at] if own else noise_all.at[slot, at]
        to = device(h, HOP[t], 0) if k == 4 else device(h, 0, HOP[t])
        f = int(forward)
        return remote(src, noise_all.at[slot, at], noise_send.at[h, k, t, f], noise_recv.at[h, k, t, f], to)

    def noise_wait(h, k, t, forward):
        back = -2 * HOP[t] if forward else -HOP[t]
        slot = place(h, back, 0) if k == 4 else place(h, STEPS[k], back)
        noise_copy(h, k, t, forward, slot).wait_recv()
        return slot

    def data_copy(index, slot, lo, size, to, own=False):
        at = pl.ds(lo, size)
        src = data_ref.at[at] if own else data_all.at[slot, at]
        return remote(src, data_all.at[slot, at], data_send.at[index], data_recv.at[index], to)

    def along_y(step, c):
        return wrap(y + step + SIDE, SIDE) * 2 + c

    sibling = (n + 1 - 2 * core, d)
    other = 1 - core
    half_cols = cols // 2

    own = place(0, 0, 0)
    for t in (0, 1):
        for h in (0, 1):
            begin(noise_copy(h, 4, t, False, own, own=True))
        begin(data_copy(t, n, 0, cols, (along_y(HOP[t], core), d), own=True))
    begin(data_copy(2, n, 0, cols, sibling, own=True))
    for t in (0, 1):
        for h in (0, 1):
            begin(noise_copy(h, 0, t, False, own, own=True))

    noise_all[own] = noise_ref[...]
    data_all[n] = data_ref[...]
    scores[...] = jnp.zeros_like(scores)
    part[...] = jnp.zeros_like(part)

    for t in (0, 1):
        slot = along_y(-HOP[t], core)
        data_copy(t, slot, 0, cols, sibling).wait_recv()
        begin(data_copy(3 + t, slot, t * half_cols, half_cols, (along_y(HOP[t], core), d)))
        begin(data_copy(5 + t, slot, 0, cols, sibling))
    for h in (0, 1):
        for t in (0, 1):
            slot = noise_wait(h, 4, t, False)
            begin(noise_copy(h, 4, t, True, slot))
            for u in (0, 1):
                begin(noise_copy(h, 1 + t, u, False, slot))
    for h in (0, 1):
        for t in (0, 1):
            begin(noise_copy(h, 0, t, True, noise_wait(h, 0, t, False)))
    far = along_y(2, core)
    for t in (0, 1):
        data_copy(3 + t, far, t * half_cols, half_cols, sibling).wait_recv()
        begin(data_copy(7 + t, far, t * half_cols, half_cols, sibling))
    for h in (0, 1):
        for t in (0, 1):
            slot = noise_wait(h, 4, t, True)
        for u in (0, 1):
            begin(noise_copy(h, 3, u, False, slot))
    for h in (0, 1):
        for k in (1, 2):
            for t in (0, 1):
                begin(noise_copy(h, k, t, True, noise_wait(h, k, t, False)))
    data_copy(2, along_y(0, other), 0, cols, sibling).wait_recv()
    for t in (0, 1):
        data_copy(5 + t, along_y(-HOP[t], other), 0, cols, sibling).wait_recv()
        data_copy(7 + t, along_y(2, other), t * half_cols, half_cols, sibling).wait_recv()

    def squares(block):
        value = block.astype(jnp.float32)
        return value * value

    def units(h, rel, lo, hi):
        pair = z // 2 if rel == 0 else 1 - z // 2
        at = pl.ds(h * half, half)

        def unit(i, carry):
            if hi - lo == 1:
                step = STEPS[lo]
            else:
                step = i + i // 2
            q = wrap(x + step + SIDE, SIDE) * 2 + pair
            left = noise_all[2 * q, at, :]
            right = noise_all[2 * q + 1, at, :]
            both = jnp.concatenate([left, right], axis=1)

            def column(m, carry):
                cut = pl.ds(pl.multiple_of(m * 256, 256), 256)
                scores[at, cut] += lax.dot_general(
                    both, data_all[q, cut, :], (((1,), (1,)), ((), ())), preferred_element_type=jnp.float32
                )
                return carry

            lax.fori_loop(0, cols // 256, column, 0)

            def norm(r, carry):
                cut = pl.ds(pl.multiple_of(h * half + r * 64, 64), 64)
                part[cut, :] += squares(noise_all[2 * q, cut, :]) + squares(noise_all[2 * q + 1, cut, :])
                return carry

            lax.fori_loop(0, half // 64, norm, 0)
            return carry

        lax.fori_loop(lo, hi, unit, 0)

    def data_norm(r, carry):
        cut = pl.ds(pl.multiple_of(r * 64, 64), 64)
        total = jnp.zeros((64, LANES), jnp.float32)
        for q in range(nsize):
            total = total + squares(data_all[q, cut, lane(0)]) + squares(data_all[q, cut, lane(1)])
        first[cut, :] = total
        return carry

    lax.fori_loop(0, cols // 64, data_norm, 0)
    for c in range(chunks):
        sqy[pl.ds(c, 1), :] = jnp.sum(first[pl.ds(c * LANES, LANES), :].T, axis=0, keepdims=True)
    units(0, 0, 0, 3)
    units(1, 0, 0, 3)
    for h in (0, 1):
        for t in (0, 1):
            begin(noise_copy(h, 3, t, True, noise_wait(h, 3, t, False)))
    units(1, 1, 0, 3)
    units(0, 0, 3, 4)
    for k in (0, 1, 2):
        for h in (0, 1):
            for t in (0, 1):
                noise_wait(h, k, t, True)
    units(0, 1, 0, 3)
    units(1, 0, 3, 4)
    for h in (0, 1):
        for t in (0, 1):
            noise_wait(h, 3, t, True)
    units(0, 1, 3, 4)
    units(1, 1, 3, 4)
    for b in range(row_blocks):
        sqx[pl.ds(b, 1), :] = jnp.sum(part[pl.ds(b * LANES, LANES), :].T, axis=0, keepdims=True)

    def fold(block, op):
        out = block[0:8]
        for r in range(1, TILE // 8):
            out = op(out, block[8 * r:8 * r + 8])
        return out

    def spread_cols():
        for c in range(chunks):
            colvec[:, lane(c)] = jnp.broadcast_to(colpack[pl.ds(c, 1), :], (8, LANES))

    factor = 2.0 * kappa / width
    for b in range(row_blocks):
        shift[pl.ds(b * LANES, LANES), :] = spread_lanes(sqx, b) * (-kappa / width)

    zero = tuple(jnp.full((8, LANES), -jnp.inf, jnp.float32) for _ in range(chunks))

    def top_step(t, accs):
        at = pl.ds(pl.multiple_of(t * TILE, TILE), TILE)
        add = shift[at, :]
        out = []
        for c in range(chunks):
            value = scores[at, lane(c)] * factor
            scores[at, lane(c)] = value
            out.append(jnp.maximum(accs[c], fold(value + add, jnp.maximum)))
        return tuple(out)

    tops = lax.fori_loop(0, tiles, top_step, zero)
    tops = tuple(jnp.max(a, axis=0, keepdims=True) for a in tops)
    for c in range(chunks):
        col_buf[0, n, 0, pl.ds(c, 1), :] = tops[c]
        colvec[:, lane(c)] = jnp.broadcast_to(tops[c], (8, LANES))

    zeros = tuple(jnp.zeros((8, LANES), jnp.float32) for _ in range(chunks))

    def tall(ref, c):
        return jnp.concatenate([ref[:, lane(c)]] * (TILE // 8), axis=0)

    def exp_step(t, accs):
        at = pl.ds(pl.multiple_of(t * TILE, TILE), TILE)
        add = shift[at, :]
        return tuple(
            accs[c] + fold(jnp.exp2(scores[at, lane(c)] + add - tall(colvec, c)), jnp.add)
            for c in range(chunks)
        )

    sums = lax.fori_loop(0, tiles, exp_step, zeros)
    for c in range(chunks):
        col_buf[0, n, 1, pl.ds(c, 1), :] = jnp.sum(sums[c], axis=0, keepdims=True)
    exchange(col_buf, col_send, col_recv, 0, 2, n, nsize, col_peer, started)
    top, total = combine(col_buf, 0, nsize)
    col_pot = -log_cols - top - jnp.log(total) * LOG2E
    colpack[...] = col_pot
    spread_cols()

    def row_step(t, carry):
        at = pl.ds(pl.multiple_of(t * TILE, TILE), TILE)
        values = [scores[at, lane(c)] + tall(colvec, c) for c in range(chunks)]
        top = values[0]
        for c in range(1, chunks):
            top = jnp.maximum(top, values[c])
        top = jnp.broadcast_to(jnp.max(top, axis=1, keepdims=True), (TILE, LANES))
        first[at, :] = top
        total = None
        for c in range(chunks):
            value = jnp.exp2(values[c] - top)
            scores[at, lane(c)] = value
            total = value if total is None else total + value
        part[at, :] = total
        return carry

    lax.fori_loop(0, tiles, row_step, 0)
    for b in range(row_blocks):
        at = pl.ds(b * LANES, LANES)
        row_buf[0, d, 0, pl.ds(b, 1), :] = first[at, :].T[0:1]
        row_buf[0, d, 1, pl.ds(b, 1), :] = jnp.sum(part[at, :].T, axis=0, keepdims=True)
    local_top = row_buf[0, d, 0]
    exchange(row_buf, row_send, row_recv, 0, 2, d, dsize, row_peer, started)
    top, total = combine(row_buf, 0, dsize)
    row_lse = top + jnp.log(total) * LOG2E
    base = jnp.exp2(local_top - row_lse)

    def spread_rows(value):
        rowpack[...] = value
        for b in range(row_blocks):
            scale[pl.ds(b * LANES, LANES), :] = spread_lanes(rowpack, b)

    spread_rows(base)

    def col_step(t, accs):
        at = pl.ds(pl.multiple_of(t * TILE, TILE), TILE)
        mul = scale[at, :]
        return tuple(accs[c] + fold(scores[at, lane(c)] * mul, jnp.add) for c in range(chunks))

    def sum_step(t, carry):
        at = pl.ds(pl.multiple_of(t * TILE, TILE), TILE)
        total = scores[at, lane(0)] * tall(colvec, 0)
        for c in range(1, chunks):
            total = total + scores[at, lane(c)] * tall(colvec, c)
        part[at, :] = total
        return carry

    for step in range(1, ITERS):
        sums = lax.fori_loop(0, tiles, col_step, zeros)
        for c in range(chunks):
            col_buf[step, n, 0, pl.ds(c, 1), :] = jnp.sum(sums[c], axis=0, keepdims=True)
        exchange(col_buf, col_send, col_recv, step, 1, n, nsize, col_peer, started)
        ratio = 1.0 / add_slots(col_buf, step, nsize)
        colpack[...] = ratio
        spread_cols()
        lax.fori_loop(0, tiles, sum_step, 0)
        for b in range(row_blocks):
            at = pl.ds(b * LANES, LANES)
            row_buf[step, d, 0, pl.ds(b, 1), :] = jnp.sum(part[at, :].T, axis=0, keepdims=True)
        row_buf[step, d, 0] = row_buf[step, d, 0] * base
        exchange(row_buf, row_send, row_recv, step, 1, d, dsize, row_peer, started)
        total = add_slots(row_buf, step, dsize)
        spread_rows(base / total)

    rows_out[...] = -(log_rows + row_lse + jnp.log(total) * LOG2E) / kappa + sqx[...] / width
    cols_out[...] = (col_pot + jnp.log(ratio) * LOG2E + (log_rows - log_cols)) / kappa + sqy[...] / width

    def weight_step(t, carry):
        at = pl.ds(pl.multiple_of(t * TILE, TILE), TILE)
        mul = scale[at, :]
        for c in range(chunks):
            weights[at, lane(c)] = (scores[at, lane(c)] * tall(colvec, c) * mul).astype(jnp.bfloat16)
        return carry

    lax.fori_loop(0, tiles, weight_step, 0)

    strip = half // STRIPS

    def product(h, s, f, i):
        at = pl.ds(h * half + s * strip, strip)
        if h == 0:
            block = data_all[f * 2 + i // 2]
        else:
            cut = pl.ds(pl.multiple_of(lax.rem(f, 2) * LANES, LANES), LANES)
            block = jnp.concatenate(
                [data_all[(i + e) * 2 + f // 2, :, cut] for e in (0, 1)], axis=1
            )
        return jnp.dot(weights[at, :], block, preferred_element_type=jnp.float32)

    def first_place(h, step):
        return wrap((x if h == 0 else z) + step + SIDE, SIDE)

    def second_place(h, step):
        return wrap((z if h == 0 else x) + step + SIDE, SIDE)

    def sum_copy(h, s, t, kind, src, dst):
        to = device(h, HOP[t], 0) if kind < 3 else device(h, 0, HOP[t])
        return remote(src, dst, sum_send.at[h, s, t, kind], sum_recv.at[h, s, t, kind], to)

    def far_part(t):
        return pl.ds(2 * t, 2)

    def near_part(t):
        return pl.ds(2 - 2 * t, 2)

    def far_copy(h, s, t):
        return sum_copy(h, s, t, 0, out_buf.at[h, s, 2, far_part(t)], far_buf.at[h, s, t])

    def direct_copy(h, s, t):
        return sum_copy(h, s, t, 1, out_buf.at[h, s, t, near_part(t)], near_buf.at[h, s, t, near_part(t)])

    def added_copy(h, s, t):
        return sum_copy(h, s, t, 2, out_buf.at[h, s, t, far_part(t)], near_buf.at[h, s, t, far_part(t)])

    def store(ref, h, s, t, i, value):
        for e in (0, 1):
            ref[h, s, t, i + e] = value[:, lane(e)].astype(jnp.bfloat16)

    for s in range(STRIPS):
        for h in (0, 1):
            f = first_place(h, 2)
            for t in (0, 1):
                store(out_buf, h, s, 2, 2 * t, product(h, s, f, 2 * t))
                begin(far_copy(h, s, t))
        for h in (0, 1):
            for t in (0, 1):
                store(out_buf, h, s, t, 2 - 2 * t, product(h, s, first_place(h, HOP[t]), 2 - 2 * t))
                begin(direct_copy(h, s, t))
        for h in (0, 1):
            for i in (0, 2):
                value = product(h, s, first_place(h, 0), i)
                for e in (0, 1):
                    own_buf[h, s, i + e] = value[:, lane(e)]
        for h in (0, 1):
            for t in (0, 1):
                value = product(h, s, first_place(h, HOP[t]), 2 * t)
                far_copy(h, s, t).wait_recv()
                for e in (0, 1):
                    out_buf[h, s, t, 2 * t + e] = (
                        value[:, lane(e)] + far_buf[h, s, t, e].astype(jnp.float32)
                    ).astype(jnp.bfloat16)
                begin(added_copy(h, s, t))

    low = strip // 2

    def far_rows(t):
        return pl.ds(t * low, low)

    def near_rows(t):
        return pl.ds((1 - t) * low, low)

    def far_copy2(h, s, t):
        return sum_copy(h, s, t, 3, own_buf.at[h, s, second_place(h, 2), far_rows(t)], far_sum.at[h, s, t])

    def direct_copy2(h, s, t):
        return sum_copy(
            h, s, t, 4, own_buf.at[h, s, second_place(h, HOP[t]), near_rows(t)], near_sum.at[h, s, t, near_rows(t)]
        )

    def added_copy2(h, s, t):
        return sum_copy(
            h, s, t, 5, own_buf.at[h, s, second_place(h, HOP[t]), far_rows(t)], near_sum.at[h, s, t, far_rows(t)]
        )

    for s in range(STRIPS):
        for h in (0, 1):
            for t in (0, 1):
                direct_copy(h, s, t).wait_recv()
                added_copy(h, s, t).wait_recv()
            for step in (2, 1, -1, 0):
                i = second_place(h, step)
                own_buf[h, s, i] = (
                    own_buf[h, s, i]
                    + near_buf[h, s, 0, i].astype(jnp.float32)
                    + near_buf[h, s, 1, i].astype(jnp.float32)
                )
            for t in (0, 1):
                begin(far_copy2(h, s, t))
            for t in (0, 1):
                begin(direct_copy2(h, s, t))
    for s in range(STRIPS):
        for h in (0, 1):
            for t in (0, 1):
                far_copy2(h, s, t).wait_recv()
                i = second_place(h, HOP[t])
                own_buf[h, s, i, far_rows(t)] = own_buf[h, s, i, far_rows(t)] + far_sum[h, s, t]
                begin(added_copy2(h, s, t))
    for s in range(STRIPS):
        for h in (0, 1):
            for t in (0, 1):
                direct_copy2(h, s, t).wait_recv()
                added_copy2(h, s, t).wait_recv()
            targets[pl.ds(h * half + s * strip, strip), :] = (
                own_buf[h, s, second_place(h, 0)] + near_sum[h, s, 0] + near_sum[h, s, 1]
            )
    for copy in started:
        copy.wait_send()


def shards(noise_latents, data_latents):
    nsize = lax.axis_size("noise")
    dsize = lax.axis_size("dp")
    rows, piece = noise_latents.shape
    cols = data_latents.shape[0]
    vmem = pl.BlockSpec(memory_space=pltpu.VMEM)
    f32, bf16 = jnp.float32, jnp.bfloat16
    strip = rows // 2 // STRIPS
    targets, rows_pot, cols_pot = pl.pallas_call(
        functools.partial(kernel, nsize, dsize, piece * dsize),
        out_shape=(
            jax.ShapeDtypeStruct((rows, piece), f32),
            jax.ShapeDtypeStruct((rows // LANES, LANES), f32),
            jax.ShapeDtypeStruct((cols // LANES, LANES), f32),
        ),
        in_specs=[vmem] * 2,
        out_specs=(vmem,) * 3,
        scratch_shapes=[
            pltpu.VMEM((dsize, rows, piece), bf16),
            pltpu.VMEM((nsize,) + data_latents.shape, bf16),
            pltpu.VMEM((rows, cols), f32),
            pltpu.VMEM((rows, cols), bf16),
            pltpu.VMEM((rows, LANES), f32),
            pltpu.VMEM((rows, LANES), f32),
            pltpu.VMEM((rows, LANES), f32),
            pltpu.VMEM((rows, LANES), f32),
            pltpu.VMEM((8, cols), f32),
            pltpu.VMEM((rows // LANES, LANES), f32),
            pltpu.VMEM((cols // LANES, LANES), f32),
            pltpu.VMEM((rows // LANES, LANES), f32),
            pltpu.VMEM((cols // LANES, LANES), f32),
            pltpu.VMEM((ITERS, nsize, 2, cols // LANES, LANES), f32),
            pltpu.VMEM((ITERS, dsize, 2, rows // LANES, LANES), f32),
            pltpu.VMEM((2, STRIPS, 3, SIDE, strip, LANES), bf16),
            pltpu.VMEM((2, STRIPS, SIDE, strip, LANES), f32),
            pltpu.VMEM((2, STRIPS, 2, 2, strip, LANES), bf16),
            pltpu.VMEM((2, STRIPS, 2, SIDE, strip, LANES), bf16),
            pltpu.VMEM((2, STRIPS, 2, strip // 2, LANES), f32),
            pltpu.VMEM((2, STRIPS, 2, strip, LANES), f32),
            pltpu.SemaphoreType.DMA((ITERS, nsize)),
            pltpu.SemaphoreType.DMA((ITERS, nsize)),
            pltpu.SemaphoreType.DMA((ITERS, dsize)),
            pltpu.SemaphoreType.DMA((ITERS, dsize)),
            pltpu.SemaphoreType.DMA((2, 5, 2, 2)),
            pltpu.SemaphoreType.DMA((2, 5, 2, 2)),
            pltpu.SemaphoreType.DMA((9,)),
            pltpu.SemaphoreType.DMA((9,)),
            pltpu.SemaphoreType.DMA((2, STRIPS, 2, 6)),
            pltpu.SemaphoreType.DMA((2, STRIPS, 2, 6)),
        ],
        compiler_params=pltpu.CompilerParams(
            collective_id=0, has_side_effects=True, vmem_limit_bytes=60 * 2**20
        ),
    )(noise_latents, data_latents)
    return targets, rows_pot.reshape(rows), cols_pot.reshape(cols)


def solution(mesh):
    return jax.shard_map(
        shards,
        mesh=mesh,
        in_specs=(P("noise", "dp"), P("dp", "noise")),
        out_specs=(P("noise", "dp"), P("noise"), P("dp")),
        check_vma=False,
    )
```

```python
import functools
import math

import jax
import jax.numpy as jnp
from jax import lax
from jax.experimental import pallas as pl
from jax.experimental.pallas import tpu as pltpu
from jax.sharding import PartitionSpec as P

ITERS = 3
EPSILON = 0.04
LOG2E = 1.0 / math.log(2.0)
MESH = pl.DeviceIdType.MESH
LANES = 128
TILE = 32
SIDE = 4
STRIPS = 4


def wrap(index, size):
    return lax.rem(index, size)


def spread_lanes(ref, row):
    return jnp.broadcast_to(ref[pl.ds(row, 1), :], (LANES, LANES)).T


def exchange(buf, send, recv, step, parts, me, size, peer_id, started):
    for k in range(1, size):
        peer = wrap(me + k, size)
        copy = pltpu.make_async_remote_copy(
            src_ref=buf.at[step, me, pl.ds(0, parts)],
            dst_ref=buf.at[step, me, pl.ds(0, parts)],
            send_sem=send.at[step, k],
            recv_sem=recv.at[step, me],
            device_id=peer_id(peer),
            device_id_type=MESH,
        )
        copy.start()
        started.append(copy)
    for k in range(1, size):
        peer = wrap(me + k, size)
        pltpu.make_async_remote_copy(
            src_ref=buf.at[step, peer, pl.ds(0, parts)],
            dst_ref=buf.at[step, peer, pl.ds(0, parts)],
            send_sem=send.at[step, k],
            recv_sem=recv.at[step, peer],
            device_id=peer_id(peer),
            device_id_type=MESH,
        ).wait_recv()


def combine(buf, step, size):
    top = buf[step, 0, 0]
    for s in range(1, size):
        top = jnp.maximum(top, buf[step, s, 0])
    total = buf[step, 0, 1] * jnp.exp2(buf[step, 0, 0] - top)
    for s in range(1, size):
        total = total + buf[step, s, 1] * jnp.exp2(buf[step, s, 0] - top)
    return top, total


def add_slots(buf, step, size):
    total = buf[step, 0, 0]
    for s in range(1, size):
        total = total + buf[step, s, 0]
    return total


def kernel(
    rsize, csize, width,
    noise_ref, data_ref,
    targets, rows_out, cols_out,
    noise_all, data_all, scores, weights,
    shift, first, scale, part, data_part, colvec, rowpack, colpack, sqx, sqy, swap,
    col_buf, row_buf, out_buf, own_buf, far_buf, near_buf, in_sum,
    col_send, col_recv, row_send, row_recv, swap_send, swap_recv,
    cross_send, cross_recv, noise_send, noise_recv, data_send, data_recv,
    sum_send, sum_recv, in_send, in_recv,
):
    rows, cols = scores.shape
    n = lax.axis_index("noise")
    d = lax.axis_index("dp")
    x, z = d // SIDE, lax.rem(d, SIDE)
    y, core = n // 2, lax.rem(n, 2)
    kind = lax.rem(x, 2)
    pair = x // 2
    home = core == kind
    kappa = LOG2E / EPSILON
    log_rows = math.log2(rows * csize)
    log_cols = math.log2(cols * rsize)
    chunks = cols // LANES
    row_blocks = rows // LANES
    tiles = rows // TILE
    started = []

    def around(value):
        return lax.rem(value + SIDE, SIDE)

    def device(xi, yi, zi, ci):
        return (yi * 2 + ci, xi * SIDE + zi)

    me_row = pair * SIDE + z
    me_col = y * 4 + kind * 2 + core

    def row_peer(p):
        return device(p // SIDE * 2 + kind, y, lax.rem(p, SIDE), core)

    def col_peer(p):
        return device(pair * 2 + lax.rem(p // 2, 2), p // 4, z, lax.rem(p, 2))

    sibling = device(x, y, z, 1 - core)
    partner = x + 1 - 2 * kind
    outside = around(x - 1 + 2 * kind)
    opposite = around(x + 2)

    barrier = pltpu.get_barrier_semaphore()
    greeted = [row_peer(wrap(me_row + k, rsize)) for k in range(1, rsize)]
    greeted += [col_peer(wrap(me_col + k, csize)) for k in range(1, csize)]
    greeted += [device(outside, y, z, 0), device(outside, y, z, 1), device(opposite, y, z, 1 - core)]
    for to in greeted:
        pl.semaphore_signal(barrier, inc=1, device_id=to, device_id_type=MESH)
    pl.semaphore_wait(barrier, len(greeted))

    def remote(src, dst, send, recv, to):
        return pltpu.make_async_remote_copy(
            src_ref=src, dst_ref=dst, send_sem=send, recv_sem=recv, device_id=to, device_id_type=MESH
        )

    def begin(copy):
        copy.start()
        started.append(copy)

    def lane(c):
        return slice(LANES * c, LANES * (c + 1))

    HOP = (1, -1)
    ORDER = (0, 1, 3, 2)
    own = x * SIDE + z

    def cross_copy(i, half, rel, to):
        return remote(
            noise_ref.at[pl.ds(half * rows, rows)], noise_all.at[own],
            cross_send.at[i], cross_recv.at[rel], to,
        )

    def cross_wait(rel):
        slot = around(x + rel) * SIDE + z
        remote(
            noise_ref.at[pl.ds(0, rows)], noise_all.at[slot], cross_send.at[0], cross_recv.at[rel], sibling
        ).wait_recv()

    there = jnp.where(home, opposite, around(x + 1))
    back = jnp.where(home, x, around(x - 1))
    far_rel = jnp.where(home, 2, 3)
    near_rel = jnp.where(home, 0, 1)
    last = cross_copy(3, core, 1, device(back, y, z, core))

    def noise_copy(rel, t, forward, slot):
        at = pl.ds(t * (rows // 2), rows // 2) if forward else pl.ds(0, rows)
        f = int(forward)
        return remote(
            noise_all.at[slot, at], noise_all.at[slot, at],
            noise_send.at[rel, t, f], noise_recv.at[rel, t, f], device(x, y, around(z + HOP[t]), core),
        )

    def noise_wait(rel, t, forward):
        slot = around(x + rel) * SIDE + around(z - HOP[t] * (2 if forward else 1))
        noise_copy(rel, t, forward, slot).wait_recv()
        return slot

    def data_copy(r, index, where, lo, size, to, own=False):
        at = pl.ds(lo, size)
        block = kind if r == 0 else 1 - kind
        dst = data_all.at[block, where, at]
        return remote(data_ref.at[at] if own else dst, dst, data_send.at[r, index], data_recv.at[r, index], to)

    half_cols = cols // 4
    full_cols = cols // 2

    def along_y(step, c):
        return around(y + step) * 2 + c

    def data_wait(r, index, where, lo, size):
        data_copy(r, index, where, lo, size, sibling).wait_recv()

    for t in (0, 1):
        begin(data_copy(0, t, n, 0, full_cols, device(x, around(y + HOP[t]), z, core), own=True))
    begin(remote(
        data_ref.at[pl.ds(0, full_cols)], data_all.at[kind, n],
        data_send.at[1, 9], data_recv.at[1, 9], device(partner, y, z, core),
    ))
    begin(cross_copy(2, 1 - core, near_rel, device(back, y, z, 1 - core)))

    @pl.when(home)
    def _():
        noise_all[own] = noise_ref[pl.ds(pl.multiple_of(core * rows, rows), rows), :]

    @pl.when(jnp.logical_not(home))
    def _():
        last.start()

    begin(cross_copy(0, 0, far_rel, device(there, y, z, 0)))
    begin(cross_copy(1, 1, far_rel, device(there, y, z, 1)))
    begin(data_copy(0, 4, n, 0, full_cols, sibling, own=True))

    data_all[kind, n] = data_ref[...]

    @pl.when(jnp.logical_not(home))
    def _():
        cross_wait(0)

    for t in (0, 1):
        begin(noise_copy(0, t, False, own))
    scores[...] = jnp.zeros_like(scores)
    part[...] = jnp.zeros_like(part)
    data_part[...] = jnp.zeros_like(data_part)
    data_wait(1, 9, n, 0, full_cols)
    for t in (0, 1):
        begin(data_copy(1, t, n, 0, full_cols, device(x, around(y + HOP[t]), z, core)))
    begin(data_copy(1, 4, n, 0, full_cols, sibling))
    for rel in ORDER[1:]:
        cross_wait(rel)
        for t in (0, 1):
            begin(noise_copy(rel, t, False, around(x + rel) * SIDE + z))
    for r in (0, 1):
        for t in (0, 1):
            where = along_y(-HOP[t], core)
            data_wait(r, t, where, 0, full_cols)
            begin(data_copy(r, 2 + t, where, t * half_cols, half_cols, device(x, around(y + HOP[t]), z, core)))
            begin(data_copy(r, 5 + t, where, 0, full_cols, sibling))
    by_data = [around(y - x + step) for step in ORDER]
    for rel in by_data:
        for t in (0, 1):
            begin(noise_copy(rel, t, True, noise_wait(rel, t, False)))
    for r in (0, 1):
        data_wait(r, 4, along_y(0, 1 - core), 0, full_cols)
        for t in (0, 1):
            data_wait(r, 5 + t, along_y(-HOP[t], 1 - core), 0, full_cols)

    def squares(block):
        value = block.astype(jnp.float32)
        return value * value

    def chunk(q):
        both = jnp.concatenate([noise_all[2 * q], noise_all[2 * q + 1]], axis=1)

        def column(m, carry):
            cut = pl.ds(pl.multiple_of(m * 256, 256), 256)
            piece = data_all[m // 4, q, pl.ds(pl.multiple_of(lax.rem(m, 4) * 256, 256), 256), :]
            scores[:, cut] += lax.dot_general(
                both, piece, (((1,), (1,)), ((), ())), preferred_element_type=jnp.float32
            )
            data_part[cut, :] += squares(piece[:, :LANES]) + squares(piece[:, LANES:])
            return carry

        lax.fori_loop(0, cols // 256, column, 0)

        def norm(r, carry):
            cut = pl.ds(pl.multiple_of(r * 64, 64), 64)
            part[cut, :] += squares(noise_all[2 * q, cut, :]) + squares(noise_all[2 * q + 1, cut, :])
            return carry

        lax.fori_loop(0, rows // 64, norm, 0)

    mine = z // 2

    def early(i, carry):
        chunk(around(y + i + i // 2) * 2 + mine)
        return carry

    lax.fori_loop(0, 3, early, 0)

    def late(step, rel):
        for t in (0, 1):
            noise_wait(rel, t, True)
        chunk(around(y + step) * 2 + 1 - mine)

    late(0, by_data[0])
    for r in (0, 1):
        for t in (0, 1):
            where = along_y(2, core)
            data_wait(r, 2 + t, where, t * half_cols, half_cols)
            begin(data_copy(r, 7 + t, where, t * half_cols, half_cols, sibling))
        if r == 0:
            late(1, by_data[1])
            late(3, by_data[2])
    for r in (0, 1):
        for t in (0, 1):
            data_wait(r, 7 + t, along_y(2, 1 - core), t * half_cols, half_cols)
    for t in (0, 1):
        noise_wait(by_data[3], t, True)

    def final(i, carry):
        chunk(around(y + 2) * 2 + lax.rem(mine + i, 2))
        return carry

    lax.fori_loop(0, 2, final, 0)
    for b in range(row_blocks):
        sqx[pl.ds(b, 1), :] = jnp.sum(part[pl.ds(b * LANES, LANES), :].T, axis=0, keepdims=True)
    for c in range(chunks):
        sqy[pl.ds(c, 1), :] = jnp.sum(data_part[pl.ds(c * LANES, LANES), :].T, axis=0, keepdims=True)

    def fold(block, op):
        out = block[0:8]
        for r in range(1, TILE // 8):
            out = op(out, block[8 * r:8 * r + 8])
        return out

    def spread_cols():
        for c in range(chunks):
            colvec[:, lane(c)] = jnp.broadcast_to(colpack[pl.ds(c, 1), :], (8, LANES))

    factor = 2.0 * kappa / width
    for b in range(row_blocks):
        shift[pl.ds(b * LANES, LANES), :] = spread_lanes(sqx, b) * (-kappa / width)

    zero = tuple(jnp.full((8, LANES), -jnp.inf, jnp.float32) for _ in range(chunks))

    def top_step(t, accs):
        at = pl.ds(pl.multiple_of(t * TILE, TILE), TILE)
        add = shift[at, :]
        out = []
        for c in range(chunks):
            value = scores[at, lane(c)] * factor
            scores[at, lane(c)] = value
            out.append(jnp.maximum(accs[c], fold(value + add, jnp.maximum)))
        return tuple(out)

    tops = lax.fori_loop(0, tiles, top_step, zero)
    tops = tuple(jnp.max(a, axis=0, keepdims=True) for a in tops)
    for c in range(chunks):
        col_buf[0, me_col, 0, pl.ds(c, 1), :] = tops[c]
        colvec[:, lane(c)] = jnp.broadcast_to(tops[c], (8, LANES))

    zeros = tuple(jnp.zeros((8, LANES), jnp.float32) for _ in range(chunks))

    def tall(ref, c):
        return jnp.concatenate([ref[:, lane(c)]] * (TILE // 8), axis=0)

    def exp_step(t, accs):
        at = pl.ds(pl.multiple_of(t * TILE, TILE), TILE)
        add = shift[at, :]
        return tuple(
            accs[c] + fold(jnp.exp2(scores[at, lane(c)] + add - tall(colvec, c)), jnp.add)
            for c in range(chunks)
        )

    sums = lax.fori_loop(0, tiles, exp_step, zeros)
    for c in range(chunks):
        col_buf[0, me_col, 1, pl.ds(c, 1), :] = jnp.sum(sums[c], axis=0, keepdims=True)
    exchange(col_buf, col_send, col_recv, 0, 2, me_col, csize, col_peer, started)
    top, total = combine(col_buf, 0, csize)
    col_pot = -log_cols - top - jnp.log(total) * LOG2E
    colpack[...] = col_pot
    spread_cols()

    def row_step(t, carry):
        at = pl.ds(pl.multiple_of(t * TILE, TILE), TILE)
        top = scores[at, lane(0)] + tall(colvec, 0)
        for c in range(1, chunks):
            top = jnp.maximum(top, scores[at, lane(c)] + tall(colvec, c))
        top = jnp.broadcast_to(jnp.max(top, axis=1, keepdims=True), (TILE, LANES))
        first[at, :] = top
        total = None
        for c in range(chunks):
            value = jnp.exp2(scores[at, lane(c)] + tall(colvec, c) - top)
            scores[at, lane(c)] = value
            total = value if total is None else total + value
        part[at, :] = total
        return carry

    lax.fori_loop(0, tiles, row_step, 0)
    for b in range(row_blocks):
        at = pl.ds(b * LANES, LANES)
        row_buf[0, me_row, 0, pl.ds(b, 1), :] = first[at, :].T[0:1]
        row_buf[0, me_row, 1, pl.ds(b, 1), :] = jnp.sum(part[at, :].T, axis=0, keepdims=True)
    local_top = row_buf[0, me_row, 0]
    exchange(row_buf, row_send, row_recv, 0, 2, me_row, rsize, row_peer, started)
    top, total = combine(row_buf, 0, rsize)
    row_lse = top + jnp.log(total) * LOG2E
    base = jnp.exp2(local_top - row_lse)

    def spread_rows(value):
        rowpack[...] = value
        for b in range(row_blocks):
            scale[pl.ds(b * LANES, LANES), :] = spread_lanes(rowpack, b)

    spread_rows(base)

    def col_step(t, accs):
        at = pl.ds(pl.multiple_of(t * TILE, TILE), TILE)
        mul = scale[at, :]
        return tuple(accs[c] + fold(scores[at, lane(c)] * mul, jnp.add) for c in range(chunks))

    def sum_step(t, carry):
        at = pl.ds(pl.multiple_of(t * TILE, TILE), TILE)
        total = scores[at, lane(0)] * tall(colvec, 0)
        for c in range(1, chunks):
            total = total + scores[at, lane(c)] * tall(colvec, c)
        part[at, :] = total
        return carry

    for step in range(1, ITERS):
        sums = lax.fori_loop(0, tiles, col_step, zeros)
        for c in range(chunks):
            col_buf[step, me_col, 0, pl.ds(c, 1), :] = jnp.sum(sums[c], axis=0, keepdims=True)
        exchange(col_buf, col_send, col_recv, step, 1, me_col, csize, col_peer, started)
        ratio = 1.0 / add_slots(col_buf, step, csize)
        colpack[...] = ratio
        spread_cols()
        lax.fori_loop(0, tiles, sum_step, 0)
        for b in range(row_blocks):
            at = pl.ds(b * LANES, LANES)
            row_buf[step, me_row, 0, pl.ds(b, 1), :] = jnp.sum(part[at, :].T, axis=0, keepdims=True)
        row_buf[step, me_row, 0] = row_buf[step, me_row, 0] * base
        exchange(row_buf, row_send, row_recv, step, 1, me_row, rsize, row_peer, started)
        total = add_slots(row_buf, step, rsize)
        spread_rows(base / total)

    cols_pot = (col_pot + jnp.log(ratio) * LOG2E + (log_rows - log_cols)) / kappa + sqy[...] / width
    colpack[...] = cols_pot
    cols_out[...] = colpack[pl.ds(pl.multiple_of(kind * 8, 8), 8), :]
    swap[0] = -(log_rows + row_lse + jnp.log(total) * LOG2E) / kappa + sqx[...] / width

    def swap_copy(i, to):
        return remote(swap.at[0], swap.at[i], swap_send.at[i], swap_recv.at[i], to)

    begin(swap_copy(1, sibling))
    for i in (0, 1):
        begin(remote(
            swap.at[0], swap.at[2 + core], swap_send.at[2 + i], swap_recv.at[2 + core], device(partner, y, z, i)
        ))

    def weight_step(t, carry):
        at = pl.ds(pl.multiple_of(t * TILE, TILE), TILE)
        mul = scale[at, :]
        for c in range(chunks):
            weights[at, lane(c)] = (scores[at, lane(c)] * tall(colvec, c) * mul).astype(jnp.bfloat16)
        return carry

    lax.fori_loop(0, tiles, weight_step, 0)

    strip = rows // STRIPS

    def product(s, to_z, i):
        at = pl.ds(pl.multiple_of(s * strip, strip), strip)
        cut = pl.ds(pl.multiple_of(lax.rem(to_z, 2) * LANES, LANES), LANES)
        total = None
        for k in (0, 1):
            block = jnp.concatenate([data_all[k, (i + e) * 2 + to_z // 2, :, cut] for e in (0, 1)], axis=1)
            value = jnp.dot(
                weights[at, k * full_cols:(k + 1) * full_cols], block, preferred_element_type=jnp.float32
            )
            total = value if total is None else total + value
        return total

    def sum_copy(s, t, index, src, dst):
        to = device(x, y, around(z + HOP[t]), core)
        return remote(src, dst, sum_send.at[s, t, index], sum_recv.at[s, t, index], to)

    def far_part(t):
        return pl.ds(2 * t, 2)

    def near_part(t):
        return pl.ds(2 - 2 * t, 2)

    def far_copy(s, t):
        return sum_copy(s, t, 0, out_buf.at[s, 2, far_part(t)], far_buf.at[s, t])

    def direct_copy(s, t):
        return sum_copy(s, t, 1, out_buf.at[s, t, near_part(t)], near_buf.at[s, t, near_part(t)])

    def added_copy(s, t):
        return sum_copy(s, t, 2, out_buf.at[s, t, far_part(t)], near_buf.at[s, t, far_part(t)])

    def in_copy(s, g, a, index, rel, to):
        at = pl.ds(pl.multiple_of(s * strip, strip), strip)
        return remote(
            own_buf.at[s, around(x + rel)], in_sum.at[g, a, at], in_send.at[s, index], in_recv.at[s, g, a], to
        )

    def in_copies(s):
        return [
            in_copy(s, 1, core, 2, 2, device(opposite, y, z, kind)),
            in_copy(s, 0, core, 0, 1, device(around(x + 1), y, z, kind)),
            in_copy(s, 1, core, 1, -1, device(around(x - 1), y, z, kind)),
        ]

    def stay_copy(s):
        return in_copy(s, 0, core, 3, 0, sibling)

    def add_strip(s):
        for t in (0, 1):
            direct_copy(s, t).wait_recv()
            added_copy(s, t).wait_recv()
        for rel in (2, 1, 3, 0):
            i = around(x + rel)
            own_buf[s, i] = (
                own_buf[s, i] + near_buf[s, 0, i].astype(jnp.float32) + near_buf[s, 1, i].astype(jnp.float32)
            )
        for copy in in_copies(s):
            copy.start()

        @pl.when(home)
        def _():
            in_sum[0, core, pl.ds(pl.multiple_of(s * strip, strip), strip), :] = own_buf[s, x]

        @pl.when(jnp.logical_not(home))
        def _():
            stay_copy(s).start()

    def send_strip(s, carry):
        for t in (0, 1):
            value = product(s, around(z + 2), 2 * t)
            for e in (0, 1):
                out_buf[s, 2, 2 * t + e] = value[:, lane(e)].astype(jnp.bfloat16)
            far_copy(s, t).start()
        for t in (0, 1):
            i = 2 - 2 * t
            value = product(s, around(z + HOP[t]), i)
            for e in (0, 1):
                out_buf[s, t, i + e] = value[:, lane(e)].astype(jnp.bfloat16)
            direct_copy(s, t).start()
        for i in (0, 2):
            value = product(s, z, i)
            for e in (0, 1):
                own_buf[s, i + e] = value[:, lane(e)]
        for t in (0, 1):
            value = product(s, around(z + HOP[t]), 2 * t)
            far_copy(s, t).wait_recv()
            for e in (0, 1):
                out_buf[s, t, 2 * t + e] = (
                    value[:, lane(e)] + far_buf[s, t, e].astype(jnp.float32)
                ).astype(jnp.bfloat16)
            added_copy(s, t).start()

        @pl.when(s > 0)
        def _():
            add_strip(jnp.maximum(s - 1, 0))

        return carry

    lax.fori_loop(0, STRIPS, send_strip, 0)
    add_strip(STRIPS - 1)

    swap_copy(1, sibling).wait_recv()
    for i in (0, 1):
        remote(swap.at[0], swap.at[2 + i], swap_send.at[2 + i], swap_recv.at[2 + i], sibling).wait_recv()
    half = rows // LANES
    for a in (0, 1):
        mine_row = jnp.where(core == a, swap[0], swap[1])
        rows_out[pl.ds(a * half, half), :] = jnp.where(home, mine_row, swap[2 + a])

    def finish(s, carry):
        at = pl.ds(pl.multiple_of(s * strip, strip), strip)
        in_copy(s, 0, 1 - core, 3, 0, sibling).wait_recv()
        in_copy(s, 1, 0, 1, 1, sibling).wait_recv()
        in_copy(s, 1, 1, 2, 1, sibling).wait_recv()

        @pl.when(jnp.logical_not(home))
        def _():
            in_copy(s, 0, core, 0, 1, sibling).wait_recv()

        for a in (0, 1):
            targets[pl.ds(pl.multiple_of(a * rows + s * strip, strip), strip), :] = (
                in_sum[0, a, at, :] + in_sum[1, a, at, :]
            )
        for t in (0, 1):
            far_copy(s, t).wait_send()
            direct_copy(s, t).wait_send()
            added_copy(s, t).wait_send()
        for copy in in_copies(s):
            copy.wait_send()

        @pl.when(jnp.logical_not(home))
        def _():
            stay_copy(s).wait_send()

        return carry

    lax.fori_loop(0, STRIPS, finish, 0)
    for copy in started:
        copy.wait_send()

    @pl.when(jnp.logical_not(home))
    def _():
        last.wait_send()


def shards(noise_latents, data_latents):
    nsize = lax.axis_size("noise")
    dsize = lax.axis_size("dp")
    block, piece = noise_latents.shape
    rows, cols = block // 2, 2 * data_latents.shape[0]
    rsize, csize = dsize // 2, nsize * 2
    vmem = pl.BlockSpec(memory_space=pltpu.VMEM)
    f32, bf16 = jnp.float32, jnp.bfloat16
    strip = rows // STRIPS
    row_vec, col_vec = (rows // LANES, LANES), (cols // LANES, LANES)
    sems = pltpu.SemaphoreType.DMA
    targets, rows_pot, cols_pot = pl.pallas_call(
        functools.partial(kernel, rsize, csize, piece * dsize),
        out_shape=(
            jax.ShapeDtypeStruct((block, piece), f32),
            jax.ShapeDtypeStruct((block // LANES, LANES), f32),
            jax.ShapeDtypeStruct((cols // 2 // LANES, LANES), f32),
        ),
        in_specs=[vmem] * 2,
        out_specs=(vmem,) * 3,
        scratch_shapes=[
            pltpu.VMEM((dsize, rows, piece), bf16),
            pltpu.VMEM((2, nsize) + data_latents.shape, bf16),
            pltpu.VMEM((rows, cols), f32),
            pltpu.VMEM((rows, cols), bf16),
            pltpu.VMEM((rows, LANES), f32),
            pltpu.VMEM((rows, LANES), f32),
            pltpu.VMEM((rows, LANES), f32),
            pltpu.VMEM((rows, LANES), f32),
            pltpu.VMEM((cols, LANES), f32),
            pltpu.VMEM((8, cols), f32),
            pltpu.VMEM(row_vec, f32),
            pltpu.VMEM(col_vec, f32),
            pltpu.VMEM(row_vec, f32),
            pltpu.VMEM(col_vec, f32),
            pltpu.VMEM((4,) + row_vec, f32),
            pltpu.VMEM((ITERS, csize, 2) + col_vec, f32),
            pltpu.VMEM((ITERS, rsize, 2) + row_vec, f32),
            pltpu.VMEM((STRIPS, 3, SIDE, strip, LANES), bf16),
            pltpu.VMEM((STRIPS, SIDE, strip, LANES), f32),
            pltpu.VMEM((STRIPS, 2, 2, strip, LANES), bf16),
            pltpu.VMEM((STRIPS, 2, SIDE, strip, LANES), bf16),
            pltpu.VMEM((2, 2, rows, LANES), f32),
            sems((ITERS, csize)),
            sems((ITERS, csize)),
            sems((ITERS, rsize)),
            sems((ITERS, rsize)),
            sems((4,)),
            sems((4,)),
            sems((4,)),
            sems((4,)),
            sems((SIDE, 2, 2)),
            sems((SIDE, 2, 2)),
            sems((2, 10)),
            sems((2, 10)),
            sems((STRIPS, 2, 3)),
            sems((STRIPS, 2, 3)),
            sems((STRIPS, 4)),
            sems((STRIPS, 2, 2)),
        ],
        compiler_params=pltpu.CompilerParams(
            collective_id=0, has_side_effects=True, vmem_limit_bytes=60 * 2**20
        ),
    )(noise_latents, data_latents)
    return targets, rows_pot.reshape(block), cols_pot.reshape(cols // 2)


def solution(mesh):
    return jax.shard_map(
        shards,
        mesh=mesh,
        in_specs=(P("noise", "dp"), P("dp", "noise")),
        out_specs=(P("noise", "dp"), P("noise"), P("dp")),
        check_vma=False,
    )
```

```python
import functools
import math

import jax
import jax.numpy as jnp
from jax import lax
from jax.experimental import pallas as pl
from jax.experimental.pallas import tpu as pltpu
from jax.sharding import PartitionSpec as P

ITERS = 3
EPSILON = 0.04
LOG2E = 1.0 / math.log(2.0)
MESH = pl.DeviceIdType.MESH
LANES = 128
TILE = 32
SIDE = 4
STRIPS = 4


def wrap(index, size):
    return lax.rem(index, size)


def spread_lanes(ref, row):
    return jnp.broadcast_to(ref[pl.ds(row, 1), :], (LANES, LANES)).T


def exchange(buf, send, recv, step, parts, me, size, peer_id, started):
    for k in range(1, size):
        peer = wrap(me + k, size)
        copy = pltpu.make_async_remote_copy(
            src_ref=buf.at[step, me, pl.ds(0, parts)],
            dst_ref=buf.at[step, me, pl.ds(0, parts)],
            send_sem=send.at[step, k],
            recv_sem=recv.at[step, me],
            device_id=peer_id(peer),
            device_id_type=MESH,
        )
        copy.start()
        started.append(copy)
    for k in range(1, size):
        peer = wrap(me + k, size)
        pltpu.make_async_remote_copy(
            src_ref=buf.at[step, peer, pl.ds(0, parts)],
            dst_ref=buf.at[step, peer, pl.ds(0, parts)],
            send_sem=send.at[step, k],
            recv_sem=recv.at[step, peer],
            device_id=peer_id(peer),
            device_id_type=MESH,
        ).wait_recv()


def combine(buf, step, size):
    top = buf[step, 0, 0]
    for s in range(1, size):
        top = jnp.maximum(top, buf[step, s, 0])
    total = buf[step, 0, 1] * jnp.exp2(buf[step, 0, 0] - top)
    for s in range(1, size):
        total = total + buf[step, s, 1] * jnp.exp2(buf[step, s, 0] - top)
    return top, total


def add_slots(buf, step, size):
    total = buf[step, 0, 0]
    for s in range(1, size):
        total = total + buf[step, s, 0]
    return total


def kernel(
    rsize, csize, width,
    noise_ref, data_ref,
    targets, rows_out, cols_out,
    noise_all, data_all, scores, weights,
    shift, first, scale, part, data_part, colvec, rowpack, colpack, sqx, sqy, swap,
    col_buf, row_buf, out_buf, own_buf, far_buf, near_buf, in_sum,
    col_send, col_recv, row_send, row_recv, swap_send, swap_recv,
    cross_send, cross_recv, noise_send, noise_recv, data_send, data_recv,
    sum_send, sum_recv, in_send, in_recv, keep,
):
    rows, cols = scores.shape
    n = lax.axis_index("noise")
    d = lax.axis_index("dp")
    x, z = d // SIDE, lax.rem(d, SIDE)
    y, core = n // 2, lax.rem(n, 2)
    kind = lax.rem((x + 1) // 2, 2)
    pair = x // 2
    side = lax.rem(x, 2)
    home = core == kind
    kappa = LOG2E / EPSILON
    log_rows = math.log2(rows * csize)
    log_cols = math.log2(cols * rsize)
    chunks = cols // LANES
    row_blocks = rows // LANES
    tiles = rows // TILE
    started = []

    def around(value):
        return lax.rem(value + SIDE, SIDE)

    def device(xi, yi, zi, ci):
        return (yi * 2 + ci, xi * SIDE + zi)

    def x_at(which, of_kind):
        return which * (3 - 2 * of_kind) + of_kind

    me_row = pair * SIDE + z
    me_col = y * 4 + kind * 2 + core

    def row_peer(p):
        return device(x_at(p // SIDE, kind), y, lax.rem(p, SIDE), core)

    def col_peer(p):
        return device(x_at(pair, lax.rem(p // 2, 2)), p // 4, z, lax.rem(p, 2))

    sibling = device(x, y, z, 1 - core)
    partner = x + 1 - 2 * side
    mate = SIDE - 1 - x
    opposite = around(x + 2)

    barrier = pltpu.get_barrier_semaphore()
    greeted = [row_peer(wrap(me_row + k, rsize)) for k in range(1, rsize)]
    greeted += [col_peer(wrap(me_col + k, csize)) for k in range(1, csize)]
    greeted += [device(opposite, y, z, 0), device(opposite, y, z, 1), device(mate, y, z, 1 - core)]
    for to in greeted:
        pl.semaphore_signal(barrier, inc=1, device_id=to, device_id_type=MESH)
    pl.semaphore_wait(barrier, len(greeted))

    def remote(src, dst, send, recv, to):
        return pltpu.make_async_remote_copy(
            src_ref=src, dst_ref=dst, send_sem=send, recv_sem=recv, device_id=to, device_id_type=MESH
        )

    def begin(copy):
        copy.start()
        started.append(copy)

    def lane(c):
        return slice(LANES * c, LANES * (c + 1))

    HOP = (1, -1)
    ORDER = (0, 1, 3, 2)
    own = x * SIDE + z

    def cross_copy(i, half, to):
        return remote(
            noise_ref.at[pl.ds(half * rows, rows)], noise_all.at[own], cross_send.at[i], cross_recv.at[x], to
        )

    def cross_wait(xi):
        remote(
            noise_ref.at[pl.ds(0, rows)], noise_all.at[xi * SIDE + z], cross_send.at[0], cross_recv.at[xi], sibling
        ).wait_recv()

    there = jnp.where(home, mate, opposite)
    back = jnp.where(home, x, partner)
    last = cross_copy(3, core, device(partner, y, z, core))

    def noise_copy(xi, t, forward, slot):
        at = pl.ds(t * (rows // 2), rows // 2) if forward else pl.ds(0, rows)
        f = int(forward)
        return remote(
            noise_all.at[slot, at], noise_all.at[slot, at],
            noise_send.at[xi, t, f], noise_recv.at[xi, t, f], device(x, y, around(z + HOP[t]), core),
        )

    def noise_wait(xi, t, forward):
        slot = xi * SIDE + around(z - HOP[t] * (2 if forward else 1))
        noise_copy(xi, t, forward, slot).wait_recv()
        return slot

    def data_copy(r, index, where, lo, size, to, own=False):
        at = pl.ds(lo, size)
        block = side if r == 0 else 1 - side
        dst = data_all.at[block, where, at]
        return remote(data_ref.at[at] if own else dst, dst, data_send.at[r, index], data_recv.at[r, index], to)

    half_cols = cols // 4
    full_cols = cols // 2

    def along_y(step, c):
        return around(y + step) * 2 + c

    def data_wait(r, index, where, lo, size):
        data_copy(r, index, where, lo, size, sibling).wait_recv()

    for t in (0, 1):
        begin(data_copy(0, t, n, 0, full_cols, device(x, around(y + HOP[t]), z, core), own=True))
    begin(remote(
        data_ref.at[pl.ds(0, full_cols)], data_all.at[side, n],
        data_send.at[1, 9], data_recv.at[1, 9], device(partner, y, z, core),
    ))
    begin(cross_copy(2, 1 - core, device(back, y, z, 1 - core)))

    @pl.when(home)
    def _():
        noise_all[own] = noise_ref[pl.ds(pl.multiple_of(core * rows, rows), rows), :]

    @pl.when(jnp.logical_not(home))
    def _():
        last.start()

    begin(cross_copy(0, 0, device(there, y, z, 0)))
    begin(cross_copy(1, 1, device(there, y, z, 1)))
    begin(data_copy(0, 4, n, 0, full_cols, sibling, own=True))

    data_all[side, n] = data_ref[...]

    @pl.when(jnp.logical_not(home))
    def _():
        cross_wait(x)

    for t in (0, 1):
        begin(noise_copy(x, t, False, own))
    scores[...] = jnp.zeros_like(scores)
    part[...] = jnp.zeros_like(part)
    data_part[...] = jnp.zeros_like(data_part)
    data_wait(1, 9, n, 0, full_cols)
    for t in (0, 1):
        begin(data_copy(1, t, n, 0, full_cols, device(x, around(y + HOP[t]), z, core)))
    begin(data_copy(1, 4, n, 0, full_cols, sibling))
    for xi in (partner, mate, opposite):
        cross_wait(xi)
        for t in (0, 1):
            begin(noise_copy(xi, t, False, xi * SIDE + z))
    for r in (0, 1):
        for t in (0, 1):
            where = along_y(-HOP[t], core)
            data_wait(r, t, where, 0, full_cols)
            begin(data_copy(r, 2 + t, where, t * half_cols, half_cols, device(x, around(y + HOP[t]), z, core)))
            begin(data_copy(r, 5 + t, where, 0, full_cols, sibling))
    by_data = [around(y + step) for step in ORDER]
    for xi in by_data:
        for t in (0, 1):
            begin(noise_copy(xi, t, True, noise_wait(xi, t, False)))
    for r in (0, 1):
        data_wait(r, 4, along_y(0, 1 - core), 0, full_cols)
        for t in (0, 1):
            data_wait(r, 5 + t, along_y(-HOP[t], 1 - core), 0, full_cols)

    def squares(block):
        value = block.astype(jnp.float32)
        return value * value

    def chunk(q):
        both = jnp.concatenate([noise_all[2 * q], noise_all[2 * q + 1]], axis=1)

        def column(m, carry):
            cut = pl.ds(pl.multiple_of(m * 256, 256), 256)
            piece = data_all[m // 4, q, pl.ds(pl.multiple_of(lax.rem(m, 4) * 256, 256), 256), :]
            scores[:, cut] += lax.dot_general(
                both, piece, (((1,), (1,)), ((), ())), preferred_element_type=jnp.float32
            )
            data_part[cut, :] += squares(piece[:, :LANES]) + squares(piece[:, LANES:])
            return carry

        lax.fori_loop(0, cols // 256, column, 0)

        def norm(r, carry):
            cut = pl.ds(pl.multiple_of(r * 64, 64), 64)
            part[cut, :] += squares(noise_all[2 * q, cut, :]) + squares(noise_all[2 * q + 1, cut, :])
            return carry

        lax.fori_loop(0, rows // 64, norm, 0)

    mine = z // 2

    def early(i, carry):
        chunk(around(y + i + i // 2) * 2 + mine)
        return carry

    lax.fori_loop(0, 3, early, 0)

    def late(xi):
        for t in (0, 1):
            noise_wait(xi, t, True)
        chunk(xi * 2 + 1 - mine)

    late(by_data[0])
    for r in (0, 1):
        for t in (0, 1):
            where = along_y(2, core)
            data_wait(r, 2 + t, where, t * half_cols, half_cols)
            begin(data_copy(r, 7 + t, where, t * half_cols, half_cols, sibling))
        if r == 0:
            late(by_data[1])
            late(by_data[2])
    for r in (0, 1):
        for t in (0, 1):
            data_wait(r, 7 + t, along_y(2, 1 - core), t * half_cols, half_cols)
    for t in (0, 1):
        noise_wait(by_data[3], t, True)

    def final(i, carry):
        chunk(around(y + 2) * 2 + lax.rem(mine + i, 2))
        return carry

    lax.fori_loop(0, 2, final, 0)
    for b in range(row_blocks):
        sqx[pl.ds(b, 1), :] = jnp.sum(part[pl.ds(b * LANES, LANES), :].T, axis=0, keepdims=True)
    for c in range(chunks):
        sqy[pl.ds(c, 1), :] = jnp.sum(data_part[pl.ds(c * LANES, LANES), :].T, axis=0, keepdims=True)

    def fold(block, op):
        out = block[0:8]
        for r in range(1, TILE // 8):
            out = op(out, block[8 * r:8 * r + 8])
        return out

    def spread_cols():
        for c in range(chunks):
            colvec[:, lane(c)] = jnp.broadcast_to(colpack[pl.ds(c, 1), :], (8, LANES))

    factor = 2.0 * kappa / width
    for b in range(row_blocks):
        shift[pl.ds(b * LANES, LANES), :] = spread_lanes(sqx, b) * (-kappa / width)

    zero = tuple(jnp.full((8, LANES), -jnp.inf, jnp.float32) for _ in range(chunks))

    def top_step(t, accs):
        at = pl.ds(pl.multiple_of(t * TILE, TILE), TILE)
        add = shift[at, :]
        out = []
        for c in range(chunks):
            value = scores[at, lane(c)] * factor
            scores[at, lane(c)] = value
            out.append(jnp.maximum(accs[c], fold(value + add, jnp.maximum)))
        return tuple(out)

    tops = lax.fori_loop(0, tiles, top_step, zero)
    tops = tuple(jnp.max(a, axis=0, keepdims=True) for a in tops)
    for c in range(chunks):
        col_buf[0, me_col, 0, pl.ds(c, 1), :] = tops[c]
        colvec[:, lane(c)] = jnp.broadcast_to(tops[c], (8, LANES))

    zeros = tuple(jnp.zeros((8, LANES), jnp.float32) for _ in range(chunks))

    def tall(ref, c):
        return jnp.concatenate([ref[:, lane(c)]] * (TILE // 8), axis=0)

    def exp_step(t, accs):
        at = pl.ds(pl.multiple_of(t * TILE, TILE), TILE)
        add = shift[at, :]
        return tuple(
            accs[c] + fold(jnp.exp2(scores[at, lane(c)] + add - tall(colvec, c)), jnp.add)
            for c in range(chunks)
        )

    sums = lax.fori_loop(0, tiles, exp_step, zeros)
    for c in range(chunks):
        col_buf[0, me_col, 1, pl.ds(c, 1), :] = jnp.sum(sums[c], axis=0, keepdims=True)
    exchange(col_buf, col_send, col_recv, 0, 2, me_col, csize, col_peer, started)
    top, total = combine(col_buf, 0, csize)
    col_pot = -log_cols - top - jnp.log(total) * LOG2E
    colpack[...] = col_pot
    spread_cols()

    def row_step(t, carry):
        at = pl.ds(pl.multiple_of(t * TILE, TILE), TILE)
        top = scores[at, lane(0)] + tall(colvec, 0)
        for c in range(1, chunks):
            top = jnp.maximum(top, scores[at, lane(c)] + tall(colvec, c))
        top = jnp.broadcast_to(jnp.max(top, axis=1, keepdims=True), (TILE, LANES))
        first[at, :] = top
        total = None
        for c in range(chunks):
            value = jnp.exp2(scores[at, lane(c)] + tall(colvec, c) - top)
            scores[at, lane(c)] = value
            total = value if total is None else total + value
        part[at, :] = total
        return carry

    lax.fori_loop(0, tiles, row_step, 0)
    for b in range(row_blocks):
        at = pl.ds(b * LANES, LANES)
        row_buf[0, me_row, 0, pl.ds(b, 1), :] = first[at, :].T[0:1]
        row_buf[0, me_row, 1, pl.ds(b, 1), :] = jnp.sum(part[at, :].T, axis=0, keepdims=True)
    local_top = row_buf[0, me_row, 0]
    exchange(row_buf, row_send, row_recv, 0, 2, me_row, rsize, row_peer, started)
    top, total = combine(row_buf, 0, rsize)
    row_lse = top + jnp.log(total) * LOG2E
    base = jnp.exp2(local_top - row_lse)

    def spread_rows(value):
        rowpack[...] = value
        for b in range(row_blocks):
            scale[pl.ds(b * LANES, LANES), :] = spread_lanes(rowpack, b)

    spread_rows(base)

    def col_step(t, accs):
        at = pl.ds(pl.multiple_of(t * TILE, TILE), TILE)
        mul = scale[at, :]
        return tuple(accs[c] + fold(scores[at, lane(c)] * mul, jnp.add) for c in range(chunks))

    def sum_step(t, carry):
        at = pl.ds(pl.multiple_of(t * TILE, TILE), TILE)
        total = scores[at, lane(0)] * tall(colvec, 0)
        for c in range(1, chunks):
            total = total + scores[at, lane(c)] * tall(colvec, c)
        part[at, :] = total
        return carry

    for step in range(1, ITERS):
        sums = lax.fori_loop(0, tiles, col_step, zeros)
        for c in range(chunks):
            col_buf[step, me_col, 0, pl.ds(c, 1), :] = jnp.sum(sums[c], axis=0, keepdims=True)
        exchange(col_buf, col_send, col_recv, step, 1, me_col, csize, col_peer, started)
        ratio = 1.0 / add_slots(col_buf, step, csize)
        colpack[...] = ratio
        spread_cols()
        lax.fori_loop(0, tiles, sum_step, 0)
        for b in range(row_blocks):
            at = pl.ds(b * LANES, LANES)
            row_buf[step, me_row, 0, pl.ds(b, 1), :] = jnp.sum(part[at, :].T, axis=0, keepdims=True)
        row_buf[step, me_row, 0] = row_buf[step, me_row, 0] * base
        exchange(row_buf, row_send, row_recv, step, 1, me_row, rsize, row_peer, started)
        total = add_slots(row_buf, step, rsize)
        spread_rows(base / total)

    cols_pot = (col_pot + jnp.log(ratio) * LOG2E + (log_rows - log_cols)) / kappa + sqy[...] / width
    colpack[...] = cols_pot
    cols_out[...] = colpack[pl.ds(pl.multiple_of(side * 8, 8), 8), :]
    swap[0] = -(log_rows + row_lse + jnp.log(total) * LOG2E) / kappa + sqx[...] / width

    def swap_copy(i, to):
        return remote(swap.at[0], swap.at[i], swap_send.at[i], swap_recv.at[i], to)

    begin(swap_copy(1, sibling))
    for i in (0, 1):
        begin(remote(
            swap.at[0], swap.at[2 + core], swap_send.at[2 + i], swap_recv.at[2 + core], device(partner, y, z, i)
        ))

    def weight_step(t, carry):
        at = pl.ds(pl.multiple_of(t * TILE, TILE), TILE)
        mul = scale[at, :]
        for c in range(chunks):
            weights[at, lane(c)] = (scores[at, lane(c)] * tall(colvec, c) * mul).astype(jnp.bfloat16)
        return carry

    lax.fori_loop(0, tiles, weight_step, 0)

    strip = rows // 2

    def strip_rows(s):
        return pl.ds(pl.multiple_of(lax.rem(s, 2) * strip, strip), strip)

    def strip_blocks(s):
        begins = s < 2
        return jnp.where(begins, opposite, mate), jnp.where(begins, partner, x)

    def product(s, to_z):
        cut = pl.ds(pl.multiple_of(lax.rem(to_z, 2) * LANES, LANES), LANES)
        total = None
        for k in (0, 1):
            block = jnp.concatenate(
                [data_all[k, xi * 2 + to_z // 2, :, cut] for xi in strip_blocks(s)], axis=1
            )
            value = jnp.dot(
                weights[strip_rows(s), k * full_cols:(k + 1) * full_cols], block,
                preferred_element_type=jnp.float32,
            )
            total = value if total is None else total + value
        return total

    def sum_copy(s, t, index, src, dst):
        to = device(x, y, around(z + HOP[t]), core)
        return remote(src, dst, sum_send.at[s, t, index], sum_recv.at[s, t, index], to)

    def far_copy(s, t):
        return sum_copy(s, t, 0, out_buf.at[s, 2, t], far_buf.at[s, t])

    def direct_copy(s, t):
        return sum_copy(s, t, 1, out_buf.at[s, t, 1 - t], near_buf.at[s, t, 1 - t])

    def added_copy(s, t):
        return sum_copy(s, t, 2, out_buf.at[s, t, t], near_buf.at[s, t, t])

    def in_copy(s, e, g, a, to):
        r = lax.rem(s, 2)
        return remote(
            own_buf.at[s, e], in_sum.at[g, a, strip_rows(s)], in_send.at[s, e], in_recv.at[r, g, a], to
        )

    def out_copy(s, e):
        return in_copy(s, e, 1 - e, core, device(strip_blocks(s)[e], y, z, kind))

    def add_strip(s):
        for t in (0, 1):
            direct_copy(s, t).wait_recv()
            added_copy(s, t).wait_recv()
        for e in (0, 1):
            own_buf[s, e] = (
                own_buf[s, e] + near_buf[s, 0, e].astype(jnp.float32) + near_buf[s, 1, e].astype(jnp.float32)
            )
            if e == 0:
                out_copy(s, 0).start()
        stays = jnp.logical_and(home, s >= 2)

        @pl.when(stays)
        def _():
            in_sum[0, core, strip_rows(s), :] = own_buf[s, 1]

        @pl.when(jnp.logical_not(stays))
        def _():
            out_copy(s, 1).start()

    def send_strip(s, carry):
        value = product(s, around(z + 2))
        for t in (0, 1):
            out_buf[s, 2, t] = value[:, lane(t)].astype(jnp.bfloat16)
            far_copy(s, t).start()
        for t in (0, 1):
            value = product(s, around(z + HOP[t]))
            out_buf[s, t, 1 - t] = value[:, lane(1 - t)].astype(jnp.bfloat16)
            direct_copy(s, t).start()
            keep[t] = value[:, lane(t)]
        value = product(s, z)
        for e in (0, 1):
            own_buf[s, e] = value[:, lane(e)]
        for t in (0, 1):
            far_copy(s, t).wait_recv()
            out_buf[s, t, t] = (keep[t] + far_buf[s, t].astype(jnp.float32)).astype(jnp.bfloat16)
            added_copy(s, t).start()

        @pl.when(s > 0)
        def _():
            add_strip(jnp.maximum(s - 1, 0))

        return carry

    lax.fori_loop(0, STRIPS, send_strip, 0)
    add_strip(STRIPS - 1)

    swap_copy(1, sibling).wait_recv()
    for i in (0, 1):
        remote(swap.at[0], swap.at[2 + i], swap_send.at[2 + i], swap_recv.at[2 + i], sibling).wait_recv()
    half = rows // LANES
    for a in (0, 1):
        mine_row = jnp.where(core == a, swap[0], swap[1])
        rows_out[pl.ds(a * half, half), :] = jnp.where(home, mine_row, swap[2 + a])

    def wait_in(r, g, a):
        in_copy(r, 0, g, a, sibling).wait_recv()

    for r in (0, 1):
        wait_in(r, 1, 0)
        wait_in(r, 1, 1)
        wait_in(r, 0, 1 - core)

        @pl.when(jnp.logical_not(home))
        def _():
            wait_in(r, 0, core)

        for a in (0, 1):
            at = pl.ds(r * strip, strip)
            targets[pl.ds(a * rows + r * strip, strip), :] = in_sum[0, a, at, :] + in_sum[1, a, at, :]

    def settle(s, carry):
        for t in (0, 1):
            far_copy(s, t).wait_send()
            direct_copy(s, t).wait_send()
            added_copy(s, t).wait_send()
        out_copy(s, 0).wait_send()

        @pl.when(jnp.logical_not(jnp.logical_and(home, s >= 2)))
        def _():
            out_copy(s, 1).wait_send()

        return carry

    lax.fori_loop(0, STRIPS, settle, 0)
    for copy in started:
        copy.wait_send()

    @pl.when(jnp.logical_not(home))
    def _():
        last.wait_send()


def shards(noise_latents, data_latents):
    nsize = lax.axis_size("noise")
    dsize = lax.axis_size("dp")
    block, piece = noise_latents.shape
    rows, cols = block // 2, 2 * data_latents.shape[0]
    rsize, csize = dsize // 2, nsize * 2
    vmem = pl.BlockSpec(memory_space=pltpu.VMEM)
    f32, bf16 = jnp.float32, jnp.bfloat16
    strip = rows // 2
    row_vec, col_vec = (rows // LANES, LANES), (cols // LANES, LANES)
    sems = pltpu.SemaphoreType.DMA
    targets, rows_pot, cols_pot = pl.pallas_call(
        functools.partial(kernel, rsize, csize, piece * dsize),
        out_shape=(
            jax.ShapeDtypeStruct((block, piece), f32),
            jax.ShapeDtypeStruct((block // LANES, LANES), f32),
            jax.ShapeDtypeStruct((cols // 2 // LANES, LANES), f32),
        ),
        in_specs=[vmem] * 2,
        out_specs=(vmem,) * 3,
        scratch_shapes=[
            pltpu.VMEM((dsize, rows, piece), bf16),
            pltpu.VMEM((2, nsize) + data_latents.shape, bf16),
            pltpu.VMEM((rows, cols), f32),
            pltpu.VMEM((rows, cols), bf16),
            pltpu.VMEM((rows, LANES), f32),
            pltpu.VMEM((rows, LANES), f32),
            pltpu.VMEM((rows, LANES), f32),
            pltpu.VMEM((rows, LANES), f32),
            pltpu.VMEM((cols, LANES), f32),
            pltpu.VMEM((8, cols), f32),
            pltpu.VMEM(row_vec, f32),
            pltpu.VMEM(col_vec, f32),
            pltpu.VMEM(row_vec, f32),
            pltpu.VMEM(col_vec, f32),
            pltpu.VMEM((4,) + row_vec, f32),
            pltpu.VMEM((ITERS, csize, 2) + col_vec, f32),
            pltpu.VMEM((ITERS, rsize, 2) + row_vec, f32),
            pltpu.VMEM((STRIPS, 3, 2, strip, LANES), bf16),
            pltpu.VMEM((STRIPS, 2, strip, LANES), f32),
            pltpu.VMEM((STRIPS, 2, strip, LANES), bf16),
            pltpu.VMEM((STRIPS, 2, 2, strip, LANES), bf16),
            pltpu.VMEM((2, 2, rows, LANES), f32),
            sems((ITERS, csize)),
            sems((ITERS, csize)),
            sems((ITERS, rsize)),
            sems((ITERS, rsize)),
            sems((4,)),
            sems((4,)),
            sems((4,)),
            sems((4,)),
            sems((SIDE, 2, 2)),
            sems((SIDE, 2, 2)),
            sems((2, 10)),
            sems((2, 10)),
            sems((STRIPS, 2, 3)),
            sems((STRIPS, 2, 3)),
            sems((STRIPS, 2)),
            sems((2, 2, 2)),
            pltpu.VMEM((2, strip, LANES), f32),
        ],
        compiler_params=pltpu.CompilerParams(
            collective_id=0, has_side_effects=True, vmem_limit_bytes=60 * 2**20
        ),
    )(noise_latents, data_latents)
    return targets, rows_pot.reshape(block), cols_pot.reshape(cols // 2)


def solution(mesh):
    return jax.shard_map(
        shards,
        mesh=mesh,
        in_specs=(P("noise", "dp"), P("dp", "noise")),
        out_specs=(P("noise", "dp"), P("noise"), P("dp")),
        check_vma=False,
    )
```

```python
import functools
import math

import jax
import jax.numpy as jnp
from jax import lax
from jax.experimental import pallas as pl
from jax.experimental.pallas import tpu as pltpu
from jax.sharding import PartitionSpec as P

ITERS = 3
EPSILON = 0.04
LOG2E = 1.0 / math.log(2.0)
MESH = pl.DeviceIdType.MESH
LANES = 128
TILE = 32
SIDE = 4
STRIPS = 4


def wrap(index, size):
    return lax.rem(index, size)


def spread_lanes(ref, row):
    return jnp.broadcast_to(ref[pl.ds(row, 1), :], (LANES, LANES)).T


def exchange(buf, send, recv, step, parts, me, size, peer_id, started):
    for k in range(1, size):
        pltpu.make_async_remote_copy(
            src_ref=buf.at[step, me, pl.ds(0, parts)],
            dst_ref=buf.at[step, me, pl.ds(0, parts)],
            send_sem=send.at[step],
            recv_sem=recv.at[step],
            device_id=peer_id(wrap(me + k, size)),
            device_id_type=MESH,
        ).start()
    slots = buf.at[step, pl.ds(0, size - 1), pl.ds(0, parts)]
    every = pltpu.make_async_remote_copy(
        src_ref=slots,
        dst_ref=slots,
        send_sem=send.at[step],
        recv_sem=recv.at[step],
        device_id=peer_id(wrap(me + 1, size)),
        device_id_type=MESH,
    )
    every.wait_recv()
    started.append(every)


def combine(buf, step, size):
    top = buf[step, 0, 0]
    for s in range(1, size):
        top = jnp.maximum(top, buf[step, s, 0])
    total = buf[step, 0, 1] * jnp.exp2(buf[step, 0, 0] - top)
    for s in range(1, size):
        total = total + buf[step, s, 1] * jnp.exp2(buf[step, s, 0] - top)
    return top, total


def add_slots(buf, step, size):
    total = buf[step, 0, 0]
    for s in range(1, size):
        total = total + buf[step, s, 0]
    return total


def kernel(
    rsize, csize, width,
    noise_ref, data_ref,
    targets, rows_out, cols_out,
    noise_all, data_all, scores, weights,
    shift, first, scale, part, data_part, colvec, rowpack, colpack, sqx, sqy, swap,
    col_buf, row_buf, out_buf, own_buf, far_buf, near_buf, in_sum,
    col_send, col_recv, row_send, row_recv, swap_send, swap_recv,
    cross_send, cross_recv, noise_send, noise_recv, data_send, data_recv,
    sum_send, sum_recv, in_send, in_recv, keep,
):
    rows, cols = scores.shape
    n = lax.axis_index("noise")
    d = lax.axis_index("dp")
    x, z = d // SIDE, lax.rem(d, SIDE)
    y, core = n // 2, lax.rem(n, 2)
    kind = lax.rem((x + 1) // 2, 2)
    pair = x // 2
    side = lax.rem(x, 2)
    home = core == kind
    kappa = LOG2E / EPSILON
    log_rows = math.log2(rows * csize)
    log_cols = math.log2(cols * rsize)
    chunks = cols // LANES
    row_blocks = rows // LANES
    tiles = rows // TILE
    started = []

    def around(value):
        return lax.rem(value + SIDE, SIDE)

    def device(xi, yi, zi, ci):
        return (yi * 2 + ci, xi * SIDE + zi)

    def x_at(which, of_kind):
        return which * (3 - 2 * of_kind) + of_kind

    me_row = pair * SIDE + z
    me_col = y * 4 + kind * 2 + core

    def row_peer(p):
        return device(x_at(p // SIDE, kind), y, lax.rem(p, SIDE), core)

    def col_peer(p):
        return device(x_at(pair, lax.rem(p // 2, 2)), p // 4, z, lax.rem(p, 2))

    sibling = device(x, y, z, 1 - core)
    partner = x + 1 - 2 * side
    mate = SIDE - 1 - x
    opposite = around(x + 2)

    barrier = pltpu.get_barrier_semaphore()
    greeted = [row_peer(wrap(me_row + k, rsize)) for k in range(1, rsize)]
    greeted += [col_peer(wrap(me_col + k, csize)) for k in range(1, csize)]
    greeted += [device(opposite, y, z, 0), device(opposite, y, z, 1), device(mate, y, z, 1 - core)]
    for to in greeted:
        pl.semaphore_signal(barrier, inc=1, device_id=to, device_id_type=MESH)
    pl.semaphore_wait(barrier, len(greeted))

    def remote(src, dst, send, recv, to):
        return pltpu.make_async_remote_copy(
            src_ref=src, dst_ref=dst, send_sem=send, recv_sem=recv, device_id=to, device_id_type=MESH
        )

    def begin(copy):
        copy.start()
        started.append(copy)

    def lane(c):
        return slice(LANES * c, LANES * (c + 1))

    HOP = (1, -1)
    ORDER = (0, 1, 3, 2)
    own = x * SIDE + z

    def cross_copy(i, half, to):
        return remote(
            noise_ref.at[pl.ds(half * rows, rows)], noise_all.at[own], cross_send.at[i], cross_recv.at[x], to
        )

    def cross_wait(xi):
        remote(
            noise_ref.at[pl.ds(0, rows)], noise_all.at[xi * SIDE + z], cross_send.at[0], cross_recv.at[xi], sibling
        ).wait_recv()

    there = jnp.where(home, mate, opposite)
    back = jnp.where(home, x, partner)
    last = cross_copy(3, core, device(partner, y, z, core))

    def noise_copy(xi, t, forward, slot):
        at = pl.ds(t * (rows // 2), rows // 2) if forward else pl.ds(0, rows)
        f = int(forward)
        return remote(
            noise_all.at[slot, at], noise_all.at[slot, at],
            noise_send.at[xi, t, f], noise_recv.at[xi, t, f], device(x, y, around(z + HOP[t]), core),
        )

    def noise_wait(xi, t, forward):
        slot = xi * SIDE + around(z - HOP[t] * (2 if forward else 1))
        noise_copy(xi, t, forward, slot).wait_recv()
        return slot

    def data_copy(r, index, where, lo, size, to, own=False):
        at = pl.ds(lo, size)
        block = side if r == 0 else 1 - side
        dst = data_all.at[block, where, at]
        return remote(data_ref.at[at] if own else dst, dst, data_send.at[r, index], data_recv.at[r, index], to)

    half_cols = cols // 4
    full_cols = cols // 2

    def along_y(step, c):
        return around(y + step) * 2 + c

    def data_wait(r, index, where, lo, size):
        data_copy(r, index, where, lo, size, sibling).wait_recv()

    for t in (0, 1):
        begin(data_copy(0, t, n, 0, full_cols, device(x, around(y + HOP[t]), z, core), own=True))
    begin(remote(
        data_ref.at[pl.ds(0, full_cols)], data_all.at[side, n],
        data_send.at[1, 9], data_recv.at[1, 9], device(partner, y, z, core),
    ))
    begin(cross_copy(2, 1 - core, device(back, y, z, 1 - core)))

    @pl.when(home)
    def _():
        noise_all[own] = noise_ref[pl.ds(pl.multiple_of(core * rows, rows), rows), :]

    @pl.when(jnp.logical_not(home))
    def _():
        last.start()

    begin(cross_copy(0, 0, device(there, y, z, 0)))
    begin(cross_copy(1, 1, device(there, y, z, 1)))
    begin(data_copy(0, 4, n, 0, full_cols, sibling, own=True))

    data_all[side, n] = data_ref[...]

    @pl.when(jnp.logical_not(home))
    def _():
        cross_wait(x)

    for t in (0, 1):
        begin(noise_copy(x, t, False, own))
    scores[...] = jnp.zeros_like(scores)
    part[...] = jnp.zeros_like(part)
    data_part[...] = jnp.zeros_like(data_part)
    data_wait(1, 9, n, 0, full_cols)
    for t in (0, 1):
        begin(data_copy(1, t, n, 0, full_cols, device(x, around(y + HOP[t]), z, core)))
    begin(data_copy(1, 4, n, 0, full_cols, sibling))
    for xi in (partner, mate, opposite):
        cross_wait(xi)
        for t in (0, 1):
            begin(noise_copy(xi, t, False, xi * SIDE + z))
    for r in (0, 1):
        for t in (0, 1):
            where = along_y(-HOP[t], core)
            data_wait(r, t, where, 0, full_cols)
            begin(data_copy(r, 2 + t, where, t * half_cols, half_cols, device(x, around(y + HOP[t]), z, core)))
            begin(data_copy(r, 5 + t, where, 0, full_cols, sibling))
    by_data = [around(y + step) for step in ORDER]
    for xi in by_data:
        for t in (0, 1):
            begin(noise_copy(xi, t, True, noise_wait(xi, t, False)))
    for r in (0, 1):
        data_wait(r, 4, along_y(0, 1 - core), 0, full_cols)
        for t in (0, 1):
            data_wait(r, 5 + t, along_y(-HOP[t], 1 - core), 0, full_cols)

    def squares(block):
        value = block.astype(jnp.float32)
        return value * value

    def chunk_product(q, m):
        both = jnp.concatenate([noise_all[2 * q], noise_all[2 * q + 1]], axis=1)
        cut = pl.ds(pl.multiple_of(m * 256, 256), 256)
        piece = data_all[m // 4, q, pl.ds(pl.multiple_of(lax.rem(m, 4) * 256, 256), 256), :]
        data_part[cut, :] += squares(piece[:, :LANES]) + squares(piece[:, LANES:])
        return lax.dot_general(both, piece, (((1,), (1,)), ((), ())), preferred_element_type=jnp.float32)

    def norms(q):
        def norm(r, carry):
            cut = pl.ds(pl.multiple_of(r * 64, 64), 64)
            part[cut, :] += squares(noise_all[2 * q, cut, :]) + squares(noise_all[2 * q + 1, cut, :])
            return carry

        lax.fori_loop(0, rows // 64, norm, 0)

    def chunk(q):
        def column(m, carry):
            cut = pl.ds(pl.multiple_of(m * 256, 256), 256)
            scores[:, cut] += chunk_product(q, m)
            return carry

        lax.fori_loop(0, cols // 256, column, 0)
        norms(q)

    mine = z // 2

    def early(i, carry):
        chunk(around(y + i + i // 2) * 2 + mine)
        return carry

    lax.fori_loop(0, 3, early, 0)

    def late(xi):
        for t in (0, 1):
            noise_wait(xi, t, True)
        chunk(xi * 2 + 1 - mine)

    late(by_data[0])
    for r in (0, 1):
        for t in (0, 1):
            where = along_y(2, core)
            data_wait(r, 2 + t, where, t * half_cols, half_cols)
            begin(data_copy(r, 7 + t, where, t * half_cols, half_cols, sibling))
        if r == 0:
            late(by_data[1])
            late(by_data[2])
    for r in (0, 1):
        for t in (0, 1):
            data_wait(r, 7 + t, along_y(2, 1 - core), t * half_cols, half_cols)
    for t in (0, 1):
        noise_wait(by_data[3], t, True)

    factor = 2.0 * kappa / width
    q_mine, q_other = around(y + 2) * 2 + mine, around(y + 2) * 2 + 1 - mine
    for q in (q_mine, q_other):
        norms(q)

    def row_shift(r, carry):
        at = pl.ds(pl.multiple_of(r * 128, 128), 128)
        total = jnp.sum(part[at, :], axis=1, keepdims=True) * (-kappa / width)
        shift[at, :] = jnp.broadcast_to(total, (128, LANES))
        return carry

    lax.fori_loop(0, rows // 128, row_shift, 0)

    def final(m, carry):
        cut = pl.ds(pl.multiple_of(m * 256, 256), 256)
        value = scores[:, cut]
        for q in (q_mine, q_other):
            value = value + chunk_product(q, m)
        value = value * factor
        scores[:, cut] = value
        for e in (0, 1):
            top = jnp.max(value[:, LANES * e:LANES * (e + 1)] + shift[...], axis=0, keepdims=True)
            col_buf[0, me_col, 0, pl.ds(2 * m + e, 1), :] = top
            colvec[:, pl.ds(pl.multiple_of(m * 256 + e * LANES, LANES), LANES)] = jnp.broadcast_to(top, (8, LANES))
        return carry

    lax.fori_loop(0, cols // 256, final, 0)

    def fold(block, op):
        out = block[0:8]
        for r in range(1, TILE // 8):
            out = op(out, block[8 * r:8 * r + 8])
        return out

    def spread_cols():
        for c in range(chunks):
            colvec[:, lane(c)] = jnp.broadcast_to(colpack[pl.ds(c, 1), :], (8, LANES))

    def tall(ref, c):
        return jnp.concatenate([ref[:, lane(c)]] * (TILE // 8), axis=0)

    def tile_at(t):
        return pl.ds(pl.multiple_of(t * TILE, TILE), TILE)

    def loop(body, init):
        return lax.fori_loop(0, tiles, body, init, unroll=2)

    zeros = tuple(jnp.zeros((8, LANES), jnp.float32) for _ in range(chunks))

    def exp_step(t, accs):
        at = tile_at(t)
        add = shift[at, :]
        return tuple(
            accs[c] + fold(jnp.exp2(scores[at, lane(c)] + add - tall(colvec, c)), jnp.add)
            for c in range(chunks)
        )

    sums = loop(exp_step, zeros)
    for c in range(chunks):
        col_buf[0, me_col, 1, pl.ds(c, 1), :] = jnp.sum(sums[c], axis=0, keepdims=True)
    exchange(col_buf, col_send, col_recv, 0, 2, me_col, csize, col_peer, started)
    top, total = combine(col_buf, 0, csize)
    col_pot = -log_cols - top - jnp.log(total) * LOG2E
    colpack[...] = col_pot
    spread_cols()

    def row_step(t, carry):
        at = tile_at(t)
        top = scores[at, lane(0)] + tall(colvec, 0)
        for c in range(1, chunks):
            top = jnp.maximum(top, scores[at, lane(c)] + tall(colvec, c))
        first[at, :] = top
        total = None
        for c in range(chunks):
            value = jnp.exp2(scores[at, lane(c)] + tall(colvec, c) - top)
            scores[at, lane(c)] = value
            total = value if total is None else total + value
        part[at, :] = total
        return carry

    loop(row_step, 0)
    for b in range(row_blocks):
        at = pl.ds(b * LANES, LANES)
        tops = first[at, :].T
        top = jnp.max(tops, axis=0, keepdims=True)
        row_buf[0, me_row, 0, pl.ds(b, 1), :] = top
        row_buf[0, me_row, 1, pl.ds(b, 1), :] = jnp.sum(part[at, :].T * jnp.exp2(tops - top), axis=0, keepdims=True)
    exchange(row_buf, row_send, row_recv, 0, 2, me_row, rsize, row_peer, started)
    top, total = combine(row_buf, 0, rsize)
    row_lse = top + jnp.log(total) * LOG2E
    rowpack[...] = row_lse
    for b in range(row_blocks):
        at = pl.ds(b * LANES, LANES)
        base = jnp.exp2(first[at, :] - spread_lanes(rowpack, b))
        first[at, :] = base
        scale[at, :] = base

    def col_step(t, accs):
        at = tile_at(t)
        mul = scale[at, :]
        return tuple(accs[c] + fold(scores[at, lane(c)] * mul, jnp.add) for c in range(chunks))

    def sum_step(keep_values):
        def body(t, carry):
            at = tile_at(t)
            total = None
            for c in range(chunks):
                value = scores[at, lane(c)] * tall(colvec, c)
                if keep_values:
                    scores[at, lane(c)] = value
                total = value if total is None else total + value
            part[at, :] = total * first[at, :]
            return carry

        return body

    for step in range(1, ITERS):
        sums = loop(col_step, zeros)
        for c in range(chunks):
            col_buf[step, me_col, 0, pl.ds(c, 1), :] = jnp.sum(sums[c], axis=0, keepdims=True)
        exchange(col_buf, col_send, col_recv, step, 1, me_col, csize, col_peer, started)
        ratio = 1.0 / add_slots(col_buf, step, csize)
        colpack[...] = ratio
        spread_cols()
        loop(sum_step(step == ITERS - 1), 0)
        for b in range(row_blocks):
            at = pl.ds(b * LANES, LANES)
            row_buf[step, me_row, 0, pl.ds(b, 1), :] = jnp.sum(part[at, :].T, axis=0, keepdims=True)
        exchange(row_buf, row_send, row_recv, step, 1, me_row, rsize, row_peer, started)
        total = add_slots(row_buf, step, rsize)
        rowpack[...] = 1.0 / total
        for b in range(row_blocks):
            at = pl.ds(b * LANES, LANES)
            scale[at, :] = first[at, :] * spread_lanes(rowpack, b)

    def weigh(r):
        def body(t, carry):
            at = pl.ds(pl.multiple_of(r * (rows // 2) + t * TILE, TILE), TILE)
            mul = scale[at, :]
            for c in range(chunks):
                weights[at, lane(c)] = (scores[at, lane(c)] * mul).astype(jnp.bfloat16)
            return carry

        lax.fori_loop(0, tiles // 2, body, 0, unroll=2)

    def swap_copy(i, to):
        return remote(swap.at[0], swap.at[i], swap_send.at[i], swap_recv.at[i], to)

    def potentials():
        for c in range(chunks):
            sqy[pl.ds(c, 1), :] = jnp.sum(data_part[pl.ds(c * LANES, LANES), :].T, axis=0, keepdims=True)
        cols_pot = (col_pot + jnp.log(ratio) * LOG2E + (log_rows - log_cols)) / kappa + sqy[...] / width
        colpack[...] = cols_pot
        cols_out[...] = colpack[pl.ds(pl.multiple_of(side * 8, 8), 8), :]
        for b in range(row_blocks):
            sqx[pl.ds(b, 1), :] = shift[pl.ds(b * LANES, LANES), :].T[0:1]
        swap[0] = -(log_rows + row_lse + jnp.log(total) * LOG2E + sqx[...]) / kappa
        begin(swap_copy(1, sibling))
        for i in (0, 1):
            begin(remote(
                swap.at[0], swap.at[2 + core], swap_send.at[2 + i], swap_recv.at[2 + core], device(partner, y, z, i)
            ))

    strip = rows // 2

    def strip_rows(s):
        return pl.ds(pl.multiple_of(lax.rem(s, 2) * strip, strip), strip)

    def strip_blocks(s):
        begins = s < 2
        return jnp.where(begins, opposite, mate), jnp.where(begins, partner, x)

    def product(s, to_z):
        cut = pl.ds(pl.multiple_of(lax.rem(to_z, 2) * LANES, LANES), LANES)
        total = None
        for k in (0, 1):
            block = jnp.concatenate(
                [data_all[k, xi * 2 + to_z // 2, :, cut] for xi in strip_blocks(s)], axis=1
            )
            value = jnp.dot(
                weights[strip_rows(s), k * full_cols:(k + 1) * full_cols], block,
                preferred_element_type=jnp.float32,
            )
            total = value if total is None else total + value
        return total

    def sum_copy(s, t, index, src, dst):
        to = device(x, y, around(z + HOP[t]), core)
        return remote(src, dst, sum_send.at[s, t, index], sum_recv.at[s, t, index], to)

    def far_copy(s, t):
        return sum_copy(s, t, 0, out_buf.at[s, 2, t], far_buf.at[s, t])

    def direct_copy(s, t):
        return sum_copy(s, t, 1, out_buf.at[s, t, 1 - t], near_buf.at[s, t, 1 - t])

    def added_copy(s, t):
        return sum_copy(s, t, 2, out_buf.at[s, t, t], near_buf.at[s, t, t])

    def in_copy(s, e, g, a, to):
        r = lax.rem(s, 2)
        return remote(
            own_buf.at[s, e], in_sum.at[g, a, strip_rows(s)], in_send.at[s, e], in_recv.at[r, g, a], to
        )

    def out_copy(s, e):
        return in_copy(s, e, 1 - e, core, device(strip_blocks(s)[e], y, z, kind))

    def add_strip(s):
        for t in (0, 1):
            direct_copy(s, t).wait_recv()
            added_copy(s, t).wait_recv()
        for e in (0, 1):
            own_buf[s, e] = (
                own_buf[s, e] + near_buf[s, 0, e].astype(jnp.float32) + near_buf[s, 1, e].astype(jnp.float32)
            )
            if e == 0:
                out_copy(s, 0).start()
        stays = jnp.logical_and(home, s >= 2)

        @pl.when(stays)
        def _():
            in_sum[0, core, strip_rows(s), :] = own_buf[s, 1]

        @pl.when(jnp.logical_not(stays))
        def _():
            out_copy(s, 1).start()

    def send_strip(s, carry):
        @pl.when(s < 2)
        def _():
            weigh(s)

        value = product(s, around(z + 2))
        for t in (0, 1):
            out_buf[s, 2, t] = value[:, lane(t)].astype(jnp.bfloat16)
            far_copy(s, t).start()
        for t in (0, 1):
            value = product(s, around(z + HOP[t]))
            out_buf[s, t, 1 - t] = value[:, lane(1 - t)].astype(jnp.bfloat16)
            direct_copy(s, t).start()
            keep[t] = value[:, lane(t)]
        value = product(s, z)
        for e in (0, 1):
            own_buf[s, e] = value[:, lane(e)]
        for t in (0, 1):
            far_copy(s, t).wait_recv()
            out_buf[s, t, t] = (keep[t] + far_buf[s, t].astype(jnp.float32)).astype(jnp.bfloat16)
            added_copy(s, t).start()

        @pl.when(s > 0)
        def _():
            add_strip(jnp.maximum(s - 1, 0))

        return carry

    lax.fori_loop(0, STRIPS, send_strip, 0)
    potentials()
    add_strip(STRIPS - 1)

    swap_copy(1, sibling).wait_recv()
    for i in (0, 1):
        remote(swap.at[0], swap.at[2 + i], swap_send.at[2 + i], swap_recv.at[2 + i], sibling).wait_recv()
    half = rows // LANES
    for a in (0, 1):
        mine_row = jnp.where(core == a, swap[0], swap[1])
        rows_out[pl.ds(a * half, half), :] = jnp.where(home, mine_row, swap[2 + a])

    def wait_in(r, g, a):
        in_copy(r, 0, g, a, sibling).wait_recv()

    for r in (0, 1):
        wait_in(r, 1, 0)
        wait_in(r, 1, 1)
        wait_in(r, 0, 1 - core)

        @pl.when(jnp.logical_not(home))
        def _():
            wait_in(r, 0, core)

        for a in (0, 1):
            at = pl.ds(r * strip, strip)
            targets[pl.ds(a * rows + r * strip, strip), :] = in_sum[0, a, at, :] + in_sum[1, a, at, :]

    def settle(s, carry):
        for t in (0, 1):
            far_copy(s, t).wait_send()
            direct_copy(s, t).wait_send()
            added_copy(s, t).wait_send()
        out_copy(s, 0).wait_send()

        @pl.when(jnp.logical_not(jnp.logical_and(home, s >= 2)))
        def _():
            out_copy(s, 1).wait_send()

        return carry

    lax.fori_loop(0, STRIPS, settle, 0)
    for copy in started:
        copy.wait_send()

    @pl.when(jnp.logical_not(home))
    def _():
        last.wait_send()


def shards(noise_latents, data_latents):
    nsize = lax.axis_size("noise")
    dsize = lax.axis_size("dp")
    block, piece = noise_latents.shape
    rows, cols = block // 2, 2 * data_latents.shape[0]
    rsize, csize = dsize // 2, nsize * 2
    vmem = pl.BlockSpec(memory_space=pltpu.VMEM)
    f32, bf16 = jnp.float32, jnp.bfloat16
    strip = rows // 2
    row_vec, col_vec = (rows // LANES, LANES), (cols // LANES, LANES)
    sems = pltpu.SemaphoreType.DMA
    targets, rows_pot, cols_pot = pl.pallas_call(
        functools.partial(kernel, rsize, csize, piece * dsize),
        out_shape=(
            jax.ShapeDtypeStruct((block, piece), f32),
            jax.ShapeDtypeStruct((block // LANES, LANES), f32),
            jax.ShapeDtypeStruct((cols // 2 // LANES, LANES), f32),
        ),
        in_specs=[vmem] * 2,
        out_specs=(vmem,) * 3,
        scratch_shapes=[
            pltpu.VMEM((dsize, rows, piece), bf16),
            pltpu.VMEM((2, nsize) + data_latents.shape, bf16),
            pltpu.VMEM((rows, cols), f32),
            pltpu.VMEM((rows, cols), bf16),
            pltpu.VMEM((rows, LANES), f32),
            pltpu.VMEM((rows, LANES), f32),
            pltpu.VMEM((rows, LANES), f32),
            pltpu.VMEM((rows, LANES), f32),
            pltpu.VMEM((cols, LANES), f32),
            pltpu.VMEM((8, cols), f32),
            pltpu.VMEM(row_vec, f32),
            pltpu.VMEM(col_vec, f32),
            pltpu.VMEM(row_vec, f32),
            pltpu.VMEM(col_vec, f32),
            pltpu.VMEM((4,) + row_vec, f32),
            pltpu.VMEM((ITERS, csize, 2) + col_vec, f32),
            pltpu.VMEM((ITERS, rsize, 2) + row_vec, f32),
            pltpu.VMEM((STRIPS, 3, 2, strip, LANES), bf16),
            pltpu.VMEM((STRIPS, 2, strip, LANES), f32),
            pltpu.VMEM((STRIPS, 2, strip, LANES), bf16),
            pltpu.VMEM((STRIPS, 2, 2, strip, LANES), bf16),
            pltpu.VMEM((2, 2, rows, LANES), f32),
            sems((ITERS,)),
            sems((ITERS,)),
            sems((ITERS,)),
            sems((ITERS,)),
            sems((4,)),
            sems((4,)),
            sems((4,)),
            sems((4,)),
            sems((SIDE, 2, 2)),
            sems((SIDE, 2, 2)),
            sems((2, 10)),
            sems((2, 10)),
            sems((STRIPS, 2, 3)),
            sems((STRIPS, 2, 3)),
            sems((STRIPS, 2)),
            sems((2, 2, 2)),
            pltpu.VMEM((2, strip, LANES), f32),
        ],
        compiler_params=pltpu.CompilerParams(
            collective_id=0, has_side_effects=True, vmem_limit_bytes=60 * 2**20
        ),
    )(noise_latents, data_latents)
    return targets, rows_pot.reshape(block), cols_pot.reshape(cols // 2)


def solution(mesh):
    return jax.shard_map(
        shards,
        mesh=mesh,
        in_specs=(P("noise", "dp"), P("dp", "noise")),
        out_specs=(P("noise", "dp"), P("noise"), P("dp")),
        check_vma=False,
    )
```

```python
import functools
import math

import jax
import jax.numpy as jnp
from jax import lax
from jax.experimental import pallas as pl
from jax.experimental.pallas import tpu as pltpu
from jax.sharding import PartitionSpec as P

ITERS = 3
EPSILON = 0.04
LOG2E = 1.0 / math.log(2.0)
MESH = pl.DeviceIdType.MESH
LANES = 128
TILE = 32
SIDE = 4
STRIPS = 4


def wrap(index, size):
    return lax.rem(index, size)


def spread_lanes(ref, row):
    return jnp.broadcast_to(ref[pl.ds(row, 1), :], (LANES, LANES)).T


def exchange(buf, send, recv, step, parts, me, size, peer_id, started):
    for k in range(1, size):
        pltpu.make_async_remote_copy(
            src_ref=buf.at[step, me, pl.ds(0, parts)],
            dst_ref=buf.at[step, me, pl.ds(0, parts)],
            send_sem=send.at[step],
            recv_sem=recv.at[step],
            device_id=peer_id(wrap(me + k, size)),
            device_id_type=MESH,
        ).start()
    slots = buf.at[step, pl.ds(0, size - 1), pl.ds(0, parts)]
    every = pltpu.make_async_remote_copy(
        src_ref=slots,
        dst_ref=slots,
        send_sem=send.at[step],
        recv_sem=recv.at[step],
        device_id=peer_id(wrap(me + 1, size)),
        device_id_type=MESH,
    )
    every.wait_recv()
    started.append(every)


def combine(buf, step, size):
    top = buf[step, 0, 0]
    for s in range(1, size):
        top = jnp.maximum(top, buf[step, s, 0])
    total = buf[step, 0, 1] * jnp.exp2(buf[step, 0, 0] - top)
    for s in range(1, size):
        total = total + buf[step, s, 1] * jnp.exp2(buf[step, s, 0] - top)
    return top, total


def add_slots(buf, step, size):
    total = buf[step, 0, 0]
    for s in range(1, size):
        total = total + buf[step, s, 0]
    return total


def kernel(
    rsize, csize, width,
    noise_ref, data_ref,
    targets, rows_out, cols_out,
    noise_all, data_all, scores, weights,
    shift, first, scale, part, data_part, colvec, rowpack, colpack, sqx, sqy, swap,
    col_buf, row_buf, out_buf, own_buf, far_buf, near_buf, in_sum,
    col_send, col_recv, row_send, row_recv, swap_send, swap_recv,
    cross_send, cross_recv, noise_send, noise_recv, data_send, data_recv,
    sum_send, sum_recv, in_send, in_recv, keep,
):
    rows, cols = scores.shape
    n = lax.axis_index("noise")
    d = lax.axis_index("dp")
    x, z = d // SIDE, lax.rem(d, SIDE)
    y, core = n // 2, lax.rem(n, 2)
    kind = lax.rem((x + 1) // 2, 2)
    pair = x // 2
    side = lax.rem(x, 2)
    home = core == kind
    kappa = LOG2E / EPSILON
    log_rows = math.log2(rows * csize)
    log_cols = math.log2(cols * rsize)
    chunks = cols // LANES
    row_blocks = rows // LANES
    tiles = rows // TILE
    started = []

    def around(value):
        return lax.rem(value + SIDE, SIDE)

    def device(xi, yi, zi, ci):
        return (yi * 2 + ci, xi * SIDE + zi)

    def x_at(which, of_kind):
        return which * (3 - 2 * of_kind) + of_kind

    me_row = pair * SIDE + z
    me_col = y * 4 + kind * 2 + core

    def row_peer(p):
        return device(x_at(p // SIDE, kind), y, lax.rem(p, SIDE), core)

    def col_peer(p):
        return device(x_at(pair, lax.rem(p // 2, 2)), p // 4, z, lax.rem(p, 2))

    sibling = device(x, y, z, 1 - core)
    partner = x + 1 - 2 * side
    mate = SIDE - 1 - x
    opposite = around(x + 2)

    barrier = pltpu.get_barrier_semaphore()
    greeted = [row_peer(wrap(me_row + k, rsize)) for k in range(1, rsize)]
    greeted += [col_peer(wrap(me_col + k, csize)) for k in range(1, csize)]
    greeted += [device(opposite, y, z, 0), device(opposite, y, z, 1), device(mate, y, z, 1 - core)]
    for to in greeted:
        pl.semaphore_signal(barrier, inc=1, device_id=to, device_id_type=MESH)
    pl.semaphore_wait(barrier, len(greeted))

    def remote(src, dst, send, recv, to):
        return pltpu.make_async_remote_copy(
            src_ref=src, dst_ref=dst, send_sem=send, recv_sem=recv, device_id=to, device_id_type=MESH
        )

    def begin(copy):
        copy.start()
        started.append(copy)

    def lane(c):
        return slice(LANES * c, LANES * (c + 1))

    HOP = (1, -1)
    ORDER = (0, 1, 3, 2)
    own = x * SIDE + z

    def cross_copy(i, half, to):
        return remote(
            noise_ref.at[pl.ds(half * rows, rows)], noise_all.at[own], cross_send.at[i], cross_recv.at[x], to
        )

    def cross_wait(xi):
        remote(
            noise_ref.at[pl.ds(0, rows)], noise_all.at[xi * SIDE + z], cross_send.at[0], cross_recv.at[xi], sibling
        ).wait_recv()

    there = jnp.where(home, mate, partner)
    aside = cross_copy(2, 1 - core, sibling)

    def noise_copy(xi, t, forward, slot):
        at = pl.ds(t * (rows // 2), rows // 2) if forward else pl.ds(0, rows)
        f = int(forward)
        return remote(
            noise_all.at[slot, at], noise_all.at[slot, at],
            noise_send.at[xi, t, f], noise_recv.at[xi, t, f], device(x, y, around(z + HOP[t]), core),
        )

    def noise_wait(xi, t, forward):
        slot = xi * SIDE + around(z - HOP[t] * (2 if forward else 1))
        noise_copy(xi, t, forward, slot).wait_recv()
        return slot

    def data_copy(r, index, where, lo, size, to, own=False):
        at = pl.ds(lo, size)
        block = side if r == 0 else 1 - side
        dst = data_all.at[block, where, at]
        return remote(data_ref.at[at] if own else dst, dst, data_send.at[r, index], data_recv.at[r, index], to)

    half_cols = cols // 4
    full_cols = cols // 2

    def along_y(step, c):
        return around(y + step) * 2 + c

    def data_wait(r, index, where, lo, size):
        data_copy(r, index, where, lo, size, sibling).wait_recv()

    HALF = 9

    def cross_data(h, own=False):
        at = pl.ds(h * half_cols, half_cols)
        dst = data_all.at[side if own else 1 - side, n, at]
        return remote(
            data_ref.at[at], dst, data_send.at[1, 11 + h], data_recv.at[1, 11 + h], device(partner, y, z, core)
        )

    def partner_y(t, h, back=0):
        where = around(y + back) * 2 + core
        to = device(x, around(y + HOP[t]), z, core)
        return t if h == 0 else HALF + t, where, h * half_cols, half_cols, to

    def partner_wait(t, h):
        data_copy(1, *partner_y(t, h, -HOP[t])).wait_recv()

    begin(cross_copy(0, 0, device(there, y, z, 0)))
    begin(cross_copy(1, 1, device(there, y, z, 1)))

    @pl.when(home)
    def _():
        aside.start()

    for t in (0, 1):
        begin(data_copy(0, t, n, 0, full_cols, device(x, around(y + HOP[t]), z, core), own=True))
    for h in (0, 1):
        begin(cross_data(h, own=True))
    begin(data_copy(0, 4, n, 0, full_cols, sibling, own=True))

    @pl.when(home)
    def _():
        noise_all[own] = noise_ref[pl.ds(pl.multiple_of(core * rows, rows), rows), :]

    @pl.when(jnp.logical_not(home))
    def _():
        cross_wait(x)

    for t in (0, 1):
        begin(noise_copy(x, t, False, own))
    data_all[side, n] = data_ref[...]
    scores[...] = jnp.zeros_like(scores)
    part[...] = jnp.zeros_like(part)
    data_part[...] = jnp.zeros_like(data_part)
    for xi in (mate, partner):
        cross_wait(xi)
        for t in (0, 1):
            begin(noise_copy(xi, t, False, xi * SIDE + z))
    slot = partner * SIDE + z
    begin(remote(
        noise_all.at[slot], noise_all.at[slot], cross_send.at[3], cross_recv.at[partner], device(mate, y, z, core)
    ))
    cross_data(0).wait_recv()
    for t in (0, 1):
        begin(data_copy(1, *partner_y(t, 0)))
    for t in (0, 1):
        where = along_y(-HOP[t], core)
        data_wait(0, t, where, 0, full_cols)
        begin(data_copy(0, 2 + t, where, t * half_cols, half_cols, device(x, around(y + HOP[t]), z, core)))
        begin(data_copy(0, 5 + t, where, 0, full_cols, sibling))
    cross_data(1).wait_recv()
    for t in (0, 1):
        begin(data_copy(1, *partner_y(t, 1)))
    begin(data_copy(1, 4, n, 0, full_cols, sibling))
    cross_wait(opposite)
    for t in (0, 1):
        begin(noise_copy(opposite, t, False, opposite * SIDE + z))
    by_data = [around(y + step) for step in ORDER]
    for xi in by_data:
        for t in (0, 1):
            begin(noise_copy(xi, t, True, noise_wait(xi, t, False)))

    def squares(block):
        value = block.astype(jnp.float32)
        return value * value

    def chunk_product(q, m):
        both = jnp.concatenate([noise_all[2 * q], noise_all[2 * q + 1]], axis=1)
        cut = pl.ds(pl.multiple_of(m * 256, 256), 256)
        piece = data_all[m // 4, q, pl.ds(pl.multiple_of(lax.rem(m, 4) * 256, 256), 256), :]
        data_part[cut, :] += squares(piece[:, :LANES]) + squares(piece[:, LANES:])
        return lax.dot_general(both, piece, (((1,), (1,)), ((), ())), preferred_element_type=jnp.float32)

    def norms(q):
        def norm(r, carry):
            cut = pl.ds(pl.multiple_of(r * 64, 64), 64)
            part[cut, :] += squares(noise_all[2 * q, cut, :]) + squares(noise_all[2 * q + 1, cut, :])
            return carry

        lax.fori_loop(0, rows // 64, norm, 0)

    near, other_block = side * 4, 4 - side * 4

    def unit(q, block):
        def column(m, carry):
            cut = pl.ds(pl.multiple_of((block + m) * 256, 256), 256)
            scores[:, cut] += chunk_product(q, block + m)
            return carry

        lax.fori_loop(0, 4, column, 0)

    mine = z // 2

    def own_unit(q):
        unit(q, near)
        norms(q)

    def forward_wait(xi):
        for t in (0, 1):
            noise_wait(xi, t, True)

    data_wait(0, 4, along_y(0, 1 - core), 0, full_cols)
    for t in (0, 1):
        data_wait(0, 5 + t, along_y(-HOP[t], 1 - core), 0, full_cols)

    def early(i, carry):
        own_unit(around(y + i + i // 2) * 2 + mine)
        return carry

    lax.fori_loop(0, 3, early, 0)

    def pass_on(t):
        where = along_y(-HOP[t], core)
        begin(data_copy(1, 2 + t, where, t * half_cols, half_cols, device(x, around(y + HOP[t]), z, core)))

    partner_wait(0, 0)
    pass_on(0)
    partner_wait(1, 0)
    for t in (0, 1):
        where = along_y(2, core)
        data_wait(0, 2 + t, where, t * half_cols, half_cols)
        begin(data_copy(0, 7 + t, where, t * half_cols, half_cols, sibling))
    forward_wait(by_data[0])
    own_unit(y * 2 + 1 - mine)
    data_wait(1, 4, along_y(0, 1 - core), 0, full_cols)

    def partner_mid(i, carry):
        unit(y * 2 + i, other_block)
        return carry

    lax.fori_loop(0, 2, partner_mid, 0)
    for t in (0, 1):
        data_wait(0, 7 + t, along_y(2, 1 - core), t * half_cols, half_cols)
    own_unit(around(y + 2) * 2 + mine)
    partner_wait(1, 1)
    pass_on(1)
    partner_wait(0, 1)
    for t in (0, 1):
        begin(data_copy(1, 5 + t, along_y(-HOP[t], core), 0, full_cols, sibling))
    for xi in by_data[1:3]:
        forward_wait(xi)
        own_unit(xi * 2 + 1 - mine)
    for t in (0, 1):
        data_wait(1, 5 + t, along_y(-HOP[t], 1 - core), 0, full_cols)

    def partner_late(i, carry):
        unit(around(y + 1 + 2 * (i // 2)) * 2 + lax.rem(i, 2), other_block)
        return carry

    lax.fori_loop(0, 4, partner_late, 0)
    for t in (0, 1):
        where = along_y(2, core)
        data_wait(1, 2 + t, where, t * half_cols, half_cols)
        begin(data_copy(1, 7 + t, where, t * half_cols, half_cols, sibling))
    forward_wait(by_data[3])
    for t in (0, 1):
        data_wait(1, 7 + t, along_y(2, 1 - core), t * half_cols, half_cols)

    factor = 2.0 * kappa / width
    q_mine, q_other = around(y + 2) * 2 + mine, around(y + 2) * 2 + 1 - mine
    norms(q_other)

    def row_shift(r, carry):
        at = pl.ds(pl.multiple_of(r * 128, 128), 128)
        total = jnp.sum(part[at, :], axis=1, keepdims=True) * (-kappa / width)
        shift[at, :] = jnp.broadcast_to(total, (128, LANES))
        return carry

    lax.fori_loop(0, rows // 128, row_shift, 0)

    def final(block, qs):
        def column(i, carry):
            m = block + i
            cut = pl.ds(pl.multiple_of(m * 256, 256), 256)
            value = scores[:, cut]
            for q in qs:
                value = value + chunk_product(q, m)
            value = value * factor
            scores[:, cut] = value
            for e in (0, 1):
                top = jnp.max(value[:, LANES * e:LANES * (e + 1)] + shift[...], axis=0, keepdims=True)
                col_buf[0, me_col, 0, pl.ds(2 * m + e, 1), :] = top
                colvec[:, pl.ds(pl.multiple_of(m * 256 + e * LANES, LANES), LANES)] = jnp.broadcast_to(top, (8, LANES))
            return carry

        lax.fori_loop(0, 4, column, 0)

    final(near, (q_other,))
    final(other_block, (q_mine, q_other))

    def fold(block, op):
        out = block[0:8]
        for r in range(1, TILE // 8):
            out = op(out, block[8 * r:8 * r + 8])
        return out

    def spread_cols():
        for c in range(chunks):
            colvec[:, lane(c)] = jnp.broadcast_to(colpack[pl.ds(c, 1), :], (8, LANES))

    def tall(ref, c):
        return jnp.concatenate([ref[:, lane(c)]] * (TILE // 8), axis=0)

    def tile_at(t):
        return pl.ds(pl.multiple_of(t * TILE, TILE), TILE)

    def loop(body, init):
        return lax.fori_loop(0, tiles, body, init, unroll=2)

    zeros = tuple(jnp.zeros((8, LANES), jnp.float32) for _ in range(chunks))

    def exp_step(t, accs):
        at = tile_at(t)
        add = shift[at, :]
        return tuple(
            accs[c] + fold(jnp.exp2(scores[at, lane(c)] + add - tall(colvec, c)), jnp.add)
            for c in range(chunks)
        )

    sums = loop(exp_step, zeros)
    for c in range(chunks):
        col_buf[0, me_col, 1, pl.ds(c, 1), :] = jnp.sum(sums[c], axis=0, keepdims=True)
    exchange(col_buf, col_send, col_recv, 0, 2, me_col, csize, col_peer, started)
    top, total = combine(col_buf, 0, csize)
    col_pot = -log_cols - top - jnp.log(total) * LOG2E
    colpack[...] = col_pot
    spread_cols()

    def row_step(t, carry):
        at = tile_at(t)
        top = scores[at, lane(0)] + tall(colvec, 0)
        for c in range(1, chunks):
            top = jnp.maximum(top, scores[at, lane(c)] + tall(colvec, c))
        first[at, :] = top
        total = None
        for c in range(chunks):
            value = jnp.exp2(scores[at, lane(c)] + tall(colvec, c) - top)
            scores[at, lane(c)] = value
            total = value if total is None else total + value
        part[at, :] = total
        return carry

    loop(row_step, 0)
    for b in range(row_blocks):
        at = pl.ds(b * LANES, LANES)
        tops = first[at, :].T
        top = jnp.max(tops, axis=0, keepdims=True)
        row_buf[0, me_row, 0, pl.ds(b, 1), :] = top
        row_buf[0, me_row, 1, pl.ds(b, 1), :] = jnp.sum(part[at, :].T * jnp.exp2(tops - top), axis=0, keepdims=True)
    exchange(row_buf, row_send, row_recv, 0, 2, me_row, rsize, row_peer, started)
    top, total = combine(row_buf, 0, rsize)
    row_lse = top + jnp.log(total) * LOG2E
    rowpack[...] = row_lse
    for b in range(row_blocks):
        at = pl.ds(b * LANES, LANES)
        base = jnp.exp2(first[at, :] - spread_lanes(rowpack, b))
        first[at, :] = base
        scale[at, :] = base

    def col_step(t, accs):
        at = tile_at(t)
        mul = scale[at, :]
        return tuple(accs[c] + fold(scores[at, lane(c)] * mul, jnp.add) for c in range(chunks))

    def sum_step(keep_values):
        def body(t, carry):
            at = tile_at(t)
            total = None
            for c in range(chunks):
                value = scores[at, lane(c)] * tall(colvec, c)
                if keep_values:
                    scores[at, lane(c)] = value
                total = value if total is None else total + value
            part[at, :] = total * first[at, :]
            return carry

        return body

    for step in range(1, ITERS):
        sums = loop(col_step, zeros)
        for c in range(chunks):
            col_buf[step, me_col, 0, pl.ds(c, 1), :] = jnp.sum(sums[c], axis=0, keepdims=True)
        exchange(col_buf, col_send, col_recv, step, 1, me_col, csize, col_peer, started)
        ratio = 1.0 / add_slots(col_buf, step, csize)
        colpack[...] = ratio
        spread_cols()
        loop(sum_step(step == ITERS - 1), 0)
        for b in range(row_blocks):
            at = pl.ds(b * LANES, LANES)
            row_buf[step, me_row, 0, pl.ds(b, 1), :] = jnp.sum(part[at, :].T, axis=0, keepdims=True)
        exchange(row_buf, row_send, row_recv, step, 1, me_row, rsize, row_peer, started)
        total = add_slots(row_buf, step, rsize)
        rowpack[...] = 1.0 / total
        for b in range(row_blocks):
            at = pl.ds(b * LANES, LANES)
            scale[at, :] = first[at, :] * spread_lanes(rowpack, b)

    def weigh(r):
        def body(t, carry):
            at = pl.ds(pl.multiple_of(r * (rows // 2) + t * TILE, TILE), TILE)
            mul = scale[at, :]
            for c in range(chunks):
                weights[at, lane(c)] = (scores[at, lane(c)] * mul).astype(jnp.bfloat16)
            return carry

        lax.fori_loop(0, tiles // 2, body, 0, unroll=2)

    def swap_copy(i, to):
        return remote(swap.at[0], swap.at[i], swap_send.at[i], swap_recv.at[i], to)

    def potentials():
        for c in range(chunks):
            sqy[pl.ds(c, 1), :] = jnp.sum(data_part[pl.ds(c * LANES, LANES), :].T, axis=0, keepdims=True)
        cols_pot = (col_pot + jnp.log(ratio) * LOG2E + (log_rows - log_cols)) / kappa + sqy[...] / width
        colpack[...] = cols_pot
        cols_out[...] = colpack[pl.ds(pl.multiple_of(side * 8, 8), 8), :]
        for b in range(row_blocks):
            sqx[pl.ds(b, 1), :] = shift[pl.ds(b * LANES, LANES), :].T[0:1]
        swap[0] = -(log_rows + row_lse + jnp.log(total) * LOG2E + sqx[...]) / kappa
        begin(swap_copy(1, sibling))
        for i in (0, 1):
            begin(remote(
                swap.at[0], swap.at[2 + core], swap_send.at[2 + i], swap_recv.at[2 + core], device(partner, y, z, i)
            ))

    strip = rows // 2

    def strip_rows(s):
        return pl.ds(pl.multiple_of(lax.rem(s, 2) * strip, strip), strip)

    def strip_blocks(s):
        begins = s < 2
        return jnp.where(begins, opposite, mate), jnp.where(begins, partner, x)

    def product(s, to_z):
        cut = pl.ds(pl.multiple_of(lax.rem(to_z, 2) * LANES, LANES), LANES)
        total = None
        for k in (0, 1):
            block = jnp.concatenate(
                [data_all[k, xi * 2 + to_z // 2, :, cut] for xi in strip_blocks(s)], axis=1
            )
            value = jnp.dot(
                weights[strip_rows(s), k * full_cols:(k + 1) * full_cols], block,
                preferred_element_type=jnp.float32,
            )
            total = value if total is None else total + value
        return total

    def sum_copy(s, t, index, src, dst):
        to = device(x, y, around(z + HOP[t]), core)
        return remote(src, dst, sum_send.at[s, t, index], sum_recv.at[s, t, index], to)

    def far_copy(s, t):
        return sum_copy(s, t, 0, out_buf.at[s, 2, t], far_buf.at[s, t])

    def direct_copy(s, t):
        return sum_copy(s, t, 1, out_buf.at[s, t, 1 - t], near_buf.at[s, t, 1 - t])

    def added_copy(s, t):
        return sum_copy(s, t, 2, out_buf.at[s, t, t], near_buf.at[s, t, t])

    def in_copy(s, e, g, a, to):
        r = lax.rem(s, 2)
        return remote(
            own_buf.at[s, e], in_sum.at[g, a, strip_rows(s)], in_send.at[s, e], in_recv.at[r, g, a], to
        )

    def out_copy(s, e):
        return in_copy(s, e, 1 - e, core, device(strip_blocks(s)[e], y, z, kind))

    def add_strip(s):
        for t in (0, 1):
            direct_copy(s, t).wait_recv()
            added_copy(s, t).wait_recv()
        for e in (0, 1):
            own_buf[s, e] = (
                own_buf[s, e] + near_buf[s, 0, e].astype(jnp.float32) + near_buf[s, 1, e].astype(jnp.float32)
            )
            if e == 0:
                out_copy(s, 0).start()
        stays = jnp.logical_and(home, s >= 2)

        @pl.when(stays)
        def _():
            in_sum[0, core, strip_rows(s), :] = own_buf[s, 1]

        @pl.when(jnp.logical_not(stays))
        def _():
            out_copy(s, 1).start()

    def send_strip(s, carry):
        @pl.when(s < 2)
        def _():
            weigh(s)

        value = product(s, around(z + 2))
        for t in (0, 1):
            out_buf[s, 2, t] = value[:, lane(t)].astype(jnp.bfloat16)
            far_copy(s, t).start()
        for t in (0, 1):
            value = product(s, around(z + HOP[t]))
            out_buf[s, t, 1 - t] = value[:, lane(1 - t)].astype(jnp.bfloat16)
            direct_copy(s, t).start()
            keep[t] = value[:, lane(t)]
        value = product(s, z)
        for e in (0, 1):
            own_buf[s, e] = value[:, lane(e)]
        for t in (0, 1):
            far_copy(s, t).wait_recv()
            out_buf[s, t, t] = (keep[t] + far_buf[s, t].astype(jnp.float32)).astype(jnp.bfloat16)
            added_copy(s, t).start()

        @pl.when(s > 0)
        def _():
            add_strip(jnp.maximum(s - 1, 0))

        return carry

    lax.fori_loop(0, STRIPS, send_strip, 0)
    potentials()
    add_strip(STRIPS - 1)

    swap_copy(1, sibling).wait_recv()
    for i in (0, 1):
        remote(swap.at[0], swap.at[2 + i], swap_send.at[2 + i], swap_recv.at[2 + i], sibling).wait_recv()
    half = rows // LANES
    for a in (0, 1):
        mine_row = jnp.where(core == a, swap[0], swap[1])
        rows_out[pl.ds(a * half, half), :] = jnp.where(home, mine_row, swap[2 + a])

    def wait_in(r, g, a):
        in_copy(r, 0, g, a, sibling).wait_recv()

    for r in (0, 1):
        wait_in(r, 1, 0)
        wait_in(r, 1, 1)
        wait_in(r, 0, 1 - core)

        @pl.when(jnp.logical_not(home))
        def _():
            wait_in(r, 0, core)

        for a in (0, 1):
            at = pl.ds(r * strip, strip)
            targets[pl.ds(a * rows + r * strip, strip), :] = in_sum[0, a, at, :] + in_sum[1, a, at, :]

    def settle(s, carry):
        for t in (0, 1):
            far_copy(s, t).wait_send()
            direct_copy(s, t).wait_send()
            added_copy(s, t).wait_send()
        out_copy(s, 0).wait_send()

        @pl.when(jnp.logical_not(jnp.logical_and(home, s >= 2)))
        def _():
            out_copy(s, 1).wait_send()

        return carry

    lax.fori_loop(0, STRIPS, settle, 0)
    for copy in started:
        copy.wait_send()

    @pl.when(home)
    def _():
        aside.wait_send()


def shards(noise_latents, data_latents):
    nsize = lax.axis_size("noise")
    dsize = lax.axis_size("dp")
    block, piece = noise_latents.shape
    rows, cols = block // 2, 2 * data_latents.shape[0]
    rsize, csize = dsize // 2, nsize * 2
    vmem = pl.BlockSpec(memory_space=pltpu.VMEM)
    f32, bf16 = jnp.float32, jnp.bfloat16
    strip = rows // 2
    row_vec, col_vec = (rows // LANES, LANES), (cols // LANES, LANES)
    sems = pltpu.SemaphoreType.DMA
    targets, rows_pot, cols_pot = pl.pallas_call(
        functools.partial(kernel, rsize, csize, piece * dsize),
        out_shape=(
            jax.ShapeDtypeStruct((block, piece), f32),
            jax.ShapeDtypeStruct((block // LANES, LANES), f32),
            jax.ShapeDtypeStruct((cols // 2 // LANES, LANES), f32),
        ),
        in_specs=[vmem] * 2,
        out_specs=(vmem,) * 3,
        scratch_shapes=[
            pltpu.VMEM((dsize, rows, piece), bf16),
            pltpu.VMEM((2, nsize) + data_latents.shape, bf16),
            pltpu.VMEM((rows, cols), f32),
            pltpu.VMEM((rows, cols), bf16),
            pltpu.VMEM((rows, LANES), f32),
            pltpu.VMEM((rows, LANES), f32),
            pltpu.VMEM((rows, LANES), f32),
            pltpu.VMEM((rows, LANES), f32),
            pltpu.VMEM((cols, LANES), f32),
            pltpu.VMEM((8, cols), f32),
            pltpu.VMEM(row_vec, f32),
            pltpu.VMEM(col_vec, f32),
            pltpu.VMEM(row_vec, f32),
            pltpu.VMEM(col_vec, f32),
            pltpu.VMEM((4,) + row_vec, f32),
            pltpu.VMEM((ITERS, csize, 2) + col_vec, f32),
            pltpu.VMEM((ITERS, rsize, 2) + row_vec, f32),
            pltpu.VMEM((STRIPS, 3, 2, strip, LANES), bf16),
            pltpu.VMEM((STRIPS, 2, strip, LANES), f32),
            pltpu.VMEM((STRIPS, 2, strip, LANES), bf16),
            pltpu.VMEM((STRIPS, 2, 2, strip, LANES), bf16),
            pltpu.VMEM((2, 2, rows, LANES), f32),
            sems((ITERS,)),
            sems((ITERS,)),
            sems((ITERS,)),
            sems((ITERS,)),
            sems((4,)),
            sems((4,)),
            sems((4,)),
            sems((4,)),
            sems((SIDE, 2, 2)),
            sems((SIDE, 2, 2)),
            sems((2, 13)),
            sems((2, 13)),
            sems((STRIPS, 2, 3)),
            sems((STRIPS, 2, 3)),
            sems((STRIPS, 2)),
            sems((2, 2, 2)),
            pltpu.VMEM((2, strip, LANES), f32),
        ],
        compiler_params=pltpu.CompilerParams(
            collective_id=0, has_side_effects=True, vmem_limit_bytes=60 * 2**20
        ),
    )(noise_latents, data_latents)
    return targets, rows_pot.reshape(block), cols_pot.reshape(cols // 2)


def solution(mesh):
    return jax.shard_map(
        shards,
        mesh=mesh,
        in_specs=(P("noise", "dp"), P("dp", "noise")),
        out_specs=(P("noise", "dp"), P("noise"), P("dp")),
        check_vma=False,
    )
```

```python
import functools
import math

import jax
import jax.numpy as jnp
from jax import lax
from jax.experimental import pallas as pl
from jax.experimental.pallas import tpu as pltpu
from jax.sharding import PartitionSpec as P

ITERS = 3
EPSILON = 0.04
LOG2E = 1.0 / math.log(2.0)
MESH = pl.DeviceIdType.MESH
LANES = 128
TILE = 32
SIDE = 4


def wrap(index, size):
    return lax.rem(index, size)


def spread_lanes(ref, row):
    return jnp.broadcast_to(ref[pl.ds(row, 1), :], (LANES, LANES)).T


def exchange(buf, send, recv, step, parts, me, size, peer_id, started):
    for k in range(1, size):
        pltpu.make_async_remote_copy(
            src_ref=buf.at[step, me, pl.ds(0, parts)],
            dst_ref=buf.at[step, me, pl.ds(0, parts)],
            send_sem=send.at[step],
            recv_sem=recv.at[step],
            device_id=peer_id(wrap(me + k, size)),
            device_id_type=MESH,
        ).start()
    slots = buf.at[step, pl.ds(0, size - 1), pl.ds(0, parts)]
    every = pltpu.make_async_remote_copy(
        src_ref=slots,
        dst_ref=slots,
        send_sem=send.at[step],
        recv_sem=recv.at[step],
        device_id=peer_id(wrap(me + 1, size)),
        device_id_type=MESH,
    )
    every.wait_recv()
    started.append(every)


def combine(buf, step, size):
    top = buf[step, 0, 0]
    for s in range(1, size):
        top = jnp.maximum(top, buf[step, s, 0])
    total = buf[step, 0, 1] * jnp.exp2(buf[step, 0, 0] - top)
    for s in range(1, size):
        total = total + buf[step, s, 1] * jnp.exp2(buf[step, s, 0] - top)
    return top, total


def add_slots(buf, step, size):
    total = buf[step, 0, 0]
    for s in range(1, size):
        total = total + buf[step, s, 0]
    return total


def kernel(
    rsize, csize, width,
    noise_ref, data_ref,
    targets, rows_out, cols_out,
    noise_all, data_all, scores, weights,
    shift, first, scale, part, data_part, colvec, rowpack, colpack, sqx, sqy, swap,
    col_buf, row_buf, out_buf, own_buf, far_buf, near_buf, in_sum,
    col_send, col_recv, row_send, row_recv, swap_send, swap_recv,
    cross_send, cross_recv, noise_send, noise_recv, data_send, data_recv,
    sum_send, sum_recv, in_send, in_recv, keep, local_sems,
):
    rows, cols = scores.shape
    n = lax.axis_index("noise")
    d = lax.axis_index("dp")
    x, z = d // SIDE, lax.rem(d, SIDE)
    y, core = n // 2, lax.rem(n, 2)
    kind = lax.rem((x + 1) // 2, 2)
    pair = x // 2
    side = lax.rem(x, 2)
    home = core == kind
    kappa = LOG2E / EPSILON
    log_rows = math.log2(rows * csize)
    log_cols = math.log2(cols * rsize)
    chunks = cols // LANES
    row_blocks = rows // LANES
    tiles = rows // TILE
    started = []

    def around(value):
        return lax.rem(value + SIDE, SIDE)

    def device(xi, yi, zi, ci):
        return (yi * 2 + ci, xi * SIDE + zi)

    def x_at(which, of_kind):
        return which * (3 - 2 * of_kind) + of_kind

    me_row = pair * SIDE + z
    me_col = y * 4 + kind * 2 + core

    def row_peer(p):
        return device(x_at(p // SIDE, kind), y, lax.rem(p, SIDE), core)

    def col_peer(p):
        return device(x_at(pair, lax.rem(p // 2, 2)), p // 4, z, lax.rem(p, 2))

    sibling = device(x, y, z, 1 - core)
    partner = x + 1 - 2 * side
    mate = SIDE - 1 - x
    opposite = around(x + 2)

    barrier = pltpu.get_barrier_semaphore()
    greeted = [row_peer(wrap(me_row + k, rsize)) for k in range(1, rsize)]
    greeted += [col_peer(wrap(me_col + k, csize)) for k in range(1, csize)]
    greeted += [device(opposite, y, z, 0), device(opposite, y, z, 1), device(mate, y, z, 1 - core)]
    for to in greeted:
        pl.semaphore_signal(barrier, inc=1, device_id=to, device_id_type=MESH)
    pl.semaphore_wait(barrier, len(greeted))

    def remote(src, dst, send, recv, to):
        return pltpu.make_async_remote_copy(
            src_ref=src, dst_ref=dst, send_sem=send, recv_sem=recv, device_id=to, device_id_type=MESH
        )

    def begin(copy):
        copy.start()
        started.append(copy)

    def lane(c):
        return slice(LANES * c, LANES * (c + 1))

    HOP = (1, -1)
    ORDER = (0, 1, 3, 2)
    own = x * SIDE + z

    def cross_copy(i, half, to):
        return remote(
            noise_ref.at[pl.ds(half * rows, rows)], noise_all.at[own], cross_send.at[i], cross_recv.at[x], to
        )

    def cross_wait(xi):
        remote(
            noise_ref.at[pl.ds(0, rows)], noise_all.at[xi * SIDE + z], cross_send.at[0], cross_recv.at[xi], sibling
        ).wait_recv()

    there = jnp.where(home, mate, partner)
    aside = cross_copy(2, 1 - core, sibling)

    def noise_copy(xi, t, forward, slot):
        at = pl.ds(t * (rows // 2), rows // 2) if forward else pl.ds(0, rows)
        f = int(forward)
        return remote(
            noise_all.at[slot, at], noise_all.at[slot, at],
            noise_send.at[xi, t, f], noise_recv.at[xi, t, f], device(x, y, around(z + HOP[t]), core),
        )

    def noise_wait(xi, t, forward):
        slot = xi * SIDE + around(z - HOP[t] * (2 if forward else 1))
        noise_copy(xi, t, forward, slot).wait_recv()
        return slot

    def data_copy(r, index, where, lo, size, to, own=False):
        at = pl.ds(lo, size)
        block = side if r == 0 else 1 - side
        dst = data_all.at[block, where, at]
        return remote(data_ref.at[at] if own else dst, dst, data_send.at[r, index], data_recv.at[r, index], to)

    half_cols = cols // 4
    full_cols = cols // 2

    def along_y(step, c):
        return around(y + step) * 2 + c

    def data_wait(r, index, where, lo, size):
        data_copy(r, index, where, lo, size, sibling).wait_recv()

    HALF = 9

    def cross_data(h, own=False):
        at = pl.ds(h * half_cols, half_cols)
        dst = data_all.at[side if own else 1 - side, n, at]
        return remote(
            data_ref.at[at], dst, data_send.at[1, 11 + h], data_recv.at[1, 11 + h], device(partner, y, z, core)
        )

    def partner_y(t, h, back=0):
        where = around(y + back) * 2 + core
        to = device(x, around(y + HOP[t]), z, core)
        return t if h == 0 else HALF + t, where, h * half_cols, half_cols, to

    def partner_wait(t, h):
        data_copy(1, *partner_y(t, h, -HOP[t])).wait_recv()

    begin(cross_copy(0, 0, device(there, y, z, 0)))
    begin(cross_copy(1, 1, device(there, y, z, 1)))

    @pl.when(home)
    def _():
        aside.start()

    for t in (0, 1):
        begin(data_copy(0, t, n, 0, full_cols, device(x, around(y + HOP[t]), z, core), own=True))
    for h in (0, 1):
        begin(cross_data(h, own=True))
    begin(data_copy(0, 4, n, 0, full_cols, sibling, own=True))

    @pl.when(home)
    def _():
        pltpu.make_async_copy(
            noise_ref.at[pl.ds(pl.multiple_of(core * rows, rows), rows)], noise_all.at[own], local_sems.at[0]
        ).start()

    data_own = pltpu.make_async_copy(data_ref, data_all.at[side, n], local_sems.at[1])
    data_own.start()

    @pl.when(home)
    def _():
        pltpu.make_async_copy(
            noise_ref.at[pl.ds(pl.multiple_of(core * rows, rows), rows)], noise_all.at[own], local_sems.at[0]
        ).wait()

    @pl.when(jnp.logical_not(home))
    def _():
        cross_wait(x)

    for t in (0, 1):
        begin(noise_copy(x, t, False, own))
    scores[...] = jnp.zeros_like(scores)
    part[...] = jnp.zeros_like(part)
    data_part[...] = jnp.zeros_like(data_part)
    for xi in (mate, partner):
        cross_wait(xi)
        for t in (0, 1):
            begin(noise_copy(xi, t, False, xi * SIDE + z))
    slot = partner * SIDE + z
    begin(remote(
        noise_all.at[slot], noise_all.at[slot], cross_send.at[3], cross_recv.at[partner], device(mate, y, z, core)
    ))
    cross_data(0).wait_recv()
    for t in (0, 1):
        begin(data_copy(1, *partner_y(t, 0)))
    for t in (0, 1):
        where = along_y(-HOP[t], core)
        data_wait(0, t, where, 0, full_cols)
        begin(data_copy(0, 2 + t, where, t * half_cols, half_cols, device(x, around(y + HOP[t]), z, core)))
        begin(data_copy(0, 5 + t, where, 0, full_cols, sibling))
    cross_data(1).wait_recv()
    for t in (0, 1):
        begin(data_copy(1, *partner_y(t, 1)))
    begin(data_copy(1, 4, n, 0, full_cols, sibling))
    cross_wait(opposite)
    for t in (0, 1):
        begin(noise_copy(opposite, t, False, opposite * SIDE + z))
    by_data = [around(y + step) for step in ORDER]
    for xi in by_data:
        for t in (0, 1):
            begin(noise_copy(xi, t, True, noise_wait(xi, t, False)))

    def squares(block):
        value = block.astype(jnp.float32)
        return value * value

    def chunk_product(q, m):
        both = jnp.concatenate([noise_all[2 * q], noise_all[2 * q + 1]], axis=1)
        cut = pl.ds(pl.multiple_of(m * 256, 256), 256)
        piece = data_all[m // 4, q, pl.ds(pl.multiple_of(lax.rem(m, 4) * 256, 256), 256), :]
        data_part[cut, :] += squares(piece[:, :LANES]) + squares(piece[:, LANES:])
        return lax.dot_general(both, piece, (((1,), (1,)), ((), ())), preferred_element_type=jnp.float32)

    def norms(q):
        def norm(r, carry):
            cut = pl.ds(pl.multiple_of(r * 64, 64), 64)
            part[cut, :] += squares(noise_all[2 * q, cut, :]) + squares(noise_all[2 * q + 1, cut, :])
            return carry

        lax.fori_loop(0, rows // 64, norm, 0)

    near, other_block = side * 4, 4 - side * 4

    def unit(q, block):
        def column(m, carry):
            cut = pl.ds(pl.multiple_of((block + m) * 256, 256), 256)
            scores[:, cut] += chunk_product(q, block + m)
            return carry

        lax.fori_loop(0, 4, column, 0)

    mine = z // 2

    def own_unit(q):
        unit(q, near)
        norms(q)

    def forward_wait(xi):
        for t in (0, 1):
            noise_wait(xi, t, True)

    data_own.wait()
    data_wait(0, 4, along_y(0, 1 - core), 0, full_cols)
    for t in (0, 1):
        data_wait(0, 5 + t, along_y(-HOP[t], 1 - core), 0, full_cols)

    def early(i, carry):
        own_unit(around(y + i + i // 2) * 2 + mine)
        return carry

    lax.fori_loop(0, 3, early, 0)

    def pass_on(t):
        where = along_y(-HOP[t], core)
        begin(data_copy(1, 2 + t, where, t * half_cols, half_cols, device(x, around(y + HOP[t]), z, core)))

    partner_wait(0, 0)
    pass_on(0)
    partner_wait(1, 0)
    for t in (0, 1):
        where = along_y(2, core)
        data_wait(0, 2 + t, where, t * half_cols, half_cols)
        begin(data_copy(0, 7 + t, where, t * half_cols, half_cols, sibling))
    forward_wait(by_data[0])
    own_unit(y * 2 + 1 - mine)
    data_wait(1, 4, along_y(0, 1 - core), 0, full_cols)

    def partner_mid(i, carry):
        unit(y * 2 + i, other_block)
        return carry

    lax.fori_loop(0, 2, partner_mid, 0)
    for t in (0, 1):
        data_wait(0, 7 + t, along_y(2, 1 - core), t * half_cols, half_cols)
    own_unit(around(y + 2) * 2 + mine)
    partner_wait(1, 1)
    pass_on(1)
    partner_wait(0, 1)
    for t in (0, 1):
        begin(data_copy(1, 5 + t, along_y(-HOP[t], core), 0, full_cols, sibling))
    for xi in by_data[1:3]:
        forward_wait(xi)
        own_unit(xi * 2 + 1 - mine)
    for t in (0, 1):
        data_wait(1, 5 + t, along_y(-HOP[t], 1 - core), 0, full_cols)

    def partner_late(i, carry):
        unit(around(y + 1 + 2 * (i // 2)) * 2 + lax.rem(i, 2), other_block)
        return carry

    lax.fori_loop(0, 4, partner_late, 0)
    for t in (0, 1):
        where = along_y(2, core)
        data_wait(1, 2 + t, where, t * half_cols, half_cols)
        begin(data_copy(1, 7 + t, where, t * half_cols, half_cols, sibling))
    forward_wait(by_data[3])
    for t in (0, 1):
        data_wait(1, 7 + t, along_y(2, 1 - core), t * half_cols, half_cols)

    factor = 2.0 * kappa / width
    q_mine, q_other = around(y + 2) * 2 + mine, around(y + 2) * 2 + 1 - mine
    norms(q_other)

    def row_shift(r, carry):
        at = pl.ds(pl.multiple_of(r * 128, 128), 128)
        total = jnp.sum(part[at, :], axis=1, keepdims=True) * (-kappa / width)
        shift[at, :] = jnp.broadcast_to(total, (128, LANES))
        return carry

    lax.fori_loop(0, rows // 128, row_shift, 0)

    def final(block, qs):
        def column(i, carry):
            m = block + i
            cut = pl.ds(pl.multiple_of(m * 256, 256), 256)
            value = scores[:, cut]
            for q in qs:
                value = value + chunk_product(q, m)
            value = value * factor
            scores[:, cut] = value
            for e in (0, 1):
                top = jnp.max(value[:, LANES * e:LANES * (e + 1)] + shift[...], axis=0, keepdims=True)
                col_buf[0, me_col, 0, pl.ds(2 * m + e, 1), :] = top
                colvec[:, pl.ds(pl.multiple_of(m * 256 + e * LANES, LANES), LANES)] = jnp.broadcast_to(top, (8, LANES))
            return carry

        lax.fori_loop(0, 4, column, 0)

    final(near, (q_other,))
    final(other_block, (q_mine, q_other))

    def fold(block, op):
        out = block[0:8]
        for r in range(1, TILE // 8):
            out = op(out, block[8 * r:8 * r + 8])
        return out

    def spread_cols():
        for c in range(chunks):
            colvec[:, lane(c)] = jnp.broadcast_to(colpack[pl.ds(c, 1), :], (8, LANES))

    def tall(ref, c):
        return jnp.concatenate([ref[:, lane(c)]] * (TILE // 8), axis=0)

    def tile_at(t):
        return pl.ds(pl.multiple_of(t * TILE, TILE), TILE)

    def loop(body, init):
        return lax.fori_loop(0, tiles, body, init, unroll=2)

    zeros = tuple(jnp.zeros((8, LANES), jnp.float32) for _ in range(chunks))

    def exp_step(t, accs):
        at = tile_at(t)
        add = shift[at, :]
        return tuple(
            accs[c] + fold(jnp.exp2(scores[at, lane(c)] + add - tall(colvec, c)), jnp.add)
            for c in range(chunks)
        )

    sums = loop(exp_step, zeros)
    for c in range(chunks):
        col_buf[0, me_col, 1, pl.ds(c, 1), :] = jnp.sum(sums[c], axis=0, keepdims=True)
    exchange(col_buf, col_send, col_recv, 0, 2, me_col, csize, col_peer, started)
    top, total = combine(col_buf, 0, csize)
    col_pot = -log_cols - top - jnp.log(total) * LOG2E
    colpack[...] = col_pot
    spread_cols()

    def row_step(t, carry):
        at = tile_at(t)
        top = scores[at, lane(0)] + tall(colvec, 0)
        for c in range(1, chunks):
            top = jnp.maximum(top, scores[at, lane(c)] + tall(colvec, c))
        first[at, :] = top
        total = None
        for c in range(chunks):
            value = jnp.exp2(scores[at, lane(c)] + tall(colvec, c) - top)
            scores[at, lane(c)] = value
            total = value if total is None else total + value
        part[at, :] = total
        return carry

    loop(row_step, 0)
    for b in range(row_blocks):
        at = pl.ds(b * LANES, LANES)
        tops = first[at, :].T
        top = jnp.max(tops, axis=0, keepdims=True)
        row_buf[0, me_row, 0, pl.ds(b, 1), :] = top
        row_buf[0, me_row, 1, pl.ds(b, 1), :] = jnp.sum(part[at, :].T * jnp.exp2(tops - top), axis=0, keepdims=True)
    exchange(row_buf, row_send, row_recv, 0, 2, me_row, rsize, row_peer, started)
    top, total = combine(row_buf, 0, rsize)
    row_lse = top + jnp.log(total) * LOG2E
    rowpack[...] = row_lse
    for b in range(row_blocks):
        at = pl.ds(b * LANES, LANES)
        base = jnp.exp2(first[at, :] - spread_lanes(rowpack, b))
        first[at, :] = base
        scale[at, :] = base

    def col_step(t, accs):
        at = tile_at(t)
        mul = scale[at, :]
        return tuple(accs[c] + fold(scores[at, lane(c)] * mul, jnp.add) for c in range(chunks))

    def sum_step(keep_values):
        def body(t, carry):
            at = tile_at(t)
            total = None
            for c in range(chunks):
                value = scores[at, lane(c)] * tall(colvec, c)
                if keep_values:
                    scores[at, lane(c)] = value
                total = value if total is None else total + value
            part[at, :] = total * first[at, :]
            return carry

        return body

    for step in range(1, ITERS):
        sums = loop(col_step, zeros)
        for c in range(chunks):
            col_buf[step, me_col, 0, pl.ds(c, 1), :] = jnp.sum(sums[c], axis=0, keepdims=True)
        exchange(col_buf, col_send, col_recv, step, 1, me_col, csize, col_peer, started)
        ratio = 1.0 / add_slots(col_buf, step, csize)
        colpack[...] = ratio
        spread_cols()
        loop(sum_step(step == ITERS - 1), 0)
        for b in range(row_blocks):
            at = pl.ds(b * LANES, LANES)
            row_buf[step, me_row, 0, pl.ds(b, 1), :] = jnp.sum(part[at, :].T, axis=0, keepdims=True)
        exchange(row_buf, row_send, row_recv, step, 1, me_row, rsize, row_peer, started)
        total = add_slots(row_buf, step, rsize)
        rowpack[...] = 1.0 / total
        for b in range(row_blocks):
            at = pl.ds(b * LANES, LANES)
            scale[at, :] = first[at, :] * spread_lanes(rowpack, b)

    def weigh(r):
        def body(t, carry):
            at = pl.ds(pl.multiple_of(r * (rows // 2) + t * TILE, TILE), TILE)
            mul = scale[at, :]
            for c in range(chunks):
                weights[at, lane(c)] = (scores[at, lane(c)] * mul).astype(jnp.bfloat16)
            return carry

        lax.fori_loop(0, tiles // 2, body, 0, unroll=2)

    def swap_copy(i, to):
        return remote(swap.at[0], swap.at[i], swap_send.at[i], swap_recv.at[i], to)

    def potentials():
        for c in range(chunks):
            sqy[pl.ds(c, 1), :] = jnp.sum(data_part[pl.ds(c * LANES, LANES), :].T, axis=0, keepdims=True)
        cols_pot = (col_pot + jnp.log(ratio) * LOG2E + (log_rows - log_cols)) / kappa + sqy[...] / width
        colpack[...] = cols_pot
        cols_out[...] = colpack[pl.ds(pl.multiple_of(side * 8, 8), 8), :]
        for b in range(row_blocks):
            sqx[pl.ds(b, 1), :] = shift[pl.ds(b * LANES, LANES), :].T[0:1]
        swap[0] = -(log_rows + row_lse + jnp.log(total) * LOG2E + sqx[...]) / kappa
        begin(swap_copy(1, sibling))
        for i in (0, 1):
            begin(remote(
                swap.at[0], swap.at[2 + core], swap_send.at[2 + i], swap_recv.at[2 + core], device(partner, y, z, i)
            ))

    strip = rows // 2

    def half_rows(r):
        return pl.ds(r * strip, strip)

    def block_x(b):
        return jnp.where(b < 2, jnp.where(b == 0, opposite, partner), jnp.where(b == 2, mate, x))

    def product(p, r, to_z):
        cut = pl.ds(pl.multiple_of(lax.rem(to_z, 2) * LANES, LANES), LANES)
        total = None
        for k in (0, 1):
            block = jnp.concatenate(
                [data_all[k, block_x(2 * p + e) * 2 + to_z // 2, :, cut] for e in (0, 1)], axis=1
            )
            value = jnp.dot(
                weights[half_rows(r), k * full_cols:(k + 1) * full_cols], block,
                preferred_element_type=jnp.float32,
            )
            total = value if total is None else total + value
        return total

    def sum_copy(b, t, index, src, dst):
        to = device(x, y, around(z + HOP[t]), core)
        return remote(src, dst, sum_send.at[b, t, index], sum_recv.at[b, t, index], to)

    def far_copy(b, t):
        return sum_copy(b, t, 0, out_buf.at[b, 2, half_rows(t)], far_buf.at[b, t])

    def direct_copy(b, t):
        at = half_rows(1 - t)
        return sum_copy(b, t, 1, out_buf.at[b, t, at], near_buf.at[b, t, at])

    def added_copy(b, t):
        at = half_rows(t)
        return sum_copy(b, t, 2, out_buf.at[b, t, at], near_buf.at[b, t, at])

    def in_copy(b, g, a, to):
        return remote(own_buf.at[b], in_sum.at[g, a], in_send.at[b], in_recv.at[g, a], to)

    def out_copy(b):
        return in_copy(b, 1 - lax.rem(b, 2), core, device(block_x(b), y, z, kind))

    def add_far(b):
        for t in (0, 1):
            far_copy(b, t).wait_recv()
            out_buf[b, t, half_rows(t), :] = (keep[b, t] + far_buf[b, t].astype(jnp.float32)).astype(jnp.bfloat16)
            added_copy(b, t).start()

    def add_near(b):
        for t in (0, 1):
            direct_copy(b, t).wait_recv()
            added_copy(b, t).wait_recv()
        own_buf[b] = own_buf[b] + near_buf[b, 0].astype(jnp.float32) + near_buf[b, 1].astype(jnp.float32)

    def send_pair(p, carry):
        @pl.when(p == 0)
        def _():
            weigh(0)

        for t in (0, 1):
            if t == 1:
                @pl.when(p == 0)
                def _():
                    weigh(1)

            value = product(p, t, around(z + 2))
            for e in (0, 1):
                out_buf[2 * p + e, 2, half_rows(t), :] = value[:, lane(e)].astype(jnp.bfloat16)
            far_copy(2 * p, t).start()

        @pl.when(p > 0)
        def _():
            add_near(0)
            out_copy(0).start()

        for t in (0, 1):
            value = product(p, 1 - t, around(z + HOP[t]))
            for e in (0, 1):
                out_buf[2 * p + e, t, half_rows(1 - t), :] = value[:, lane(e)].astype(jnp.bfloat16)
            direct_copy(2 * p, t).start()
            value = product(p, t, around(z + HOP[t]))
            for e in (0, 1):
                keep[2 * p + e, t] = value[:, lane(e)]

        @pl.when(p > 0)
        def _():
            add_far(1)

        @pl.when(p == 0)
        def _():
            add_far(0)

        for t in (0, 1):
            far_copy(2 * p + 1, t).start()
        for t in (0, 1):
            direct_copy(2 * p + 1, t).start()
        for r in (0, 1):
            value = product(p, r, z)
            for e in (0, 1):
                own_buf[2 * p + e, half_rows(r), :] = value[:, lane(e)]
        return carry

    lax.fori_loop(0, 2, send_pair, 0)
    add_far(2)
    potentials()
    add_near(1)
    out_copy(1).start()
    add_near(2)
    out_copy(2).start()
    add_far(3)

    swap_copy(1, sibling).wait_recv()
    for i in (0, 1):
        remote(swap.at[0], swap.at[2 + i], swap_send.at[2 + i], swap_recv.at[2 + i], sibling).wait_recv()
    half = rows // LANES
    for a in (0, 1):
        mine_row = jnp.where(core == a, swap[0], swap[1])
        rows_out[pl.ds(a * half, half), :] = jnp.where(home, mine_row, swap[2 + a])

    add_near(3)

    @pl.when(home)
    def _():
        in_sum[0, core] = own_buf[3]

    @pl.when(jnp.logical_not(home))
    def _():
        out_copy(3).start()

    def wait_in(g, a):
        in_copy(0, g, a, sibling).wait_recv()

    wait_in(1, 0)
    wait_in(1, 1)
    wait_in(0, 1 - core)

    @pl.when(jnp.logical_not(home))
    def _():
        wait_in(0, core)

    for a in (0, 1):
        in_sum[0, a] = in_sum[0, a] + in_sum[1, a]
        pltpu.make_async_copy(in_sum.at[0, a], targets.at[pl.ds(a * rows, rows)], local_sems.at[a]).start()

    def settle(b, carry):
        for t in (0, 1):
            far_copy(b, t).wait_send()
            direct_copy(b, t).wait_send()
            added_copy(b, t).wait_send()
        return carry

    lax.fori_loop(0, SIDE, settle, 0)
    for a in (0, 1):
        pltpu.make_async_copy(in_sum.at[0, a], targets.at[pl.ds(a * rows, rows)], local_sems.at[a]).wait()
    for b in range(SIDE - 1):
        out_copy(b).wait_send()

    @pl.when(jnp.logical_not(home))
    def _():
        out_copy(3).wait_send()

    for copy in started:
        copy.wait_send()

    @pl.when(home)
    def _():
        aside.wait_send()


def shards(noise_latents, data_latents):
    nsize = lax.axis_size("noise")
    dsize = lax.axis_size("dp")
    block, piece = noise_latents.shape
    rows, cols = block // 2, 2 * data_latents.shape[0]
    rsize, csize = dsize // 2, nsize * 2
    vmem = pl.BlockSpec(memory_space=pltpu.VMEM)
    f32, bf16 = jnp.float32, jnp.bfloat16
    strip = rows // 2
    row_vec, col_vec = (rows // LANES, LANES), (cols // LANES, LANES)
    sems = pltpu.SemaphoreType.DMA
    targets, rows_pot, cols_pot = pl.pallas_call(
        functools.partial(kernel, rsize, csize, piece * dsize),
        out_shape=(
            jax.ShapeDtypeStruct((block, piece), f32),
            jax.ShapeDtypeStruct((block // LANES, LANES), f32),
            jax.ShapeDtypeStruct((cols // 2 // LANES, LANES), f32),
        ),
        in_specs=[pl.BlockSpec(memory_space=pl.ANY)] * 2,
        out_specs=(pl.BlockSpec(memory_space=pl.ANY), vmem, vmem),
        scratch_shapes=[
            pltpu.VMEM((dsize, rows, piece), bf16),
            pltpu.VMEM((2, nsize) + data_latents.shape, bf16),
            pltpu.VMEM((rows, cols), f32),
            pltpu.VMEM((rows, cols), bf16),
            pltpu.VMEM((rows, LANES), f32),
            pltpu.VMEM((rows, LANES), f32),
            pltpu.VMEM((rows, LANES), f32),
            pltpu.VMEM((rows, LANES), f32),
            pltpu.VMEM((cols, LANES), f32),
            pltpu.VMEM((8, cols), f32),
            pltpu.VMEM(row_vec, f32),
            pltpu.VMEM(col_vec, f32),
            pltpu.VMEM(row_vec, f32),
            pltpu.VMEM(col_vec, f32),
            pltpu.VMEM((4,) + row_vec, f32),
            pltpu.VMEM((ITERS, csize, 2) + col_vec, f32),
            pltpu.VMEM((ITERS, rsize, 2) + row_vec, f32),
            pltpu.VMEM((SIDE, 3, rows, LANES), bf16),
            pltpu.VMEM((SIDE, rows, LANES), f32),
            pltpu.VMEM((SIDE, 2, strip, LANES), bf16),
            pltpu.VMEM((SIDE, 2, rows, LANES), bf16),
            pltpu.VMEM((2, 2, rows, LANES), f32),
            sems((ITERS,)),
            sems((ITERS,)),
            sems((ITERS,)),
            sems((ITERS,)),
            sems((4,)),
            sems((4,)),
            sems((4,)),
            sems((4,)),
            sems((SIDE, 2, 2)),
            sems((SIDE, 2, 2)),
            sems((2, 13)),
            sems((2, 13)),
            sems((SIDE, 2, 3)),
            sems((SIDE, 2, 3)),
            sems((SIDE,)),
            sems((2, 2)),
            pltpu.VMEM((SIDE, 2, strip, LANES), f32),
            sems((2,)),
        ],
        compiler_params=pltpu.CompilerParams(
            collective_id=0, has_side_effects=True, vmem_limit_bytes=60 * 2**20
        ),
    )(noise_latents, data_latents)
    return targets, rows_pot.reshape(block), cols_pot.reshape(cols // 2)


def solution(mesh):
    return jax.shard_map(
        shards,
        mesh=mesh,
        in_specs=(P("noise", "dp"), P("dp", "noise")),
        out_specs=(P("noise", "dp"), P("noise"), P("dp")),
        check_vma=False,
    )
```

```python
import functools
import math

import jax
import jax.numpy as jnp
from jax import lax
from jax.experimental import pallas as pl
from jax.experimental.pallas import tpu as pltpu
from jax.sharding import PartitionSpec as P

ITERS = 3
EPSILON = 0.04
LOG2E = 1.0 / math.log(2.0)
MESH = pl.DeviceIdType.MESH
LANES = 128
TILE = 32
SIDE = 4


def wrap(index, size):
    return lax.rem(index, size)


def spread_lanes(ref, row):
    return jnp.broadcast_to(ref[pl.ds(row, 1), :], (LANES, LANES)).T


def exchange(buf, send, recv, step, parts, me, size, peer_id, started):
    for k in range(1, size):
        pltpu.make_async_remote_copy(
            src_ref=buf.at[step, me, pl.ds(0, parts)],
            dst_ref=buf.at[step, me, pl.ds(0, parts)],
            send_sem=send.at[step],
            recv_sem=recv.at[step],
            device_id=peer_id(wrap(me + k, size)),
            device_id_type=MESH,
        ).start()
    slots = buf.at[step, pl.ds(0, size - 1), pl.ds(0, parts)]
    every = pltpu.make_async_remote_copy(
        src_ref=slots,
        dst_ref=slots,
        send_sem=send.at[step],
        recv_sem=recv.at[step],
        device_id=peer_id(wrap(me + 1, size)),
        device_id_type=MESH,
    )
    every.wait_recv()
    started.append(every)


def combine(buf, step, size):
    top = buf[step, 0, 0]
    for s in range(1, size):
        top = jnp.maximum(top, buf[step, s, 0])
    total = buf[step, 0, 1] * jnp.exp2(buf[step, 0, 0] - top)
    for s in range(1, size):
        total = total + buf[step, s, 1] * jnp.exp2(buf[step, s, 0] - top)
    return top, total


def add_slots(buf, step, size):
    total = buf[step, 0, 0]
    for s in range(1, size):
        total = total + buf[step, s, 0]
    return total


def kernel(
    rsize, csize, width,
    noise_ref, data_ref,
    targets, rows_out, cols_out,
    noise_all, data_all, scores, weights,
    shift, first, scale, part, data_part, colvec, rowpack, colpack, sqx, sqy, swap,
    col_buf, row_buf, out_buf, own_buf, far_buf, near_buf, in_sum,
    col_send, col_recv, row_send, row_recv, swap_send, swap_recv,
    cross_send, cross_recv, noise_send, noise_recv, data_send, data_recv,
    sum_send, sum_recv, in_send, in_recv, keep, local_sems, relay_in, mate_out, mate_in,
):
    rows, cols = scores.shape
    n = lax.axis_index("noise")
    d = lax.axis_index("dp")
    x, z = d // SIDE, lax.rem(d, SIDE)
    y, core = n // 2, lax.rem(n, 2)
    kind = lax.rem((x + 1) // 2, 2)
    pair = x // 2
    side = lax.rem(x, 2)
    home = core == kind
    kappa = LOG2E / EPSILON
    log_rows = math.log2(rows * csize)
    log_cols = math.log2(cols * rsize)
    chunks = cols // LANES
    row_blocks = rows // LANES
    tiles = rows // TILE
    started = []

    def around(value):
        return lax.rem(value + SIDE, SIDE)

    def device(xi, yi, zi, ci):
        return (yi * 2 + ci, xi * SIDE + zi)

    def x_at(which, of_kind):
        return which * (3 - 2 * of_kind) + of_kind

    me_row = pair * SIDE + z
    me_col = y * 4 + kind * 2 + core

    def row_peer(p):
        return device(x_at(p // SIDE, kind), y, lax.rem(p, SIDE), core)

    def col_peer(p):
        return device(x_at(pair, lax.rem(p // 2, 2)), p // 4, z, lax.rem(p, 2))

    sibling = device(x, y, z, 1 - core)
    partner = x + 1 - 2 * side
    mate = SIDE - 1 - x
    opposite = around(x + 2)

    barrier = pltpu.get_barrier_semaphore()
    greeted = [row_peer(wrap(me_row + k, rsize)) for k in range(1, rsize)]
    greeted += [col_peer(wrap(me_col + k, csize)) for k in range(1, csize)]
    greeted += [device(opposite, y, z, 0), device(opposite, y, z, 1), device(mate, y, z, 1 - core)]
    for to in greeted:
        pl.semaphore_signal(barrier, inc=1, device_id=to, device_id_type=MESH)
    pl.semaphore_wait(barrier, len(greeted))

    def remote(src, dst, send, recv, to):
        return pltpu.make_async_remote_copy(
            src_ref=src, dst_ref=dst, send_sem=send, recv_sem=recv, device_id=to, device_id_type=MESH
        )

    def begin(copy):
        copy.start()
        started.append(copy)

    def lane(c):
        return slice(LANES * c, LANES * (c + 1))

    HOP = (1, -1)
    ORDER = (0, 1, 3, 2)
    own = x * SIDE + z

    def cross_copy(i, half, to):
        return remote(
            noise_ref.at[pl.ds(half * rows, rows)], noise_all.at[own], cross_send.at[i], cross_recv.at[x], to
        )

    def cross_wait(xi):
        remote(
            noise_ref.at[pl.ds(0, rows)], noise_all.at[xi * SIDE + z], cross_send.at[0], cross_recv.at[xi], sibling
        ).wait_recv()

    there = jnp.where(home, mate, partner)
    aside = cross_copy(2, 1 - core, sibling)

    def noise_copy(xi, t, forward, slot):
        at = pl.ds(t * (rows // 2), rows // 2) if forward else pl.ds(0, rows)
        f = int(forward)
        return remote(
            noise_all.at[slot, at], noise_all.at[slot, at],
            noise_send.at[xi, t, f], noise_recv.at[xi, t, f], device(x, y, around(z + HOP[t]), core),
        )

    def noise_wait(xi, t, forward):
        slot = xi * SIDE + around(z - HOP[t] * (2 if forward else 1))
        noise_copy(xi, t, forward, slot).wait_recv()
        return slot

    def data_copy(r, index, where, lo, size, to, own=False):
        at = pl.ds(lo, size)
        block = side if r == 0 else 1 - side
        dst = data_all.at[block, where, at]
        return remote(data_ref.at[at] if own else dst, dst, data_send.at[r, index], data_recv.at[r, index], to)

    half_cols = cols // 4
    full_cols = cols // 2

    def along_y(step, c):
        return around(y + step) * 2 + c

    def data_wait(r, index, where, lo, size):
        data_copy(r, index, where, lo, size, sibling).wait_recv()

    HALF = 9

    def cross_data(h, own=False):
        at = pl.ds(h * half_cols, half_cols)
        dst = data_all.at[side if own else 1 - side, n, at]
        return remote(
            data_ref.at[at], dst, data_send.at[1, 11 + h], data_recv.at[1, 11 + h], device(partner, y, z, core)
        )

    def partner_y(t, h, back=0):
        where = around(y + back) * 2 + core
        to = device(x, around(y + HOP[t]), z, core)
        return t if h == 0 else HALF + t, where, h * half_cols, half_cols, to

    def partner_wait(t, h):
        data_copy(1, *partner_y(t, h, -HOP[t])).wait_recv()

    begin(cross_copy(0, 0, device(there, y, z, 0)))
    begin(cross_copy(1, 1, device(there, y, z, 1)))

    @pl.when(home)
    def _():
        aside.start()

    for t in (0, 1):
        begin(data_copy(0, t, n, 0, full_cols, device(x, around(y + HOP[t]), z, core), own=True))
    for h in (0, 1):
        begin(cross_data(h, own=True))
    begin(data_copy(0, 4, n, 0, full_cols, sibling, own=True))

    @pl.when(home)
    def _():
        pltpu.make_async_copy(
            noise_ref.at[pl.ds(pl.multiple_of(core * rows, rows), rows)], noise_all.at[own], local_sems.at[0]
        ).start()

    data_own = pltpu.make_async_copy(data_ref, data_all.at[side, n], local_sems.at[1])
    data_own.start()

    @pl.when(home)
    def _():
        pltpu.make_async_copy(
            noise_ref.at[pl.ds(pl.multiple_of(core * rows, rows), rows)], noise_all.at[own], local_sems.at[0]
        ).wait()

    @pl.when(jnp.logical_not(home))
    def _():
        cross_wait(x)

    for t in (0, 1):
        begin(noise_copy(x, t, False, own))
    scores[...] = jnp.zeros_like(scores)
    part[...] = jnp.zeros_like(part)
    data_part[...] = jnp.zeros_like(data_part)
    for xi in (mate, partner):
        cross_wait(xi)
        for t in (0, 1):
            begin(noise_copy(xi, t, False, xi * SIDE + z))
    slot = partner * SIDE + z
    begin(remote(
        noise_all.at[slot], noise_all.at[slot], cross_send.at[3], cross_recv.at[partner], device(mate, y, z, core)
    ))
    cross_data(0).wait_recv()
    for t in (0, 1):
        begin(data_copy(1, *partner_y(t, 0)))
    for t in (0, 1):
        where = along_y(-HOP[t], core)
        data_wait(0, t, where, 0, full_cols)
        begin(data_copy(0, 2 + t, where, t * half_cols, half_cols, device(x, around(y + HOP[t]), z, core)))
        begin(data_copy(0, 5 + t, where, 0, full_cols, sibling))
    cross_data(1).wait_recv()
    for t in (0, 1):
        begin(data_copy(1, *partner_y(t, 1)))
    begin(data_copy(1, 4, n, 0, full_cols, sibling))
    cross_wait(opposite)
    for t in (0, 1):
        begin(noise_copy(opposite, t, False, opposite * SIDE + z))
    by_data = [around(y + step) for step in ORDER]
    for xi in by_data:
        for t in (0, 1):
            begin(noise_copy(xi, t, True, noise_wait(xi, t, False)))

    def squares(block):
        value = block.astype(jnp.float32)
        return value * value

    def chunk_product(q, m):
        both = jnp.concatenate([noise_all[2 * q], noise_all[2 * q + 1]], axis=1)
        cut = pl.ds(pl.multiple_of(m * 256, 256), 256)
        piece = data_all[m // 4, q, pl.ds(pl.multiple_of(lax.rem(m, 4) * 256, 256), 256), :]
        data_part[cut, :] += squares(piece[:, :LANES]) + squares(piece[:, LANES:])
        return lax.dot_general(both, piece, (((1,), (1,)), ((), ())), preferred_element_type=jnp.float32)

    def norms(q):
        def norm(r, carry):
            cut = pl.ds(pl.multiple_of(r * 64, 64), 64)
            part[cut, :] += squares(noise_all[2 * q, cut, :]) + squares(noise_all[2 * q + 1, cut, :])
            return carry

        lax.fori_loop(0, rows // 64, norm, 0)

    near, other_block = side * 4, 4 - side * 4

    def unit(q, block):
        def column(m, carry):
            cut = pl.ds(pl.multiple_of((block + m) * 256, 256), 256)
            scores[:, cut] += chunk_product(q, block + m)
            return carry

        lax.fori_loop(0, 4, column, 0)

    mine = z // 2

    def own_unit(q):
        unit(q, near)
        norms(q)

    def forward_wait(xi):
        for t in (0, 1):
            noise_wait(xi, t, True)

    def pass_on(t):
        where = along_y(-HOP[t], core)
        begin(data_copy(1, 2 + t, where, t * half_cols, half_cols, device(x, around(y + HOP[t]), z, core)))

    partner_wait(0, 0)
    pass_on(0)
    partner_wait(1, 0)
    data_own.wait()
    data_wait(0, 4, along_y(0, 1 - core), 0, full_cols)
    for t in (0, 1):
        data_wait(0, 5 + t, along_y(-HOP[t], 1 - core), 0, full_cols)

    def early(i, carry):
        own_unit(around(y + i + i // 2) * 2 + mine)
        return carry

    lax.fori_loop(0, 3, early, 0)
    for t in (0, 1):
        where = along_y(2, core)
        data_wait(0, 2 + t, where, t * half_cols, half_cols)
        begin(data_copy(0, 7 + t, where, t * half_cols, half_cols, sibling))

    forward_wait(by_data[0])
    own_unit(y * 2 + 1 - mine)
    data_wait(1, 4, along_y(0, 1 - core), 0, full_cols)

    def partner_mid(i, carry):
        unit(y * 2 + i, other_block)
        return carry

    lax.fori_loop(0, 2, partner_mid, 0)
    for t in (0, 1):
        data_wait(0, 7 + t, along_y(2, 1 - core), t * half_cols, half_cols)
    own_unit(around(y + 2) * 2 + mine)
    partner_wait(1, 1)
    pass_on(1)
    partner_wait(0, 1)
    for t in (0, 1):
        begin(data_copy(1, 5 + t, along_y(-HOP[t], core), 0, full_cols, sibling))
    for xi in by_data[1:3]:
        forward_wait(xi)
        own_unit(xi * 2 + 1 - mine)
    for t in (0, 1):
        data_wait(1, 5 + t, along_y(-HOP[t], 1 - core), 0, full_cols)

    def partner_late(i, carry):
        unit(around(y + 1 + 2 * (i // 2)) * 2 + lax.rem(i, 2), other_block)
        return carry

    lax.fori_loop(0, 4, partner_late, 0)
    for t in (0, 1):
        where = along_y(2, core)
        data_wait(1, 2 + t, where, t * half_cols, half_cols)
        begin(data_copy(1, 7 + t, where, t * half_cols, half_cols, sibling))
    forward_wait(by_data[3])
    for t in (0, 1):
        data_wait(1, 7 + t, along_y(2, 1 - core), t * half_cols, half_cols)

    factor = 2.0 * kappa / width
    q_mine, q_other = around(y + 2) * 2 + mine, around(y + 2) * 2 + 1 - mine
    norms(q_other)

    def row_shift(r, carry):
        at = pl.ds(pl.multiple_of(r * 128, 128), 128)
        total = jnp.sum(part[at, :], axis=1, keepdims=True) * (-kappa / width)
        shift[at, :] = jnp.broadcast_to(total, (128, LANES))
        return carry

    lax.fori_loop(0, rows // 128, row_shift, 0)

    def final(block, qs):
        def column(i, carry):
            m = block + i
            cut = pl.ds(pl.multiple_of(m * 256, 256), 256)
            value = scores[:, cut]
            for q in qs:
                value = value + chunk_product(q, m)
            value = value * factor
            scores[:, cut] = value
            for e in (0, 1):
                top = jnp.max(value[:, LANES * e:LANES * (e + 1)] + shift[...], axis=0, keepdims=True)
                col_buf[0, me_col, 0, pl.ds(2 * m + e, 1), :] = top
                colvec[:, pl.ds(pl.multiple_of(m * 256 + e * LANES, LANES), LANES)] = jnp.broadcast_to(top, (8, LANES))
            return carry

        lax.fori_loop(0, 4, column, 0)

    final(near, (q_other,))
    final(other_block, (q_mine, q_other))

    def fold(block, op):
        out = block[0:8]
        for r in range(1, TILE // 8):
            out = op(out, block[8 * r:8 * r + 8])
        return out

    def spread_cols():
        for c in range(chunks):
            colvec[:, lane(c)] = jnp.broadcast_to(colpack[pl.ds(c, 1), :], (8, LANES))

    def tall(ref, c):
        return jnp.concatenate([ref[:, lane(c)]] * (TILE // 8), axis=0)

    def tile_at(t):
        return pl.ds(pl.multiple_of(t * TILE, TILE), TILE)

    def loop(body, init):
        return lax.fori_loop(0, tiles, body, init, unroll=2)

    zeros = tuple(jnp.zeros((8, LANES), jnp.float32) for _ in range(chunks))

    def exp_step(t, accs):
        at = tile_at(t)
        add = shift[at, :]
        return tuple(
            accs[c] + fold(jnp.exp2(scores[at, lane(c)] + add - tall(colvec, c)), jnp.add)
            for c in range(chunks)
        )

    sums = loop(exp_step, zeros)
    for c in range(chunks):
        col_buf[0, me_col, 1, pl.ds(c, 1), :] = jnp.sum(sums[c], axis=0, keepdims=True)
    exchange(col_buf, col_send, col_recv, 0, 2, me_col, csize, col_peer, started)
    top, total = combine(col_buf, 0, csize)
    col_pot = -log_cols - top - jnp.log(total) * LOG2E
    colpack[...] = col_pot
    spread_cols()

    def row_step(t, carry):
        at = tile_at(t)
        top = scores[at, lane(0)] + tall(colvec, 0)
        for c in range(1, chunks):
            top = jnp.maximum(top, scores[at, lane(c)] + tall(colvec, c))
        first[at, :] = top
        total = None
        for c in range(chunks):
            value = jnp.exp2(scores[at, lane(c)] + tall(colvec, c) - top)
            scores[at, lane(c)] = value
            total = value if total is None else total + value
        part[at, :] = total
        return carry

    loop(row_step, 0)
    for b in range(row_blocks):
        at = pl.ds(b * LANES, LANES)
        tops = first[at, :].T
        top = jnp.max(tops, axis=0, keepdims=True)
        row_buf[0, me_row, 0, pl.ds(b, 1), :] = top
        row_buf[0, me_row, 1, pl.ds(b, 1), :] = jnp.sum(part[at, :].T * jnp.exp2(tops - top), axis=0, keepdims=True)
    exchange(row_buf, row_send, row_recv, 0, 2, me_row, rsize, row_peer, started)
    top, total = combine(row_buf, 0, rsize)
    row_lse = top + jnp.log(total) * LOG2E
    rowpack[...] = row_lse
    for b in range(row_blocks):
        at = pl.ds(b * LANES, LANES)
        base = jnp.exp2(first[at, :] - spread_lanes(rowpack, b))
        first[at, :] = base
        scale[at, :] = base

    def col_step(t, accs):
        at = tile_at(t)
        mul = scale[at, :]
        return tuple(accs[c] + fold(scores[at, lane(c)] * mul, jnp.add) for c in range(chunks))

    def sum_step(keep_values):
        def body(t, carry):
            at = tile_at(t)
            total = None
            for c in range(chunks):
                value = scores[at, lane(c)] * tall(colvec, c)
                if keep_values:
                    scores[at, lane(c)] = value
                total = value if total is None else total + value
            part[at, :] = total * first[at, :]
            return carry

        return body

    for step in range(1, ITERS):
        sums = loop(col_step, zeros)
        for c in range(chunks):
            col_buf[step, me_col, 0, pl.ds(c, 1), :] = jnp.sum(sums[c], axis=0, keepdims=True)
        exchange(col_buf, col_send, col_recv, step, 1, me_col, csize, col_peer, started)
        ratio = 1.0 / add_slots(col_buf, step, csize)
        colpack[...] = ratio
        spread_cols()
        loop(sum_step(step == ITERS - 1), 0)
        for b in range(row_blocks):
            at = pl.ds(b * LANES, LANES)
            row_buf[step, me_row, 0, pl.ds(b, 1), :] = jnp.sum(part[at, :].T, axis=0, keepdims=True)
        exchange(row_buf, row_send, row_recv, step, 1, me_row, rsize, row_peer, started)
        total = add_slots(row_buf, step, rsize)
        rowpack[...] = 1.0 / total
        for b in range(row_blocks):
            at = pl.ds(b * LANES, LANES)
            scale[at, :] = first[at, :] * spread_lanes(rowpack, b)

    def weigh(r):
        def body(t, carry):
            at = pl.ds(pl.multiple_of(r * (rows // 2) + t * TILE, TILE), TILE)
            mul = scale[at, :]
            for c in range(chunks):
                weights[at, lane(c)] = (scores[at, lane(c)] * mul).astype(jnp.bfloat16)
            return carry

        lax.fori_loop(0, tiles // 2, body, 0, unroll=2)

    def swap_copy(i, to):
        return remote(swap.at[0], swap.at[i], swap_send.at[i], swap_recv.at[i], to)

    def potentials():
        for c in range(chunks):
            sqy[pl.ds(c, 1), :] = jnp.sum(data_part[pl.ds(c * LANES, LANES), :].T, axis=0, keepdims=True)
        cols_pot = (col_pot + jnp.log(ratio) * LOG2E + (log_rows - log_cols)) / kappa + sqy[...] / width
        colpack[...] = cols_pot
        cols_out[...] = colpack[pl.ds(pl.multiple_of(side * 8, 8), 8), :]
        for b in range(row_blocks):
            sqx[pl.ds(b, 1), :] = shift[pl.ds(b * LANES, LANES), :].T[0:1]
        swap[0] = -(log_rows + row_lse + jnp.log(total) * LOG2E + sqx[...]) / kappa
        begin(swap_copy(1, sibling))
        for i in (0, 1):
            begin(remote(
                swap.at[0], swap.at[2 + core], swap_send.at[2 + i], swap_recv.at[2 + core], device(partner, y, z, i)
            ))

    strip = rows // 2

    def half_rows(r):
        return pl.ds(r * strip, strip)

    def block_x(b):
        return jnp.where(b < 2, jnp.where(b == 0, opposite, partner), jnp.where(b == 2, mate, x))

    def product(p, r, to_z):
        cut = pl.ds(pl.multiple_of(lax.rem(to_z, 2) * LANES, LANES), LANES)
        total = None
        for k in (0, 1):
            block = jnp.concatenate(
                [data_all[k, block_x(2 * p + e) * 2 + to_z // 2, :, cut] for e in (0, 1)], axis=1
            )
            value = jnp.dot(
                weights[half_rows(r), k * full_cols:(k + 1) * full_cols], block,
                preferred_element_type=jnp.float32,
            )
            total = value if total is None else total + value
        return total

    def sum_copy(b, t, index, src, dst):
        to = device(x, y, around(z + HOP[t]), core)
        return remote(src, dst, sum_send.at[b, t, index], sum_recv.at[b, t, index], to)

    def far_copy(b, t):
        return sum_copy(b, t, 0, out_buf.at[b, 2, half_rows(t)], far_buf.at[b, t])

    def direct_copy(b, t):
        at = half_rows(1 - t)
        return sum_copy(b, t, 1, out_buf.at[b, t, at], near_buf.at[b, t, at])

    def added_copy(b, t):
        at = half_rows(t)
        return sum_copy(b, t, 2, out_buf.at[b, t, at], near_buf.at[b, t, at])

    def relay_copy():
        return remote(own_buf.at[0], relay_in, in_send.at[0], in_recv.at[4], device(mate, y, z, core))

    def partner_copy(a):
        return remote(own_buf.at[1], in_sum.at[a], in_send.at[1], in_recv.at[a], device(partner, y, z, kind))

    def mate_copy(a):
        return remote(mate_out, mate_in.at[a], in_send.at[2], in_recv.at[2 + a], device(mate, y, z, kind))

    def stay_copy(a):
        return remote(own_buf.at[3], in_sum.at[a], in_send.at[3], in_recv.at[a], sibling)

    def add_far(b):
        for t in (0, 1):
            far_copy(b, t).wait_recv()
            out_buf[b, t, half_rows(t), :] = (keep[b, t] + far_buf[b, t].astype(jnp.float32)).astype(jnp.bfloat16)
            added_copy(b, t).start()

    def add_near(b):
        for t in (0, 1):
            direct_copy(b, t).wait_recv()
            added_copy(b, t).wait_recv()
        own_buf[b] = own_buf[b] + near_buf[b, 0].astype(jnp.float32) + near_buf[b, 1].astype(jnp.float32)

    def send_pair(p, carry):
        @pl.when(p == 0)
        def _():
            weigh(0)

        for t in (0, 1):
            if t == 1:
                @pl.when(p == 0)
                def _():
                    weigh(1)

            value = product(p, t, around(z + 2))
            for e in (0, 1):
                out_buf[2 * p + e, 2, half_rows(t), :] = value[:, lane(e)].astype(jnp.bfloat16)
            far_copy(2 * p, t).start()

        @pl.when(p > 0)
        def _():
            add_near(0)
            relay_copy().start()

        for t in (0, 1):
            value = product(p, 1 - t, around(z + HOP[t]))
            for e in (0, 1):
                out_buf[2 * p + e, t, half_rows(1 - t), :] = value[:, lane(e)].astype(jnp.bfloat16)
            direct_copy(2 * p, t).start()
            value = product(p, t, around(z + HOP[t]))
            for e in (0, 1):
                keep[2 * p + e, t] = value[:, lane(e)]

        @pl.when(p > 0)
        def _():
            add_far(1)

        @pl.when(p == 0)
        def _():
            add_far(0)

        for t in (0, 1):
            far_copy(2 * p + 1, t).start()
        for t in (0, 1):
            direct_copy(2 * p + 1, t).start()
        for r in (0, 1):
            value = product(p, r, z)
            for e in (0, 1):
                own_buf[2 * p + e, half_rows(r), :] = value[:, lane(e)]
        return carry

    lax.fori_loop(0, 2, send_pair, 0)
    add_far(2)
    potentials()
    add_near(1)
    relay_copy().wait_recv()
    own_buf[1] = own_buf[1] + relay_in[...]
    partner_copy(core).start()
    add_near(2)
    mate_out[...] = own_buf[2].astype(jnp.bfloat16)
    mate_copy(core).start()
    add_far(3)

    swap_copy(1, sibling).wait_recv()
    for i in (0, 1):
        remote(swap.at[0], swap.at[2 + i], swap_send.at[2 + i], swap_recv.at[2 + i], sibling).wait_recv()
    half = rows // LANES
    for a in (0, 1):
        mine_row = jnp.where(core == a, swap[0], swap[1])
        rows_out[pl.ds(a * half, half), :] = jnp.where(home, mine_row, swap[2 + a])

    add_near(3)

    @pl.when(home)
    def _():
        in_sum[core] = own_buf[3]
        stay_copy(1 - core).wait_recv()
        for a in (0, 1):
            mate_copy(a).wait_recv()
            in_sum[a] = in_sum[a] + mate_in[a].astype(jnp.float32)

    @pl.when(jnp.logical_not(home))
    def _():
        stay_copy(core).start()
        for a in (0, 1):
            partner_copy(a).wait_recv()

    def result_copy(a):
        return pltpu.make_async_copy(in_sum.at[a], targets.at[pl.ds(a * rows, rows)], local_sems.at[a])

    for a in (0, 1):
        result_copy(a).start()

    def settle(b, carry):
        for t in (0, 1):
            far_copy(b, t).wait_send()
            direct_copy(b, t).wait_send()
            added_copy(b, t).wait_send()
        return carry

    lax.fori_loop(0, SIDE, settle, 0)
    for a in (0, 1):
        result_copy(a).wait()
    relay_copy().wait_send()
    partner_copy(core).wait_send()
    mate_copy(core).wait_send()

    @pl.when(jnp.logical_not(home))
    def _():
        stay_copy(core).wait_send()

    for copy in started:
        copy.wait_send()

    @pl.when(home)
    def _():
        aside.wait_send()


def shards(noise_latents, data_latents):
    nsize = lax.axis_size("noise")
    dsize = lax.axis_size("dp")
    block, piece = noise_latents.shape
    rows, cols = block // 2, 2 * data_latents.shape[0]
    rsize, csize = dsize // 2, nsize * 2
    vmem = pl.BlockSpec(memory_space=pltpu.VMEM)
    f32, bf16 = jnp.float32, jnp.bfloat16
    strip = rows // 2
    row_vec, col_vec = (rows // LANES, LANES), (cols // LANES, LANES)
    sems = pltpu.SemaphoreType.DMA
    targets, rows_pot, cols_pot = pl.pallas_call(
        functools.partial(kernel, rsize, csize, piece * dsize),
        out_shape=(
            jax.ShapeDtypeStruct((block, piece), f32),
            jax.ShapeDtypeStruct((block // LANES, LANES), f32),
            jax.ShapeDtypeStruct((cols // 2 // LANES, LANES), f32),
        ),
        in_specs=[pl.BlockSpec(memory_space=pl.ANY)] * 2,
        out_specs=(pl.BlockSpec(memory_space=pl.ANY), vmem, vmem),
        scratch_shapes=[
            pltpu.VMEM((dsize, rows, piece), bf16),
            pltpu.VMEM((2, nsize) + data_latents.shape, bf16),
            pltpu.VMEM((rows, cols), f32),
            pltpu.VMEM((rows, cols), bf16),
            pltpu.VMEM((rows, LANES), f32),
            pltpu.VMEM((rows, LANES), f32),
            pltpu.VMEM((rows, LANES), f32),
            pltpu.VMEM((rows, LANES), f32),
            pltpu.VMEM((cols, LANES), f32),
            pltpu.VMEM((8, cols), f32),
            pltpu.VMEM(row_vec, f32),
            pltpu.VMEM(col_vec, f32),
            pltpu.VMEM(row_vec, f32),
            pltpu.VMEM(col_vec, f32),
            pltpu.VMEM((4,) + row_vec, f32),
            pltpu.VMEM((ITERS, csize, 2) + col_vec, f32),
            pltpu.VMEM((ITERS, rsize, 2) + row_vec, f32),
            pltpu.VMEM((SIDE, 3, rows, LANES), bf16),
            pltpu.VMEM((SIDE, rows, LANES), f32),
            pltpu.VMEM((SIDE, 2, strip, LANES), bf16),
            pltpu.VMEM((SIDE, 2, rows, LANES), bf16),
            pltpu.VMEM((2, rows, LANES), f32),
            sems((ITERS,)),
            sems((ITERS,)),
            sems((ITERS,)),
            sems((ITERS,)),
            sems((4,)),
            sems((4,)),
            sems((4,)),
            sems((4,)),
            sems((SIDE, 2, 2)),
            sems((SIDE, 2, 2)),
            sems((2, 13)),
            sems((2, 13)),
            sems((SIDE, 2, 3)),
            sems((SIDE, 2, 3)),
            sems((SIDE,)),
            sems((5,)),
            pltpu.VMEM((SIDE, 2, strip, LANES), f32),
            sems((2,)),
            pltpu.VMEM((rows, LANES), f32),
            pltpu.VMEM((rows, LANES), bf16),
            pltpu.VMEM((2, rows, LANES), bf16),
        ],
        compiler_params=pltpu.CompilerParams(
            collective_id=0, has_side_effects=True, vmem_limit_bytes=60 * 2**20
        ),
    )(noise_latents, data_latents)
    return targets, rows_pot.reshape(block), cols_pot.reshape(cols // 2)


def solution(mesh):
    return jax.shard_map(
        shards,
        mesh=mesh,
        in_specs=(P("noise", "dp"), P("dp", "noise")),
        out_specs=(P("noise", "dp"), P("noise"), P("dp")),
        check_vma=False,
    )
```

```python
import functools
import math

import jax
import jax.numpy as jnp
from jax import lax
from jax.experimental import pallas as pl
from jax.experimental.pallas import tpu as pltpu
from jax.sharding import PartitionSpec as P

ITERS = 3
EPSILON = 0.04
LOG2E = 1.0 / math.log(2.0)
MESH = pl.DeviceIdType.MESH
LANES = 128
TILE = 32
SIDE = 4
PARTS = 4


def wrap(index, size):
    return lax.rem(index, size)


def spread_lanes(ref, row):
    return jnp.broadcast_to(ref[pl.ds(row, 1), :], (LANES, LANES)).T


def exchange(buf, send, recv, step, parts, me, size, peer_id, started):
    for k in range(1, size):
        pltpu.make_async_remote_copy(
            src_ref=buf.at[step, me, pl.ds(0, parts)],
            dst_ref=buf.at[step, me, pl.ds(0, parts)],
            send_sem=send.at[step],
            recv_sem=recv.at[step],
            device_id=peer_id(wrap(me + k, size)),
            device_id_type=MESH,
        ).start()
    slots = buf.at[step, pl.ds(0, size - 1), pl.ds(0, parts)]
    every = pltpu.make_async_remote_copy(
        src_ref=slots,
        dst_ref=slots,
        send_sem=send.at[step],
        recv_sem=recv.at[step],
        device_id=peer_id(wrap(me + 1, size)),
        device_id_type=MESH,
    )
    every.wait_recv()
    started.append(every)


def combine(buf, step, size):
    top = buf[step, 0, 0]
    for s in range(1, size):
        top = jnp.maximum(top, buf[step, s, 0])
    total = buf[step, 0, 1] * jnp.exp2(buf[step, 0, 0] - top)
    for s in range(1, size):
        total = total + buf[step, s, 1] * jnp.exp2(buf[step, s, 0] - top)
    return top, total


def add_slots(buf, step, size):
    total = buf[step, 0, 0]
    for s in range(1, size):
        total = total + buf[step, s, 0]
    return total


def kernel(
    rsize, csize, width,
    noise_ref, data_ref,
    targets, rows_out, cols_out,
    noise_all, data_all, scores, weights,
    shift, first, scale, part, data_part, colvec, rowpack, colpack, sqx, sqy, swap,
    ring_buf, quad_buf, row_buf, out_buf, own_buf, far_buf, near_buf, in_sum,
    ring_send, ring_recv, quad_send, quad_recv, row_send, row_recv, swap_send, swap_recv,
    cross_send, cross_recv, noise_send, noise_recv, data_send, data_recv,
    sum_send, sum_recv, in_send, in_recv, keep, local_sems, relay_in, mate_out, mate_in,
):
    rows, cols = scores.shape
    n = lax.axis_index("noise")
    d = lax.axis_index("dp")
    x, z = d // SIDE, lax.rem(d, SIDE)
    y, core = n // 2, lax.rem(n, 2)
    kind = lax.rem((x + 1) // 2, 2)
    pair = x // 2
    side = lax.rem(x, 2)
    home = core == kind
    kappa = LOG2E / EPSILON
    log_rows = math.log2(rows * csize)
    log_cols = math.log2(cols * rsize)
    chunks = cols // LANES
    row_blocks = rows // LANES
    tiles = rows // TILE
    started = []

    def around(value):
        return lax.rem(value + SIDE, SIDE)

    def device(xi, yi, zi, ci):
        return (yi * 2 + ci, xi * SIDE + zi)

    def x_at(which, of_kind):
        return which * (3 - 2 * of_kind) + of_kind

    me_row = pair * SIDE + z
    me_quad = kind * 2 + core

    def row_peer(p):
        return device(x_at(p // SIDE, kind), y, lax.rem(p, SIDE), core)

    def ring_peer(p):
        return device(x, p, z, core)

    def quad_peer(p, yi=y):
        return device(x_at(pair, p // 2), yi, z, lax.rem(p, 2))

    sibling = device(x, y, z, 1 - core)
    partner = x + 1 - 2 * side
    mate = SIDE - 1 - x
    opposite = around(x + 2)

    barrier = pltpu.get_barrier_semaphore()
    greeted = [row_peer(wrap(me_row + k, rsize)) for k in range(1, rsize)]
    greeted += [ring_peer(around(y + k)) for k in (1, 2, 3)]
    greeted += [quad_peer(around(me_quad + k)) for k in (1, 2, 3)]
    greeted += [device(opposite, y, z, 0), device(opposite, y, z, 1), device(mate, y, z, 1 - core)]
    for to in greeted:
        pl.semaphore_signal(barrier, inc=1, device_id=to, device_id_type=MESH)
    pl.semaphore_wait(barrier, len(greeted))

    def remote(src, dst, send, recv, to):
        return pltpu.make_async_remote_copy(
            src_ref=src, dst_ref=dst, send_sem=send, recv_sem=recv, device_id=to, device_id_type=MESH
        )

    def begin(copy):
        copy.start()
        started.append(copy)

    def lane(c):
        return slice(LANES * c, LANES * (c + 1))

    HOP = (1, -1)
    ORDER = (0, 1, 3, 2)
    own = x * SIDE + z

    def cross_copy(i, half, to):
        return remote(
            noise_ref.at[pl.ds(half * rows, rows)], noise_all.at[own], cross_send.at[i], cross_recv.at[x], to
        )

    def cross_wait(xi):
        remote(
            noise_ref.at[pl.ds(0, rows)], noise_all.at[xi * SIDE + z], cross_send.at[0], cross_recv.at[xi], sibling
        ).wait_recv()

    there = jnp.where(home, mate, partner)
    aside = cross_copy(2, 1 - core, sibling)

    def noise_copy(xi, t, forward, slot):
        at = pl.ds(t * (rows // 2), rows // 2) if forward else pl.ds(0, rows)
        f = int(forward)
        return remote(
            noise_all.at[slot, at], noise_all.at[slot, at],
            noise_send.at[xi, t, f], noise_recv.at[xi, t, f], device(x, y, around(z + HOP[t]), core),
        )

    def noise_wait(xi, t, forward):
        slot = xi * SIDE + around(z - HOP[t] * (2 if forward else 1))
        noise_copy(xi, t, forward, slot).wait_recv()
        return slot

    def data_copy(r, index, where, lo, size, to, own=False):
        at = pl.ds(lo, size)
        block = side if r == 0 else 1 - side
        dst = data_all.at[block, where, at]
        return remote(data_ref.at[at] if own else dst, dst, data_send.at[r, index], data_recv.at[r, index], to)

    half_cols = cols // 4
    full_cols = cols // 2

    def along_y(step, c):
        return around(y + step) * 2 + c

    def data_wait(r, index, where, lo, size):
        data_copy(r, index, where, lo, size, sibling).wait_recv()

    HALF = 9

    def cross_data(h, own=False):
        at = pl.ds(h * half_cols, half_cols)
        dst = data_all.at[side if own else 1 - side, n, at]
        return remote(
            data_ref.at[at], dst, data_send.at[1, 11 + h], data_recv.at[1, 11 + h], device(partner, y, z, core)
        )

    def partner_y(t, h, back=0):
        where = around(y + back) * 2 + core
        to = device(x, around(y + HOP[t]), z, core)
        return t if h == 0 else HALF + t, where, h * half_cols, half_cols, to

    def partner_wait(t, h):
        data_copy(1, *partner_y(t, h, -HOP[t])).wait_recv()

    begin(cross_copy(0, 0, device(there, y, z, 0)))
    begin(cross_copy(1, 1, device(there, y, z, 1)))

    @pl.when(home)
    def _():
        aside.start()

    for t in (0, 1):
        begin(data_copy(0, t, n, 0, full_cols, device(x, around(y + HOP[t]), z, core), own=True))
    for h in (0, 1):
        begin(cross_data(h, own=True))
    begin(data_copy(0, 4, n, 0, full_cols, sibling, own=True))

    @pl.when(home)
    def _():
        pltpu.make_async_copy(
            noise_ref.at[pl.ds(pl.multiple_of(core * rows, rows), rows)], noise_all.at[own], local_sems.at[0]
        ).start()

    data_own = pltpu.make_async_copy(data_ref, data_all.at[side, n], local_sems.at[1])
    data_own.start()

    @pl.when(home)
    def _():
        pltpu.make_async_copy(
            noise_ref.at[pl.ds(pl.multiple_of(core * rows, rows), rows)], noise_all.at[own], local_sems.at[0]
        ).wait()

    @pl.when(jnp.logical_not(home))
    def _():
        cross_wait(x)

    for t in (0, 1):
        begin(noise_copy(x, t, False, own))
    scores[...] = jnp.zeros_like(scores)
    part[...] = jnp.zeros_like(part)
    data_part[...] = jnp.zeros_like(data_part)
    for xi in (mate, partner):
        cross_wait(xi)
        for t in (0, 1):
            begin(noise_copy(xi, t, False, xi * SIDE + z))
    slot = partner * SIDE + z
    begin(remote(
        noise_all.at[slot], noise_all.at[slot], cross_send.at[3], cross_recv.at[partner], device(mate, y, z, core)
    ))
    cross_data(0).wait_recv()
    for t in (0, 1):
        begin(data_copy(1, *partner_y(t, 0)))
    for t in (0, 1):
        where = along_y(-HOP[t], core)
        data_wait(0, t, where, 0, full_cols)
        begin(data_copy(0, 2 + t, where, t * half_cols, half_cols, device(x, around(y + HOP[t]), z, core)))
        begin(data_copy(0, 5 + t, where, 0, full_cols, sibling))
    cross_data(1).wait_recv()
    for t in (0, 1):
        begin(data_copy(1, *partner_y(t, 1)))
    begin(data_copy(1, 4, n, 0, full_cols, sibling))
    cross_wait(opposite)
    for t in (0, 1):
        begin(noise_copy(opposite, t, False, opposite * SIDE + z))
    by_data = [around(y + step) for step in ORDER]
    for xi in by_data:
        for t in (0, 1):
            begin(noise_copy(xi, t, True, noise_wait(xi, t, False)))

    def squares(block):
        value = block.astype(jnp.float32)
        return value * value

    def chunk_product(q, m):
        both = jnp.concatenate([noise_all[2 * q], noise_all[2 * q + 1]], axis=1)
        cut = pl.ds(pl.multiple_of(m * 256, 256), 256)
        piece = data_all[m // 4, q, pl.ds(pl.multiple_of(lax.rem(m, 4) * 256, 256), 256), :]
        data_part[cut, :] += squares(piece[:, :LANES]) + squares(piece[:, LANES:])
        return lax.dot_general(both, piece, (((1,), (1,)), ((), ())), preferred_element_type=jnp.float32)

    def norms(q):
        def norm(r, carry):
            cut = pl.ds(pl.multiple_of(r * 64, 64), 64)
            part[cut, :] += squares(noise_all[2 * q, cut, :]) + squares(noise_all[2 * q + 1, cut, :])
            return carry

        lax.fori_loop(0, rows // 64, norm, 0)

    near, other_block = side * 4, 4 - side * 4

    def unit(q, block):
        def column(m, carry):
            cut = pl.ds(pl.multiple_of((block + m) * 256, 256), 256)
            scores[:, cut] += chunk_product(q, block + m)
            return carry

        lax.fori_loop(0, 4, column, 0)

    mine = z // 2

    def own_unit(q):
        unit(q, near)
        norms(q)

    def forward_wait(xi):
        for t in (0, 1):
            noise_wait(xi, t, True)

    def pass_on(t):
        where = along_y(-HOP[t], core)
        begin(data_copy(1, 2 + t, where, t * half_cols, half_cols, device(x, around(y + HOP[t]), z, core)))

    partner_wait(0, 0)
    pass_on(0)
    partner_wait(1, 0)
    data_own.wait()
    data_wait(0, 4, along_y(0, 1 - core), 0, full_cols)
    for t in (0, 1):
        data_wait(0, 5 + t, along_y(-HOP[t], 1 - core), 0, full_cols)

    def early(i, carry):
        own_unit(around(y + i + i // 2) * 2 + mine)
        return carry

    lax.fori_loop(0, 3, early, 0)
    for t in (0, 1):
        where = along_y(2, core)
        data_wait(0, 2 + t, where, t * half_cols, half_cols)
        begin(data_copy(0, 7 + t, where, t * half_cols, half_cols, sibling))

    forward_wait(by_data[0])
    own_unit(y * 2 + 1 - mine)
    data_wait(1, 4, along_y(0, 1 - core), 0, full_cols)

    def partner_mid(i, carry):
        unit(y * 2 + i, other_block)
        return carry

    lax.fori_loop(0, 2, partner_mid, 0)
    for t in (0, 1):
        data_wait(0, 7 + t, along_y(2, 1 - core), t * half_cols, half_cols)
    own_unit(around(y + 2) * 2 + mine)
    partner_wait(1, 1)
    pass_on(1)
    partner_wait(0, 1)
    for t in (0, 1):
        begin(data_copy(1, 5 + t, along_y(-HOP[t], core), 0, full_cols, sibling))
    for xi in by_data[1:3]:
        forward_wait(xi)
        own_unit(xi * 2 + 1 - mine)
    for t in (0, 1):
        data_wait(1, 5 + t, along_y(-HOP[t], 1 - core), 0, full_cols)

    def partner_late(i, carry):
        unit(around(y + 1 + 2 * (i // 2)) * 2 + lax.rem(i, 2), other_block)
        return carry

    lax.fori_loop(0, 4, partner_late, 0)
    for t in (0, 1):
        where = along_y(2, core)
        data_wait(1, 2 + t, where, t * half_cols, half_cols)
        begin(data_copy(1, 7 + t, where, t * half_cols, half_cols, sibling))
    forward_wait(by_data[3])
    for t in (0, 1):
        data_wait(1, 7 + t, along_y(2, 1 - core), t * half_cols, half_cols)

    factor = 2.0 * kappa / width
    q_mine, q_other = around(y + 2) * 2 + mine, around(y + 2) * 2 + 1 - mine
    norms(q_other)

    def row_shift(r, carry):
        at = pl.ds(pl.multiple_of(r * 128, 128), 128)
        total = jnp.sum(part[at, :], axis=1, keepdims=True) * (-kappa / width)
        shift[at, :] = jnp.broadcast_to(total, (128, LANES))
        return carry

    lax.fori_loop(0, rows // 128, row_shift, 0)

    def final(block, qs):
        def column(i, carry):
            m = block + i
            cut = pl.ds(pl.multiple_of(m * 256, 256), 256)
            value = scores[:, cut]
            for q in qs:
                value = value + chunk_product(q, m)
            value = value * factor
            scores[:, cut] = value
            for e in (0, 1):
                top = jnp.max(value[:, LANES * e:LANES * (e + 1)] + shift[...], axis=0, keepdims=True)
                ring_buf[0, y, 0, pl.ds(2 * m + e, 1), :] = top
                colvec[:, pl.ds(pl.multiple_of(m * 256 + e * LANES, LANES), LANES)] = jnp.broadcast_to(top, (8, LANES))
            return carry

        lax.fori_loop(0, 4, column, 0)

    final(near, (q_other,))
    final(other_block, (q_mine, q_other))

    def fold(block, op):
        out = block[0:8]
        for r in range(1, TILE // 8):
            out = op(out, block[8 * r:8 * r + 8])
        return out

    def spread_cols():
        for c in range(chunks):
            colvec[:, lane(c)] = jnp.broadcast_to(colpack[pl.ds(c, 1), :], (8, LANES))

    def tall(ref, c):
        return jnp.concatenate([ref[:, lane(c)]] * (TILE // 8), axis=0)

    def tile_at(t):
        return pl.ds(pl.multiple_of(t * TILE, TILE), TILE)

    def loop(body, init):
        return lax.fori_loop(0, tiles, body, init, unroll=2)

    zeros = tuple(jnp.zeros((8, LANES), jnp.float32) for _ in range(chunks))

    def exp_step(t, accs):
        at = tile_at(t)
        add = shift[at, :]
        return tuple(
            accs[c] + fold(jnp.exp2(scores[at, lane(c)] + add - tall(colvec, c)), jnp.add)
            for c in range(chunks)
        )

    sums = loop(exp_step, zeros)
    for c in range(chunks):
        ring_buf[0, y, 1, pl.ds(c, 1), :] = jnp.sum(sums[c], axis=0, keepdims=True)
    exchange(ring_buf, ring_send, ring_recv, 0, 2, y, SIDE, ring_peer, started)
    top, total = combine(ring_buf, 0, SIDE)
    quad_buf[0, me_quad, 0] = top
    quad_buf[0, me_quad, 1] = total
    exchange(quad_buf, quad_send, quad_recv, 0, 2, me_quad, SIDE, quad_peer, started)
    top, total = combine(quad_buf, 0, SIDE)
    col_pot = -log_cols - top - jnp.log(total) * LOG2E
    colpack[...] = col_pot
    spread_cols()

    def row_step(t, carry):
        at = tile_at(t)
        top = scores[at, lane(0)] + tall(colvec, 0)
        for c in range(1, chunks):
            top = jnp.maximum(top, scores[at, lane(c)] + tall(colvec, c))
        first[at, :] = top
        total = None
        for c in range(chunks):
            value = jnp.exp2(scores[at, lane(c)] + tall(colvec, c) - top)
            scores[at, lane(c)] = value
            total = value if total is None else total + value
        part[at, :] = total
        return carry

    loop(row_step, 0)
    for b in range(row_blocks):
        at = pl.ds(b * LANES, LANES)
        tops = first[at, :].T
        top = jnp.max(tops, axis=0, keepdims=True)
        row_buf[0, me_row, 0, pl.ds(b, 1), :] = top
        row_buf[0, me_row, 1, pl.ds(b, 1), :] = jnp.sum(part[at, :].T * jnp.exp2(tops - top), axis=0, keepdims=True)
    exchange(row_buf, row_send, row_recv, 0, 2, me_row, rsize, row_peer, started)
    top, total = combine(row_buf, 0, rsize)
    row_lse = top + jnp.log(total) * LOG2E
    rowpack[...] = row_lse
    for b in range(row_blocks):
        at = pl.ds(b * LANES, LANES)
        base = jnp.exp2(first[at, :] - spread_lanes(rowpack, b))
        first[at, :] = base
        scale[at, :] = base

    def col_step(t, accs):
        at = tile_at(t)
        mul = scale[at, :]
        return tuple(accs[c] + fold(scores[at, lane(c)] * mul, jnp.add) for c in range(chunks))

    def sum_step(keep_values):
        def body(t, carry):
            at = tile_at(t)
            total = None
            for c in range(chunks):
                value = scores[at, lane(c)] * tall(colvec, c)
                if keep_values:
                    scores[at, lane(c)] = value
                total = value if total is None else total + value
            part[at, :] = total * first[at, :]
            return carry

        return body

    for step in range(1, ITERS):
        sums = loop(col_step, zeros)
        for c in range(chunks):
            ring_buf[step, y, 0, pl.ds(c, 1), :] = jnp.sum(sums[c], axis=0, keepdims=True)
        exchange(ring_buf, ring_send, ring_recv, step, 1, y, SIDE, ring_peer, started)
        quad_buf[step, me_quad, 0] = add_slots(ring_buf, step, SIDE)
        exchange(quad_buf, quad_send, quad_recv, step, 1, me_quad, SIDE, quad_peer, started)
        ratio = 1.0 / add_slots(quad_buf, step, SIDE)
        colpack[...] = ratio
        spread_cols()
        loop(sum_step(step == ITERS - 1), 0)
        for b in range(row_blocks):
            at = pl.ds(b * LANES, LANES)
            row_buf[step, me_row, 0, pl.ds(b, 1), :] = jnp.sum(part[at, :].T, axis=0, keepdims=True)
        exchange(row_buf, row_send, row_recv, step, 1, me_row, rsize, row_peer, started)
        total = add_slots(row_buf, step, rsize)
        rowpack[...] = 1.0 / total
        for b in range(row_blocks):
            at = pl.ds(b * LANES, LANES)
            scale[at, :] = first[at, :] * spread_lanes(rowpack, b)

    def weigh(r):
        def body(t, carry):
            at = pl.ds(pl.multiple_of(r * (rows // 2) + t * TILE, TILE), TILE)
            mul = scale[at, :]
            for c in range(chunks):
                weights[at, lane(c)] = (scores[at, lane(c)] * mul).astype(jnp.bfloat16)
            return carry

        lax.fori_loop(0, tiles // 2, body, 0, unroll=2)

    def swap_copy(i, to):
        return remote(swap.at[0], swap.at[i], swap_send.at[i], swap_recv.at[i], to)

    def potentials():
        for c in range(chunks):
            sqy[pl.ds(c, 1), :] = jnp.sum(data_part[pl.ds(c * LANES, LANES), :].T, axis=0, keepdims=True)
        cols_pot = (col_pot + jnp.log(ratio) * LOG2E + (log_rows - log_cols)) / kappa + sqy[...] / width
        colpack[...] = cols_pot
        cols_out[...] = colpack[pl.ds(pl.multiple_of(side * 8, 8), 8), :]
        for b in range(row_blocks):
            sqx[pl.ds(b, 1), :] = shift[pl.ds(b * LANES, LANES), :].T[0:1]
        swap[0] = -(log_rows + row_lse + jnp.log(total) * LOG2E + sqx[...]) / kappa
        begin(swap_copy(1, sibling))
        for i in (0, 1):
            begin(remote(
                swap.at[0], swap.at[2 + core], swap_send.at[2 + i], swap_recv.at[2 + core], device(partner, y, z, i)
            ))

    strip = rows // 2

    def half_rows(r):
        return pl.ds(r * strip, strip)

    def block_x(b):
        return jnp.where(b < 2, jnp.where(b == 0, opposite, partner), jnp.where(b == 2, mate, x))

    def product(p, r, to_z):
        cut = pl.ds(pl.multiple_of(lax.rem(to_z, 2) * LANES, LANES), LANES)
        total = None
        for k in (0, 1):
            block = jnp.concatenate(
                [data_all[k, block_x(2 * p + e) * 2 + to_z // 2, :, cut] for e in (0, 1)], axis=1
            )
            value = jnp.dot(
                weights[half_rows(r), k * full_cols:(k + 1) * full_cols], block,
                preferred_element_type=jnp.float32,
            )
            total = value if total is None else total + value
        return total

    def sum_copy(b, t, index, src, dst):
        to = device(x, y, around(z + HOP[t]), core)
        return remote(src, dst, sum_send.at[b, t, index], sum_recv.at[b, t, index], to)

    def far_copy(b, t):
        return sum_copy(b, t, 0, out_buf.at[b, 2, half_rows(t)], far_buf.at[b, t])

    def direct_copy(b, t):
        at = half_rows(1 - t)
        return sum_copy(b, t, 1, out_buf.at[b, t, at], near_buf.at[b, t, at])

    def added_copy(b, t):
        at = half_rows(t)
        return sum_copy(b, t, 2, out_buf.at[b, t, at], near_buf.at[b, t, at])

    def relay_copy():
        return remote(own_buf.at[0], relay_in, in_send.at[0], in_recv.at[4], device(mate, y, z, core))

    def partner_copy(a):
        return remote(own_buf.at[1], in_sum.at[a], in_send.at[1], in_recv.at[a], device(partner, y, z, kind))

    def mate_copy(a):
        return remote(mate_out, mate_in.at[a], in_send.at[2], in_recv.at[2 + a], device(mate, y, z, kind))

    def stay_copy(a):
        return remote(own_buf.at[3], in_sum.at[a], in_send.at[3], in_recv.at[a], sibling)

    def add_far(b):
        for t in (0, 1):
            far_copy(b, t).wait_recv()
            out_buf[b, t, half_rows(t), :] = (keep[b, t] + far_buf[b, t].astype(jnp.float32)).astype(jnp.bfloat16)
            added_copy(b, t).start()

    def add_near(b):
        for t in (0, 1):
            direct_copy(b, t).wait_recv()
            added_copy(b, t).wait_recv()
        own_buf[b] = own_buf[b] + near_buf[b, 0].astype(jnp.float32) + near_buf[b, 1].astype(jnp.float32)

    def send_pair(p, carry):
        @pl.when(p == 0)
        def _():
            weigh(0)

        for t in (0, 1):
            if t == 1:
                @pl.when(p == 0)
                def _():
                    weigh(1)

            value = product(p, t, around(z + 2))
            for e in (0, 1):
                out_buf[2 * p + e, 2, half_rows(t), :] = value[:, lane(e)].astype(jnp.bfloat16)
            far_copy(2 * p, t).start()

        @pl.when(p > 0)
        def _():
            add_near(0)
            relay_copy().start()

        for t in (0, 1):
            value = product(p, 1 - t, around(z + HOP[t]))
            for e in (0, 1):
                out_buf[2 * p + e, t, half_rows(1 - t), :] = value[:, lane(e)].astype(jnp.bfloat16)
            direct_copy(2 * p, t).start()
            value = product(p, t, around(z + HOP[t]))
            for e in (0, 1):
                keep[2 * p + e, t] = value[:, lane(e)]

        @pl.when(p > 0)
        def _():
            add_far(1)

        @pl.when(p == 0)
        def _():
            add_far(0)

        for t in (0, 1):
            far_copy(2 * p + 1, t).start()
        for t in (0, 1):
            direct_copy(2 * p + 1, t).start()
        for r in (0, 1):
            value = product(p, r, z)
            for e in (0, 1):
                own_buf[2 * p + e, half_rows(r), :] = value[:, lane(e)]
        return carry

    lax.fori_loop(0, 2, send_pair, 0)
    add_far(2)
    potentials()
    add_near(1)
    relay_copy().wait_recv()
    own_buf[1] = own_buf[1] + relay_in[...]
    partner_copy(core).start()
    add_near(2)
    mate_out[...] = own_buf[2].astype(jnp.bfloat16)
    mate_copy(core).start()
    add_far(3)

    swap_copy(1, sibling).wait_recv()
    for i in (0, 1):
        remote(swap.at[0], swap.at[2 + i], swap_send.at[2 + i], swap_recv.at[2 + i], sibling).wait_recv()
    half = rows // LANES
    for a in (0, 1):
        mine_row = jnp.where(core == a, swap[0], swap[1])
        rows_out[pl.ds(a * half, half), :] = jnp.where(home, mine_row, swap[2 + a])

    add_near(3)

    @pl.when(home)
    def _():
        in_sum[core] = own_buf[3]
        stay_copy(1 - core).wait_recv()
        for a in (0, 1):
            mate_copy(a).wait_recv()
            in_sum[a] = in_sum[a] + mate_in[a].astype(jnp.float32)

    @pl.when(jnp.logical_not(home))
    def _():
        stay_copy(core).start()
        for a in (0, 1):
            partner_copy(a).wait_recv()

    def result_copy(a):
        return pltpu.make_async_copy(in_sum.at[a], targets.at[pl.ds(a * rows, rows)], local_sems.at[a])

    for a in (0, 1):
        result_copy(a).start()

    def settle(b, carry):
        for t in (0, 1):
            far_copy(b, t).wait_send()
            direct_copy(b, t).wait_send()
            added_copy(b, t).wait_send()
        return carry

    lax.fori_loop(0, SIDE, settle, 0)
    for a in (0, 1):
        result_copy(a).wait()
    relay_copy().wait_send()
    partner_copy(core).wait_send()
    mate_copy(core).wait_send()

    @pl.when(jnp.logical_not(home))
    def _():
        stay_copy(core).wait_send()

    for copy in started:
        copy.wait_send()

    @pl.when(home)
    def _():
        aside.wait_send()


def hand_on(targets, rows_pot, cols_pot, targets_out, rows_out, cols_out, sems):
    size = targets.shape[0] // PARTS
    copies = [
        pltpu.make_async_copy(targets.at[pl.ds(i * size, size)], targets_out.at[pl.ds(i * size, size)], sems.at[i])
        for i in range(PARTS)
    ]
    copies.append(pltpu.make_async_copy(rows_pot, rows_out, sems.at[PARTS]))
    copies.append(pltpu.make_async_copy(cols_pot, cols_out, sems.at[PARTS + 1]))
    for copy in copies:
        copy.start()
    for copy in copies:
        copy.wait()


def shards(noise_latents, data_latents):
    nsize = lax.axis_size("noise")
    dsize = lax.axis_size("dp")
    block, piece = noise_latents.shape
    rows, cols = block // 2, 2 * data_latents.shape[0]
    rsize, csize = dsize // 2, nsize * 2
    vmem = pl.BlockSpec(memory_space=pltpu.VMEM)
    f32, bf16 = jnp.float32, jnp.bfloat16
    strip = rows // 2
    row_vec, col_vec = (rows // LANES, LANES), (cols // LANES, LANES)
    sems = pltpu.SemaphoreType.DMA
    targets, rows_pot, cols_pot = pl.pallas_call(
        functools.partial(kernel, rsize, csize, piece * dsize),
        out_shape=(
            jax.ShapeDtypeStruct((block, piece), f32),
            jax.ShapeDtypeStruct((block // LANES, LANES), f32),
            jax.ShapeDtypeStruct((cols // 2 // LANES, LANES), f32),
        ),
        in_specs=[pl.BlockSpec(memory_space=pl.ANY)] * 2,
        out_specs=(pl.BlockSpec(memory_space=pl.ANY), vmem, vmem),
        scratch_shapes=[
            pltpu.VMEM((dsize, rows, piece), bf16),
            pltpu.VMEM((2, nsize) + data_latents.shape, bf16),
            pltpu.VMEM((rows, cols), f32),
            pltpu.VMEM((rows, cols), bf16),
            pltpu.VMEM((rows, LANES), f32),
            pltpu.VMEM((rows, LANES), f32),
            pltpu.VMEM((rows, LANES), f32),
            pltpu.VMEM((rows, LANES), f32),
            pltpu.VMEM((cols, LANES), f32),
            pltpu.VMEM((8, cols), f32),
            pltpu.VMEM(row_vec, f32),
            pltpu.VMEM(col_vec, f32),
            pltpu.VMEM(row_vec, f32),
            pltpu.VMEM(col_vec, f32),
            pltpu.VMEM((4,) + row_vec, f32),
            pltpu.VMEM((ITERS, SIDE, 2) + col_vec, f32),
            pltpu.VMEM((ITERS, SIDE, 2) + col_vec, f32),
            pltpu.VMEM((ITERS, rsize, 2) + row_vec, f32),
            pltpu.VMEM((SIDE, 3, rows, LANES), bf16),
            pltpu.VMEM((SIDE, rows, LANES), f32),
            pltpu.VMEM((SIDE, 2, strip, LANES), bf16),
            pltpu.VMEM((SIDE, 2, rows, LANES), bf16),
            pltpu.VMEM((2, rows, LANES), f32),
            sems((ITERS,)),
            sems((ITERS,)),
            sems((ITERS,)),
            sems((ITERS,)),
            sems((ITERS,)),
            sems((ITERS,)),
            sems((4,)),
            sems((4,)),
            sems((4,)),
            sems((4,)),
            sems((SIDE, 2, 2)),
            sems((SIDE, 2, 2)),
            sems((2, 13)),
            sems((2, 13)),
            sems((SIDE, 2, 3)),
            sems((SIDE, 2, 3)),
            sems((SIDE,)),
            sems((5,)),
            pltpu.VMEM((SIDE, 2, strip, LANES), f32),
            sems((2,)),
            pltpu.VMEM((rows, LANES), f32),
            pltpu.VMEM((rows, LANES), bf16),
            pltpu.VMEM((2, rows, LANES), bf16),
        ],
        compiler_params=pltpu.CompilerParams(
            collective_id=0, has_side_effects=True, vmem_limit_bytes=60 * 2**20
        ),
    )(noise_latents, data_latents)
    results = (targets, rows_pot, cols_pot)
    targets, rows_pot, cols_pot = pl.pallas_call(
        hand_on,
        out_shape=tuple(jax.ShapeDtypeStruct(a.shape, a.dtype) for a in results),
        in_specs=[pl.BlockSpec(memory_space=pl.ANY)] * 3,
        out_specs=(pl.BlockSpec(memory_space=pl.ANY),) * 3,
        scratch_shapes=[sems((PARTS + 2,))],
        compiler_params=pltpu.CompilerParams(vmem_limit_bytes=60 * 2**20),
    )(*results)
    return targets, rows_pot.reshape(block), cols_pot.reshape(cols // 2)


def solution(mesh):
    return jax.shard_map(
        shards,
        mesh=mesh,
        in_specs=(P("noise", "dp"), P("dp", "noise")),
        out_specs=(P("noise", "dp"), P("noise"), P("dp")),
        check_vma=False,
    )
```

```python
import functools
import math

import jax
import jax.numpy as jnp
from jax import lax
from jax.experimental import pallas as pl
from jax.experimental.pallas import tpu as pltpu
from jax.sharding import PartitionSpec as P

ITERS = 3
EPSILON = 0.04
LOG2E = 1.0 / math.log(2.0)
MESH = pl.DeviceIdType.MESH
LANES = 128
TILE = 32
SIDE = 4
PARTS = 4


def wrap(index, size):
    return lax.rem(index, size)


def spread_lanes(ref, row):
    return jnp.broadcast_to(ref[pl.ds(row, 1), :], (LANES, LANES)).T


def exchange(buf, send, recv, step, me, size, peer_id, started):
    for k in range(1, size):
        pltpu.make_async_remote_copy(
            src_ref=buf.at[step, me],
            dst_ref=buf.at[step, me],
            send_sem=send.at[step],
            recv_sem=recv.at[step],
            device_id=peer_id(wrap(me + k, size)),
            device_id_type=MESH,
        ).start()
    slots = buf.at[step, pl.ds(0, size - 1)]
    every = pltpu.make_async_remote_copy(
        src_ref=slots,
        dst_ref=slots,
        send_sem=send.at[step],
        recv_sem=recv.at[step],
        device_id=peer_id(wrap(me + 1, size)),
        device_id_type=MESH,
    )
    every.wait_recv()
    started.append(every)


def combine(buf, step, size):
    top = buf[step, 0]
    for s in range(1, size):
        top = jnp.maximum(top, buf[step, s])
    total = jnp.exp2(buf[step, 0] - top)
    for s in range(1, size):
        total = total + jnp.exp2(buf[step, s] - top)
    return top + jnp.log(total) * LOG2E


def add_slots(buf, step, size):
    total = buf[step, 0]
    for s in range(1, size):
        total = total + buf[step, s]
    return total


def kernel(
    rsize, csize, width,
    noise_ref, data_ref,
    targets, rows_out, cols_out,
    noise_all, data_all, scores, weights,
    shift, first, scale, part, data_part, colvec, rowpack, colpack, sqx, sqy, swap,
    col_buf, row_buf, out_buf, own_buf, far_buf, near_buf, in_sum,
    col_send, col_recv, row_send, row_recv, swap_send, swap_recv,
    cross_send, cross_recv, noise_send, noise_recv, data_send, data_recv,
    sum_send, sum_recv, in_send, in_recv, keep, local_sems, own_send, relay_in, mate_out, mate_in,
):
    rows, cols = scores.shape
    n = lax.axis_index("noise")
    d = lax.axis_index("dp")
    x, z = d // SIDE, lax.rem(d, SIDE)
    y, core = n // 2, lax.rem(n, 2)
    kind = lax.rem((x + 1) // 2, 2)
    pair = x // 2
    side = lax.rem(x, 2)
    home = core == kind
    kappa = LOG2E / EPSILON
    log_rows = math.log2(rows * csize)
    log_cols = math.log2(cols * rsize)
    chunks = cols // LANES
    row_blocks = rows // LANES
    tiles = rows // TILE
    started = []

    def around(value):
        return lax.rem(value + SIDE, SIDE)

    def device(xi, yi, zi, ci):
        return (yi * 2 + ci, xi * SIDE + zi)

    def x_at(which, of_kind):
        return which * (3 - 2 * of_kind) + of_kind

    me_row = pair * SIDE + z
    me_col = y * 4 + kind * 2 + core

    def row_peer(p):
        return device(x_at(p // SIDE, kind), y, lax.rem(p, SIDE), core)

    def col_peer(p):
        return device(x_at(pair, lax.rem(p // 2, 2)), p // 4, z, lax.rem(p, 2))

    sibling = device(x, y, z, 1 - core)
    partner = x + 1 - 2 * side
    mate = SIDE - 1 - x
    opposite = around(x + 2)

    barrier = pltpu.get_barrier_semaphore()
    greeted = [row_peer(wrap(me_row + k, rsize)) for k in range(1, rsize)]
    greeted += [col_peer(wrap(me_col + k, csize)) for k in range(1, csize)]
    greeted += [device(opposite, y, z, 0), device(opposite, y, z, 1), device(mate, y, z, 1 - core)]
    greeted += [device(x, y, around(z + step), 1 - core) for step in (1, -1)]
    for to in greeted:
        pl.semaphore_signal(barrier, inc=1, device_id=to, device_id_type=MESH)
    pl.semaphore_wait(barrier, len(greeted))

    def remote(src, dst, send, recv, to):
        return pltpu.make_async_remote_copy(
            src_ref=src, dst_ref=dst, send_sem=send, recv_sem=recv, device_id=to, device_id_type=MESH
        )

    def begin(copy):
        copy.start()
        started.append(copy)

    def lane(c):
        return slice(LANES * c, LANES * (c + 1))

    HOP = (1, -1)
    own = x * SIDE + z

    def cross_copy(i, half, to):
        return remote(
            noise_ref.at[pl.ds(half * rows, rows)], noise_all.at[own], cross_send.at[i], cross_recv.at[x], to
        )

    def cross_wait(xi):
        remote(
            noise_ref.at[pl.ds(0, rows)], noise_all.at[xi * SIDE + z], cross_send.at[0], cross_recv.at[xi], sibling
        ).wait_recv()

    there = jnp.where(home, mate, partner)
    aside = cross_copy(2, 1 - core, sibling)

    def noise_copy(xi, t, forward, slot):
        at = pl.ds(t * (rows // 2), rows // 2) if forward else pl.ds(0, rows)
        f = int(forward)
        return remote(
            noise_all.at[slot, at], noise_all.at[slot, at],
            noise_send.at[xi, t, f], noise_recv.at[xi, t, f], device(x, y, around(z + HOP[t]), core),
        )

    def noise_wait(xi, t, forward):
        slot = xi * SIDE + around(z - HOP[t] * (2 if forward else 1))
        noise_copy(xi, t, forward, slot).wait_recv()
        return slot

    def data_copy(r, index, where, lo, size, to, own=False):
        at = pl.ds(lo, size)
        block = side if r == 0 else 1 - side
        dst = data_all.at[block, where, at]
        return remote(data_ref.at[at] if own else dst, dst, data_send.at[r, index], data_recv.at[r, index], to)

    half_cols = cols // 4
    full_cols = cols // 2

    def along_y(step, c):
        return around(y + step) * 2 + c

    def data_wait(r, index, where, lo, size):
        data_copy(r, index, where, lo, size, sibling).wait_recv()

    HALF = 9

    def cross_data(h, own=False):
        at = pl.ds(h * half_cols, half_cols)
        dst = data_all.at[side if own else 1 - side, n, at]
        return remote(
            data_ref.at[at], dst, data_send.at[1, 11 + h], data_recv.at[1, 11 + h], device(partner, y, z, core)
        )

    def partner_y(t, h, back=0):
        where = around(y + back) * 2 + core
        to = device(x, around(y + HOP[t]), z, core)
        return t if h == 0 else HALF + t, where, h * half_cols, half_cols, to

    def partner_wait(t, h):
        data_copy(1, *partner_y(t, h, -HOP[t])).wait_recv()

    def own_round(t, a):
        return remote(
            noise_ref.at[pl.ds(a * rows, rows)], noise_all.at[own],
            own_send.at[t, a], noise_recv.at[x, t, 0], device(x, y, around(z + HOP[t]), a),
        )

    def own_half():
        return pltpu.make_async_copy(
            noise_ref.at[pl.ds(pl.multiple_of(core * rows, rows), rows)], noise_all.at[own], local_sems.at[0]
        )

    @pl.when(home)
    def _():
        for t in (0, 1):
            for a in (0, 1):
                own_round(t, a).start()
        aside.start()

    begin(cross_copy(0, 0, device(there, y, z, 0)))
    begin(cross_copy(1, 1, device(there, y, z, 1)))
    for t in (0, 1):
        begin(data_copy(0, t, n, 0, full_cols, device(x, around(y + HOP[t]), z, core), own=True))
    for h in (0, 1):
        begin(cross_data(h, own=True))

    @pl.when(home)
    def _():
        own_half().start()

    data_own = pltpu.make_async_copy(data_ref, data_all.at[side, n], local_sems.at[1])
    data_own.start()
    scores[...] = jnp.zeros_like(scores)
    part[...] = jnp.zeros_like(part)
    data_part[...] = jnp.zeros_like(data_part)
    for xi in (mate, partner):
        cross_wait(xi)
        for t in (0, 1):
            begin(noise_copy(xi, t, False, xi * SIDE + z))
    slot = partner * SIDE + z
    begin(remote(
        noise_all.at[slot], noise_all.at[slot], cross_send.at[3], cross_recv.at[partner], device(mate, y, z, core)
    ))
    begin(data_copy(0, 4, n, 0, full_cols, sibling, own=True))
    cross_data(0).wait_recv()
    for t in (0, 1):
        begin(data_copy(1, *partner_y(t, 0)))
    for t in (0, 1):
        where = along_y(-HOP[t], core)
        data_wait(0, t, where, 0, full_cols)
        begin(data_copy(0, 2 + t, where, t * half_cols, half_cols, device(x, around(y + HOP[t]), z, core)))
        begin(data_copy(0, 5 + t, where, 0, full_cols, sibling))
    cross_data(1).wait_recv()
    for t in (0, 1):
        begin(data_copy(1, *partner_y(t, 1)))
    begin(data_copy(1, 4, n, 0, full_cols, sibling))
    cross_wait(opposite)
    for t in (0, 1):
        begin(noise_copy(opposite, t, False, opposite * SIDE + z))
    swapped = opposite == y
    following = around(y + 1)
    by_data = [jnp.where(swapped, following, y), jnp.where(swapped, y, following), around(y - 1), around(y + 2)]
    for xi in by_data:
        for t in (0, 1):
            begin(noise_copy(xi, t, True, noise_wait(xi, t, False)))

    def squares(block):
        value = block.astype(jnp.float32)
        return value * value

    def chunk_product(q, m):
        both = jnp.concatenate([noise_all[2 * q], noise_all[2 * q + 1]], axis=1)
        cut = pl.ds(pl.multiple_of(m * 256, 256), 256)
        piece = data_all[m // 4, q, pl.ds(pl.multiple_of(lax.rem(m, 4) * 256, 256), 256), :]
        data_part[cut, :] += squares(piece[:, :LANES]) + squares(piece[:, LANES:])
        return lax.dot_general(both, piece, (((1,), (1,)), ((), ())), preferred_element_type=jnp.float32)

    def norms(q):
        def norm(r, carry):
            cut = pl.ds(pl.multiple_of(r * 64, 64), 64)
            part[cut, :] += squares(noise_all[2 * q, cut, :]) + squares(noise_all[2 * q + 1, cut, :])
            return carry

        lax.fori_loop(0, rows // 64, norm, 0)

    near, other_block = side * 4, 4 - side * 4

    def unit(q, block):
        def column(m, carry):
            cut = pl.ds(pl.multiple_of((block + m) * 256, 256), 256)
            scores[:, cut] += chunk_product(q, block + m)
            return carry

        lax.fori_loop(0, 4, column, 0)

    mine = z // 2

    def own_unit(q):
        unit(q, near)
        norms(q)

    def forward_wait(xi):
        for t in (0, 1):
            noise_wait(xi, t, True)

    def pass_on(t):
        where = along_y(-HOP[t], core)
        begin(data_copy(1, 2 + t, where, t * half_cols, half_cols, device(x, around(y + HOP[t]), z, core)))

    partner_wait(0, 0)
    pass_on(0)
    partner_wait(1, 0)
    data_own.wait()
    data_wait(0, 4, along_y(0, 1 - core), 0, full_cols)
    for t in (0, 1):
        data_wait(0, 5 + t, along_y(-HOP[t], 1 - core), 0, full_cols)

    def early(i, carry):
        own_unit(around(y + i + i // 2) * 2 + mine)
        return carry

    @pl.when(home)
    def _():
        own_half().wait()

    @pl.when(jnp.logical_not(home))
    def _():
        cross_wait(x)

    lax.fori_loop(0, 3, early, 0)
    for t in (0, 1):
        where = along_y(2, core)
        data_wait(0, 2 + t, where, t * half_cols, half_cols)
        begin(data_copy(0, 7 + t, where, t * half_cols, half_cols, sibling))
    data_wait(1, 4, along_y(0, 1 - core), 0, full_cols)
    unit(y * 2 + mine, other_block)
    forward_wait(by_data[0])
    own_unit(by_data[0] * 2 + 1 - mine)
    partner_wait(1, 1)
    pass_on(1)
    partner_wait(0, 1)
    for t in (0, 1):
        begin(data_copy(1, 5 + t, along_y(-HOP[t], core), 0, full_cols, sibling))
    for t in (0, 1):
        data_wait(0, 7 + t, along_y(2, 1 - core), t * half_cols, half_cols)
    own_unit(around(y + 2) * 2 + mine)
    forward_wait(by_data[1])
    own_unit(by_data[1] * 2 + 1 - mine)
    unit(y * 2 + 1 - mine, other_block)
    forward_wait(by_data[2])
    own_unit(by_data[2] * 2 + 1 - mine)
    for t in (0, 1):
        data_wait(1, 5 + t, along_y(-HOP[t], 1 - core), 0, full_cols)

    def partner_late(i, carry):
        unit(around(y + 1 + 2 * (i // 2)) * 2 + lax.rem(i, 2), other_block)
        return carry

    lax.fori_loop(0, 4, partner_late, 0)
    for t in (0, 1):
        where = along_y(2, core)
        data_wait(1, 2 + t, where, t * half_cols, half_cols)
        begin(data_copy(1, 7 + t, where, t * half_cols, half_cols, sibling))
    forward_wait(by_data[3])
    for t in (0, 1):
        data_wait(1, 7 + t, along_y(2, 1 - core), t * half_cols, half_cols)

    factor = 2.0 * kappa / width
    q_mine, q_other = around(y + 2) * 2 + mine, around(y + 2) * 2 + 1 - mine
    norms(q_other)

    def row_shift(r, carry):
        at = pl.ds(pl.multiple_of(r * 128, 128), 128)
        total = jnp.sum(part[at, :], axis=1, keepdims=True) * (-kappa / width)
        shift[at, :] = jnp.broadcast_to(total, (128, LANES))
        return carry

    lax.fori_loop(0, rows // 128, row_shift, 0)

    def final(block, qs):
        def column(i, carry):
            m = block + i
            cut = pl.ds(pl.multiple_of(m * 256, 256), 256)
            value = scores[:, cut]
            for q in qs:
                value = value + chunk_product(q, m)
            value = value * factor
            scores[:, cut] = value
            for e in (0, 1):
                top = jnp.max(value[:, LANES * e:LANES * (e + 1)] + shift[...], axis=0, keepdims=True)
                colvec[:, pl.ds(pl.multiple_of(m * 256 + e * LANES, LANES), LANES)] = jnp.broadcast_to(top, (8, LANES))
            return carry

        lax.fori_loop(0, 4, column, 0)

    final(near, (q_other,))
    final(other_block, (q_mine, q_other))

    def fold(block, op):
        out = block[0:8]
        for r in range(1, TILE // 8):
            out = op(out, block[8 * r:8 * r + 8])
        return out

    def spread_cols():
        for c in range(chunks):
            colvec[:, lane(c)] = jnp.broadcast_to(colpack[pl.ds(c, 1), :], (8, LANES))

    def tall(ref, c):
        return jnp.concatenate([ref[:, lane(c)]] * (TILE // 8), axis=0)

    def tile_at(t):
        return pl.ds(pl.multiple_of(t * TILE, TILE), TILE)

    def loop(body, init):
        return lax.fori_loop(0, tiles, body, init, unroll=2)

    zeros = tuple(jnp.zeros((8, LANES), jnp.float32) for _ in range(chunks))

    def exp_step(t, accs):
        at = tile_at(t)
        add = shift[at, :]
        return tuple(
            accs[c] + fold(jnp.exp2(scores[at, lane(c)] + add - tall(colvec, c)), jnp.add)
            for c in range(chunks)
        )

    sums = loop(exp_step, zeros)
    for c in range(chunks):
        total = jnp.sum(sums[c], axis=0, keepdims=True)
        col_buf[0, me_col, pl.ds(c, 1), :] = colvec[0:1, lane(c)] + jnp.log(total) * LOG2E
    exchange(col_buf, col_send, col_recv, 0, me_col, csize, col_peer, started)
    col_pot = -log_cols - combine(col_buf, 0, csize)
    colpack[...] = col_pot
    spread_cols()

    def row_step(t, carry):
        at = tile_at(t)
        top = scores[at, lane(0)] + tall(colvec, 0)
        for c in range(1, chunks):
            top = jnp.maximum(top, scores[at, lane(c)] + tall(colvec, c))
        first[at, :] = top
        total = None
        for c in range(chunks):
            value = jnp.exp2(scores[at, lane(c)] + tall(colvec, c) - top)
            scores[at, lane(c)] = value
            total = value if total is None else total + value
        part[at, :] = total
        return carry

    loop(row_step, 0)
    for b in range(row_blocks):
        at = pl.ds(b * LANES, LANES)
        tops = first[at, :].T
        top = jnp.max(tops, axis=0, keepdims=True)
        total = jnp.sum(part[at, :].T * jnp.exp2(tops - top), axis=0, keepdims=True)
        row_buf[0, me_row, pl.ds(b, 1), :] = top + jnp.log(total) * LOG2E
    exchange(row_buf, row_send, row_recv, 0, me_row, rsize, row_peer, started)
    row_lse = combine(row_buf, 0, rsize)
    rowpack[...] = row_lse
    for b in range(row_blocks):
        at = pl.ds(b * LANES, LANES)
        base = jnp.exp2(first[at, :] - spread_lanes(rowpack, b))
        first[at, :] = base
        scale[at, :] = base

    def col_step(t, accs):
        at = tile_at(t)
        mul = scale[at, :]
        return tuple(accs[c] + fold(scores[at, lane(c)] * mul, jnp.add) for c in range(chunks))

    def sum_step(keep_values):
        def body(t, carry):
            at = tile_at(t)
            total = None
            for c in range(chunks):
                value = scores[at, lane(c)] * tall(colvec, c)
                if keep_values:
                    scores[at, lane(c)] = value
                total = value if total is None else total + value
            part[at, :] = total * first[at, :]
            return carry

        return body

    for step in range(1, ITERS):
        sums = loop(col_step, zeros)
        for c in range(chunks):
            col_buf[step, me_col, pl.ds(c, 1), :] = jnp.sum(sums[c], axis=0, keepdims=True)
        exchange(col_buf, col_send, col_recv, step, me_col, csize, col_peer, started)
        ratio = 1.0 / add_slots(col_buf, step, csize)
        colpack[...] = ratio
        spread_cols()
        loop(sum_step(step == ITERS - 1), 0)
        for b in range(row_blocks):
            at = pl.ds(b * LANES, LANES)
            row_buf[step, me_row, pl.ds(b, 1), :] = jnp.sum(part[at, :].T, axis=0, keepdims=True)
        exchange(row_buf, row_send, row_recv, step, me_row, rsize, row_peer, started)
        total = add_slots(row_buf, step, rsize)
        rowpack[...] = 1.0 / total
        for b in range(row_blocks):
            at = pl.ds(b * LANES, LANES)
            scale[at, :] = first[at, :] * spread_lanes(rowpack, b)

    def weigh(r):
        def body(t, carry):
            at = pl.ds(pl.multiple_of(r * (rows // 2) + t * TILE, TILE), TILE)
            mul = scale[at, :]
            for c in range(chunks):
                weights[at, lane(c)] = (scores[at, lane(c)] * mul).astype(jnp.bfloat16)
            return carry

        lax.fori_loop(0, tiles // 2, body, 0, unroll=2)

    def swap_copy(i, to):
        return remote(swap.at[0], swap.at[i], swap_send.at[i], swap_recv.at[i], to)

    def potentials():
        for c in range(chunks):
            sqy[pl.ds(c, 1), :] = jnp.sum(data_part[pl.ds(c * LANES, LANES), :].T, axis=0, keepdims=True)
        cols_pot = (col_pot + jnp.log(ratio) * LOG2E + (log_rows - log_cols)) / kappa + sqy[...] / width
        colpack[...] = cols_pot
        cols_out[...] = colpack[pl.ds(pl.multiple_of(side * 8, 8), 8), :]
        for b in range(row_blocks):
            sqx[pl.ds(b, 1), :] = shift[pl.ds(b * LANES, LANES), :].T[0:1]
        swap[0] = -(log_rows + row_lse + jnp.log(total) * LOG2E + sqx[...]) / kappa
        begin(swap_copy(1, sibling))
        for i in (0, 1):
            begin(remote(
                swap.at[0], swap.at[2 + core], swap_send.at[2 + i], swap_recv.at[2 + core], device(partner, y, z, i)
            ))

    strip = rows // 2

    def half_rows(r):
        return pl.ds(r * strip, strip)

    def block_x(b):
        return jnp.where(b < 2, jnp.where(b == 0, opposite, partner), jnp.where(b == 2, mate, x))

    def product(p, r, to_z):
        cut = pl.ds(pl.multiple_of(lax.rem(to_z, 2) * LANES, LANES), LANES)
        total = None
        for k in (0, 1):
            block = jnp.concatenate(
                [data_all[k, block_x(2 * p + e) * 2 + to_z // 2, :, cut] for e in (0, 1)], axis=1
            )
            value = jnp.dot(
                weights[half_rows(r), k * full_cols:(k + 1) * full_cols], block,
                preferred_element_type=jnp.float32,
            )
            total = value if total is None else total + value
        return total

    def sum_copy(b, t, index, src, dst):
        to = device(x, y, around(z + HOP[t]), core)
        return remote(src, dst, sum_send.at[b, t, index], sum_recv.at[b, t, index], to)

    def far_copy(b, t):
        return sum_copy(b, t, 0, out_buf.at[b, 2, half_rows(t)], far_buf.at[b, t])

    def direct_copy(b, t):
        at = half_rows(1 - t)
        return sum_copy(b, t, 1, out_buf.at[b, t, at], near_buf.at[b, t, at])

    def added_copy(b, t):
        at = half_rows(t)
        return sum_copy(b, t, 2, out_buf.at[b, t, at], near_buf.at[b, t, at])

    def relay_copy():
        return remote(own_buf.at[0], relay_in, in_send.at[0], in_recv.at[4], device(mate, y, z, core))

    def partner_copy(a):
        return remote(own_buf.at[1], in_sum.at[a], in_send.at[1], in_recv.at[a], device(partner, y, z, kind))

    def mate_copy(a):
        return remote(mate_out, mate_in.at[a], in_send.at[2], in_recv.at[2 + a], device(mate, y, z, kind))

    def stay_copy(a):
        return remote(own_buf.at[3], in_sum.at[a], in_send.at[3], in_recv.at[a], sibling)

    def add_far(b):
        for t in (0, 1):
            far_copy(b, t).wait_recv()
            out_buf[b, t, half_rows(t), :] = (keep[b, t] + far_buf[b, t].astype(jnp.float32)).astype(jnp.bfloat16)
            added_copy(b, t).start()

    def add_near(b):
        for t in (0, 1):
            direct_copy(b, t).wait_recv()
            added_copy(b, t).wait_recv()
        own_buf[b] = own_buf[b] + near_buf[b, 0].astype(jnp.float32) + near_buf[b, 1].astype(jnp.float32)

    def send_pair(p, carry):
        @pl.when(p == 0)
        def _():
            weigh(0)

        for t in (0, 1):
            if t == 1:
                @pl.when(p == 0)
                def _():
                    weigh(1)

            value = product(p, t, around(z + 2))
            for e in (0, 1):
                out_buf[2 * p + e, 2, half_rows(t), :] = value[:, lane(e)].astype(jnp.bfloat16)
            far_copy(2 * p, t).start()

        @pl.when(p > 0)
        def _():
            add_near(0)
            relay_copy().start()

        for t in (0, 1):
            value = product(p, 1 - t, around(z + HOP[t]))
            for e in (0, 1):
                out_buf[2 * p + e, t, half_rows(1 - t), :] = value[:, lane(e)].astype(jnp.bfloat16)
            direct_copy(2 * p, t).start()
            value = product(p, t, around(z + HOP[t]))
            for e in (0, 1):
                keep[2 * p + e, t] = value[:, lane(e)]

        @pl.when(p > 0)
        def _():
            add_far(1)

        @pl.when(p == 0)
        def _():
            add_far(0)

        for t in (0, 1):
            far_copy(2 * p + 1, t).start()
        for t in (0, 1):
            direct_copy(2 * p + 1, t).start()
        for r in (0, 1):
            value = product(p, r, z)
            for e in (0, 1):
                own_buf[2 * p + e, half_rows(r), :] = value[:, lane(e)]
        return carry

    lax.fori_loop(0, 2, send_pair, 0)
    add_far(2)
    potentials()
    add_near(1)
    relay_copy().wait_recv()
    own_buf[1] = own_buf[1] + relay_in[...]
    partner_copy(core).start()
    add_near(2)
    mate_out[...] = own_buf[2].astype(jnp.bfloat16)
    mate_copy(core).start()
    add_far(3)

    swap_copy(1, sibling).wait_recv()
    for i in (0, 1):
        remote(swap.at[0], swap.at[2 + i], swap_send.at[2 + i], swap_recv.at[2 + i], sibling).wait_recv()
    half = rows // LANES
    for a in (0, 1):
        mine_row = jnp.where(core == a, swap[0], swap[1])
        rows_out[pl.ds(a * half, half), :] = jnp.where(home, mine_row, swap[2 + a])

    add_near(3)

    @pl.when(home)
    def _():
        in_sum[core] = own_buf[3]
        stay_copy(1 - core).wait_recv()
        for a in (0, 1):
            mate_copy(a).wait_recv()
            in_sum[a] = in_sum[a] + mate_in[a].astype(jnp.float32)

    @pl.when(jnp.logical_not(home))
    def _():
        stay_copy(core).start()
        for a in (0, 1):
            partner_copy(a).wait_recv()

    def result_copy(a):
        return pltpu.make_async_copy(in_sum.at[a], targets.at[pl.ds(a * rows, rows)], local_sems.at[a])

    for a in (0, 1):
        result_copy(a).start()

    def settle(b, carry):
        for t in (0, 1):
            far_copy(b, t).wait_send()
            direct_copy(b, t).wait_send()
            added_copy(b, t).wait_send()
        return carry

    lax.fori_loop(0, SIDE, settle, 0)
    for a in (0, 1):
        result_copy(a).wait()
    relay_copy().wait_send()
    partner_copy(core).wait_send()
    mate_copy(core).wait_send()

    @pl.when(jnp.logical_not(home))
    def _():
        stay_copy(core).wait_send()

    for copy in started:
        copy.wait_send()

    @pl.when(home)
    def _():
        aside.wait_send()
        for t in (0, 1):
            for a in (0, 1):
                own_round(t, a).wait_send()


def hand_on(targets, rows_pot, cols_pot, targets_out, rows_out, cols_out, sems):
    size = targets.shape[0] // PARTS
    copies = [
        pltpu.make_async_copy(targets.at[pl.ds(i * size, size)], targets_out.at[pl.ds(i * size, size)], sems.at[i])
        for i in range(PARTS)
    ]
    copies.append(pltpu.make_async_copy(rows_pot, rows_out, sems.at[PARTS]))
    copies.append(pltpu.make_async_copy(cols_pot, cols_out, sems.at[PARTS + 1]))
    for copy in copies:
        copy.start()
    for copy in copies:
        copy.wait()


def shards(noise_latents, data_latents):
    nsize = lax.axis_size("noise")
    dsize = lax.axis_size("dp")
    block, piece = noise_latents.shape
    rows, cols = block // 2, 2 * data_latents.shape[0]
    rsize, csize = dsize // 2, nsize * 2
    vmem = pl.BlockSpec(memory_space=pltpu.VMEM)
    f32, bf16 = jnp.float32, jnp.bfloat16
    strip = rows // 2
    row_vec, col_vec = (rows // LANES, LANES), (cols // LANES, LANES)
    sems = pltpu.SemaphoreType.DMA
    targets, rows_pot, cols_pot = pl.pallas_call(
        functools.partial(kernel, rsize, csize, piece * dsize),
        out_shape=(
            jax.ShapeDtypeStruct((block, piece), f32),
            jax.ShapeDtypeStruct((block // LANES, LANES), f32),
            jax.ShapeDtypeStruct((cols // 2 // LANES, LANES), f32),
        ),
        in_specs=[pl.BlockSpec(memory_space=pl.ANY)] * 2,
        out_specs=(pl.BlockSpec(memory_space=pl.ANY), vmem, vmem),
        scratch_shapes=[
            pltpu.VMEM((dsize, rows, piece), bf16),
            pltpu.VMEM((2, nsize) + data_latents.shape, bf16),
            pltpu.VMEM((rows, cols), f32),
            pltpu.VMEM((rows, cols), bf16),
            pltpu.VMEM((rows, LANES), f32),
            pltpu.VMEM((rows, LANES), f32),
            pltpu.VMEM((rows, LANES), f32),
            pltpu.VMEM((rows, LANES), f32),
            pltpu.VMEM((cols, LANES), f32),
            pltpu.VMEM((8, cols), f32),
            pltpu.VMEM(row_vec, f32),
            pltpu.VMEM(col_vec, f32),
            pltpu.VMEM(row_vec, f32),
            pltpu.VMEM(col_vec, f32),
            pltpu.VMEM((4,) + row_vec, f32),
            pltpu.VMEM((ITERS, csize) + col_vec, f32),
            pltpu.VMEM((ITERS, rsize) + row_vec, f32),
            pltpu.VMEM((SIDE, 3, rows, LANES), bf16),
            pltpu.VMEM((SIDE, rows, LANES), f32),
            pltpu.VMEM((SIDE, 2, strip, LANES), bf16),
            pltpu.VMEM((SIDE, 2, rows, LANES), bf16),
            pltpu.VMEM((2, rows, LANES), f32),
            sems((ITERS,)),
            sems((ITERS,)),
            sems((ITERS,)),
            sems((ITERS,)),
            sems((4,)),
            sems((4,)),
            sems((4,)),
            sems((4,)),
            sems((SIDE, 2, 2)),
            sems((SIDE, 2, 2)),
            sems((2, 13)),
            sems((2, 13)),
            sems((SIDE, 2, 3)),
            sems((SIDE, 2, 3)),
            sems((SIDE,)),
            sems((5,)),
            pltpu.VMEM((SIDE, 2, strip, LANES), f32),
            sems((2,)),
            sems((2, 2)),
            pltpu.VMEM((rows, LANES), f32),
            pltpu.VMEM((rows, LANES), bf16),
            pltpu.VMEM((2, rows, LANES), bf16),
        ],
        compiler_params=pltpu.CompilerParams(
            collective_id=0, has_side_effects=True, vmem_limit_bytes=50 * 2**20
        ),
    )(noise_latents, data_latents)
    results = (targets, rows_pot, cols_pot)
    targets, rows_pot, cols_pot = pl.pallas_call(
        hand_on,
        out_shape=tuple(jax.ShapeDtypeStruct(a.shape, a.dtype) for a in results),
        in_specs=[pl.BlockSpec(memory_space=pl.ANY)] * 3,
        out_specs=(pl.BlockSpec(memory_space=pl.ANY),) * 3,
        scratch_shapes=[sems((PARTS + 2,))],
    )(*results)
    return targets, rows_pot.reshape(block), cols_pot.reshape(cols // 2)


def solution(mesh):
    return jax.shard_map(
        shards,
        mesh=mesh,
        in_specs=(P("noise", "dp"), P("dp", "noise")),
        out_specs=(P("noise", "dp"), P("noise"), P("dp")),
        check_vma=False,
    )
```

```python
import functools
import math

import jax
import jax.numpy as jnp
from jax import lax
from jax.experimental import pallas as pl
from jax.experimental.pallas import tpu as pltpu
from jax.sharding import PartitionSpec as P

ITERS = 3
EPSILON = 0.04
LOG2E = 1.0 / math.log(2.0)
MESH = pl.DeviceIdType.MESH
LANES = 128
TILE = 32
SIDE = 4
PARTS = 4


def wrap(index, size):
    return lax.rem(index, size)


def spread_lanes(ref, row):
    return jnp.broadcast_to(ref[pl.ds(row, 1), :], (LANES, LANES)).T


def exchange(buf, send, recv, step, me, size, peer_id, started):
    for k in range(1, size):
        pltpu.make_async_remote_copy(
            src_ref=buf.at[step, me],
            dst_ref=buf.at[step, me],
            send_sem=send.at[step],
            recv_sem=recv.at[step],
            device_id=peer_id(wrap(me + k, size)),
            device_id_type=MESH,
        ).start()
    slots = buf.at[step, pl.ds(0, size - 1)]
    every = pltpu.make_async_remote_copy(
        src_ref=slots,
        dst_ref=slots,
        send_sem=send.at[step],
        recv_sem=recv.at[step],
        device_id=peer_id(wrap(me + 1, size)),
        device_id_type=MESH,
    )
    every.wait_recv()
    started.append(every)


def combine(buf, step, size):
    top = buf[step, 0]
    for s in range(1, size):
        top = jnp.maximum(top, buf[step, s])
    total = jnp.exp2(buf[step, 0] - top)
    for s in range(1, size):
        total = total + jnp.exp2(buf[step, s] - top)
    return top + jnp.log(total) * LOG2E


def add_slots(buf, step, size):
    total = buf[step, 0]
    for s in range(1, size):
        total = total + buf[step, s]
    return total


def kernel(
    rsize, csize, width,
    noise_ref, data_ref,
    targets, rows_out, cols_out,
    noise_all, data_all, scores, weights,
    shift, first, scale, part, data_part, colvec, rowpack, colpack, sqx, sqy, swap,
    col_buf, row_buf, out_buf, own_buf, far_buf, near_buf, in_sum,
    col_send, col_recv, row_send, row_recv, swap_send, swap_recv,
    cross_send, cross_recv, noise_send, noise_recv, data_send, data_recv,
    sum_send, sum_recv, in_send, in_recv, keep, local_sems, own_send, far_send, relay_in, mate_out, mate_in,
):
    rows, cols = scores.shape
    n = lax.axis_index("noise")
    d = lax.axis_index("dp")
    x, z = d // SIDE, lax.rem(d, SIDE)
    y, core = n // 2, lax.rem(n, 2)
    kind = lax.rem((x + 1) // 2, 2)
    pair = x // 2
    side = lax.rem(x, 2)
    home = core == kind
    kappa = LOG2E / EPSILON
    log_rows = math.log2(rows * csize)
    log_cols = math.log2(cols * rsize)
    chunks = cols // LANES
    row_blocks = rows // LANES
    tiles = rows // TILE
    started = []

    def around(value):
        return lax.rem(value + SIDE, SIDE)

    def device(xi, yi, zi, ci):
        return (yi * 2 + ci, xi * SIDE + zi)

    def x_at(which, of_kind):
        return which * (3 - 2 * of_kind) + of_kind

    me_row = pair * SIDE + z
    me_col = y * 4 + kind * 2 + core

    def row_peer(p):
        return device(x_at(p // SIDE, kind), y, lax.rem(p, SIDE), core)

    def col_peer(p):
        return device(x_at(pair, lax.rem(p // 2, 2)), p // 4, z, lax.rem(p, 2))

    sibling = device(x, y, z, 1 - core)
    partner = x + 1 - 2 * side
    mate = SIDE - 1 - x
    opposite = around(x + 2)

    barrier = pltpu.get_barrier_semaphore()
    greeted = [row_peer(wrap(me_row + k, rsize)) for k in range(1, rsize)]
    greeted += [col_peer(wrap(me_col + k, csize)) for k in range(1, csize)]
    greeted += [device(opposite, y, z, 0), device(opposite, y, z, 1), device(mate, y, z, 1 - core)]
    greeted += [device(x, y, around(z + step), 1 - core) for step in (1, -1)]
    for to in greeted:
        pl.semaphore_signal(barrier, inc=1, device_id=to, device_id_type=MESH)
    pl.semaphore_wait(barrier, len(greeted))

    def remote(src, dst, send, recv, to):
        return pltpu.make_async_remote_copy(
            src_ref=src, dst_ref=dst, send_sem=send, recv_sem=recv, device_id=to, device_id_type=MESH
        )

    def begin(copy):
        copy.start()
        started.append(copy)

    def lane(c):
        return slice(LANES * c, LANES * (c + 1))

    HOP = (1, -1)
    own = x * SIDE + z

    def cross_copy(i, half, to):
        return remote(
            noise_ref.at[pl.ds(half * rows, rows)], noise_all.at[own], cross_send.at[i], cross_recv.at[x], to
        )

    def cross_wait(xi):
        remote(
            noise_ref.at[pl.ds(0, rows)], noise_all.at[xi * SIDE + z], cross_send.at[0], cross_recv.at[xi], sibling
        ).wait_recv()

    there = jnp.where(home, mate, partner)
    aside = cross_copy(2, 1 - core, sibling)

    def noise_copy(xi, t, forward, slot):
        at = pl.ds(t * (rows // 2), rows // 2) if forward else pl.ds(0, rows)
        f = int(forward)
        return remote(
            noise_all.at[slot, at], noise_all.at[slot, at],
            noise_send.at[xi, t, f], noise_recv.at[xi, t, f], device(x, y, around(z + HOP[t]), core),
        )

    def noise_wait(xi, t, forward):
        slot = xi * SIDE + around(z - HOP[t] * (2 if forward else 1))
        noise_copy(xi, t, forward, slot).wait_recv()
        return slot

    def data_copy(r, index, where, lo, size, to, own=False):
        at = pl.ds(lo, size)
        block = side if r == 0 else 1 - side
        dst = data_all.at[block, where, at]
        return remote(data_ref.at[at] if own else dst, dst, data_send.at[r, index], data_recv.at[r, index], to)

    half_cols = cols // 4
    full_cols = cols // 2

    def along_y(step, c):
        return around(y + step) * 2 + c

    def data_wait(r, index, where, lo, size):
        data_copy(r, index, where, lo, size, sibling).wait_recv()

    HALF = 9

    def cross_data(h, own=False):
        at = pl.ds(h * half_cols, half_cols)
        dst = data_all.at[side if own else 1 - side, n, at]
        return remote(
            data_ref.at[at], dst, data_send.at[1, 11 + h], data_recv.at[1, 11 + h], device(partner, y, z, core)
        )

    def partner_y(t, h, back=0):
        where = around(y + back) * 2 + core
        to = device(x, around(y + HOP[t]), z, core)
        return t if h == 0 else HALF + t, where, h * half_cols, half_cols, to

    def partner_wait(t, h):
        data_copy(1, *partner_y(t, h, -HOP[t])).wait_recv()

    def own_round(t, a):
        return remote(
            noise_ref.at[pl.ds(a * rows, rows)], noise_all.at[own],
            own_send.at[t, a], noise_recv.at[x, t, 0], device(x, y, around(z + HOP[t]), a),
        )

    def own_half():
        return pltpu.make_async_copy(
            noise_ref.at[pl.ds(pl.multiple_of(core * rows, rows), rows)], noise_all.at[own], local_sems.at[0]
        )

    @pl.when(home)
    def _():
        for t in (0, 1):
            for a in (0, 1):
                own_round(t, a).start()
        aside.start()

    begin(cross_copy(0, 0, device(there, y, z, 0)))
    begin(cross_copy(1, 1, device(there, y, z, 1)))
    for t in (0, 1):
        begin(data_copy(0, t, n, 0, full_cols, device(x, around(y + HOP[t]), z, core), own=True))
    @pl.when(home)
    def _():
        own_half().start()

    data_own = pltpu.make_async_copy(data_ref, data_all.at[side, n], local_sems.at[1])
    data_own.start()
    part[...] = jnp.zeros_like(part)
    data_part[...] = jnp.zeros_like(data_part)

    def round_z(xi):
        for t in (0, 1):
            begin(noise_copy(xi, t, False, xi * SIDE + z))

    def forward_z(xi):
        for t in (0, 1):
            begin(noise_copy(xi, t, True, noise_wait(xi, t, False)))

    def far_noise(xi, t):
        slot = xi * SIDE + around(z + 2)
        at = pl.ds(t * (rows // 2), rows // 2)
        return remote(
            noise_all.at[slot, at], noise_all.at[slot, at],
            far_send.at[xi, t], noise_recv.at[xi, t, 1], device(mate, y, z, core),
        )

    def share_far(xi):
        for t in (0, 1):
            noise_wait(xi, t, True)
            begin(far_noise(xi, t))

    def far_wait(xi):
        for t in (0, 1):
            far_noise(xi, t).wait_recv()

    def far_data(t, block):
        where = along_y(2, core)
        at = pl.ds(t * half_cols, half_cols)
        dst = data_all.at[block, where, at]
        return remote(dst, dst, data_send.at[1, 2 + t], data_recv.at[1, 2 + t], device(partner, y, z, core))

    cross_wait(partner)
    slot = partner * SIDE + z
    begin(remote(
        noise_all.at[slot], noise_all.at[slot], cross_send.at[3], cross_recv.at[partner], device(mate, y, z, core)
    ))
    round_z(partner)
    for h in (0, 1):
        begin(cross_data(h, own=True))
    begin(data_copy(0, 4, n, 0, full_cols, sibling, own=True))
    forward_z(x)
    cross_wait(mate)
    round_z(mate)
    for t in (0, 1):
        where = along_y(-HOP[t], core)
        data_wait(0, t, where, 0, full_cols)
        begin(data_copy(0, 2 + t, where, t * half_cols, half_cols, device(x, around(y + HOP[t]), z, core)))
        begin(data_copy(0, 5 + t, where, 0, full_cols, sibling))
    cross_data(0).wait_recv()
    for t in (0, 1):
        begin(data_copy(1, *partner_y(t, 0)))
    forward_z(partner)
    cross_wait(opposite)
    round_z(opposite)
    share_far(x)
    cross_data(1).wait_recv()
    for t in (0, 1):
        begin(data_copy(1, *partner_y(t, 1)))
    begin(data_copy(1, 4, n, 0, full_cols, sibling))
    for t in (0, 1):
        where = along_y(2, core)
        data_wait(0, 2 + t, where, t * half_cols, half_cols)
        begin(far_data(t, side))
        begin(data_copy(0, 7 + t, where, t * half_cols, half_cols, sibling))

    def squares(block):
        value = block.astype(jnp.float32)
        return value * value

    def chunk_product(xi, m):
        left = jnp.concatenate([noise_all[xi * SIDE + i] for i in range(SIDE)], axis=1)
        cut = pl.ds(pl.multiple_of(m * 256, 256), 256)
        here = pl.ds(pl.multiple_of(lax.rem(m, 4) * 256, 256), 256)
        pieces = [data_all[m // 4, xi * 2 + i, here, :] for i in (0, 1)]
        total = data_part[cut, :]
        for piece in pieces:
            total = total + squares(piece[:, :LANES]) + squares(piece[:, LANES:])
        data_part[cut, :] = total
        return lax.dot_general(
            left, jnp.concatenate(pieces, axis=1), (((1,), (1,)), ((), ())), preferred_element_type=jnp.float32
        )

    def norms(xi):
        def norm(r, carry):
            cut = pl.ds(pl.multiple_of(r * 64, 64), 64)
            total = part[cut, :]
            for i in range(SIDE):
                total = total + squares(noise_all[xi * SIDE + i, cut, :])
            part[cut, :] = total
            return carry

        lax.fori_loop(0, rows // 64, norm, 0)

    near, other_block = side * 4, 4 - side * 4

    def unit(block, xs, fresh):
        def column(i, carry):
            m = block + i
            cut = pl.ds(pl.multiple_of(m * 256, 256), 256)
            value = None if fresh else scores[:, cut]
            for xi in xs:
                value = chunk_product(xi, m) if value is None else value + chunk_product(xi, m)
            scores[:, cut] = value
            return carry

        lax.fori_loop(0, 4, column, 0)

    data_own.wait()
    data_wait(0, 4, along_y(0, 1 - core), 0, full_cols)
    for t in (0, 1):
        data_wait(0, 5 + t, along_y(-HOP[t], 1 - core), 0, full_cols)
    for t in (0, 1):
        data_wait(0, 7 + t, along_y(2, 1 - core), t * half_cols, half_cols)

    @pl.when(home)
    def _():
        own_half().wait()

    @pl.when(jnp.logical_not(home))
    def _():
        cross_wait(x)

    unit(near, (x,), True)
    share_far(partner)
    norms(x)
    for t in (0, 1):
        noise_wait(mate, t, False)
    far_wait(mate)
    unit(near, (mate,), False)
    norms(mate)
    for h in (0, 1):
        for t in (0, 1):
            partner_wait(t, h)
    for t in (0, 1):
        begin(data_copy(1, 5 + t, along_y(-HOP[t], core), 0, full_cols, sibling))
    unit(near, (partner,), False)
    norms(partner)
    for t in (0, 1):
        noise_wait(opposite, t, False)
    far_wait(opposite)
    for t in (0, 1):
        far_data(t, 1 - side).wait_recv()
        begin(data_copy(1, 7 + t, along_y(2, core), t * half_cols, half_cols, sibling))
    norms(opposite)

    factor = 2.0 * kappa / width

    def row_shift(r, carry):
        at = pl.ds(pl.multiple_of(r * 128, 128), 128)
        total = jnp.sum(part[at, :], axis=1, keepdims=True) * (-kappa / width)
        shift[at, :] = jnp.broadcast_to(total, (128, LANES))
        return carry

    lax.fori_loop(0, rows // 128, row_shift, 0)

    def final(block, xi):
        def column(i, carry):
            m = block + i
            cut = pl.ds(pl.multiple_of(m * 256, 256), 256)
            value = (scores[:, cut] + chunk_product(xi, m)) * factor
            scores[:, cut] = value
            for e in (0, 1):
                top = jnp.max(value[:, LANES * e:LANES * (e + 1)] + shift[...], axis=0, keepdims=True)
                colvec[:, pl.ds(pl.multiple_of(m * 256 + e * LANES, LANES), LANES)] = jnp.broadcast_to(top, (8, LANES))
            return carry

        lax.fori_loop(0, 4, column, 0)

    final(near, opposite)
    data_wait(1, 4, along_y(0, 1 - core), 0, full_cols)
    for t in (0, 1):
        data_wait(1, 5 + t, along_y(-HOP[t], 1 - core), 0, full_cols)
    unit(other_block, (y, around(y + 1), around(y - 1)), True)
    for t in (0, 1):
        data_wait(1, 7 + t, along_y(2, 1 - core), t * half_cols, half_cols)
    final(other_block, around(y + 2))

    def fold(block, op):
        out = block[0:8]
        for r in range(1, TILE // 8):
            out = op(out, block[8 * r:8 * r + 8])
        return out

    def spread_cols():
        for c in range(chunks):
            colvec[:, lane(c)] = jnp.broadcast_to(colpack[pl.ds(c, 1), :], (8, LANES))

    def tall(ref, c):
        return jnp.concatenate([ref[:, lane(c)]] * (TILE // 8), axis=0)

    def tile_at(t):
        return pl.ds(pl.multiple_of(t * TILE, TILE), TILE)

    def loop(body, init):
        return lax.fori_loop(0, tiles, body, init, unroll=2)

    zeros = tuple(jnp.zeros((8, LANES), jnp.float32) for _ in range(chunks))

    def exp_step(t, accs):
        at = tile_at(t)
        add = shift[at, :]
        return tuple(
            accs[c] + fold(jnp.exp2(scores[at, lane(c)] + add - tall(colvec, c)), jnp.add)
            for c in range(chunks)
        )

    sums = loop(exp_step, zeros)
    for c in range(chunks):
        total = jnp.sum(sums[c], axis=0, keepdims=True)
        col_buf[0, me_col, pl.ds(c, 1), :] = colvec[0:1, lane(c)] + jnp.log(total) * LOG2E
    exchange(col_buf, col_send, col_recv, 0, me_col, csize, col_peer, started)
    col_pot = -log_cols - combine(col_buf, 0, csize)
    colpack[...] = col_pot
    spread_cols()

    def row_step(t, carry):
        at = tile_at(t)
        top = scores[at, lane(0)] + tall(colvec, 0)
        for c in range(1, chunks):
            top = jnp.maximum(top, scores[at, lane(c)] + tall(colvec, c))
        first[at, :] = top
        total = None
        for c in range(chunks):
            value = jnp.exp2(scores[at, lane(c)] + tall(colvec, c) - top)
            scores[at, lane(c)] = value
            total = value if total is None else total + value
        part[at, :] = total
        return carry

    loop(row_step, 0)
    for b in range(row_blocks):
        at = pl.ds(b * LANES, LANES)
        tops = first[at, :].T
        top = jnp.max(tops, axis=0, keepdims=True)
        total = jnp.sum(part[at, :].T * jnp.exp2(tops - top), axis=0, keepdims=True)
        row_buf[0, me_row, pl.ds(b, 1), :] = top + jnp.log(total) * LOG2E
    exchange(row_buf, row_send, row_recv, 0, me_row, rsize, row_peer, started)
    row_lse = combine(row_buf, 0, rsize)
    rowpack[...] = row_lse
    for b in range(row_blocks):
        at = pl.ds(b * LANES, LANES)
        base = jnp.exp2(first[at, :] - spread_lanes(rowpack, b))
        first[at, :] = base
        scale[at, :] = base

    def col_step(t, accs):
        at = tile_at(t)
        mul = scale[at, :]
        return tuple(accs[c] + fold(scores[at, lane(c)] * mul, jnp.add) for c in range(chunks))

    def sum_step(keep_values):
        def body(t, carry):
            at = tile_at(t)
            total = None
            for c in range(chunks):
                value = scores[at, lane(c)] * tall(colvec, c)
                if keep_values:
                    scores[at, lane(c)] = value
                total = value if total is None else total + value
            part[at, :] = total * first[at, :]
            return carry

        return body

    for step in range(1, ITERS):
        sums = loop(col_step, zeros)
        for c in range(chunks):
            col_buf[step, me_col, pl.ds(c, 1), :] = jnp.sum(sums[c], axis=0, keepdims=True)
        exchange(col_buf, col_send, col_recv, step, me_col, csize, col_peer, started)
        ratio = 1.0 / add_slots(col_buf, step, csize)
        colpack[...] = ratio
        spread_cols()
        loop(sum_step(step == ITERS - 1), 0)
        for b in range(row_blocks):
            at = pl.ds(b * LANES, LANES)
            row_buf[step, me_row, pl.ds(b, 1), :] = jnp.sum(part[at, :].T, axis=0, keepdims=True)
        exchange(row_buf, row_send, row_recv, step, me_row, rsize, row_peer, started)
        total = add_slots(row_buf, step, rsize)
        rowpack[...] = 1.0 / total
        for b in range(row_blocks):
            at = pl.ds(b * LANES, LANES)
            scale[at, :] = first[at, :] * spread_lanes(rowpack, b)

    def weigh(r):
        def body(t, carry):
            at = pl.ds(pl.multiple_of(r * (rows // 2) + t * TILE, TILE), TILE)
            mul = scale[at, :]
            for c in range(chunks):
                weights[at, lane(c)] = (scores[at, lane(c)] * mul).astype(jnp.bfloat16)
            return carry

        lax.fori_loop(0, tiles // 2, body, 0, unroll=2)

    def swap_copy(i, to):
        return remote(swap.at[0], swap.at[i], swap_send.at[i], swap_recv.at[i], to)

    def potentials():
        for c in range(chunks):
            sqy[pl.ds(c, 1), :] = jnp.sum(data_part[pl.ds(c * LANES, LANES), :].T, axis=0, keepdims=True)
        cols_pot = (col_pot + jnp.log(ratio) * LOG2E + (log_rows - log_cols)) / kappa + sqy[...] / width
        colpack[...] = cols_pot
        cols_out[...] = colpack[pl.ds(pl.multiple_of(side * 8, 8), 8), :]
        for b in range(row_blocks):
            sqx[pl.ds(b, 1), :] = shift[pl.ds(b * LANES, LANES), :].T[0:1]
        swap[0] = -(log_rows + row_lse + jnp.log(total) * LOG2E + sqx[...]) / kappa
        begin(swap_copy(1, sibling))
        for i in (0, 1):
            begin(remote(
                swap.at[0], swap.at[2 + core], swap_send.at[2 + i], swap_recv.at[2 + core], device(partner, y, z, i)
            ))

    strip = rows // 2

    def half_rows(r):
        return pl.ds(r * strip, strip)

    def block_x(b):
        return jnp.where(b < 2, jnp.where(b == 0, opposite, partner), jnp.where(b == 2, mate, x))

    def product(p, r, to_z):
        cut = pl.ds(pl.multiple_of(lax.rem(to_z, 2) * LANES, LANES), LANES)
        total = None
        for k in (0, 1):
            block = jnp.concatenate(
                [data_all[k, block_x(2 * p + e) * 2 + to_z // 2, :, cut] for e in (0, 1)], axis=1
            )
            value = jnp.dot(
                weights[half_rows(r), k * full_cols:(k + 1) * full_cols], block,
                preferred_element_type=jnp.float32,
            )
            total = value if total is None else total + value
        return total

    def sum_copy(b, t, index, src, dst):
        to = device(x, y, around(z + HOP[t]), core)
        return remote(src, dst, sum_send.at[b, t, index], sum_recv.at[b, t, index], to)

    def far_copy(b, t):
        return sum_copy(b, t, 0, out_buf.at[b, 2, half_rows(t)], far_buf.at[b, t])

    def direct_copy(b, t):
        at = half_rows(1 - t)
        return sum_copy(b, t, 1, out_buf.at[b, t, at], near_buf.at[b, t, at])

    def added_copy(b, t):
        at = half_rows(t)
        return sum_copy(b, t, 2, out_buf.at[b, t, at], near_buf.at[b, t, at])

    def relay_copy():
        return remote(own_buf.at[0], relay_in, in_send.at[0], in_recv.at[4], device(mate, y, z, core))

    def partner_copy(a):
        return remote(own_buf.at[1], in_sum.at[a], in_send.at[1], in_recv.at[a], device(partner, y, z, kind))

    def mate_copy(a):
        return remote(mate_out, mate_in.at[a], in_send.at[2], in_recv.at[2 + a], device(mate, y, z, kind))

    def stay_copy(a):
        return remote(own_buf.at[3], in_sum.at[a], in_send.at[3], in_recv.at[a], sibling)

    def add_far(b):
        for t in (0, 1):
            far_copy(b, t).wait_recv()
            out_buf[b, t, half_rows(t), :] = (keep[b, t] + far_buf[b, t].astype(jnp.float32)).astype(jnp.bfloat16)
            added_copy(b, t).start()

    def add_near(b):
        for t in (0, 1):
            direct_copy(b, t).wait_recv()
            added_copy(b, t).wait_recv()
        own_buf[b] = own_buf[b] + near_buf[b, 0].astype(jnp.float32) + near_buf[b, 1].astype(jnp.float32)

    def send_pair(p, carry):
        @pl.when(p == 0)
        def _():
            weigh(0)

        for t in (0, 1):
            if t == 1:
                @pl.when(p == 0)
                def _():
                    weigh(1)

            value = product(p, t, around(z + 2))
            for e in (0, 1):
                out_buf[2 * p + e, 2, half_rows(t), :] = value[:, lane(e)].astype(jnp.bfloat16)
            far_copy(2 * p, t).start()

        @pl.when(p > 0)
        def _():
            add_near(0)
            relay_copy().start()

        for t in (0, 1):
            value = product(p, 1 - t, around(z + HOP[t]))
            for e in (0, 1):
                out_buf[2 * p + e, t, half_rows(1 - t), :] = value[:, lane(e)].astype(jnp.bfloat16)
            direct_copy(2 * p, t).start()
            value = product(p, t, around(z + HOP[t]))
            for e in (0, 1):
                keep[2 * p + e, t] = value[:, lane(e)]

        @pl.when(p > 0)
        def _():
            add_far(1)

        @pl.when(p == 0)
        def _():
            add_far(0)

        for t in (0, 1):
            far_copy(2 * p + 1, t).start()
        for t in (0, 1):
            direct_copy(2 * p + 1, t).start()
        for r in (0, 1):
            value = product(p, r, z)
            for e in (0, 1):
                own_buf[2 * p + e, half_rows(r), :] = value[:, lane(e)]
        return carry

    lax.fori_loop(0, 2, send_pair, 0)
    add_far(2)
    potentials()
    add_near(1)
    relay_copy().wait_recv()
    own_buf[1] = own_buf[1] + relay_in[...]
    partner_copy(core).start()
    add_near(2)
    mate_out[...] = own_buf[2].astype(jnp.bfloat16)
    mate_copy(core).start()
    add_far(3)

    swap_copy(1, sibling).wait_recv()
    for i in (0, 1):
        remote(swap.at[0], swap.at[2 + i], swap_send.at[2 + i], swap_recv.at[2 + i], sibling).wait_recv()
    half = rows // LANES
    for a in (0, 1):
        mine_row = jnp.where(core == a, swap[0], swap[1])
        rows_out[pl.ds(a * half, half), :] = jnp.where(home, mine_row, swap[2 + a])

    add_near(3)

    @pl.when(home)
    def _():
        in_sum[core] = own_buf[3]
        stay_copy(1 - core).wait_recv()
        for a in (0, 1):
            mate_copy(a).wait_recv()
            in_sum[a] = in_sum[a] + mate_in[a].astype(jnp.float32)

    @pl.when(jnp.logical_not(home))
    def _():
        stay_copy(core).start()
        for a in (0, 1):
            partner_copy(a).wait_recv()

    def result_copy(a):
        return pltpu.make_async_copy(in_sum.at[a], targets.at[pl.ds(a * rows, rows)], local_sems.at[a])

    for a in (0, 1):
        result_copy(a).start()

    def settle(b, carry):
        for t in (0, 1):
            far_copy(b, t).wait_send()
            direct_copy(b, t).wait_send()
            added_copy(b, t).wait_send()
        return carry

    lax.fori_loop(0, SIDE, settle, 0)
    for a in (0, 1):
        result_copy(a).wait()
    relay_copy().wait_send()
    partner_copy(core).wait_send()
    mate_copy(core).wait_send()

    @pl.when(jnp.logical_not(home))
    def _():
        stay_copy(core).wait_send()

    for copy in started:
        copy.wait_send()

    @pl.when(home)
    def _():
        aside.wait_send()
        for t in (0, 1):
            for a in (0, 1):
                own_round(t, a).wait_send()


def hand_on(targets, rows_pot, cols_pot, targets_out, rows_out, cols_out, stage, row_stage, col_stage, sems):
    size = targets.shape[0] // PARTS
    legs = [
        (targets.at[pl.ds(i * size, size)], stage.at[i], targets_out.at[pl.ds(i * size, size)]) for i in range(PARTS)
    ]
    legs += [(rows_pot, row_stage, rows_out), (cols_pot, col_stage, cols_out)]
    first = [pltpu.make_async_copy(src, mid, sems.at[i, 0]) for i, (src, mid, _) in enumerate(legs)]
    second = [pltpu.make_async_copy(mid, dst, sems.at[i, 1]) for i, (_, mid, dst) in enumerate(legs)]
    for copy in first:
        copy.start()
    for before, copy in zip(first, second):
        before.wait()
        copy.start()
    for copy in second:
        copy.wait()


def shards(noise_latents, data_latents):
    nsize = lax.axis_size("noise")
    dsize = lax.axis_size("dp")
    block, piece = noise_latents.shape
    rows, cols = block // 2, 2 * data_latents.shape[0]
    rsize, csize = dsize // 2, nsize * 2
    vmem = pl.BlockSpec(memory_space=pltpu.VMEM)
    f32, bf16 = jnp.float32, jnp.bfloat16
    strip = rows // 2
    row_vec, col_vec = (rows // LANES, LANES), (cols // LANES, LANES)
    sems = pltpu.SemaphoreType.DMA
    targets, rows_pot, cols_pot = pl.pallas_call(
        functools.partial(kernel, rsize, csize, piece * dsize),
        out_shape=(
            jax.ShapeDtypeStruct((block, piece), f32),
            jax.ShapeDtypeStruct((block // LANES, LANES), f32),
            jax.ShapeDtypeStruct((cols // 2 // LANES, LANES), f32),
        ),
        in_specs=[pl.BlockSpec(memory_space=pl.ANY)] * 2,
        out_specs=(pl.BlockSpec(memory_space=pl.ANY), vmem, vmem),
        scratch_shapes=[
            pltpu.VMEM((dsize, rows, piece), bf16),
            pltpu.VMEM((2, nsize) + data_latents.shape, bf16),
            pltpu.VMEM((rows, cols), f32),
            pltpu.VMEM((rows, cols), bf16),
            pltpu.VMEM((rows, LANES), f32),
            pltpu.VMEM((rows, LANES), f32),
            pltpu.VMEM((rows, LANES), f32),
            pltpu.VMEM((rows, LANES), f32),
            pltpu.VMEM((cols, LANES), f32),
            pltpu.VMEM((8, cols), f32),
            pltpu.VMEM(row_vec, f32),
            pltpu.VMEM(col_vec, f32),
            pltpu.VMEM(row_vec, f32),
            pltpu.VMEM(col_vec, f32),
            pltpu.VMEM((4,) + row_vec, f32),
            pltpu.VMEM((ITERS, csize) + col_vec, f32),
            pltpu.VMEM((ITERS, rsize) + row_vec, f32),
            pltpu.VMEM((SIDE, 3, rows, LANES), bf16),
            pltpu.VMEM((SIDE, rows, LANES), f32),
            pltpu.VMEM((SIDE, 2, strip, LANES), bf16),
            pltpu.VMEM((SIDE, 2, rows, LANES), bf16),
            pltpu.VMEM((2, rows, LANES), f32),
            sems((ITERS,)),
            sems((ITERS,)),
            sems((ITERS,)),
            sems((ITERS,)),
            sems((4,)),
            sems((4,)),
            sems((4,)),
            sems((4,)),
            sems((SIDE, 2, 2)),
            sems((SIDE, 2, 2)),
            sems((2, 13)),
            sems((2, 13)),
            sems((SIDE, 2, 3)),
            sems((SIDE, 2, 3)),
            sems((SIDE,)),
            sems((5,)),
            pltpu.VMEM((SIDE, 2, strip, LANES), f32),
            sems((2,)),
            sems((2, 2)),
            sems((SIDE, 2)),
            pltpu.VMEM((rows, LANES), f32),
            pltpu.VMEM((rows, LANES), bf16),
            pltpu.VMEM((2, rows, LANES), bf16),
        ],
        compiler_params=pltpu.CompilerParams(
            collective_id=0, has_side_effects=True, vmem_limit_bytes=60 * 2**20
        ),
    )(noise_latents, data_latents)
    results = (targets, rows_pot, cols_pot)
    targets, rows_pot, cols_pot = pl.pallas_call(
        hand_on,
        out_shape=tuple(jax.ShapeDtypeStruct(a.shape, a.dtype) for a in results),
        in_specs=[pl.BlockSpec(memory_space=pl.ANY)] * 3,
        out_specs=(pl.BlockSpec(memory_space=pl.ANY),) * 3,
        scratch_shapes=[
            pltpu.VMEM((PARTS, block // PARTS, piece), f32),
            pltpu.VMEM(rows_pot.shape, f32),
            pltpu.VMEM(cols_pot.shape, f32),
            sems((PARTS + 2, 2)),
        ],
        compiler_params=pltpu.CompilerParams(vmem_limit_bytes=60 * 2**20),
    )(*results)
    return targets, rows_pot.reshape(block), cols_pot.reshape(cols // 2)


def solution(mesh):
    return jax.shard_map(
        shards,
        mesh=mesh,
        in_specs=(P("noise", "dp"), P("dp", "noise")),
        out_specs=(P("noise", "dp"), P("noise"), P("dp")),
        check_vma=False,
    )
```

```python
import functools
import math

import jax
import jax.numpy as jnp
from jax import lax
from jax.experimental import pallas as pl
from jax.experimental.pallas import tpu as pltpu
from jax.sharding import PartitionSpec as P

ITERS = 3
EPSILON = 0.04
LOG2E = 1.0 / math.log(2.0)
MESH = pl.DeviceIdType.MESH
LANES = 128
TILE = 32
SIDE = 4
PARTS = 4


def wrap(index, size):
    return lax.rem(index, size)


def spread_lanes(ref, row):
    return jnp.broadcast_to(ref[pl.ds(row, 1), :], (LANES, LANES)).T


def exchange(buf, send, recv, step, me, size, peer_id, started):
    for k in range(1, size):
        pltpu.make_async_remote_copy(
            src_ref=buf.at[step, me],
            dst_ref=buf.at[step, me],
            send_sem=send.at[step],
            recv_sem=recv.at[step],
            device_id=peer_id(wrap(me + k, size)),
            device_id_type=MESH,
        ).start()
    slots = buf.at[step, pl.ds(0, size - 1)]
    every = pltpu.make_async_remote_copy(
        src_ref=slots,
        dst_ref=slots,
        send_sem=send.at[step],
        recv_sem=recv.at[step],
        device_id=peer_id(wrap(me + 1, size)),
        device_id_type=MESH,
    )
    every.wait_recv()
    started.append(every)


def combine(buf, step, size):
    top = buf[step, 0]
    for s in range(1, size):
        top = jnp.maximum(top, buf[step, s])
    total = jnp.exp2(buf[step, 0] - top)
    for s in range(1, size):
        total = total + jnp.exp2(buf[step, s] - top)
    return top + jnp.log(total) * LOG2E


def add_slots(buf, step, size):
    total = buf[step, 0]
    for s in range(1, size):
        total = total + buf[step, s]
    return total


def kernel(
    rsize, csize, width,
    noise_ref, data_ref,
    targets, rows_out, cols_out,
    noise_all, data_all, scores, weights,
    shift, first, scale, part, data_part, colvec, rowpack, colpack, sqx, sqy, swap,
    col_buf, row_buf, out_buf, own_buf, far_buf, near_buf, in_sum,
    col_send, col_recv, row_send, row_recv, swap_send, swap_recv,
    cross_send, cross_recv, noise_send, noise_recv, data_send, data_recv,
    sum_send, sum_recv, in_send, in_recv, keep, far_keep, given, give_send, give_recv, part_recv, local_sems, own_send, far_send, relay_in, mate_out, mate_in,
):
    rows, cols = scores.shape
    n = lax.axis_index("noise")
    d = lax.axis_index("dp")
    x, z = d // SIDE, lax.rem(d, SIDE)
    y, core = n // 2, lax.rem(n, 2)
    kind = lax.rem((x + 1) // 2, 2)
    pair = x // 2
    side = lax.rem(x, 2)
    home = core == kind
    kappa = LOG2E / EPSILON
    log_rows = math.log2(rows * csize)
    log_cols = math.log2(cols * rsize)
    chunks = cols // LANES
    row_blocks = rows // LANES
    tiles = rows // TILE
    started = []

    def around(value):
        return lax.rem(value + SIDE, SIDE)

    def device(xi, yi, zi, ci):
        return (yi * 2 + ci, xi * SIDE + zi)

    def x_at(which, of_kind):
        return which * (3 - 2 * of_kind) + of_kind

    me_row = pair * SIDE + z
    me_col = y * 4 + kind * 2 + core

    def row_peer(p):
        return device(x_at(p // SIDE, kind), y, lax.rem(p, SIDE), core)

    def col_peer(p):
        return device(x_at(pair, lax.rem(p // 2, 2)), p // 4, z, lax.rem(p, 2))

    sibling = device(x, y, z, 1 - core)
    partner = x + 1 - 2 * side
    mate = SIDE - 1 - x
    opposite = around(x + 2)

    barrier = pltpu.get_barrier_semaphore()
    greeted = [row_peer(wrap(me_row + k, rsize)) for k in range(1, rsize)]
    greeted += [col_peer(wrap(me_col + k, csize)) for k in range(1, csize)]
    greeted += [device(opposite, y, z, 0), device(opposite, y, z, 1), device(mate, y, z, 1 - core)]
    greeted += [device(x, y, around(z + step), 1 - core) for step in (1, -1)]
    for to in greeted:
        pl.semaphore_signal(barrier, inc=1, device_id=to, device_id_type=MESH)
    pl.semaphore_wait(barrier, len(greeted))

    def remote(src, dst, send, recv, to):
        return pltpu.make_async_remote_copy(
            src_ref=src, dst_ref=dst, send_sem=send, recv_sem=recv, device_id=to, device_id_type=MESH
        )

    def begin(copy):
        copy.start()
        started.append(copy)

    def lane(c):
        return slice(LANES * c, LANES * (c + 1))

    HOP = (1, -1)
    own = x * SIDE + z

    def cross_copy(i, half, to):
        return remote(
            noise_ref.at[pl.ds(half * rows, rows)], noise_all.at[own], cross_send.at[i], cross_recv.at[x], to
        )

    def cross_wait(xi):
        remote(
            noise_ref.at[pl.ds(0, rows)], noise_all.at[xi * SIDE + z], cross_send.at[0], cross_recv.at[xi], sibling
        ).wait_recv()

    there = jnp.where(home, mate, partner)
    aside = cross_copy(2, 1 - core, sibling)

    def noise_copy(xi, t, forward, slot):
        at = pl.ds(t * (rows // 2), rows // 2) if forward else pl.ds(0, rows)
        f = int(forward)
        return remote(
            noise_all.at[slot, at], noise_all.at[slot, at],
            noise_send.at[xi, t, f], noise_recv.at[xi, t, f], device(x, y, around(z + HOP[t]), core),
        )

    def noise_wait(xi, t, forward):
        slot = xi * SIDE + around(z - HOP[t] * (2 if forward else 1))
        noise_copy(xi, t, forward, slot).wait_recv()
        return slot

    def data_copy(r, index, where, lo, size, to, own=False):
        at = pl.ds(lo, size)
        block = side if r == 0 else 1 - side
        dst = data_all.at[block, where, at]
        return remote(data_ref.at[at] if own else dst, dst, data_send.at[r, index], data_recv.at[r, index], to)

    half_cols = cols // 4
    full_cols = cols // 2

    def along_y(step, c):
        return around(y + step) * 2 + c

    def data_wait(r, index, where, lo, size):
        data_copy(r, index, where, lo, size, sibling).wait_recv()

    HALF = 9

    def cross_data(h, own=False):
        at = pl.ds(h * half_cols, half_cols)
        dst = data_all.at[side if own else 1 - side, n, at]
        return remote(
            data_ref.at[at], dst, data_send.at[1, 11 + h], data_recv.at[1, 11 + h], device(partner, y, z, core)
        )

    def partner_y(t, h, back=0):
        where = around(y + back) * 2 + core
        to = device(x, around(y + HOP[t]), z, core)
        return t if h == 0 else HALF + t, where, h * half_cols, half_cols, to

    def partner_wait(t, h):
        data_copy(1, *partner_y(t, h, -HOP[t])).wait_recv()

    def own_round(t, a):
        return remote(
            noise_ref.at[pl.ds(a * rows, rows)], noise_all.at[own],
            own_send.at[t, a], noise_recv.at[x, t, 0], device(x, y, around(z + HOP[t]), a),
        )

    def own_half():
        return pltpu.make_async_copy(
            noise_ref.at[pl.ds(pl.multiple_of(core * rows, rows), rows)], noise_all.at[own], local_sems.at[0]
        )

    @pl.when(home)
    def _():
        for t in (0, 1):
            for a in (0, 1):
                own_round(t, a).start()
        aside.start()

    begin(cross_copy(0, 0, device(there, y, z, 0)))
    begin(cross_copy(1, 1, device(there, y, z, 1)))
    for t in (0, 1):
        begin(data_copy(0, t, n, 0, full_cols, device(x, around(y + HOP[t]), z, core), own=True))
    @pl.when(home)
    def _():
        own_half().start()

    data_own = pltpu.make_async_copy(data_ref, data_all.at[side, n], local_sems.at[1])
    data_own.start()
    part[...] = jnp.zeros_like(part)
    data_part[...] = jnp.zeros_like(data_part)

    def round_z(xi):
        for t in (0, 1):
            begin(noise_copy(xi, t, False, xi * SIDE + z))

    def forward_z(xi):
        for t in (0, 1):
            begin(noise_copy(xi, t, True, noise_wait(xi, t, False)))

    def far_noise(xi, t):
        slot = xi * SIDE + around(z + 2)
        at = pl.ds(t * (rows // 2), rows // 2)
        return remote(
            noise_all.at[slot, at], noise_all.at[slot, at],
            far_send.at[xi, t], noise_recv.at[xi, t, 1], device(mate, y, z, core),
        )

    def share_far(xi):
        for t in (0, 1):
            noise_wait(xi, t, True)
            begin(far_noise(xi, t))

    def far_wait(xi):
        for t in (0, 1):
            far_noise(xi, t).wait_recv()

    def far_data(t, block):
        where = along_y(2, core)
        at = pl.ds(t * half_cols, half_cols)
        dst = data_all.at[block, where, at]
        return remote(dst, dst, data_send.at[1, 2 + t], data_recv.at[1, 2 + t], device(partner, y, z, core))

    cross_wait(partner)
    slot = partner * SIDE + z
    begin(remote(
        noise_all.at[slot], noise_all.at[slot], cross_send.at[3], cross_recv.at[partner], device(mate, y, z, core)
    ))
    round_z(partner)
    for h in (0, 1):
        begin(cross_data(h, own=True))
    begin(data_copy(0, 4, n, 0, full_cols, sibling, own=True))
    forward_z(x)
    cross_wait(mate)
    round_z(mate)
    for t in (0, 1):
        where = along_y(-HOP[t], core)
        data_wait(0, t, where, 0, full_cols)
        begin(data_copy(0, 2 + t, where, t * half_cols, half_cols, device(x, around(y + HOP[t]), z, core)))
        begin(data_copy(0, 5 + t, where, 0, full_cols, sibling))
    cross_data(0).wait_recv()
    for t in (0, 1):
        begin(data_copy(1, *partner_y(t, 0)))
    forward_z(partner)
    cross_wait(opposite)
    round_z(opposite)
    share_far(x)
    cross_data(1).wait_recv()
    for t in (0, 1):
        begin(data_copy(1, *partner_y(t, 1)))
    begin(data_copy(1, 4, n, 0, full_cols, sibling))
    for t in (0, 1):
        where = along_y(2, core)
        data_wait(0, 2 + t, where, t * half_cols, half_cols)
        begin(far_data(t, side))
        begin(data_copy(0, 7 + t, where, t * half_cols, half_cols, sibling))

    def squares(block):
        value = block.astype(jnp.float32)
        return value * value

    def chunk_product(xi, m):
        left = jnp.concatenate([noise_all[xi * SIDE + i] for i in range(SIDE)], axis=1)
        cut = pl.ds(pl.multiple_of(m * 256, 256), 256)
        here = pl.ds(pl.multiple_of(lax.rem(m, 4) * 256, 256), 256)
        pieces = [data_all[m // 4, xi * 2 + i, here, :] for i in (0, 1)]
        total = data_part[cut, :]
        for piece in pieces:
            total = total + squares(piece[:, :LANES]) + squares(piece[:, LANES:])
        data_part[cut, :] = total
        return lax.dot_general(
            left, jnp.concatenate(pieces, axis=1), (((1,), (1,)), ((), ())), preferred_element_type=jnp.float32
        )

    def norms(xi):
        def norm(r, carry):
            cut = pl.ds(pl.multiple_of(r * 64, 64), 64)
            total = part[cut, :]
            for i in range(SIDE):
                total = total + squares(noise_all[xi * SIDE + i, cut, :])
            part[cut, :] = total
            return carry

        lax.fori_loop(0, rows // 64, norm, 0)

    near, other_block = side * 4, 4 - side * 4

    def unit(block, xs, fresh):
        def column(i, carry):
            m = block + i
            cut = pl.ds(pl.multiple_of(m * 256, 256), 256)
            value = None if fresh else scores[:, cut]
            for xi in xs:
                value = chunk_product(xi, m) if value is None else value + chunk_product(xi, m)
            scores[:, cut] = value
            return carry

        lax.fori_loop(0, 4, column, 0)

    data_own.wait()
    data_wait(0, 4, along_y(0, 1 - core), 0, full_cols)
    for t in (0, 1):
        data_wait(0, 5 + t, along_y(-HOP[t], 1 - core), 0, full_cols)
    for t in (0, 1):
        data_wait(0, 7 + t, along_y(2, 1 - core), t * half_cols, half_cols)

    @pl.when(home)
    def _():
        own_half().wait()

    @pl.when(jnp.logical_not(home))
    def _():
        cross_wait(x)

    unit(near, (x,), True)
    share_far(partner)
    norms(x)
    for t in (0, 1):
        noise_wait(mate, t, False)
    far_wait(mate)
    unit(near, (mate,), False)
    norms(mate)
    for h in (0, 1):
        for t in (0, 1):
            partner_wait(t, h)
    for t in (0, 1):
        begin(data_copy(1, 5 + t, along_y(-HOP[t], core), 0, full_cols, sibling))
    unit(near, (partner,), False)
    norms(partner)
    for t in (0, 1):
        noise_wait(opposite, t, False)
    far_wait(opposite)
    for t in (0, 1):
        far_data(t, 1 - side).wait_recv()
        begin(data_copy(1, 7 + t, along_y(2, core), t * half_cols, half_cols, sibling))
    norms(opposite)

    factor = 2.0 * kappa / width

    def row_shift(r, carry):
        at = pl.ds(pl.multiple_of(r * 128, 128), 128)
        total = jnp.sum(part[at, :], axis=1, keepdims=True) * (-kappa / width)
        shift[at, :] = jnp.broadcast_to(total, (128, LANES))
        return carry

    lax.fori_loop(0, rows // 128, row_shift, 0)

    def final(block, xi):
        def column(i, carry):
            m = block + i
            cut = pl.ds(pl.multiple_of(m * 256, 256), 256)
            value = (scores[:, cut] + chunk_product(xi, m)) * factor
            scores[:, cut] = value
            for e in (0, 1):
                top = jnp.max(value[:, LANES * e:LANES * (e + 1)] + shift[...], axis=0, keepdims=True)
                colvec[:, pl.ds(pl.multiple_of(m * 256 + e * LANES, LANES), LANES)] = jnp.broadcast_to(top, (8, LANES))
            return carry

        lax.fori_loop(0, 4, column, 0)

    final(near, opposite)
    data_wait(1, 4, along_y(0, 1 - core), 0, full_cols)
    for t in (0, 1):
        data_wait(1, 5 + t, along_y(-HOP[t], 1 - core), 0, full_cols)
    unit(other_block, (y, around(y + 1), around(y - 1)), True)
    for t in (0, 1):
        data_wait(1, 7 + t, along_y(2, 1 - core), t * half_cols, half_cols)
    final(other_block, around(y + 2))

    def fold(block, op):
        out = block[0:8]
        for r in range(1, TILE // 8):
            out = op(out, block[8 * r:8 * r + 8])
        return out

    def spread_cols():
        for c in range(chunks):
            colvec[:, lane(c)] = jnp.broadcast_to(colpack[pl.ds(c, 1), :], (8, LANES))

    def tall(ref, c):
        return jnp.concatenate([ref[:, lane(c)]] * (TILE // 8), axis=0)

    def tile_at(t):
        return pl.ds(pl.multiple_of(t * TILE, TILE), TILE)

    def loop(body, init):
        return lax.fori_loop(0, tiles, body, init, unroll=2)

    zeros = tuple(jnp.zeros((8, LANES), jnp.float32) for _ in range(chunks))

    def exp_step(t, accs):
        at = tile_at(t)
        add = shift[at, :]
        return tuple(
            accs[c] + fold(jnp.exp2(scores[at, lane(c)] + add - tall(colvec, c)), jnp.add)
            for c in range(chunks)
        )

    sums = loop(exp_step, zeros)
    for c in range(chunks):
        total = jnp.sum(sums[c], axis=0, keepdims=True)
        col_buf[0, me_col, pl.ds(c, 1), :] = colvec[0:1, lane(c)] + jnp.log(total) * LOG2E
    exchange(col_buf, col_send, col_recv, 0, me_col, csize, col_peer, started)
    col_pot = -log_cols - combine(col_buf, 0, csize)
    colpack[...] = col_pot
    spread_cols()

    def row_step(t, carry):
        at = tile_at(t)
        top = scores[at, lane(0)] + tall(colvec, 0)
        for c in range(1, chunks):
            top = jnp.maximum(top, scores[at, lane(c)] + tall(colvec, c))
        first[at, :] = top
        total = None
        for c in range(chunks):
            value = jnp.exp2(scores[at, lane(c)] + tall(colvec, c) - top)
            scores[at, lane(c)] = value
            total = value if total is None else total + value
        part[at, :] = total
        return carry

    loop(row_step, 0)
    for b in range(row_blocks):
        at = pl.ds(b * LANES, LANES)
        tops = first[at, :].T
        top = jnp.max(tops, axis=0, keepdims=True)
        total = jnp.sum(part[at, :].T * jnp.exp2(tops - top), axis=0, keepdims=True)
        row_buf[0, me_row, pl.ds(b, 1), :] = top + jnp.log(total) * LOG2E
    exchange(row_buf, row_send, row_recv, 0, me_row, rsize, row_peer, started)
    row_lse = combine(row_buf, 0, rsize)
    rowpack[...] = row_lse
    for b in range(row_blocks):
        at = pl.ds(b * LANES, LANES)
        base = jnp.exp2(first[at, :] - spread_lanes(rowpack, b))
        first[at, :] = base
        scale[at, :] = base

    def col_step(t, accs):
        at = tile_at(t)
        mul = scale[at, :]
        return tuple(accs[c] + fold(scores[at, lane(c)] * mul, jnp.add) for c in range(chunks))

    def sum_step(keep_values):
        def body(t, carry):
            at = tile_at(t)
            total = None
            for c in range(chunks):
                value = scores[at, lane(c)] * tall(colvec, c)
                if keep_values:
                    scores[at, lane(c)] = value
                total = value if total is None else total + value
            part[at, :] = total * first[at, :]
            return carry

        return body

    for step in range(1, ITERS):
        sums = loop(col_step, zeros)
        for c in range(chunks):
            col_buf[step, me_col, pl.ds(c, 1), :] = jnp.sum(sums[c], axis=0, keepdims=True)
        exchange(col_buf, col_send, col_recv, step, me_col, csize, col_peer, started)
        ratio = 1.0 / add_slots(col_buf, step, csize)
        colpack[...] = ratio
        spread_cols()
        loop(sum_step(step == ITERS - 1), 0)
        for b in range(row_blocks):
            at = pl.ds(b * LANES, LANES)
            row_buf[step, me_row, pl.ds(b, 1), :] = jnp.sum(part[at, :].T, axis=0, keepdims=True)
        exchange(row_buf, row_send, row_recv, step, me_row, rsize, row_peer, started)
        total = add_slots(row_buf, step, rsize)
        rowpack[...] = 1.0 / total
        for b in range(row_blocks):
            at = pl.ds(b * LANES, LANES)
            scale[at, :] = first[at, :] * spread_lanes(rowpack, b)

    def weigh(r):
        def body(t, carry):
            at = pl.ds(pl.multiple_of(r * (rows // 2) + t * TILE, TILE), TILE)
            mul = scale[at, :]
            for c in range(chunks):
                weights[at, lane(c)] = (scores[at, lane(c)] * mul).astype(jnp.bfloat16)
            return carry

        lax.fori_loop(0, tiles // 2, body, 0, unroll=2)

    def swap_copy(i, to):
        return remote(swap.at[0], swap.at[i], swap_send.at[i], swap_recv.at[i], to)

    def potentials():
        for c in range(chunks):
            sqy[pl.ds(c, 1), :] = jnp.sum(data_part[pl.ds(c * LANES, LANES), :].T, axis=0, keepdims=True)
        cols_pot = (col_pot + jnp.log(ratio) * LOG2E + (log_rows - log_cols)) / kappa + sqy[...] / width
        colpack[...] = cols_pot
        cols_out[...] = colpack[pl.ds(pl.multiple_of(side * 8, 8), 8), :]
        for b in range(row_blocks):
            sqx[pl.ds(b, 1), :] = shift[pl.ds(b * LANES, LANES), :].T[0:1]
        swap[0] = -(log_rows + row_lse + jnp.log(total) * LOG2E + sqx[...]) / kappa
        begin(swap_copy(1, sibling))
        for i in (0, 1):
            begin(remote(
                swap.at[0], swap.at[2 + core], swap_send.at[2 + i], swap_recv.at[2 + core], device(partner, y, z, i)
            ))

    strip = rows // 2

    def half_rows(r):
        return pl.ds(pl.multiple_of(r * strip, strip), strip)

    def block_x(b):
        return jnp.where(b < 2, jnp.where(b == 0, opposite, mate), jnp.where(b == 2, partner, x))

    def product(p, r, to_z):
        cut = pl.ds(pl.multiple_of(lax.rem(to_z, 2) * LANES, LANES), LANES)
        total = None
        for k in (0, 1):
            block = jnp.concatenate(
                [data_all[k, block_x(2 * p + e) * 2 + to_z // 2, :, cut] for e in (0, 1)], axis=1
            )
            value = jnp.dot(
                weights[half_rows(r), k * full_cols:(k + 1) * full_cols], block,
                preferred_element_type=jnp.float32,
            )
            total = value if total is None else total + value
        return total

    def hop(t):
        return 1 - 2 * t

    def sum_copy(b, t, index, src, dst):
        to = device(x, y, around(z + hop(t)), core)
        return remote(src, dst, sum_send.at[b, t, index], sum_recv.at[b, t, index], to)

    def far_copy(b, t):
        return sum_copy(b, t, 0, out_buf.at[b, 2, half_rows(t)], far_buf.at[b - 2, t])

    def direct_copy(b, t):
        at = half_rows(1 - t)
        return sum_copy(b, t, 1, out_buf.at[b, t, at], near_buf.at[b, t, at])

    def added_copy(b, t):
        at = half_rows(t)
        return sum_copy(b, t, 2, out_buf.at[b, t, at], near_buf.at[b, t, at])

    def give_copy(b, r):
        at = half_rows(r)
        return remote(
            out_buf.at[b, 2, at], given.at[b, at], give_send.at[b, r], give_recv.at[b, r], device(mate, y, z, core)
        )

    def relay_copy(r):
        at = half_rows(r)
        return remote(own_buf.at[0, at], relay_in.at[at], in_send.at[r], in_recv.at[4 + r], device(mate, y, z, core))

    def partner_copy(a, r):
        at = half_rows(r)
        return remote(
            own_buf.at[2, at], in_sum.at[a, at], in_send.at[2 + r], part_recv.at[a, r], device(partner, y, z, kind)
        )

    def mate_copy(a):
        return remote(mate_out, mate_in.at[a], in_send.at[4], in_recv.at[2 + a], device(mate, y, z, kind))

    def stay_copy(a):
        return remote(own_buf.at[3], in_sum.at[a], in_send.at[5], in_recv.at[a], sibling)

    def add_far(b):
        for t in (0, 1):
            far_copy(b, t).wait_recv()
            out_buf[b, t, half_rows(t), :] = (
                keep[b - 2, t, half_rows(t), :] + far_buf[b - 2, t].astype(jnp.float32)
            ).astype(jnp.bfloat16)
            added_copy(b, t).start()

    def add_near(b):
        for t in (0, 1):
            direct_copy(b, t).wait_recv()
            added_copy(b, t).wait_recv()
        own_buf[b] = own_buf[b] + near_buf[b, 0].astype(jnp.float32) + near_buf[b, 1].astype(jnp.float32)

    def add_given(b):
        for r in (0, 1):
            at = half_rows(r)
            give_copy(b - 2, r).wait_recv()
            out_buf[b, 2, at, :] = (far_keep[b - 2, at, :] + given[b - 2, at, :].astype(jnp.float32)).astype(jnp.bfloat16)
            far_copy(b, r).start()

    def halves(body):
        def step(r, carry):
            body(r)
            return carry

        lax.fori_loop(0, 2, step, 0)

    def give(r):
        weigh(r)
        value = product(0, r, around(z + 2))
        for e in (0, 1):
            out_buf[e, 2, half_rows(r), :] = value[:, lane(e)].astype(jnp.bfloat16)
        give_copy(0, r).start()

    def near_products(p):
        def along(t):
            def part_of(r):
                value = product(p, r, around(z + hop(t)))
                for e in (0, 1):
                    block = value[:, lane(e)]
                    out_buf[2 * p + e, t, half_rows(r), :] = block.astype(jnp.bfloat16)
                    if p == 1:
                        keep[e, t, half_rows(r), :] = block

            halves(part_of)
            direct_copy(2 * p, t).start()
            if p == 0:
                added_copy(0, t).start()

        halves(along)

    def far_products(r):
        value = product(1, r, around(z + 2))
        for e in (0, 1):
            far_keep[e, half_rows(r), :] = value[:, lane(e)]

    def own_products(p):
        def part_of(r):
            value = product(p, r, z)
            for e in (0, 1):
                own_buf[2 * p + e, half_rows(r), :] = value[:, lane(e)]

        halves(part_of)

    halves(give)
    for r in (0, 1):
        give_copy(1, r).start()
    near_products(1)
    near_products(0)
    halves(far_products)
    add_given(2)
    for t in (0, 1):
        direct_copy(1, t).start()
        added_copy(1, t).start()
    halves(own_products)
    add_near(0)
    for r in (0, 1):
        relay_copy(r).start()
    add_far(2)
    add_given(3)
    for t in (0, 1):
        direct_copy(3, t).start()
    add_near(1)
    mate_out[...] = own_buf[1].astype(jnp.bfloat16)
    mate_copy(core).start()
    potentials()
    add_near(2)

    def to_partner(r):
        relay_copy(r).wait_recv()
        own_buf[2, half_rows(r), :] = own_buf[2, half_rows(r), :] + relay_in[half_rows(r), :]
        partner_copy(core, r).start()

    to_partner(0)
    add_far(3)
    to_partner(1)

    swap_copy(1, sibling).wait_recv()
    for i in (0, 1):
        remote(swap.at[0], swap.at[2 + i], swap_send.at[2 + i], swap_recv.at[2 + i], sibling).wait_recv()
    half = rows // LANES
    for a in (0, 1):
        mine_row = jnp.where(core == a, swap[0], swap[1])
        rows_out[pl.ds(a * half, half), :] = jnp.where(home, mine_row, swap[2 + a])

    add_near(3)

    @pl.when(home)
    def _():
        in_sum[core] = own_buf[3]
        stay_copy(1 - core).wait_recv()
        for a in (0, 1):
            mate_copy(a).wait_recv()
            in_sum[a] = in_sum[a] + mate_in[a].astype(jnp.float32)

    @pl.when(jnp.logical_not(home))
    def _():
        stay_copy(core).start()
        for a in (0, 1):
            for r in (0, 1):
                partner_copy(a, r).wait_recv()

    def result_copy(a):
        return pltpu.make_async_copy(in_sum.at[a], targets.at[pl.ds(a * rows, rows)], local_sems.at[a])

    for a in (0, 1):
        result_copy(a).start()

    def settle(b, carry):
        for t in (0, 1):
            direct_copy(b, t).wait_send()
            added_copy(b, t).wait_send()

            @pl.when(b < 2)
            def _():
                give_copy(jnp.minimum(b, 1), t).wait_send()

            @pl.when(b >= 2)
            def _():
                far_copy(jnp.maximum(b, 2), t).wait_send()

        return carry

    lax.fori_loop(0, SIDE, settle, 0)
    for a in (0, 1):
        result_copy(a).wait()
    for r in (0, 1):
        relay_copy(r).wait_send()
        partner_copy(core, r).wait_send()
    mate_copy(core).wait_send()

    @pl.when(jnp.logical_not(home))
    def _():
        stay_copy(core).wait_send()

    for copy in started:
        copy.wait_send()

    @pl.when(home)
    def _():
        aside.wait_send()
        for t in (0, 1):
            for a in (0, 1):
                own_round(t, a).wait_send()


def hand_on(targets, rows_pot, cols_pot, targets_out, rows_out, cols_out, stage, row_stage, col_stage, sems):
    size = targets.shape[0] // PARTS
    legs = [
        (targets.at[pl.ds(i * size, size)], stage.at[i], targets_out.at[pl.ds(i * size, size)]) for i in range(PARTS)
    ]
    legs += [(rows_pot, row_stage, rows_out), (cols_pot, col_stage, cols_out)]
    first = [pltpu.make_async_copy(src, mid, sems.at[i, 0]) for i, (src, mid, _) in enumerate(legs)]
    second = [pltpu.make_async_copy(mid, dst, sems.at[i, 1]) for i, (_, mid, dst) in enumerate(legs)]
    for copy in first:
        copy.start()
    for before, copy in zip(first, second):
        before.wait()
        copy.start()
    for copy in second:
        copy.wait()


def shards(noise_latents, data_latents):
    nsize = lax.axis_size("noise")
    dsize = lax.axis_size("dp")
    block, piece = noise_latents.shape
    rows, cols = block // 2, 2 * data_latents.shape[0]
    rsize, csize = dsize // 2, nsize * 2
    vmem = pl.BlockSpec(memory_space=pltpu.VMEM)
    f32, bf16 = jnp.float32, jnp.bfloat16
    strip = rows // 2
    row_vec, col_vec = (rows // LANES, LANES), (cols // LANES, LANES)
    sems = pltpu.SemaphoreType.DMA
    targets, rows_pot, cols_pot = pl.pallas_call(
        functools.partial(kernel, rsize, csize, piece * dsize),
        out_shape=(
            jax.ShapeDtypeStruct((block, piece), f32),
            jax.ShapeDtypeStruct((block // LANES, LANES), f32),
            jax.ShapeDtypeStruct((cols // 2 // LANES, LANES), f32),
        ),
        in_specs=[pl.BlockSpec(memory_space=pl.ANY)] * 2,
        out_specs=(pl.BlockSpec(memory_space=pl.ANY), vmem, vmem),
        scratch_shapes=[
            pltpu.VMEM((dsize, rows, piece), bf16),
            pltpu.VMEM((2, nsize) + data_latents.shape, bf16),
            pltpu.VMEM((rows, cols), f32),
            pltpu.VMEM((rows, cols), bf16),
            pltpu.VMEM((rows, LANES), f32),
            pltpu.VMEM((rows, LANES), f32),
            pltpu.VMEM((rows, LANES), f32),
            pltpu.VMEM((rows, LANES), f32),
            pltpu.VMEM((cols, LANES), f32),
            pltpu.VMEM((8, cols), f32),
            pltpu.VMEM(row_vec, f32),
            pltpu.VMEM(col_vec, f32),
            pltpu.VMEM(row_vec, f32),
            pltpu.VMEM(col_vec, f32),
            pltpu.VMEM((4,) + row_vec, f32),
            pltpu.VMEM((ITERS, csize) + col_vec, f32),
            pltpu.VMEM((ITERS, rsize) + row_vec, f32),
            pltpu.VMEM((SIDE, 3, rows, LANES), bf16),
            pltpu.VMEM((SIDE, rows, LANES), f32),
            pltpu.VMEM((2, 2, strip, LANES), bf16),
            pltpu.VMEM((SIDE, 2, rows, LANES), bf16),
            pltpu.VMEM((2, rows, LANES), f32),
            sems((ITERS,)),
            sems((ITERS,)),
            sems((ITERS,)),
            sems((ITERS,)),
            sems((4,)),
            sems((4,)),
            sems((4,)),
            sems((4,)),
            sems((SIDE, 2, 2)),
            sems((SIDE, 2, 2)),
            sems((2, 13)),
            sems((2, 13)),
            sems((SIDE, 2, 3)),
            sems((SIDE, 2, 3)),
            sems((6,)),
            sems((6,)),
            pltpu.VMEM((2, 2, rows, LANES), f32),
            pltpu.VMEM((2, rows, LANES), f32),
            pltpu.VMEM((2, rows, LANES), bf16),
            sems((2, 2)),
            sems((2, 2)),
            sems((2, 2)),
            sems((2,)),
            sems((2, 2)),
            sems((SIDE, 2)),
            pltpu.VMEM((rows, LANES), f32),
            pltpu.VMEM((rows, LANES), bf16),
            pltpu.VMEM((2, rows, LANES), bf16),
        ],
        compiler_params=pltpu.CompilerParams(
            collective_id=0, has_side_effects=True, vmem_limit_bytes=60 * 2**20
        ),
    )(noise_latents, data_latents)
    results = (targets, rows_pot, cols_pot)
    targets, rows_pot, cols_pot = pl.pallas_call(
        hand_on,
        out_shape=tuple(jax.ShapeDtypeStruct(a.shape, a.dtype) for a in results),
        in_specs=[pl.BlockSpec(memory_space=pl.ANY)] * 3,
        out_specs=(pl.BlockSpec(memory_space=pl.ANY),) * 3,
        scratch_shapes=[
            pltpu.VMEM((PARTS, block // PARTS, piece), f32),
            pltpu.VMEM(rows_pot.shape, f32),
            pltpu.VMEM(cols_pot.shape, f32),
            sems((PARTS + 2, 2)),
        ],
        compiler_params=pltpu.CompilerParams(vmem_limit_bytes=60 * 2**20),
    )(*results)
    return targets, rows_pot.reshape(block), cols_pot.reshape(cols // 2)


def solution(mesh):
    return jax.shard_map(
        shards,
        mesh=mesh,
        in_specs=(P("noise", "dp"), P("dp", "noise")),
        out_specs=(P("noise", "dp"), P("noise"), P("dp")),
        check_vma=False,
    )
```

```python
import functools
import math

import jax
import jax.numpy as jnp
from jax import lax
from jax.experimental import pallas as pl
from jax.experimental.pallas import tpu as pltpu
from jax.sharding import PartitionSpec as P

ITERS = 3
EPSILON = 0.04
LOG2E = 1.0 / math.log(2.0)
MESH = pl.DeviceIdType.MESH
LANES = 128
TILE = 32
SIDE = 4
PARTS = 4


def spread_lanes(ref, row):
    return jnp.broadcast_to(ref[pl.ds(row, 1), :], (LANES, LANES)).T


def exchange(buf, send, recv, step, me, peers, started):
    for peer in peers:
        pltpu.make_async_remote_copy(
            src_ref=buf.at[step, me],
            dst_ref=buf.at[step, me],
            send_sem=send.at[step],
            recv_sem=recv.at[step],
            device_id=peer,
            device_id_type=MESH,
        ).start()
    slots = buf.at[step, pl.ds(0, len(peers))]
    every = pltpu.make_async_remote_copy(
        src_ref=slots,
        dst_ref=slots,
        send_sem=send.at[step],
        recv_sem=recv.at[step],
        device_id=peers[0],
        device_id_type=MESH,
    )
    every.wait_recv()
    started.append(every)


def combine(buf, step, size):
    top = buf[step, 0]
    for s in range(1, size):
        top = jnp.maximum(top, buf[step, s])
    total = jnp.exp2(buf[step, 0] - top)
    for s in range(1, size):
        total = total + jnp.exp2(buf[step, s] - top)
    return top + jnp.log(total) * LOG2E


def add_slots(buf, step, size):
    total = buf[step, 0]
    for s in range(1, size):
        total = total + buf[step, s]
    return total


def kernel(
    rsize, csize, width,
    noise_ref, data_ref,
    targets, rows_out, cols_out,
    noise_all, data_all, scores, weights,
    shift, first, scale, part, data_part, colvec, rowpack, colpack, sqx, sqy, swap,
    col_buf, row_buf, out_buf, own_buf, far_buf, near_buf, in_sum,
    col_send, col_recv, row_send, row_recv, swap_send, swap_recv,
    cross_send, cross_recv, noise_send, noise_recv, data_send, data_recv,
    sum_send, sum_recv, in_send, in_recv, keep, far_keep, given, give_send, give_recv, part_recv, local_sems, own_send, far_send, relay_in, mate_out, mate_in,
):
    rows, cols = scores.shape
    n = lax.axis_index("noise")
    d = lax.axis_index("dp")
    x, z = d // SIDE, lax.rem(d, SIDE)
    y, core = n // 2, lax.rem(n, 2)
    kind = lax.rem((x + 1) // 2, 2)
    pair = x // 2
    side = lax.rem(x, 2)
    home = core == kind
    kappa = LOG2E / EPSILON
    log_rows = math.log2(rows * csize)
    log_cols = math.log2(cols * rsize)
    chunks = cols // LANES
    row_blocks = rows // LANES
    tiles = rows // TILE
    started = []

    def around(value):
        return lax.rem(value + SIDE, SIDE)

    def device(xi, yi, zi, ci):
        return (yi * 2 + ci, xi * SIDE + zi)

    me_row = pair * SIDE + z
    me_col = y * 4 + kind * 2 + core

    sibling = device(x, y, z, 1 - core)
    partner = x + 1 - 2 * side
    mate = SIDE - 1 - x
    opposite = around(x + 2)

    barrier = pltpu.get_barrier_semaphore()
    ys, zs = [around(y + k) for k in range(SIDE)], [around(z + k) for k in range(SIDE)]
    rings = [yi * 2 + ci for yi in (ys[2], ys[1], ys[3], ys[0]) for ci in (1 - core, core)]
    col_peers = [(r, di) for di in (partner * SIDE + z, d) for r in rings][:-1]
    row_peers = [(n, xi * SIDE + zi) for xi in (mate, x) for zi in (zs[2], zs[1], zs[3], zs[0])][:-1]
    greeted = row_peers + col_peers
    greeted += [device(opposite, y, z, 0), device(opposite, y, z, 1), device(mate, y, z, 1 - core)]
    greeted += [device(x, y, around(z + step), 1 - core) for step in (1, -1)]
    for to in greeted:
        pl.semaphore_signal(barrier, inc=1, device_id=to, device_id_type=MESH)
    pl.semaphore_wait(barrier, len(greeted))

    def remote(src, dst, send, recv, to):
        return pltpu.make_async_remote_copy(
            src_ref=src, dst_ref=dst, send_sem=send, recv_sem=recv, device_id=to, device_id_type=MESH
        )

    def begin(copy):
        copy.start()
        started.append(copy)

    def lane(c):
        return slice(LANES * c, LANES * (c + 1))

    HOP = (1, -1)
    own = x * SIDE + z

    def cross_copy(i, half, to):
        return remote(
            noise_ref.at[pl.ds(half * rows, rows)], noise_all.at[own], cross_send.at[i], cross_recv.at[x], to
        )

    def cross_wait(xi):
        remote(
            noise_ref.at[pl.ds(0, rows)], noise_all.at[xi * SIDE + z], cross_send.at[0], cross_recv.at[xi], sibling
        ).wait_recv()

    there = jnp.where(home, mate, partner)
    aside = cross_copy(2, 1 - core, sibling)

    def noise_copy(xi, t, forward, slot):
        at = pl.ds(t * (rows // 2), rows // 2) if forward else pl.ds(0, rows)
        f = int(forward)
        return remote(
            noise_all.at[slot, at], noise_all.at[slot, at],
            noise_send.at[xi, t, f], noise_recv.at[xi, t, f], device(x, y, around(z + HOP[t]), core),
        )

    def noise_wait(xi, t, forward):
        slot = xi * SIDE + around(z - HOP[t] * (2 if forward else 1))
        noise_copy(xi, t, forward, slot).wait_recv()
        return slot

    def data_copy(r, index, where, lo, size, to, own=False):
        at = pl.ds(lo, size)
        block = side if r == 0 else 1 - side
        dst = data_all.at[block, where, at]
        return remote(data_ref.at[at] if own else dst, dst, data_send.at[r, index], data_recv.at[r, index], to)

    half_cols = cols // 4
    full_cols = cols // 2

    def along_y(step, c):
        return around(y + step) * 2 + c

    def data_wait(r, index, where, lo, size):
        data_copy(r, index, where, lo, size, sibling).wait_recv()

    HALF = 9

    def cross_data(h, own=False):
        at = pl.ds(h * half_cols, half_cols)
        dst = data_all.at[side if own else 1 - side, n, at]
        return remote(
            data_ref.at[at], dst, data_send.at[1, 11 + h], data_recv.at[1, 11 + h], device(partner, y, z, core)
        )

    def partner_y(t, h, back=0):
        where = around(y + back) * 2 + core
        to = device(x, around(y + HOP[t]), z, core)
        return t if h == 0 else HALF + t, where, h * half_cols, half_cols, to

    def partner_wait(t, h):
        data_copy(1, *partner_y(t, h, -HOP[t])).wait_recv()

    def own_round(t, a):
        return remote(
            noise_ref.at[pl.ds(a * rows, rows)], noise_all.at[own],
            own_send.at[t, a], noise_recv.at[x, t, 0], device(x, y, around(z + HOP[t]), a),
        )

    def own_half():
        return pltpu.make_async_copy(
            noise_ref.at[pl.ds(pl.multiple_of(core * rows, rows), rows)], noise_all.at[own], local_sems.at[0]
        )

    @pl.when(home)
    def _():
        for t in (0, 1):
            for a in (0, 1):
                own_round(t, a).start()
        aside.start()

    begin(cross_copy(0, 0, device(there, y, z, 0)))
    begin(cross_copy(1, 1, device(there, y, z, 1)))
    for t in (0, 1):
        begin(data_copy(0, t, n, 0, full_cols, device(x, around(y + HOP[t]), z, core), own=True))
    @pl.when(home)
    def _():
        own_half().start()

    data_own = pltpu.make_async_copy(data_ref, data_all.at[side, n], local_sems.at[1])
    data_own.start()
    scores[...] = jnp.zeros_like(scores)
    part[...] = jnp.zeros_like(part)
    data_part[...] = jnp.zeros_like(data_part)

    def round_z(xi):
        for t in (0, 1):
            begin(noise_copy(xi, t, False, xi * SIDE + z))

    def forward_z(xi):
        for t in (0, 1):
            begin(noise_copy(xi, t, True, noise_wait(xi, t, False)))

    def far_noise(xi, t):
        slot = xi * SIDE + around(z + 2)
        at = pl.ds(t * (rows // 2), rows // 2)
        return remote(
            noise_all.at[slot, at], noise_all.at[slot, at],
            far_send.at[xi, t], noise_recv.at[xi, t, 1], device(mate, y, z, core),
        )

    def share_far(xi):
        for t in (0, 1):
            noise_wait(xi, t, True)
            begin(far_noise(xi, t))

    def far_wait(xi):
        for t in (0, 1):
            far_noise(xi, t).wait_recv()

    def far_data(t, block):
        where = along_y(2, core)
        at = pl.ds(t * half_cols, half_cols)
        dst = data_all.at[block, where, at]
        return remote(dst, dst, data_send.at[1, 2 + t], data_recv.at[1, 2 + t], device(partner, y, z, core))

    cross_wait(partner)
    slot = partner * SIDE + z
    begin(remote(
        noise_all.at[slot], noise_all.at[slot], cross_send.at[3], cross_recv.at[partner], device(mate, y, z, core)
    ))
    round_z(partner)
    for h in (0, 1):
        begin(cross_data(h, own=True))
    begin(data_copy(0, 4, n, 0, full_cols, sibling, own=True))
    forward_z(x)
    cross_wait(mate)
    round_z(mate)
    for t in (0, 1):
        where = along_y(-HOP[t], core)
        data_wait(0, t, where, 0, full_cols)
        begin(data_copy(0, 2 + t, where, t * half_cols, half_cols, device(x, around(y + HOP[t]), z, core)))
        begin(data_copy(0, 5 + t, where, 0, full_cols, sibling))
    cross_data(0).wait_recv()
    for t in (0, 1):
        begin(data_copy(1, *partner_y(t, 0)))
    forward_z(partner)
    cross_wait(opposite)
    round_z(opposite)
    share_far(x)
    cross_data(1).wait_recv()
    for t in (0, 1):
        begin(data_copy(1, *partner_y(t, 1)))
    begin(data_copy(1, 4, n, 0, full_cols, sibling))
    for t in (0, 1):
        where = along_y(2, core)
        data_wait(0, 2 + t, where, t * half_cols, half_cols)
        begin(far_data(t, side))
        begin(data_copy(0, 7 + t, where, t * half_cols, half_cols, sibling))

    def squares(block):
        value = block.astype(jnp.float32)
        return value * value

    def chunk_product(xi, m):
        left = jnp.concatenate([noise_all[xi * SIDE + i] for i in range(SIDE)], axis=1)
        cut = pl.ds(pl.multiple_of(m * 256, 256), 256)
        here = pl.ds(pl.multiple_of(lax.rem(m, 4) * 256, 256), 256)
        pieces = [data_all[m // 4, xi * 2 + i, here, :] for i in (0, 1)]
        total = data_part[cut, :]
        for piece in pieces:
            total = total + squares(piece[:, :LANES]) + squares(piece[:, LANES:])
        data_part[cut, :] = total
        return lax.dot_general(
            left, jnp.concatenate(pieces, axis=1), (((1,), (1,)), ((), ())), preferred_element_type=jnp.float32
        )

    def norms(xi):
        def norm(r, carry):
            cut = pl.ds(pl.multiple_of(r * 64, 64), 64)
            total = part[cut, :]
            for i in range(SIDE):
                total = total + squares(noise_all[xi * SIDE + i, cut, :])
            part[cut, :] = total
            return carry

        lax.fori_loop(0, rows // 64, norm, 0)

    near, other_block = side * 4, 4 - side * 4

    def unit(block, xs, fresh, count=4):
        def column(i, carry):
            m = block + i
            cut = pl.ds(pl.multiple_of(m * 256, 256), 256)
            value = None if fresh else scores[:, cut]
            for xi in xs:
                value = chunk_product(xi, m) if value is None else value + chunk_product(xi, m)
            scores[:, cut] = value
            return carry

        lax.fori_loop(0, count, column, 0)

    def add_unit(block, count, xi):
        unit(block, (xi,), False, count)

    data_own.wait()
    data_wait(0, 4, along_y(0, 1 - core), 0, full_cols)
    for t in (0, 1):
        data_wait(0, 5 + t, along_y(-HOP[t], 1 - core), 0, full_cols)
    for t in (0, 1):
        data_wait(0, 7 + t, along_y(2, 1 - core), t * half_cols, half_cols)

    @pl.when(home)
    def _():
        own_half().wait()

    @pl.when(jnp.logical_not(home))
    def _():
        cross_wait(x)

    unit(near, (x,), True)
    share_far(partner)
    norms(x)
    for t in (0, 1):
        noise_wait(mate, t, False)
    far_wait(mate)
    unit(near, (mate,), False)
    norms(mate)

    def beside(t, h, c):
        return data_copy(1, (5 if h == 0 else 13) + t, along_y(-HOP[t], c), h * half_cols, half_cols, sibling)

    for t in (0, 1):
        partner_wait(t, 0)
        begin(beside(t, 0, core))
    unit(near, (partner,), False)
    norms(partner)
    data_wait(1, 4, along_y(0, 1 - core), 0, full_cols)
    for t in (0, 1):
        beside(t, 0, 1 - core).wait_recv()

    def ahead(i, carry):
        xi = around(y + i + i // 2)
        add_unit(other_block, jnp.where(xi == opposite, 0, jnp.where(i == 0, 4, 2)), xi)
        return carry

    lax.fori_loop(0, 3, ahead, 0)
    for t in (0, 1):
        partner_wait(t, 1)
        begin(beside(t, 1, core))
    for t in (0, 1):
        noise_wait(opposite, t, False)
    far_wait(opposite)
    for t in (0, 1):
        far_data(t, 1 - side).wait_recv()
        begin(data_copy(1, 7 + t, along_y(2, core), t * half_cols, half_cols, sibling))
    norms(opposite)

    factor = 2.0 * kappa / width

    def row_shift(r, carry):
        at = pl.ds(pl.multiple_of(r * 128, 128), 128)
        total = jnp.sum(part[at, :], axis=1, keepdims=True) * (-kappa / width)
        shift[at, :] = jnp.broadcast_to(total, (128, LANES))
        return carry

    lax.fori_loop(0, rows // 128, row_shift, 0)

    def final(block, xi):
        def column(i, carry):
            m = block + i
            cut = pl.ds(pl.multiple_of(m * 256, 256), 256)
            value = (scores[:, cut] + chunk_product(xi, m)) * factor
            scores[:, cut] = value
            for e in (0, 1):
                top = jnp.max(value[:, LANES * e:LANES * (e + 1)] + shift[...], axis=0, keepdims=True)
                colvec[:, pl.ds(pl.multiple_of(m * 256 + e * LANES, LANES), LANES)] = jnp.broadcast_to(top, (8, LANES))
            return carry

        lax.fori_loop(0, 4, column, 0)

    final(near, opposite)
    add_unit(other_block, jnp.where(opposite == y, 4, jnp.where(opposite == around(y + 2), 0, 2)), opposite)
    for t in (0, 1):
        beside(t, 1, 1 - core).wait_recv()
    unit(other_block + 2, (around(y + 1), around(y - 1)), False, 2)
    for t in (0, 1):
        data_wait(1, 7 + t, along_y(2, 1 - core), t * half_cols, half_cols)
    final(other_block, around(y + 2))

    def fold(block, op):
        out = block[0:8]
        for r in range(1, TILE // 8):
            out = op(out, block[8 * r:8 * r + 8])
        return out

    def spread_cols():
        for c in range(chunks):
            colvec[:, lane(c)] = jnp.broadcast_to(colpack[pl.ds(c, 1), :], (8, LANES))

    def tall(ref, c):
        return jnp.concatenate([ref[:, lane(c)]] * (TILE // 8), axis=0)

    def tile_at(t):
        return pl.ds(pl.multiple_of(t * TILE, TILE), TILE)

    def loop(body, init):
        return lax.fori_loop(0, tiles, body, init, unroll=2)

    zeros = tuple(jnp.zeros((8, LANES), jnp.float32) for _ in range(chunks))

    def exp_step(t, accs):
        at = tile_at(t)
        add = shift[at, :]
        return tuple(
            accs[c] + fold(jnp.exp2(scores[at, lane(c)] + add - tall(colvec, c)), jnp.add)
            for c in range(chunks)
        )

    sums = loop(exp_step, zeros)
    for c in range(chunks):
        total = jnp.sum(sums[c], axis=0, keepdims=True)
        col_buf[0, me_col, pl.ds(c, 1), :] = colvec[0:1, lane(c)] + jnp.log(total) * LOG2E
    exchange(col_buf, col_send, col_recv, 0, me_col, col_peers, started)
    col_pot = -log_cols - combine(col_buf, 0, csize)
    colpack[...] = col_pot
    spread_cols()

    def row_step(t, carry):
        at = tile_at(t)
        top = scores[at, lane(0)] + tall(colvec, 0)
        for c in range(1, chunks):
            top = jnp.maximum(top, scores[at, lane(c)] + tall(colvec, c))
        first[at, :] = top
        total = None
        for c in range(chunks):
            value = jnp.exp2(scores[at, lane(c)] + tall(colvec, c) - top)
            scores[at, lane(c)] = value
            total = value if total is None else total + value
        part[at, :] = total
        return carry

    loop(row_step, 0)
    for b in range(row_blocks):
        at = pl.ds(b * LANES, LANES)
        tops = first[at, :].T
        top = jnp.max(tops, axis=0, keepdims=True)
        total = jnp.sum(part[at, :].T * jnp.exp2(tops - top), axis=0, keepdims=True)
        row_buf[0, me_row, pl.ds(b, 1), :] = top + jnp.log(total) * LOG2E
    exchange(row_buf, row_send, row_recv, 0, me_row, row_peers, started)
    row_lse = combine(row_buf, 0, rsize)
    rowpack[...] = row_lse
    for b in range(row_blocks):
        at = pl.ds(b * LANES, LANES)
        base = jnp.exp2(first[at, :] - spread_lanes(rowpack, b))
        first[at, :] = base
        scale[at, :] = base

    def col_step(t, accs):
        at = tile_at(t)
        mul = scale[at, :]
        return tuple(accs[c] + fold(scores[at, lane(c)] * mul, jnp.add) for c in range(chunks))

    def sum_step(keep_values):
        def body(t, carry):
            at = tile_at(t)
            total = None
            for c in range(chunks):
                value = scores[at, lane(c)] * tall(colvec, c)
                if keep_values:
                    scores[at, lane(c)] = value
                total = value if total is None else total + value
            part[at, :] = total * first[at, :]
            return carry

        return body

    for step in range(1, ITERS):
        sums = loop(col_step, zeros)
        for c in range(chunks):
            col_buf[step, me_col, pl.ds(c, 1), :] = jnp.sum(sums[c], axis=0, keepdims=True)
        exchange(col_buf, col_send, col_recv, step, me_col, col_peers, started)
        ratio = 1.0 / add_slots(col_buf, step, csize)
        colpack[...] = ratio
        spread_cols()
        loop(sum_step(step == ITERS - 1), 0)
        for b in range(row_blocks):
            at = pl.ds(b * LANES, LANES)
            row_buf[step, me_row, pl.ds(b, 1), :] = jnp.sum(part[at, :].T, axis=0, keepdims=True)
        exchange(row_buf, row_send, row_recv, step, me_row, row_peers, started)
        total = add_slots(row_buf, step, rsize)
        rowpack[...] = 1.0 / total
        for b in range(row_blocks):
            at = pl.ds(b * LANES, LANES)
            scale[at, :] = first[at, :] * spread_lanes(rowpack, b)

    def weigh(r):
        def body(t, carry):
            at = pl.ds(pl.multiple_of(r * (rows // 2) + t * TILE, TILE), TILE)
            mul = scale[at, :]
            for c in range(chunks):
                weights[at, lane(c)] = (scores[at, lane(c)] * mul).astype(jnp.bfloat16)
            return carry

        lax.fori_loop(0, tiles // 2, body, 0, unroll=2)

    def swap_copy(i, to):
        return remote(swap.at[0], swap.at[i], swap_send.at[i], swap_recv.at[i], to)

    def potentials():
        for c in range(chunks):
            sqy[pl.ds(c, 1), :] = jnp.sum(data_part[pl.ds(c * LANES, LANES), :].T, axis=0, keepdims=True)
        cols_pot = (col_pot + jnp.log(ratio) * LOG2E + (log_rows - log_cols)) / kappa + sqy[...] / width
        colpack[...] = cols_pot
        cols_out[...] = colpack[pl.ds(pl.multiple_of(side * 8, 8), 8), :]
        for b in range(row_blocks):
            sqx[pl.ds(b, 1), :] = shift[pl.ds(b * LANES, LANES), :].T[0:1]
        swap[0] = -(log_rows + row_lse + jnp.log(total) * LOG2E + sqx[...]) / kappa
        begin(swap_copy(1, sibling))
        for i in (0, 1):
            begin(remote(
                swap.at[0], swap.at[2 + core], swap_send.at[2 + i], swap_recv.at[2 + core], device(partner, y, z, i)
            ))

    strip = rows // 2

    def half_rows(r):
        return pl.ds(pl.multiple_of(r * strip, strip), strip)

    def block_x(b):
        return jnp.where(b < 2, jnp.where(b == 0, opposite, mate), jnp.where(b == 2, partner, x))

    def product(p, r, to_z):
        cut = pl.ds(pl.multiple_of(lax.rem(to_z, 2) * LANES, LANES), LANES)
        total = None
        for k in (0, 1):
            block = jnp.concatenate(
                [data_all[k, block_x(2 * p + e) * 2 + to_z // 2, :, cut] for e in (0, 1)], axis=1
            )
            value = jnp.dot(
                weights[half_rows(r), k * full_cols:(k + 1) * full_cols], block,
                preferred_element_type=jnp.float32,
            )
            total = value if total is None else total + value
        return total

    def hop(t):
        return 1 - 2 * t

    def sum_copy(b, t, index, src, dst):
        to = device(x, y, around(z + hop(t)), core)
        return remote(src, dst, sum_send.at[b, t, index], sum_recv.at[b, t, index], to)

    def far_copy(b, t):
        return sum_copy(b, t, 0, out_buf.at[b, 2, half_rows(t)], far_buf.at[b - 2, t])

    def direct_copy(b, t):
        at = half_rows(1 - t)
        return sum_copy(b, t, 1, out_buf.at[b, t, at], near_buf.at[b, t, at])

    def added_copy(b, t):
        at = half_rows(t)
        return sum_copy(b, t, 2, out_buf.at[b, t, at], near_buf.at[b, t, at])

    def give_copy(b, r):
        at = half_rows(r)
        return remote(
            out_buf.at[b, 2, at], given.at[b, at], give_send.at[b, r], give_recv.at[b, r], device(mate, y, z, core)
        )

    def relay_copy(r):
        at = half_rows(r)
        return remote(own_buf.at[0, at], relay_in.at[at], in_send.at[r], in_recv.at[4 + r], device(mate, y, z, core))

    def partner_copy(a, r):
        at = half_rows(r)
        return remote(
            own_buf.at[2, at], in_sum.at[a, at], in_send.at[2 + r], part_recv.at[a, r], device(partner, y, z, kind)
        )

    def mate_copy(a):
        return remote(mate_out, mate_in.at[a], in_send.at[4], in_recv.at[2 + a], device(mate, y, z, kind))

    def stay_copy(a):
        return remote(own_buf.at[3], in_sum.at[a], in_send.at[5], in_recv.at[a], sibling)

    def add_far(b):
        for t in (0, 1):
            far_copy(b, t).wait_recv()
            out_buf[b, t, half_rows(t), :] = (
                keep[b - 2, t, half_rows(t), :] + far_buf[b - 2, t].astype(jnp.float32)
            ).astype(jnp.bfloat16)
            added_copy(b, t).start()

    def add_near(b):
        for t in (0, 1):
            direct_copy(b, t).wait_recv()
            added_copy(b, t).wait_recv()
        own_buf[b] = own_buf[b] + near_buf[b, 0].astype(jnp.float32) + near_buf[b, 1].astype(jnp.float32)

    def add_given(b):
        for r in (0, 1):
            at = half_rows(r)
            give_copy(b - 2, r).wait_recv()
            out_buf[b, 2, at, :] = (far_keep[b - 2, at, :] + given[b - 2, at, :].astype(jnp.float32)).astype(jnp.bfloat16)
            far_copy(b, r).start()

    def halves(body):
        def step(r, carry):
            body(r)
            return carry

        lax.fori_loop(0, 2, step, 0)

    def give(r):
        weigh(r)
        value = product(0, r, around(z + 2))
        for e in (0, 1):
            out_buf[e, 2, half_rows(r), :] = value[:, lane(e)].astype(jnp.bfloat16)
        give_copy(0, r).start()

    def near_products(p):
        def along(t):
            def part_of(r):
                value = product(p, r, around(z + hop(t)))
                for e in (0, 1):
                    block = value[:, lane(e)]
                    out_buf[2 * p + e, t, half_rows(r), :] = block.astype(jnp.bfloat16)
                    if p == 1:
                        keep[e, t, half_rows(r), :] = block

            halves(part_of)
            direct_copy(2 * p, t).start()
            if p == 0:
                added_copy(0, t).start()

        halves(along)

    def far_products(r):
        value = product(1, r, around(z + 2))
        for e in (0, 1):
            far_keep[e, half_rows(r), :] = value[:, lane(e)]

    def own_products(p):
        def part_of(r):
            value = product(p, r, z)
            for e in (0, 1):
                own_buf[2 * p + e, half_rows(r), :] = value[:, lane(e)]

        halves(part_of)

    halves(give)
    for r in (0, 1):
        give_copy(1, r).start()
    near_products(1)
    near_products(0)
    halves(far_products)
    add_given(2)
    for t in (0, 1):
        direct_copy(1, t).start()
        added_copy(1, t).start()
    halves(own_products)
    add_near(0)
    for r in (0, 1):
        relay_copy(r).start()
    add_far(2)
    add_given(3)
    for t in (0, 1):
        direct_copy(3, t).start()
    add_near(1)
    mate_out[...] = own_buf[1].astype(jnp.bfloat16)
    mate_copy(core).start()
    potentials()
    add_near(2)

    def to_partner(r):
        relay_copy(r).wait_recv()
        own_buf[2, half_rows(r), :] = own_buf[2, half_rows(r), :] + relay_in[half_rows(r), :]
        partner_copy(core, r).start()

    to_partner(0)
    add_far(3)
    to_partner(1)

    swap_copy(1, sibling).wait_recv()
    for i in (0, 1):
        remote(swap.at[0], swap.at[2 + i], swap_send.at[2 + i], swap_recv.at[2 + i], sibling).wait_recv()
    half = rows // LANES
    for a in (0, 1):
        mine_row = jnp.where(core == a, swap[0], swap[1])
        rows_out[pl.ds(a * half, half), :] = jnp.where(home, mine_row, swap[2 + a])

    add_near(3)

    @pl.when(home)
    def _():
        in_sum[core] = own_buf[3]
        stay_copy(1 - core).wait_recv()
        for a in (0, 1):
            mate_copy(a).wait_recv()
            in_sum[a] = in_sum[a] + mate_in[a].astype(jnp.float32)

    @pl.when(jnp.logical_not(home))
    def _():
        stay_copy(core).start()
        for a in (0, 1):
            for r in (0, 1):
                partner_copy(a, r).wait_recv()

    def result_copy(a):
        return pltpu.make_async_copy(in_sum.at[a], targets.at[pl.ds(a * rows, rows)], local_sems.at[a])

    for a in (0, 1):
        result_copy(a).start()

    def settle(b, carry):
        for t in (0, 1):
            direct_copy(b, t).wait_send()
            added_copy(b, t).wait_send()

            @pl.when(b < 2)
            def _():
                give_copy(jnp.minimum(b, 1), t).wait_send()

            @pl.when(b >= 2)
            def _():
                far_copy(jnp.maximum(b, 2), t).wait_send()

        return carry

    lax.fori_loop(0, SIDE, settle, 0)
    for a in (0, 1):
        result_copy(a).wait()
    for r in (0, 1):
        relay_copy(r).wait_send()
        partner_copy(core, r).wait_send()
    mate_copy(core).wait_send()

    @pl.when(jnp.logical_not(home))
    def _():
        stay_copy(core).wait_send()

    for copy in started:
        copy.wait_send()

    @pl.when(home)
    def _():
        aside.wait_send()
        for t in (0, 1):
            for a in (0, 1):
                own_round(t, a).wait_send()


def hand_on(targets, rows_pot, cols_pot, targets_out, rows_out, cols_out, stage, row_stage, col_stage, sems):
    size = targets.shape[0] // PARTS
    legs = [
        (targets.at[pl.ds(i * size, size)], stage.at[i], targets_out.at[pl.ds(i * size, size)]) for i in range(PARTS)
    ]
    legs += [(rows_pot, row_stage, rows_out), (cols_pot, col_stage, cols_out)]
    first = [pltpu.make_async_copy(src, mid, sems.at[i, 0]) for i, (src, mid, _) in enumerate(legs)]
    second = [pltpu.make_async_copy(mid, dst, sems.at[i, 1]) for i, (_, mid, dst) in enumerate(legs)]
    for copy in first:
        copy.start()
    for before, copy in zip(first, second):
        before.wait()
        copy.start()
    for copy in second:
        copy.wait()


def shards(noise_latents, data_latents):
    nsize = lax.axis_size("noise")
    dsize = lax.axis_size("dp")
    block, piece = noise_latents.shape
    rows, cols = block // 2, 2 * data_latents.shape[0]
    rsize, csize = dsize // 2, nsize * 2
    vmem = pl.BlockSpec(memory_space=pltpu.VMEM)
    f32, bf16 = jnp.float32, jnp.bfloat16
    strip = rows // 2
    row_vec, col_vec = (rows // LANES, LANES), (cols // LANES, LANES)
    sems = pltpu.SemaphoreType.DMA
    targets, rows_pot, cols_pot = pl.pallas_call(
        functools.partial(kernel, rsize, csize, piece * dsize),
        out_shape=(
            jax.ShapeDtypeStruct((block, piece), f32),
            jax.ShapeDtypeStruct((block // LANES, LANES), f32),
            jax.ShapeDtypeStruct((cols // 2 // LANES, LANES), f32),
        ),
        in_specs=[pl.BlockSpec(memory_space=pl.ANY)] * 2,
        out_specs=(pl.BlockSpec(memory_space=pl.ANY), vmem, vmem),
        scratch_shapes=[
            pltpu.VMEM((dsize, rows, piece), bf16),
            pltpu.VMEM((2, nsize) + data_latents.shape, bf16),
            pltpu.VMEM((rows, cols), f32),
            pltpu.VMEM((rows, cols), bf16),
            pltpu.VMEM((rows, LANES), f32),
            pltpu.VMEM((rows, LANES), f32),
            pltpu.VMEM((rows, LANES), f32),
            pltpu.VMEM((rows, LANES), f32),
            pltpu.VMEM((cols, LANES), f32),
            pltpu.VMEM((8, cols), f32),
            pltpu.VMEM(row_vec, f32),
            pltpu.VMEM(col_vec, f32),
            pltpu.VMEM(row_vec, f32),
            pltpu.VMEM(col_vec, f32),
            pltpu.VMEM((4,) + row_vec, f32),
            pltpu.VMEM((ITERS, csize) + col_vec, f32),
            pltpu.VMEM((ITERS, rsize) + row_vec, f32),
            pltpu.VMEM((SIDE, 3, rows, LANES), bf16),
            pltpu.VMEM((SIDE, rows, LANES), f32),
            pltpu.VMEM((2, 2, strip, LANES), bf16),
            pltpu.VMEM((SIDE, 2, rows, LANES), bf16),
            pltpu.VMEM((2, rows, LANES), f32),
            sems((ITERS,)),
            sems((ITERS,)),
            sems((ITERS,)),
            sems((ITERS,)),
            sems((4,)),
            sems((4,)),
            sems((4,)),
            sems((4,)),
            sems((SIDE, 2, 2)),
            sems((SIDE, 2, 2)),
            sems((2, 15)),
            sems((2, 15)),
            sems((SIDE, 2, 3)),
            sems((SIDE, 2, 3)),
            sems((6,)),
            sems((6,)),
            pltpu.VMEM((2, 2, rows, LANES), f32),
            pltpu.VMEM((2, rows, LANES), f32),
            pltpu.VMEM((2, rows, LANES), bf16),
            sems((2, 2)),
            sems((2, 2)),
            sems((2, 2)),
            sems((2,)),
            sems((2, 2)),
            sems((SIDE, 2)),
            pltpu.VMEM((rows, LANES), f32),
            pltpu.VMEM((rows, LANES), bf16),
            pltpu.VMEM((2, rows, LANES), bf16),
        ],
        compiler_params=pltpu.CompilerParams(
            collective_id=0, has_side_effects=True, vmem_limit_bytes=60 * 2**20
        ),
    )(noise_latents, data_latents)
    results = (targets, rows_pot, cols_pot)
    targets, rows_pot, cols_pot = pl.pallas_call(
        hand_on,
        out_shape=tuple(jax.ShapeDtypeStruct(a.shape, a.dtype) for a in results),
        in_specs=[pl.BlockSpec(memory_space=pl.ANY)] * 3,
        out_specs=(pl.BlockSpec(memory_space=pl.ANY),) * 3,
        scratch_shapes=[
            pltpu.VMEM((PARTS, block // PARTS, piece), f32),
            pltpu.VMEM(rows_pot.shape, f32),
            pltpu.VMEM(cols_pot.shape, f32),
            sems((PARTS + 2, 2)),
        ],
        compiler_params=pltpu.CompilerParams(vmem_limit_bytes=60 * 2**20),
    )(*results)
    return targets, rows_pot.reshape(block), cols_pot.reshape(cols // 2)


def solution(mesh):
    return jax.shard_map(
        shards,
        mesh=mesh,
        in_specs=(P("noise", "dp"), P("dp", "noise")),
        out_specs=(P("noise", "dp"), P("noise"), P("dp")),
        check_vma=False,
    )
```

```python
import functools
import math

import jax
import jax.numpy as jnp
from jax import lax
from jax.experimental import pallas as pl
from jax.experimental.pallas import tpu as pltpu
from jax.sharding import PartitionSpec as P

ITERS = 3
EPSILON = 0.04
LOG2E = 1.0 / math.log(2.0)
MESH = pl.DeviceIdType.MESH
LANES = 128
TILE = 32
SIDE = 4
PARTS = 4


def spread_lanes(ref, row):
    return jnp.broadcast_to(ref[pl.ds(row, 1), :], (LANES, LANES)).T


def exchange(buf, send, recv, step, me, peers, started):
    for peer in peers:
        pltpu.make_async_remote_copy(
            src_ref=buf.at[step, me],
            dst_ref=buf.at[step, me],
            send_sem=send.at[step],
            recv_sem=recv.at[step],
            device_id=peer,
            device_id_type=MESH,
        ).start()
    slots = buf.at[step, pl.ds(0, len(peers))]
    every = pltpu.make_async_remote_copy(
        src_ref=slots,
        dst_ref=slots,
        send_sem=send.at[step],
        recv_sem=recv.at[step],
        device_id=peers[0],
        device_id_type=MESH,
    )
    every.wait_recv()
    started.append(every)


def combine(buf, step, size):
    top = buf[step, 0]
    for s in range(1, size):
        top = jnp.maximum(top, buf[step, s])
    total = jnp.exp2(buf[step, 0] - top)
    for s in range(1, size):
        total = total + jnp.exp2(buf[step, s] - top)
    return top + jnp.log(total) * LOG2E


def add_slots(buf, step, size):
    total = buf[step, 0]
    for s in range(1, size):
        total = total + buf[step, s]
    return total


def kernel(
    rsize, csize, width,
    noise_ref, data_ref,
    targets, rows_out, cols_out,
    noise_all, data_all, scores, weights,
    shift, first, scale, part, data_part, colvec, rowpack, colpack, sqx, sqy, swap,
    col_buf, row_buf, out_buf, own_buf, far_buf, near_buf, in_sum,
    col_send, col_recv, row_send, row_recv, swap_send, swap_recv,
    cross_send, cross_recv, noise_send, noise_recv, data_send, data_recv,
    sum_send, sum_recv, in_send, in_recv, keep, far_keep, given, give_send, give_recv, part_recv, local_sems, own_send, far_send, relay_in, mate_out, mate_in,
):
    rows, cols = scores.shape
    n = lax.axis_index("noise")
    d = lax.axis_index("dp")
    x, z = d // SIDE, lax.rem(d, SIDE)
    y, core = n // 2, lax.rem(n, 2)
    kind = lax.rem((x + 1) // 2, 2)
    pair = x // 2
    side = lax.rem(x, 2)
    home = core == kind
    kappa = LOG2E / EPSILON
    log_rows = math.log2(rows * csize)
    log_cols = math.log2(cols * rsize)
    chunks = cols // LANES
    row_blocks = rows // LANES
    tiles = rows // TILE
    started = []

    def around(value):
        return lax.rem(value + SIDE, SIDE)

    def device(xi, yi, zi, ci):
        return (yi * 2 + ci, xi * SIDE + zi)

    me_row = pair * SIDE + z
    me_col = y * 4 + kind * 2 + core

    sibling = device(x, y, z, 1 - core)
    partner = x + 1 - 2 * side
    mate = SIDE - 1 - x
    opposite = around(x + 2)

    barrier = pltpu.get_barrier_semaphore()
    ys, zs = [around(y + k) for k in range(SIDE)], [around(z + k) for k in range(SIDE)]
    rings = [yi * 2 + ci for yi in (ys[2], ys[1], ys[3], ys[0]) for ci in (1 - core, core)]
    col_peers = [(r, di) for di in (partner * SIDE + z, d) for r in rings][:-1]
    row_peers = [(n, xi * SIDE + zi) for xi in (mate, x) for zi in (zs[2], zs[1], zs[3], zs[0])][:-1]
    greeted = row_peers + col_peers
    greeted += [device(opposite, y, z, 0), device(opposite, y, z, 1), device(mate, y, z, 1 - core)]
    greeted += [device(x, y, around(z + step), 1 - core) for step in (1, -1)]
    for to in greeted:
        pl.semaphore_signal(barrier, inc=1, device_id=to, device_id_type=MESH)
    pl.semaphore_wait(barrier, len(greeted))

    def remote(src, dst, send, recv, to):
        return pltpu.make_async_remote_copy(
            src_ref=src, dst_ref=dst, send_sem=send, recv_sem=recv, device_id=to, device_id_type=MESH
        )

    def begin(copy):
        copy.start()
        started.append(copy)

    def lane(c):
        return slice(LANES * c, LANES * (c + 1))

    HOP = (1, -1)

    def noise_slot(xi, zi, at):
        return noise_all.at[xi, at, pl.ds(pl.multiple_of(zi * LANES, LANES), LANES)]

    own = noise_slot(x, z, pl.ds(0, rows))

    def cross_copy(i, half, to):
        return remote(
            noise_ref.at[pl.ds(half * rows, rows)], own, cross_send.at[i], cross_recv.at[x], to
        )

    def cross_wait(xi):
        remote(
            noise_ref.at[pl.ds(0, rows)], noise_slot(xi, z, pl.ds(0, rows)), cross_send.at[0], cross_recv.at[xi], sibling
        ).wait_recv()

    there = jnp.where(home, mate, partner)
    aside = cross_copy(2, 1 - core, sibling)

    def noise_copy(xi, t, forward, zi):
        at = pl.ds(t * (rows // 2), rows // 2) if forward else pl.ds(0, rows)
        f = int(forward)
        slot = noise_slot(xi, zi, at)
        return remote(
            slot, slot, noise_send.at[xi, t, f], noise_recv.at[xi, t, f], device(x, y, around(z + HOP[t]), core)
        )

    def noise_wait(xi, t, forward):
        zi = around(z - HOP[t] * (2 if forward else 1))
        noise_copy(xi, t, forward, zi).wait_recv()
        return zi

    def data_slot(block, where, at):
        width_at = pl.ds(pl.multiple_of(lax.rem(where, 2) * 256, 256), 256)
        return data_all.at[block, where // 2, at, width_at]

    def data_copy(r, index, where, lo, size, to, own=False):
        at = pl.ds(lo, size)
        block = side if r == 0 else 1 - side
        dst = data_slot(block, where, at)
        return remote(data_ref.at[at] if own else dst, dst, data_send.at[r, index], data_recv.at[r, index], to)

    half_cols = cols // 4
    full_cols = cols // 2

    def along_y(step, c):
        return around(y + step) * 2 + c

    def data_wait(r, index, where, lo, size):
        data_copy(r, index, where, lo, size, sibling).wait_recv()

    HALF = 9

    def cross_data(h, own=False):
        at = pl.ds(h * half_cols, half_cols)
        dst = data_slot(side if own else 1 - side, n, at)
        return remote(
            data_ref.at[at], dst, data_send.at[1, 11 + h], data_recv.at[1, 11 + h], device(partner, y, z, core)
        )

    def partner_y(t, h, back=0):
        where = around(y + back) * 2 + core
        to = device(x, around(y + HOP[t]), z, core)
        return t if h == 0 else HALF + t, where, h * half_cols, half_cols, to

    def partner_wait(t, h):
        data_copy(1, *partner_y(t, h, -HOP[t])).wait_recv()

    def own_round(t, a):
        return remote(
            noise_ref.at[pl.ds(a * rows, rows)], own,
            own_send.at[t, a], noise_recv.at[x, t, 0], device(x, y, around(z + HOP[t]), a),
        )

    def own_half():
        return pltpu.make_async_copy(
            noise_ref.at[pl.ds(pl.multiple_of(core * rows, rows), rows)], own, local_sems.at[0]
        )

    @pl.when(home)
    def _():
        for t in (0, 1):
            for a in (0, 1):
                own_round(t, a).start()
        aside.start()

    begin(cross_copy(0, 0, device(there, y, z, 0)))
    begin(cross_copy(1, 1, device(there, y, z, 1)))
    for t in (0, 1):
        begin(data_copy(0, t, n, 0, full_cols, device(x, around(y + HOP[t]), z, core), own=True))
    @pl.when(home)
    def _():
        own_half().start()

    data_own = pltpu.make_async_copy(data_ref, data_slot(side, n, pl.ds(0, full_cols)), local_sems.at[1])
    data_own.start()
    scores[...] = jnp.zeros_like(scores)
    part[...] = jnp.zeros_like(part)
    data_part[...] = jnp.zeros_like(data_part)

    def round_z(xi):
        for t in (0, 1):
            begin(noise_copy(xi, t, False, z))

    def forward_z(xi):
        for t in (0, 1):
            begin(noise_copy(xi, t, True, noise_wait(xi, t, False)))

    def far_noise(xi, t):
        slot = noise_slot(xi, around(z + 2), pl.ds(t * (rows // 2), rows // 2))
        return remote(slot, slot, far_send.at[xi, t], noise_recv.at[xi, t, 1], device(mate, y, z, core))

    def share_far(xi):
        for t in (0, 1):
            noise_wait(xi, t, True)
            begin(far_noise(xi, t))

    def far_wait(xi):
        for t in (0, 1):
            far_noise(xi, t).wait_recv()

    def far_data(t, block):
        where = along_y(2, core)
        at = pl.ds(t * half_cols, half_cols)
        dst = data_slot(block, where, at)
        return remote(dst, dst, data_send.at[1, 2 + t], data_recv.at[1, 2 + t], device(partner, y, z, core))

    cross_wait(partner)
    slot = noise_slot(partner, z, pl.ds(0, rows))
    begin(remote(slot, slot, cross_send.at[3], cross_recv.at[partner], device(mate, y, z, core)))
    round_z(partner)
    for h in (0, 1):
        begin(cross_data(h, own=True))
    begin(data_copy(0, 4, n, 0, full_cols, sibling, own=True))
    forward_z(x)
    cross_wait(mate)
    round_z(mate)
    for t in (0, 1):
        where = along_y(-HOP[t], core)
        data_wait(0, t, where, 0, full_cols)
        begin(data_copy(0, 2 + t, where, t * half_cols, half_cols, device(x, around(y + HOP[t]), z, core)))
        begin(data_copy(0, 5 + t, where, 0, full_cols, sibling))
    cross_data(0).wait_recv()
    for t in (0, 1):
        begin(data_copy(1, *partner_y(t, 0)))
    forward_z(partner)
    cross_wait(opposite)
    round_z(opposite)
    share_far(x)
    cross_data(1).wait_recv()
    for t in (0, 1):
        begin(data_copy(1, *partner_y(t, 1)))
    begin(data_copy(1, 4, n, 0, full_cols, sibling))
    for t in (0, 1):
        where = along_y(2, core)
        data_wait(0, 2 + t, where, t * half_cols, half_cols)
        begin(far_data(t, side))
        begin(data_copy(0, 7 + t, where, t * half_cols, half_cols, sibling))

    def squares(block):
        value = block.astype(jnp.float32)
        return value * value

    def chunk_product(xi, m):
        cut = pl.ds(pl.multiple_of(m * 256, 256), 256)
        here = pl.ds(pl.multiple_of(lax.rem(m, 4) * 256, 256), 256)
        total = data_part[cut, :]
        for i in range(SIDE):
            total = total + squares(data_all[m // 4, xi, here, lane(i)])
        data_part[cut, :] = total
        return lax.dot_general(
            noise_all[xi], data_all[m // 4, xi, here, :], (((1,), (1,)), ((), ())),
            preferred_element_type=jnp.float32,
        )

    def norms(xi):
        def norm(r, carry):
            cut = pl.ds(pl.multiple_of(r * 64, 64), 64)
            total = part[cut, :]
            for i in range(SIDE):
                total = total + squares(noise_all[xi, cut, lane(i)])
            part[cut, :] = total
            return carry

        lax.fori_loop(0, rows // 64, norm, 0)

    near, other_block = side * 4, 4 - side * 4

    def unit(block, xs, fresh, count=4):
        def column(i, carry):
            m = block + i
            cut = pl.ds(pl.multiple_of(m * 256, 256), 256)
            value = None if fresh else scores[:, cut]
            for xi in xs:
                value = chunk_product(xi, m) if value is None else value + chunk_product(xi, m)
            scores[:, cut] = value
            return carry

        lax.fori_loop(0, count, column, 0)

    def add_unit(block, count, xi):
        unit(block, (xi,), False, count)

    data_own.wait()
    data_wait(0, 4, along_y(0, 1 - core), 0, full_cols)
    for t in (0, 1):
        data_wait(0, 5 + t, along_y(-HOP[t], 1 - core), 0, full_cols)
    for t in (0, 1):
        data_wait(0, 7 + t, along_y(2, 1 - core), t * half_cols, half_cols)

    @pl.when(home)
    def _():
        own_half().wait()

    @pl.when(jnp.logical_not(home))
    def _():
        cross_wait(x)

    unit(near, (x,), True)
    share_far(partner)
    norms(x)
    for t in (0, 1):
        noise_wait(mate, t, False)
    far_wait(mate)
    unit(near, (mate,), False)
    norms(mate)

    def beside(t, h, c):
        return data_copy(1, (5 if h == 0 else 13) + t, along_y(-HOP[t], c), h * half_cols, half_cols, sibling)

    for t in (0, 1):
        partner_wait(t, 0)
        begin(beside(t, 0, core))
    unit(near, (partner,), False)
    norms(partner)
    data_wait(1, 4, along_y(0, 1 - core), 0, full_cols)
    for t in (0, 1):
        beside(t, 0, 1 - core).wait_recv()

    def ahead(i, carry):
        xi = around(y + i + i // 2)
        add_unit(other_block, jnp.where(xi == opposite, 0, jnp.where(i == 0, 4, 2)), xi)
        return carry

    lax.fori_loop(0, 3, ahead, 0)
    for t in (0, 1):
        partner_wait(t, 1)
        begin(beside(t, 1, core))
    for t in (0, 1):
        noise_wait(opposite, t, False)
    far_wait(opposite)
    for t in (0, 1):
        far_data(t, 1 - side).wait_recv()
        begin(data_copy(1, 7 + t, along_y(2, core), t * half_cols, half_cols, sibling))
    norms(opposite)

    factor = 2.0 * kappa / width

    def row_shift(r, carry):
        at = pl.ds(pl.multiple_of(r * 128, 128), 128)
        total = jnp.sum(part[at, :], axis=1, keepdims=True) * (-kappa / width)
        shift[at, :] = jnp.broadcast_to(total, (128, LANES))
        return carry

    lax.fori_loop(0, rows // 128, row_shift, 0)

    def final(block, xi):
        def column(i, carry):
            m = block + i
            cut = pl.ds(pl.multiple_of(m * 256, 256), 256)
            value = (scores[:, cut] + chunk_product(xi, m)) * factor
            scores[:, cut] = value
            for e in (0, 1):
                top = jnp.max(value[:, LANES * e:LANES * (e + 1)] + shift[...], axis=0, keepdims=True)
                colvec[:, pl.ds(pl.multiple_of(m * 256 + e * LANES, LANES), LANES)] = jnp.broadcast_to(top, (8, LANES))
            return carry

        lax.fori_loop(0, 4, column, 0)

    final(near, opposite)
    add_unit(other_block, jnp.where(opposite == y, 4, jnp.where(opposite == around(y + 2), 0, 2)), opposite)
    for t in (0, 1):
        beside(t, 1, 1 - core).wait_recv()
    unit(other_block + 2, (around(y + 1), around(y - 1)), False, 2)
    for t in (0, 1):
        data_wait(1, 7 + t, along_y(2, 1 - core), t * half_cols, half_cols)
    final(other_block, around(y + 2))

    def fold(block, op):
        out = block[0:8]
        for r in range(1, TILE // 8):
            out = op(out, block[8 * r:8 * r + 8])
        return out

    def spread_cols():
        for c in range(chunks):
            colvec[:, lane(c)] = jnp.broadcast_to(colpack[pl.ds(c, 1), :], (8, LANES))

    def tall(ref, c):
        return jnp.concatenate([ref[:, lane(c)]] * (TILE // 8), axis=0)

    def tile_at(t):
        return pl.ds(pl.multiple_of(t * TILE, TILE), TILE)

    def loop(body, init):
        return lax.fori_loop(0, tiles, body, init, unroll=2)

    zeros = tuple(jnp.zeros((8, LANES), jnp.float32) for _ in range(chunks))

    def exp_step(t, accs):
        at = tile_at(t)
        add = shift[at, :]
        return tuple(
            accs[c] + fold(jnp.exp2(scores[at, lane(c)] + add - tall(colvec, c)), jnp.add)
            for c in range(chunks)
        )

    sums = loop(exp_step, zeros)
    for c in range(chunks):
        total = jnp.sum(sums[c], axis=0, keepdims=True)
        col_buf[0, me_col, pl.ds(c, 1), :] = colvec[0:1, lane(c)] + jnp.log(total) * LOG2E
    exchange(col_buf, col_send, col_recv, 0, me_col, col_peers, started)
    col_pot = -log_cols - combine(col_buf, 0, csize)
    colpack[...] = col_pot
    spread_cols()

    def row_step(t, carry):
        at = tile_at(t)
        top = scores[at, lane(0)] + tall(colvec, 0)
        for c in range(1, chunks):
            top = jnp.maximum(top, scores[at, lane(c)] + tall(colvec, c))
        first[at, :] = top
        total = None
        for c in range(chunks):
            value = jnp.exp2(scores[at, lane(c)] + tall(colvec, c) - top)
            scores[at, lane(c)] = value
            total = value if total is None else total + value
        part[at, :] = total
        return carry

    loop(row_step, 0)
    for b in range(row_blocks):
        at = pl.ds(b * LANES, LANES)
        tops = first[at, :].T
        top = jnp.max(tops, axis=0, keepdims=True)
        total = jnp.sum(part[at, :].T * jnp.exp2(tops - top), axis=0, keepdims=True)
        row_buf[0, me_row, pl.ds(b, 1), :] = top + jnp.log(total) * LOG2E
    exchange(row_buf, row_send, row_recv, 0, me_row, row_peers, started)
    row_lse = combine(row_buf, 0, rsize)
    rowpack[...] = row_lse
    for b in range(row_blocks):
        at = pl.ds(b * LANES, LANES)
        base = jnp.exp2(first[at, :] - spread_lanes(rowpack, b))
        first[at, :] = base
        scale[at, :] = base

    def col_step(t, accs):
        at = tile_at(t)
        mul = scale[at, :]
        return tuple(accs[c] + fold(scores[at, lane(c)] * mul, jnp.add) for c in range(chunks))

    def sum_step(keep_values):
        def body(t, carry):
            at = tile_at(t)
            total = None
            for c in range(chunks):
                value = scores[at, lane(c)] * tall(colvec, c)
                if keep_values:
                    scores[at, lane(c)] = value
                total = value if total is None else total + value
            part[at, :] = total * first[at, :]
            return carry

        return body

    for step in range(1, ITERS):
        sums = loop(col_step, zeros)
        for c in range(chunks):
            col_buf[step, me_col, pl.ds(c, 1), :] = jnp.sum(sums[c], axis=0, keepdims=True)
        exchange(col_buf, col_send, col_recv, step, me_col, col_peers, started)
        ratio = 1.0 / add_slots(col_buf, step, csize)
        colpack[...] = ratio
        spread_cols()
        loop(sum_step(step == ITERS - 1), 0)
        for b in range(row_blocks):
            at = pl.ds(b * LANES, LANES)
            row_buf[step, me_row, pl.ds(b, 1), :] = jnp.sum(part[at, :].T, axis=0, keepdims=True)
        exchange(row_buf, row_send, row_recv, step, me_row, row_peers, started)
        total = add_slots(row_buf, step, rsize)
        rowpack[...] = 1.0 / total
        for b in range(row_blocks):
            at = pl.ds(b * LANES, LANES)
            scale[at, :] = first[at, :] * spread_lanes(rowpack, b)

    def weigh(r):
        def body(t, carry):
            at = pl.ds(pl.multiple_of(r * (rows // 2) + t * TILE, TILE), TILE)
            mul = scale[at, :]
            for c in range(chunks):
                weights[at, lane(c)] = (scores[at, lane(c)] * mul).astype(jnp.bfloat16)
            return carry

        lax.fori_loop(0, tiles // 2, body, 0, unroll=2)

    def swap_copy(i, to):
        return remote(swap.at[0], swap.at[i], swap_send.at[i], swap_recv.at[i], to)

    def potentials():
        for c in range(chunks):
            sqy[pl.ds(c, 1), :] = jnp.sum(data_part[pl.ds(c * LANES, LANES), :].T, axis=0, keepdims=True)
        cols_pot = (col_pot + jnp.log(ratio) * LOG2E + (log_rows - log_cols)) / kappa + sqy[...] / width
        colpack[...] = cols_pot
        cols_out[...] = colpack[pl.ds(pl.multiple_of(side * 8, 8), 8), :]
        for b in range(row_blocks):
            sqx[pl.ds(b, 1), :] = shift[pl.ds(b * LANES, LANES), :].T[0:1]
        swap[0] = -(log_rows + row_lse + jnp.log(total) * LOG2E + sqx[...]) / kappa
        begin(swap_copy(1, sibling))
        for i in (0, 1):
            begin(remote(
                swap.at[0], swap.at[2 + core], swap_send.at[2 + i], swap_recv.at[2 + core], device(partner, y, z, i)
            ))

    strip = rows // 2

    def half_rows(r):
        return pl.ds(pl.multiple_of(r * strip, strip), strip)

    def block_x(b):
        return jnp.where(b < 2, jnp.where(b == 0, opposite, mate), jnp.where(b == 2, partner, x))

    def product(p, r, to_z):
        cut = pl.ds(pl.multiple_of(to_z * LANES, LANES), LANES)
        total = None
        for k in (0, 1):
            block = jnp.concatenate(
                [data_all[k, block_x(2 * p + e), :, cut] for e in (0, 1)], axis=1
            )
            value = jnp.dot(
                weights[half_rows(r), k * full_cols:(k + 1) * full_cols], block,
                preferred_element_type=jnp.float32,
            )
            total = value if total is None else total + value
        return total

    def hop(t):
        return 1 - 2 * t

    def sum_copy(b, t, index, src, dst):
        to = device(x, y, around(z + hop(t)), core)
        return remote(src, dst, sum_send.at[b, t, index], sum_recv.at[b, t, index], to)

    def far_copy(b, t):
        return sum_copy(b, t, 0, out_buf.at[b, 2, half_rows(t)], far_buf.at[b - 2, t])

    def direct_copy(b, t):
        at = half_rows(1 - t)
        return sum_copy(b, t, 1, out_buf.at[b, t, at], near_buf.at[b, t, at])

    def added_copy(b, t):
        at = half_rows(t)
        return sum_copy(b, t, 2, out_buf.at[b, t, at], near_buf.at[b, t, at])

    def give_copy(b, r):
        at = half_rows(r)
        return remote(
            out_buf.at[b, 2, at], given.at[b, at], give_send.at[b, r], give_recv.at[b, r], device(mate, y, z, core)
        )

    def relay_copy(r):
        at = half_rows(r)
        return remote(own_buf.at[0, at], relay_in.at[at], in_send.at[r], in_recv.at[4 + r], device(mate, y, z, core))

    def partner_copy(a, r):
        at = half_rows(r)
        return remote(
            own_buf.at[2, at], in_sum.at[a, at], in_send.at[2 + r], part_recv.at[a, r], device(partner, y, z, kind)
        )

    def mate_copy(a):
        return remote(mate_out, mate_in.at[a], in_send.at[4], in_recv.at[2 + a], device(mate, y, z, kind))

    def stay_copy(a):
        return remote(own_buf.at[3], in_sum.at[a], in_send.at[5], in_recv.at[a], sibling)

    def add_far(b):
        for t in (0, 1):
            far_copy(b, t).wait_recv()
            out_buf[b, t, half_rows(t), :] = (
                keep[b - 2, t, half_rows(t), :] + far_buf[b - 2, t].astype(jnp.float32)
            ).astype(jnp.bfloat16)
            added_copy(b, t).start()

    def add_near(b):
        for t in (0, 1):
            direct_copy(b, t).wait_recv()
            added_copy(b, t).wait_recv()
        own_buf[b] = own_buf[b] + near_buf[b, 0].astype(jnp.float32) + near_buf[b, 1].astype(jnp.float32)

    def add_given(b):
        for r in (0, 1):
            at = half_rows(r)
            give_copy(b - 2, r).wait_recv()
            out_buf[b, 2, at, :] = (far_keep[b - 2, at, :] + given[b - 2, at, :].astype(jnp.float32)).astype(jnp.bfloat16)
            far_copy(b, r).start()

    def halves(body):
        def step(r, carry):
            body(r)
            return carry

        lax.fori_loop(0, 2, step, 0)

    def give(r):
        weigh(r)
        value = product(0, r, around(z + 2))
        for e in (0, 1):
            out_buf[e, 2, half_rows(r), :] = value[:, lane(e)].astype(jnp.bfloat16)
        give_copy(0, r).start()

    def near_products(p):
        def along(t):
            def part_of(r):
                value = product(p, r, around(z + hop(t)))
                for e in (0, 1):
                    block = value[:, lane(e)]
                    out_buf[2 * p + e, t, half_rows(r), :] = block.astype(jnp.bfloat16)
                    if p == 1:
                        keep[e, t, half_rows(r), :] = block

            halves(part_of)
            direct_copy(2 * p, t).start()
            if p == 0:
                added_copy(0, t).start()

        halves(along)

    def far_products(r):
        value = product(1, r, around(z + 2))
        for e in (0, 1):
            far_keep[e, half_rows(r), :] = value[:, lane(e)]

    def own_products(p):
        def part_of(r):
            value = product(p, r, z)
            for e in (0, 1):
                own_buf[2 * p + e, half_rows(r), :] = value[:, lane(e)]

        halves(part_of)

    halves(give)
    for r in (0, 1):
        give_copy(1, r).start()
    near_products(1)
    near_products(0)
    halves(far_products)
    add_given(2)
    for t in (0, 1):
        direct_copy(1, t).start()
        added_copy(1, t).start()
    halves(own_products)
    add_near(0)
    for r in (0, 1):
        relay_copy(r).start()
    add_far(2)
    add_given(3)
    for t in (0, 1):
        direct_copy(3, t).start()
    add_near(1)
    mate_out[...] = own_buf[1].astype(jnp.bfloat16)
    mate_copy(core).start()
    potentials()
    add_near(2)

    def to_partner(r):
        relay_copy(r).wait_recv()
        own_buf[2, half_rows(r), :] = own_buf[2, half_rows(r), :] + relay_in[half_rows(r), :]
        partner_copy(core, r).start()

    to_partner(0)
    add_far(3)
    to_partner(1)

    swap_copy(1, sibling).wait_recv()
    for i in (0, 1):
        remote(swap.at[0], swap.at[2 + i], swap_send.at[2 + i], swap_recv.at[2 + i], sibling).wait_recv()
    half = rows // LANES
    for a in (0, 1):
        mine_row = jnp.where(core == a, swap[0], swap[1])
        rows_out[pl.ds(a * half, half), :] = jnp.where(home, mine_row, swap[2 + a])

    add_near(3)

    @pl.when(home)
    def _():
        in_sum[core] = own_buf[3]
        stay_copy(1 - core).wait_recv()
        for a in (0, 1):
            mate_copy(a).wait_recv()
            in_sum[a] = in_sum[a] + mate_in[a].astype(jnp.float32)

    @pl.when(jnp.logical_not(home))
    def _():
        stay_copy(core).start()
        for a in (0, 1):
            for r in (0, 1):
                partner_copy(a, r).wait_recv()

    def result_copy(a):
        return pltpu.make_async_copy(in_sum.at[a], targets.at[pl.ds(a * rows, rows)], local_sems.at[a])

    for a in (0, 1):
        result_copy(a).start()

    def settle(b, carry):
        for t in (0, 1):
            direct_copy(b, t).wait_send()
            added_copy(b, t).wait_send()

            @pl.when(b < 2)
            def _():
                give_copy(jnp.minimum(b, 1), t).wait_send()

            @pl.when(b >= 2)
            def _():
                far_copy(jnp.maximum(b, 2), t).wait_send()

        return carry

    lax.fori_loop(0, SIDE, settle, 0)
    for a in (0, 1):
        result_copy(a).wait()
    for r in (0, 1):
        relay_copy(r).wait_send()
        partner_copy(core, r).wait_send()
    mate_copy(core).wait_send()

    @pl.when(jnp.logical_not(home))
    def _():
        stay_copy(core).wait_send()

    for copy in started:
        copy.wait_send()

    @pl.when(home)
    def _():
        aside.wait_send()
        for t in (0, 1):
            for a in (0, 1):
                own_round(t, a).wait_send()


def hand_on(targets, rows_pot, cols_pot, targets_out, rows_out, cols_out, stage, row_stage, col_stage, sems):
    size = targets.shape[0] // PARTS
    legs = [
        (targets.at[pl.ds(i * size, size)], stage.at[i], targets_out.at[pl.ds(i * size, size)]) for i in range(PARTS)
    ]
    legs += [(rows_pot, row_stage, rows_out), (cols_pot, col_stage, cols_out)]
    first = [pltpu.make_async_copy(src, mid, sems.at[i, 0]) for i, (src, mid, _) in enumerate(legs)]
    second = [pltpu.make_async_copy(mid, dst, sems.at[i, 1]) for i, (_, mid, dst) in enumerate(legs)]
    for copy in first:
        copy.start()
    for before, copy in zip(first, second):
        before.wait()
        copy.start()
    for copy in second:
        copy.wait()


def shards(noise_latents, data_latents):
    nsize = lax.axis_size("noise")
    dsize = lax.axis_size("dp")
    block, piece = noise_latents.shape
    rows, cols = block // 2, 2 * data_latents.shape[0]
    rsize, csize = dsize // 2, nsize * 2
    vmem = pl.BlockSpec(memory_space=pltpu.VMEM)
    f32, bf16 = jnp.float32, jnp.bfloat16
    strip = rows // 2
    row_vec, col_vec = (rows // LANES, LANES), (cols // LANES, LANES)
    sems = pltpu.SemaphoreType.DMA
    targets, rows_pot, cols_pot = pl.pallas_call(
        functools.partial(kernel, rsize, csize, piece * dsize),
        out_shape=(
            jax.ShapeDtypeStruct((block, piece), f32),
            jax.ShapeDtypeStruct((block // LANES, LANES), f32),
            jax.ShapeDtypeStruct((cols // 2 // LANES, LANES), f32),
        ),
        in_specs=[pl.BlockSpec(memory_space=pl.ANY)] * 2,
        out_specs=(pl.BlockSpec(memory_space=pl.ANY), vmem, vmem),
        scratch_shapes=[
            pltpu.VMEM((SIDE, rows, SIDE * piece), bf16),
            pltpu.VMEM((2, SIDE, cols // 2, nsize // SIDE * data_latents.shape[1]), bf16),
            pltpu.VMEM((rows, cols), f32),
            pltpu.VMEM((rows, cols), bf16),
            pltpu.VMEM((rows, LANES), f32),
            pltpu.VMEM((rows, LANES), f32),
            pltpu.VMEM((rows, LANES), f32),
            pltpu.VMEM((rows, LANES), f32),
            pltpu.VMEM((cols, LANES), f32),
            pltpu.VMEM((8, cols), f32),
            pltpu.VMEM(row_vec, f32),
            pltpu.VMEM(col_vec, f32),
            pltpu.VMEM(row_vec, f32),
            pltpu.VMEM(col_vec, f32),
            pltpu.VMEM((4,) + row_vec, f32),
            pltpu.VMEM((ITERS, csize) + col_vec, f32),
            pltpu.VMEM((ITERS, rsize) + row_vec, f32),
            pltpu.VMEM((SIDE, 3, rows, LANES), bf16),
            pltpu.VMEM((SIDE, rows, LANES), f32),
            pltpu.VMEM((2, 2, strip, LANES), bf16),
            pltpu.VMEM((SIDE, 2, rows, LANES), bf16),
            pltpu.VMEM((2, rows, LANES), f32),
            sems((ITERS,)),
            sems((ITERS,)),
            sems((ITERS,)),
            sems((ITERS,)),
            sems((4,)),
            sems((4,)),
            sems((4,)),
            sems((4,)),
            sems((SIDE, 2, 2)),
            sems((SIDE, 2, 2)),
            sems((2, 15)),
            sems((2, 15)),
            sems((SIDE, 2, 3)),
            sems((SIDE, 2, 3)),
            sems((6,)),
            sems((6,)),
            pltpu.VMEM((2, 2, rows, LANES), f32),
            pltpu.VMEM((2, rows, LANES), f32),
            pltpu.VMEM((2, rows, LANES), bf16),
            sems((2, 2)),
            sems((2, 2)),
            sems((2, 2)),
            sems((2,)),
            sems((2, 2)),
            sems((SIDE, 2)),
            pltpu.VMEM((rows, LANES), f32),
            pltpu.VMEM((rows, LANES), bf16),
            pltpu.VMEM((2, rows, LANES), bf16),
        ],
        compiler_params=pltpu.CompilerParams(
            collective_id=0, has_side_effects=True, vmem_limit_bytes=60 * 2**20
        ),
    )(noise_latents, data_latents)
    results = (targets, rows_pot, cols_pot)
    targets, rows_pot, cols_pot = pl.pallas_call(
        hand_on,
        out_shape=tuple(jax.ShapeDtypeStruct(a.shape, a.dtype) for a in results),
        in_specs=[pl.BlockSpec(memory_space=pl.ANY)] * 3,
        out_specs=(pl.BlockSpec(memory_space=pl.ANY),) * 3,
        scratch_shapes=[
            pltpu.VMEM((PARTS, block // PARTS, piece), f32),
            pltpu.VMEM(rows_pot.shape, f32),
            pltpu.VMEM(cols_pot.shape, f32),
            sems((PARTS + 2, 2)),
        ],
        compiler_params=pltpu.CompilerParams(vmem_limit_bytes=60 * 2**20),
    )(*results)
    return targets, rows_pot.reshape(block), cols_pot.reshape(cols // 2)


def solution(mesh):
    return jax.shard_map(
        shards,
        mesh=mesh,
        in_specs=(P("noise", "dp"), P("dp", "noise")),
        out_specs=(P("noise", "dp"), P("noise"), P("dp")),
        check_vma=False,
    )
```

```python
import functools
import math

import jax
import jax.numpy as jnp
from jax import lax
from jax.experimental import pallas as pl
from jax.experimental.pallas import tpu as pltpu
from jax.sharding import PartitionSpec as P

ITERS = 3
EPSILON = 0.04
LOG2E = 1.0 / math.log(2.0)
MESH = pl.DeviceIdType.MESH
LANES = 128
TILE = 32
SIDE = 4
PARTS = 4


def spread_lanes(ref, row):
    return jnp.broadcast_to(ref[pl.ds(row, 1), :], (LANES, LANES)).T


def exchange(buf, send, recv, step, me, peers, started):
    for peer in peers:
        pltpu.make_async_remote_copy(
            src_ref=buf.at[step, me],
            dst_ref=buf.at[step, me],
            send_sem=send.at[step],
            recv_sem=recv.at[step],
            device_id=peer,
            device_id_type=MESH,
        ).start()
    slots = buf.at[step, pl.ds(0, len(peers))]
    every = pltpu.make_async_remote_copy(
        src_ref=slots,
        dst_ref=slots,
        send_sem=send.at[step],
        recv_sem=recv.at[step],
        device_id=peers[0],
        device_id_type=MESH,
    )
    every.wait_recv()
    started.append(every)


def combine(buf, step, size):
    top = buf[step, 0]
    for s in range(1, size):
        top = jnp.maximum(top, buf[step, s])
    total = jnp.exp2(buf[step, 0] - top)
    for s in range(1, size):
        total = total + jnp.exp2(buf[step, s] - top)
    return top + jnp.log(total) * LOG2E


def add_slots(buf, step, size):
    total = buf[step, 0]
    for s in range(1, size):
        total = total + buf[step, s]
    return total


def kernel(
    rsize, csize, width,
    noise_ref, data_ref,
    targets, rows_out, cols_out,
    noise_all, data_all, scores, weights,
    shift, first, factor_of, scale, part, data_part, colvec, rowpack, colpack, sqx, sqy, swap,
    col_buf, row_buf, out_buf, own_buf, far_buf, near_buf, in_sum,
    col_send, col_recv, row_send, row_recv, swap_send, swap_recv,
    cross_send, cross_recv, noise_send, noise_recv, data_send, data_recv,
    sum_send, sum_recv, in_send, in_recv, keep, far_keep, given, give_send, give_recv, part_recv, local_sems, own_send, far_send, relay_in, mate_out, mate_in,
):
    rows, cols = scores.shape
    n = lax.axis_index("noise")
    d = lax.axis_index("dp")
    x, z = d // SIDE, lax.rem(d, SIDE)
    y, core = n // 2, lax.rem(n, 2)
    kind = lax.rem((x + 1) // 2, 2)
    pair = x // 2
    side = lax.rem(x, 2)
    home = core == kind
    kappa = LOG2E / EPSILON
    log_rows = math.log2(rows * csize)
    log_cols = math.log2(cols * rsize)
    chunks = cols // LANES
    row_blocks = rows // LANES
    tiles = rows // TILE
    started = []

    def around(value):
        return lax.rem(value + SIDE, SIDE)

    def device(xi, yi, zi, ci):
        return (yi * 2 + ci, xi * SIDE + zi)

    me_row = pair * SIDE + z
    me_col = y * 4 + kind * 2 + core

    sibling = device(x, y, z, 1 - core)
    partner = x + 1 - 2 * side
    mate = SIDE - 1 - x
    opposite = around(x + 2)

    barrier = pltpu.get_barrier_semaphore()
    ys, zs = [around(y + k) for k in range(SIDE)], [around(z + k) for k in range(SIDE)]
    rings = [yi * 2 + ci for yi in (ys[2], ys[1], ys[3], ys[0]) for ci in (1 - core, core)]
    col_peers = [(r, di) for di in (partner * SIDE + z, d) for r in rings][:-1]
    row_peers = [(n, xi * SIDE + zi) for xi in (mate, x) for zi in (zs[2], zs[1], zs[3], zs[0])][:-1]
    greeted = [sibling]
    for ci in (0, 1):
        greeted += [device(partner, y, z, ci), device(mate, y, z, ci), device(x, y, zs[1], ci), device(x, y, zs[3], ci)]
    greeted += [device(x, ys[1], z, core), device(x, ys[3], z, core)]
    for to in greeted:
        pl.semaphore_signal(barrier, inc=1, device_id=to, device_id_type=MESH)
    pl.semaphore_wait(barrier, len(greeted))

    def remote(src, dst, send, recv, to):
        return pltpu.make_async_remote_copy(
            src_ref=src, dst_ref=dst, send_sem=send, recv_sem=recv, device_id=to, device_id_type=MESH
        )

    def begin(copy):
        copy.start()
        started.append(copy)

    def lane(c):
        return slice(LANES * c, LANES * (c + 1))

    HOP = (1, -1)

    def noise_slot(xi, zi, at):
        return noise_all.at[xi, at, pl.ds(pl.multiple_of(zi * LANES, LANES), LANES)]

    own = noise_slot(x, z, pl.ds(0, rows))

    def cross_copy(i, half, to):
        return remote(
            noise_ref.at[pl.ds(half * rows, rows)], own, cross_send.at[i], cross_recv.at[x], to
        )

    def cross_wait(xi):
        remote(
            noise_ref.at[pl.ds(0, rows)], noise_slot(xi, z, pl.ds(0, rows)), cross_send.at[0], cross_recv.at[xi], sibling
        ).wait_recv()

    there = jnp.where(home, mate, partner)
    aside = cross_copy(2, 1 - core, sibling)

    def noise_copy(xi, t, forward, zi):
        at = pl.ds(t * (rows // 2), rows // 2) if forward else pl.ds(0, rows)
        f = int(forward)
        slot = noise_slot(xi, zi, at)
        return remote(
            slot, slot, noise_send.at[xi, t, f], noise_recv.at[xi, t, f], device(x, y, around(z + HOP[t]), core)
        )

    def noise_wait(xi, t, forward):
        zi = around(z - HOP[t] * (2 if forward else 1))
        noise_copy(xi, t, forward, zi).wait_recv()
        return zi

    def data_slot(block, where, at):
        width_at = pl.ds(pl.multiple_of(lax.rem(where, 2) * 256, 256), 256)
        return data_all.at[block, where // 2, at, width_at]

    def data_copy(r, index, where, lo, size, to, own=False):
        at = pl.ds(lo, size)
        block = side if r == 0 else 1 - side
        dst = data_slot(block, where, at)
        return remote(data_ref.at[at] if own else dst, dst, data_send.at[r, index], data_recv.at[r, index], to)

    half_cols = cols // 4
    full_cols = cols // 2

    def along_y(step, c):
        return around(y + step) * 2 + c

    def data_wait(r, index, where, lo, size):
        data_copy(r, index, where, lo, size, sibling).wait_recv()

    HALF = 9

    def cross_data(h, own=False):
        at = pl.ds(h * half_cols, half_cols)
        dst = data_slot(side if own else 1 - side, n, at)
        return remote(
            data_ref.at[at], dst, data_send.at[1, 11 + h], data_recv.at[1, 11 + h], device(partner, y, z, core)
        )

    def partner_y(t, h, back=0):
        where = around(y + back) * 2 + core
        to = device(x, around(y + HOP[t]), z, core)
        return t if h == 0 else HALF + t, where, h * half_cols, half_cols, to

    def partner_wait(t, h):
        data_copy(1, *partner_y(t, h, -HOP[t])).wait_recv()

    def own_round(t, a):
        return remote(
            noise_ref.at[pl.ds(a * rows, rows)], own,
            own_send.at[t, a], noise_recv.at[x, t, 0], device(x, y, around(z + HOP[t]), a),
        )

    def own_half():
        return pltpu.make_async_copy(
            noise_ref.at[pl.ds(pl.multiple_of(core * rows, rows), rows)], own, local_sems.at[0]
        )

    @pl.when(home)
    def _():
        for t in (0, 1):
            for a in (0, 1):
                own_round(t, a).start()
        aside.start()

    begin(cross_copy(0, 0, device(there, y, z, 0)))
    begin(cross_copy(1, 1, device(there, y, z, 1)))
    for t in (0, 1):
        begin(data_copy(0, t, n, 0, full_cols, device(x, around(y + HOP[t]), z, core), own=True))
    @pl.when(home)
    def _():
        own_half().start()

    data_own = pltpu.make_async_copy(data_ref, data_slot(side, n, pl.ds(0, full_cols)), local_sems.at[1])
    data_own.start()
    scores[...] = jnp.zeros_like(scores)
    part[...] = jnp.zeros_like(part)
    data_part[...] = jnp.zeros_like(data_part)

    def round_z(xi):
        for t in (0, 1):
            begin(noise_copy(xi, t, False, z))

    def forward_z(xi):
        for t in (0, 1):
            begin(noise_copy(xi, t, True, noise_wait(xi, t, False)))

    def far_noise(xi, t):
        slot = noise_slot(xi, around(z + 2), pl.ds(t * (rows // 2), rows // 2))
        return remote(slot, slot, far_send.at[xi, t], noise_recv.at[xi, t, 1], device(mate, y, z, core))

    def share_far(xi):
        for t in (0, 1):
            noise_wait(xi, t, True)
            begin(far_noise(xi, t))

    def far_wait(xi):
        for t in (0, 1):
            far_noise(xi, t).wait_recv()

    def far_data(t, block):
        where = along_y(2, core)
        at = pl.ds(t * half_cols, half_cols)
        dst = data_slot(block, where, at)
        return remote(dst, dst, data_send.at[1, 2 + t], data_recv.at[1, 2 + t], device(partner, y, z, core))

    cross_wait(partner)
    slot = noise_slot(partner, z, pl.ds(0, rows))
    begin(remote(slot, slot, cross_send.at[3], cross_recv.at[partner], device(mate, y, z, core)))
    round_z(partner)
    for h in (0, 1):
        begin(cross_data(h, own=True))
    begin(data_copy(0, 4, n, 0, full_cols, sibling, own=True))
    forward_z(x)
    cross_wait(mate)
    round_z(mate)
    for t in (0, 1):
        where = along_y(-HOP[t], core)
        data_wait(0, t, where, 0, full_cols)
        begin(data_copy(0, 2 + t, where, t * half_cols, half_cols, device(x, around(y + HOP[t]), z, core)))
        begin(data_copy(0, 5 + t, where, 0, full_cols, sibling))
    cross_data(0).wait_recv()
    for t in (0, 1):
        begin(data_copy(1, *partner_y(t, 0)))
    forward_z(partner)
    cross_wait(opposite)
    round_z(opposite)
    share_far(x)
    cross_data(1).wait_recv()
    for t in (0, 1):
        begin(data_copy(1, *partner_y(t, 1)))
    begin(data_copy(1, 4, n, 0, full_cols, sibling))
    for t in (0, 1):
        where = along_y(2, core)
        data_wait(0, 2 + t, where, t * half_cols, half_cols)
        begin(far_data(t, side))
        begin(data_copy(0, 7 + t, where, t * half_cols, half_cols, sibling))

    def squares(block):
        value = block.astype(jnp.float32)
        return value * value

    def chunk_product(xi, m):
        cut = pl.ds(pl.multiple_of(m * 256, 256), 256)
        here = pl.ds(pl.multiple_of(lax.rem(m, 4) * 256, 256), 256)
        total = data_part[cut, :]
        for i in range(SIDE):
            total = total + squares(data_all[m // 4, xi, here, lane(i)])
        data_part[cut, :] = total
        return lax.dot_general(
            noise_all[xi], data_all[m // 4, xi, here, :], (((1,), (1,)), ((), ())),
            preferred_element_type=jnp.float32,
        )

    def norms(xi):
        def norm(r, carry):
            cut = pl.ds(pl.multiple_of(r * 64, 64), 64)
            total = part[cut, :]
            for i in range(SIDE):
                total = total + squares(noise_all[xi, cut, lane(i)])
            part[cut, :] = total
            return carry

        lax.fori_loop(0, rows // 64, norm, 0)

    near, other_block = side * 4, 4 - side * 4

    def unit(block, xs, fresh, count=4):
        def column(i, carry):
            m = block + i
            cut = pl.ds(pl.multiple_of(m * 256, 256), 256)
            value = None if fresh else scores[:, cut]
            for xi in xs:
                value = chunk_product(xi, m) if value is None else value + chunk_product(xi, m)
            scores[:, cut] = value
            return carry

        lax.fori_loop(0, count, column, 0)

    def add_unit(block, count, xi):
        unit(block, (xi,), False, count)

    data_own.wait()
    data_wait(0, 4, along_y(0, 1 - core), 0, full_cols)
    for t in (0, 1):
        data_wait(0, 5 + t, along_y(-HOP[t], 1 - core), 0, full_cols)
    for t in (0, 1):
        data_wait(0, 7 + t, along_y(2, 1 - core), t * half_cols, half_cols)

    @pl.when(home)
    def _():
        own_half().wait()

    @pl.when(jnp.logical_not(home))
    def _():
        cross_wait(x)

    unit(near, (x,), True)
    share_far(partner)
    norms(x)
    for t in (0, 1):
        noise_wait(mate, t, False)
    far_wait(mate)
    unit(near, (mate,), False)
    norms(mate)

    def beside(t, h, c):
        return data_copy(1, (5 if h == 0 else 13) + t, along_y(-HOP[t], c), h * half_cols, half_cols, sibling)

    for t in (0, 1):
        partner_wait(t, 0)
        begin(beside(t, 0, core))
    unit(near, (partner,), False)
    norms(partner)
    data_wait(1, 4, along_y(0, 1 - core), 0, full_cols)
    for t in (0, 1):
        beside(t, 0, 1 - core).wait_recv()

    def ahead(i, carry):
        xi = around(y + i + i // 2)
        add_unit(other_block, jnp.where(xi == opposite, 0, jnp.where(i == 0, 4, 2)), xi)
        return carry

    lax.fori_loop(0, 3, ahead, 0)
    for t in (0, 1):
        partner_wait(t, 1)
        begin(beside(t, 1, core))
    for t in (0, 1):
        noise_wait(opposite, t, False)
    far_wait(opposite)
    for t in (0, 1):
        far_data(t, 1 - side).wait_recv()
        begin(data_copy(1, 7 + t, along_y(2, core), t * half_cols, half_cols, sibling))
    norms(opposite)

    factor = 2.0 * kappa / width

    def row_shift(r, carry):
        at = pl.ds(pl.multiple_of(r * 128, 128), 128)
        total = jnp.sum(part[at, :], axis=1, keepdims=True) * (-kappa / width)
        shift[at, :] = jnp.broadcast_to(total, (128, LANES))
        return carry

    lax.fori_loop(0, rows // 128, row_shift, 0)

    def final(block, xi):
        def column(i, carry):
            m = block + i
            cut = pl.ds(pl.multiple_of(m * 256, 256), 256)
            value = (scores[:, cut] + chunk_product(xi, m)) * factor
            scores[:, cut] = value
            for e in (0, 1):
                top = jnp.max(value[:, LANES * e:LANES * (e + 1)] + shift[...], axis=0, keepdims=True)
                colvec[:, pl.ds(pl.multiple_of(m * 256 + e * LANES, LANES), LANES)] = jnp.broadcast_to(top, (8, LANES))
            return carry

        lax.fori_loop(0, 4, column, 0)

    final(near, opposite)
    add_unit(other_block, jnp.where(opposite == y, 4, jnp.where(opposite == around(y + 2), 0, 2)), opposite)
    for t in (0, 1):
        beside(t, 1, 1 - core).wait_recv()
    unit(other_block + 2, (around(y + 1), around(y - 1)), False, 2)
    for t in (0, 1):
        data_wait(1, 7 + t, along_y(2, 1 - core), t * half_cols, half_cols)
    final(other_block, around(y + 2))

    def fold(block, op):
        out = block[0:8]
        for r in range(1, TILE // 8):
            out = op(out, block[8 * r:8 * r + 8])
        return out

    def spread_cols():
        for c in range(chunks):
            colvec[:, lane(c)] = jnp.broadcast_to(colpack[pl.ds(c, 1), :], (8, LANES))

    def tall(ref, c):
        return jnp.concatenate([ref[:, lane(c)]] * (TILE // 8), axis=0)

    def tile_at(t):
        return pl.ds(pl.multiple_of(t * TILE, TILE), TILE)

    def loop(body, init):
        return lax.fori_loop(0, tiles, body, init, unroll=2)

    zeros = tuple(jnp.zeros((8, LANES), jnp.float32) for _ in range(chunks))

    def exp_step(t, accs):
        at = tile_at(t)
        add = shift[at, :]
        return tuple(
            accs[c] + fold(jnp.exp2(scores[at, lane(c)] + add - tall(colvec, c)), jnp.add)
            for c in range(chunks)
        )

    sums = loop(exp_step, zeros)
    for c in range(chunks):
        total = jnp.sum(sums[c], axis=0, keepdims=True)
        col_buf[0, me_col, pl.ds(c, 1), :] = colvec[0:1, lane(c)] + jnp.log(total) * LOG2E
    exchange(col_buf, col_send, col_recv, 0, me_col, col_peers, started)
    col_pot = -log_cols - combine(col_buf, 0, csize)
    colpack[...] = col_pot
    spread_cols()

    def block_at(b):
        return pl.ds(pl.multiple_of(b * LANES, LANES), LANES)

    def tiles_of(b):
        return [pl.ds(pl.multiple_of(b * LANES + q * TILE, TILE), TILE) for q in range(LANES // TILE)]

    def behind(body, compact):
        def step(b, carry):
            compact(jnp.maximum(b - 1, 0))
            for at in tiles_of(b):
                body(at)
            return carry

        lax.fori_loop(0, row_blocks, step, 0)
        compact(row_blocks - 1)

    def row_step(at):
        top = scores[at, lane(0)] + tall(colvec, 0)
        for c in range(1, chunks):
            top = jnp.maximum(top, scores[at, lane(c)] + tall(colvec, c))
        first[at, :] = top
        total = None
        for c in range(chunks):
            value = jnp.exp2(scores[at, lane(c)] + tall(colvec, c) - top)
            scores[at, lane(c)] = value
            total = value if total is None else total + value
        part[at, :] = total

    def compact_lse(b):
        tops = first[block_at(b), :].T
        top = jnp.max(tops, axis=0, keepdims=True)
        total = jnp.sum(part[block_at(b), :].T * jnp.exp2(tops - top), axis=0, keepdims=True)
        row_buf[0, me_row, pl.ds(b, 1), :] = top + jnp.log(total) * LOG2E

    first[pl.ds(0, LANES), :] = jnp.zeros((LANES, LANES), jnp.float32)
    behind(row_step, compact_lse)
    exchange(row_buf, row_send, row_recv, 0, me_row, row_peers, started)
    row_lse = combine(row_buf, 0, rsize)
    rowpack[...] = row_lse

    def spread_first(b):
        base = jnp.exp2(first[block_at(b), :] - spread_lanes(rowpack, b))
        factor_of[block_at(b), :] = base
        scale[block_at(b), :] = base

    def spread(b):
        scale[block_at(b), :] = factor_of[block_at(b), :] * spread_lanes(rowpack, b)

    def col_pass(ahead):
        def step(b, accs):
            accs = list(accs)
            for at in tiles_of(b):
                mul = scale[at, :]
                for c in range(chunks):
                    accs[c] = accs[c] + fold(scores[at, lane(c)] * mul, jnp.add)
            ahead(jnp.minimum(b + 1, row_blocks - 1))
            return tuple(accs)

        ahead(0)
        return lax.fori_loop(0, row_blocks, step, zeros)

    def sum_step(keep_values):
        def body(at):
            total = None
            for c in range(chunks):
                value = scores[at, lane(c)] * tall(colvec, c)
                if keep_values:
                    scores[at, lane(c)] = value
                total = value if total is None else total + value
            part[at, :] = total * factor_of[at, :]

        return body

    for step in range(1, ITERS):
        sums = col_pass(spread_first if step == 1 else spread)
        for c in range(chunks):
            col_buf[step, me_col, pl.ds(c, 1), :] = jnp.sum(sums[c], axis=0, keepdims=True)
        exchange(col_buf, col_send, col_recv, step, me_col, col_peers, started)
        ratio = 1.0 / add_slots(col_buf, step, csize)
        colpack[...] = ratio
        spread_cols()

        def compact(b, step=step):
            row_buf[step, me_row, pl.ds(b, 1), :] = jnp.sum(part[block_at(b), :].T, axis=0, keepdims=True)

        behind(sum_step(step == ITERS - 1), compact)
        exchange(row_buf, row_send, row_recv, step, me_row, row_peers, started)
        total = add_slots(row_buf, step, rsize)
        rowpack[...] = 1.0 / total
    spread(0)

    def weigh(r):
        blocks = row_blocks // 2

        def body(i, carry):
            b = r * blocks + i
            for at in tiles_of(b):
                mul = scale[at, :]
                for c in range(chunks):
                    weights[at, lane(c)] = (scores[at, lane(c)] * mul).astype(jnp.bfloat16)
            spread(jnp.minimum(b + 1, row_blocks - 1))
            return carry

        lax.fori_loop(0, blocks, body, 0)

    def swap_copy(i, to):
        return remote(swap.at[0], swap.at[i], swap_send.at[i], swap_recv.at[i], to)

    def potentials():
        for c in range(chunks):
            sqy[pl.ds(c, 1), :] = jnp.sum(data_part[pl.ds(c * LANES, LANES), :].T, axis=0, keepdims=True)
        cols_pot = (col_pot + jnp.log(ratio) * LOG2E + (log_rows - log_cols)) / kappa + sqy[...] / width
        colpack[...] = cols_pot
        cols_out[...] = colpack[pl.ds(pl.multiple_of(side * 8, 8), 8), :]
        for b in range(row_blocks):
            sqx[pl.ds(b, 1), :] = shift[pl.ds(b * LANES, LANES), :].T[0:1]
        swap[0] = -(log_rows + row_lse + jnp.log(total) * LOG2E + sqx[...]) / kappa
        begin(swap_copy(1, sibling))
        for i in (0, 1):
            begin(remote(
                swap.at[0], swap.at[2 + core], swap_send.at[2 + i], swap_recv.at[2 + core], device(partner, y, z, i)
            ))

    strip = rows // 2

    def half_rows(r):
        return pl.ds(pl.multiple_of(r * strip, strip), strip)

    def block_x(b):
        return jnp.where(b < 2, jnp.where(b == 0, opposite, mate), jnp.where(b == 2, partner, x))

    def product(p, r, to_z):
        cut = pl.ds(pl.multiple_of(to_z * LANES, LANES), LANES)
        total = None
        for k in (0, 1):
            block = jnp.concatenate(
                [data_all[k, block_x(2 * p + e), :, cut] for e in (0, 1)], axis=1
            )
            value = jnp.dot(
                weights[half_rows(r), k * full_cols:(k + 1) * full_cols], block,
                preferred_element_type=jnp.float32,
            )
            total = value if total is None else total + value
        return total

    def hop(t):
        return 1 - 2 * t

    def sum_copy(b, t, index, src, dst):
        to = device(x, y, around(z + hop(t)), core)
        return remote(src, dst, sum_send.at[b, t, index], sum_recv.at[b, t, index], to)

    def far_copy(b, t):
        return sum_copy(b, t, 0, out_buf.at[b, 2, half_rows(t)], far_buf.at[b - 2, t])

    def direct_copy(b, t):
        at = half_rows(1 - t)
        return sum_copy(b, t, 1, out_buf.at[b, t, at], near_buf.at[b, t, at])

    def added_copy(b, t):
        at = half_rows(t)
        return sum_copy(b, t, 2, out_buf.at[b, t, at], near_buf.at[b, t, at])

    def give_copy(b, r):
        at = half_rows(r)
        return remote(
            out_buf.at[b, 2, at], given.at[b, at], give_send.at[b, r], give_recv.at[b, r], device(mate, y, z, core)
        )

    def relay_copy(r):
        at = half_rows(r)
        return remote(own_buf.at[0, at], relay_in.at[at], in_send.at[r], in_recv.at[4 + r], device(mate, y, z, core))

    def partner_copy(a, r):
        at = half_rows(r)
        return remote(
            own_buf.at[2, at], in_sum.at[a, at], in_send.at[2 + r], part_recv.at[a, r], device(partner, y, z, kind)
        )

    def mate_copy(a):
        return remote(mate_out, mate_in.at[a], in_send.at[4], in_recv.at[2 + a], device(mate, y, z, kind))

    def stay_copy(a):
        return remote(own_buf.at[3], in_sum.at[a], in_send.at[5], in_recv.at[a], sibling)

    def add_far(b):
        for t in (0, 1):
            far_copy(b, t).wait_recv()
            out_buf[b, t, half_rows(t), :] = (
                keep[b - 2, t, half_rows(t), :] + far_buf[b - 2, t].astype(jnp.float32)
            ).astype(jnp.bfloat16)
            added_copy(b, t).start()

    def add_near(b):
        for t in (0, 1):
            direct_copy(b, t).wait_recv()
            added_copy(b, t).wait_recv()
        own_buf[b] = own_buf[b] + near_buf[b, 0].astype(jnp.float32) + near_buf[b, 1].astype(jnp.float32)

    def add_given(b):
        for r in (0, 1):
            at = half_rows(r)
            give_copy(b - 2, r).wait_recv()
            out_buf[b, 2, at, :] = (far_keep[b - 2, at, :] + given[b - 2, at, :].astype(jnp.float32)).astype(jnp.bfloat16)
            far_copy(b, r).start()

    def halves(body):
        def step(r, carry):
            body(r)
            return carry

        lax.fori_loop(0, 2, step, 0)

    def give(r):
        weigh(r)
        value = product(0, r, around(z + 2))
        for e in (0, 1):
            out_buf[e, 2, half_rows(r), :] = value[:, lane(e)].astype(jnp.bfloat16)
        give_copy(0, r).start()

    def near_products(p):
        def along(t):
            def part_of(r):
                value = product(p, r, around(z + hop(t)))
                for e in (0, 1):
                    block = value[:, lane(e)]
                    out_buf[2 * p + e, t, half_rows(r), :] = block.astype(jnp.bfloat16)
                    if p == 1:
                        keep[e, t, half_rows(r), :] = block

            halves(part_of)
            direct_copy(2 * p, t).start()
            if p == 0:
                added_copy(0, t).start()

        halves(along)

    def far_products(r):
        value = product(1, r, around(z + 2))
        for e in (0, 1):
            far_keep[e, half_rows(r), :] = value[:, lane(e)]

    def own_products(p):
        def part_of(r):
            value = product(p, r, z)
            for e in (0, 1):
                own_buf[2 * p + e, half_rows(r), :] = value[:, lane(e)]

        halves(part_of)

    halves(give)
    for r in (0, 1):
        give_copy(1, r).start()
    near_products(1)
    near_products(0)
    halves(far_products)
    add_given(2)
    for t in (0, 1):
        direct_copy(1, t).start()
        added_copy(1, t).start()
    halves(own_products)
    add_near(0)
    for r in (0, 1):
        relay_copy(r).start()
    add_far(2)
    add_given(3)
    for t in (0, 1):
        direct_copy(3, t).start()
    add_near(1)
    mate_out[...] = own_buf[1].astype(jnp.bfloat16)
    mate_copy(core).start()
    potentials()
    add_near(2)

    def to_partner(r):
        relay_copy(r).wait_recv()
        own_buf[2, half_rows(r), :] = own_buf[2, half_rows(r), :] + relay_in[half_rows(r), :]
        partner_copy(core, r).start()

    to_partner(0)
    add_far(3)
    to_partner(1)

    swap_copy(1, sibling).wait_recv()
    for i in (0, 1):
        remote(swap.at[0], swap.at[2 + i], swap_send.at[2 + i], swap_recv.at[2 + i], sibling).wait_recv()
    half = rows // LANES
    for a in (0, 1):
        mine_row = jnp.where(core == a, swap[0], swap[1])
        rows_out[pl.ds(a * half, half), :] = jnp.where(home, mine_row, swap[2 + a])

    add_near(3)

    @pl.when(home)
    def _():
        in_sum[core] = own_buf[3]
        stay_copy(1 - core).wait_recv()
        for a in (0, 1):
            mate_copy(a).wait_recv()
            in_sum[a] = in_sum[a] + mate_in[a].astype(jnp.float32)

    @pl.when(jnp.logical_not(home))
    def _():
        stay_copy(core).start()
        for a in (0, 1):
            for r in (0, 1):
                partner_copy(a, r).wait_recv()

    def result_copy(a):
        return pltpu.make_async_copy(in_sum.at[a], targets.at[pl.ds(a * rows, rows)], local_sems.at[a])

    for a in (0, 1):
        result_copy(a).start()

    def settle(b, carry):
        for t in (0, 1):
            direct_copy(b, t).wait_send()
            added_copy(b, t).wait_send()

            @pl.when(b < 2)
            def _():
                give_copy(jnp.minimum(b, 1), t).wait_send()

            @pl.when(b >= 2)
            def _():
                far_copy(jnp.maximum(b, 2), t).wait_send()

        return carry

    lax.fori_loop(0, SIDE, settle, 0)
    for a in (0, 1):
        result_copy(a).wait()
    for r in (0, 1):
        relay_copy(r).wait_send()
        partner_copy(core, r).wait_send()
    mate_copy(core).wait_send()

    @pl.when(jnp.logical_not(home))
    def _():
        stay_copy(core).wait_send()

    for copy in started:
        copy.wait_send()

    @pl.when(home)
    def _():
        aside.wait_send()
        for t in (0, 1):
            for a in (0, 1):
                own_round(t, a).wait_send()


def hand_on(targets, rows_pot, cols_pot, targets_out, rows_out, cols_out, stage, row_stage, col_stage, sems):
    size = targets.shape[0] // PARTS
    legs = [
        (targets.at[pl.ds(i * size, size)], stage.at[i], targets_out.at[pl.ds(i * size, size)]) for i in range(PARTS)
    ]
    legs += [(rows_pot, row_stage, rows_out), (cols_pot, col_stage, cols_out)]
    first = [pltpu.make_async_copy(src, mid, sems.at[i, 0]) for i, (src, mid, _) in enumerate(legs)]
    second = [pltpu.make_async_copy(mid, dst, sems.at[i, 1]) for i, (_, mid, dst) in enumerate(legs)]
    for copy in first:
        copy.start()
    for before, copy in zip(first, second):
        before.wait()
        copy.start()
    for copy in second:
        copy.wait()


def shards(noise_latents, data_latents):
    nsize = lax.axis_size("noise")
    dsize = lax.axis_size("dp")
    block, piece = noise_latents.shape
    rows, cols = block // 2, 2 * data_latents.shape[0]
    rsize, csize = dsize // 2, nsize * 2
    vmem = pl.BlockSpec(memory_space=pltpu.VMEM)
    f32, bf16 = jnp.float32, jnp.bfloat16
    strip = rows // 2
    row_vec, col_vec = (rows // LANES, LANES), (cols // LANES, LANES)
    sems = pltpu.SemaphoreType.DMA
    targets, rows_pot, cols_pot = pl.pallas_call(
        functools.partial(kernel, rsize, csize, piece * dsize),
        out_shape=(
            jax.ShapeDtypeStruct((block, piece), f32),
            jax.ShapeDtypeStruct((block // LANES, LANES), f32),
            jax.ShapeDtypeStruct((cols // 2 // LANES, LANES), f32),
        ),
        in_specs=[pl.BlockSpec(memory_space=pl.ANY)] * 2,
        out_specs=(pl.BlockSpec(memory_space=pl.ANY), vmem, vmem),
        scratch_shapes=[
            pltpu.VMEM((SIDE, rows, SIDE * piece), bf16),
            pltpu.VMEM((2, SIDE, cols // 2, nsize // SIDE * data_latents.shape[1]), bf16),
            pltpu.VMEM((rows, cols), f32),
            pltpu.VMEM((rows, cols), bf16),
            pltpu.VMEM((rows, LANES), f32),
            pltpu.VMEM((rows, LANES), f32),
            pltpu.VMEM((rows, LANES), f32),
            pltpu.VMEM((rows, LANES), f32),
            pltpu.VMEM((rows, LANES), f32),
            pltpu.VMEM((cols, LANES), f32),
            pltpu.VMEM((8, cols), f32),
            pltpu.VMEM(row_vec, f32),
            pltpu.VMEM(col_vec, f32),
            pltpu.VMEM(row_vec, f32),
            pltpu.VMEM(col_vec, f32),
            pltpu.VMEM((4,) + row_vec, f32),
            pltpu.VMEM((ITERS, csize) + col_vec, f32),
            pltpu.VMEM((ITERS, rsize) + row_vec, f32),
            pltpu.VMEM((SIDE, 3, rows, LANES), bf16),
            pltpu.VMEM((SIDE, rows, LANES), f32),
            pltpu.VMEM((2, 2, strip, LANES), bf16),
            pltpu.VMEM((SIDE, 2, rows, LANES), bf16),
            pltpu.VMEM((2, rows, LANES), f32),
            sems((ITERS,)),
            sems((ITERS,)),
            sems((ITERS,)),
            sems((ITERS,)),
            sems((4,)),
            sems((4,)),
            sems((4,)),
            sems((4,)),
            sems((SIDE, 2, 2)),
            sems((SIDE, 2, 2)),
            sems((2, 15)),
            sems((2, 15)),
            sems((SIDE, 2, 3)),
            sems((SIDE, 2, 3)),
            sems((6,)),
            sems((6,)),
            pltpu.VMEM((2, 2, rows, LANES), f32),
            pltpu.VMEM((2, rows, LANES), f32),
            pltpu.VMEM((2, rows, LANES), bf16),
            sems((2, 2)),
            sems((2, 2)),
            sems((2, 2)),
            sems((2,)),
            sems((2, 2)),
            sems((SIDE, 2)),
            pltpu.VMEM((rows, LANES), f32),
            pltpu.VMEM((rows, LANES), bf16),
            pltpu.VMEM((2, rows, LANES), bf16),
        ],
        compiler_params=pltpu.CompilerParams(
            collective_id=0, has_side_effects=True, vmem_limit_bytes=60 * 2**20
        ),
    )(noise_latents, data_latents)
    results = (targets, rows_pot, cols_pot)
    targets, rows_pot, cols_pot = pl.pallas_call(
        hand_on,
        out_shape=tuple(jax.ShapeDtypeStruct(a.shape, a.dtype) for a in results),
        in_specs=[pl.BlockSpec(memory_space=pl.ANY)] * 3,
        out_specs=(pl.BlockSpec(memory_space=pl.ANY),) * 3,
        scratch_shapes=[
            pltpu.VMEM((PARTS, block // PARTS, piece), f32),
            pltpu.VMEM(rows_pot.shape, f32),
            pltpu.VMEM(cols_pot.shape, f32),
            sems((PARTS + 2, 2)),
        ],
        compiler_params=pltpu.CompilerParams(vmem_limit_bytes=60 * 2**20),
    )(*results)
    return targets, rows_pot.reshape(block), cols_pot.reshape(cols // 2)


def solution(mesh):
    return jax.shard_map(
        shards,
        mesh=mesh,
        in_specs=(P("noise", "dp"), P("dp", "noise")),
        out_specs=(P("noise", "dp"), P("noise"), P("dp")),
        check_vma=False,
    )
```

```python
import functools
import math

import jax
import jax.numpy as jnp
from jax import lax
from jax.experimental import pallas as pl
from jax.experimental.pallas import tpu as pltpu
from jax.sharding import PartitionSpec as P

ITERS = 3
EPSILON = 0.04
LOG2E = 1.0 / math.log(2.0)
MESH = pl.DeviceIdType.MESH
LANES = 128
TILE = 32
SIDE = 4
PARTS = 4


def spread_lanes(ref, row):
    return jnp.broadcast_to(ref[pl.ds(row, 1), :], (LANES, LANES)).T


def exchange(buf, send, recv, step, me, peers, started):
    for peer in peers:
        pltpu.make_async_remote_copy(
            src_ref=buf.at[step, me],
            dst_ref=buf.at[step, me],
            send_sem=send.at[step],
            recv_sem=recv.at[step],
            device_id=peer,
            device_id_type=MESH,
        ).start()
    slots = buf.at[step, pl.ds(0, len(peers))]
    every = pltpu.make_async_remote_copy(
        src_ref=slots,
        dst_ref=slots,
        send_sem=send.at[step],
        recv_sem=recv.at[step],
        device_id=peers[0],
        device_id_type=MESH,
    )
    every.wait_recv()
    started.append(every)


def combine(buf, step, size):
    top = buf[step, 0]
    for s in range(1, size):
        top = jnp.maximum(top, buf[step, s])
    total = jnp.exp2(buf[step, 0] - top)
    for s in range(1, size):
        total = total + jnp.exp2(buf[step, s] - top)
    return top + jnp.log(total) * LOG2E


def add_slots(buf, step, size):
    total = buf[step, 0]
    for s in range(1, size):
        total = total + buf[step, s]
    return total


def kernel(
    rsize, csize, width,
    noise_ref, data_ref,
    targets, rows_out, cols_out,
    noise_all, data_all, scores, weights,
    shift, first, scale, part, data_part, colvec, rowpack, colpack, sqx, sqy, swap,
    col_buf, row_buf, out_buf, own_buf, far_buf, near_buf, in_sum,
    col_send, col_recv, row_send, row_recv, swap_send, swap_recv,
    cross_send, cross_recv, noise_send, noise_recv, data_send, data_recv,
    sum_send, sum_recv, in_send, in_recv, keep, far_keep, given, give_send, give_recv, part_recv, local_sems, own_send, far_send, relay_in, mate_out, mate_in,
):
    rows, cols = scores.shape
    n = lax.axis_index("noise")
    d = lax.axis_index("dp")
    x, z = d // SIDE, lax.rem(d, SIDE)
    y, core = n // 2, lax.rem(n, 2)
    kind = lax.rem((x + 1) // 2, 2)
    pair = x // 2
    side = lax.rem(x, 2)
    home = core == kind
    kappa = LOG2E / EPSILON
    log_rows = math.log2(rows * csize)
    log_cols = math.log2(cols * rsize)
    chunks = cols // LANES
    row_blocks = rows // LANES
    tiles = rows // TILE
    started = []

    def around(value):
        return lax.rem(value + SIDE, SIDE)

    def device(xi, yi, zi, ci):
        return (yi * 2 + ci, xi * SIDE + zi)

    me_row = pair * SIDE + z
    me_col = y * 4 + kind * 2 + core

    sibling = device(x, y, z, 1 - core)
    partner = x + 1 - 2 * side
    mate = SIDE - 1 - x
    opposite = around(x + 2)

    barrier = pltpu.get_barrier_semaphore()
    ys, zs = [around(y + k) for k in range(SIDE)], [around(z + k) for k in range(SIDE)]
    rings = [yi * 2 + ci for yi in (ys[2], ys[1], ys[3], ys[0]) for ci in (1 - core, core)]
    col_peers = [(r, di) for di in (partner * SIDE + z, d) for r in rings][:-1]
    row_peers = [(n, xi * SIDE + zi) for xi in (mate, x) for zi in (zs[2], zs[1], zs[3], zs[0])][:-1]
    greeted = [sibling]
    for ci in (0, 1):
        greeted += [device(partner, y, z, ci), device(mate, y, z, ci), device(x, y, zs[1], ci), device(x, y, zs[3], ci)]
    greeted += [device(x, ys[1], z, core), device(x, ys[3], z, core)]
    for to in greeted:
        pl.semaphore_signal(barrier, inc=1, device_id=to, device_id_type=MESH)
    pl.semaphore_wait(barrier, len(greeted))

    def remote(src, dst, send, recv, to):
        return pltpu.make_async_remote_copy(
            src_ref=src, dst_ref=dst, send_sem=send, recv_sem=recv, device_id=to, device_id_type=MESH
        )

    def begin(copy):
        copy.start()
        started.append(copy)

    def lane(c):
        return slice(LANES * c, LANES * (c + 1))

    HOP = (1, -1)

    def noise_slot(xi, zi, at):
        return noise_all.at[xi, at, pl.ds(pl.multiple_of(zi * LANES, LANES), LANES)]

    own = noise_slot(x, z, pl.ds(0, rows))

    def cross_copy(i, half, to):
        return remote(
            noise_ref.at[pl.ds(half * rows, rows)], own, cross_send.at[i], cross_recv.at[x], to
        )

    def cross_wait(xi):
        remote(
            noise_ref.at[pl.ds(0, rows)], noise_slot(xi, z, pl.ds(0, rows)), cross_send.at[0], cross_recv.at[xi], sibling
        ).wait_recv()

    there = jnp.where(home, mate, partner)
    aside = cross_copy(2, 1 - core, sibling)

    def noise_copy(xi, t, forward, zi):
        at = pl.ds(t * (rows // 2), rows // 2) if forward else pl.ds(0, rows)
        f = int(forward)
        slot = noise_slot(xi, zi, at)
        return remote(
            slot, slot, noise_send.at[xi, t, f], noise_recv.at[xi, t, f], device(x, y, around(z + HOP[t]), core)
        )

    def noise_wait(xi, t, forward):
        zi = around(z - HOP[t] * (2 if forward else 1))
        noise_copy(xi, t, forward, zi).wait_recv()
        return zi

    def data_slot(block, where, at):
        width_at = pl.ds(pl.multiple_of(lax.rem(where, 2) * 256, 256), 256)
        return data_all.at[block, where // 2, at, width_at]

    def data_copy(r, index, where, lo, size, to, own=False):
        at = pl.ds(lo, size)
        block = side if r == 0 else 1 - side
        dst = data_slot(block, where, at)
        return remote(data_ref.at[at] if own else dst, dst, data_send.at[r, index], data_recv.at[r, index], to)

    half_cols = cols // 4
    full_cols = cols // 2

    def along_y(step, c):
        return around(y + step) * 2 + c

    def data_wait(r, index, where, lo, size):
        data_copy(r, index, where, lo, size, sibling).wait_recv()

    HALF = 9

    def cross_data(h, own=False):
        at = pl.ds(h * half_cols, half_cols)
        dst = data_slot(side if own else 1 - side, n, at)
        return remote(
            data_ref.at[at], dst, data_send.at[1, 11 + h], data_recv.at[1, 11 + h], device(partner, y, z, core)
        )

    def partner_y(t, h, back=0):
        where = around(y + back) * 2 + core
        to = device(x, around(y + HOP[t]), z, core)
        return t if h == 0 else HALF + t, where, h * half_cols, half_cols, to

    def partner_wait(t, h):
        data_copy(1, *partner_y(t, h, -HOP[t])).wait_recv()

    def own_round(t, a):
        return remote(
            noise_ref.at[pl.ds(a * rows, rows)], own,
            own_send.at[t, a], noise_recv.at[x, t, 0], device(x, y, around(z + HOP[t]), a),
        )

    def own_half():
        return pltpu.make_async_copy(
            noise_ref.at[pl.ds(pl.multiple_of(core * rows, rows), rows)], own, local_sems.at[0]
        )

    @pl.when(home)
    def _():
        for t in (0, 1):
            for a in (0, 1):
                own_round(t, a).start()
        aside.start()

    begin(cross_copy(0, 0, device(there, y, z, 0)))
    begin(cross_copy(1, 1, device(there, y, z, 1)))
    for t in (0, 1):
        begin(data_copy(0, t, n, 0, full_cols, device(x, around(y + HOP[t]), z, core), own=True))
    @pl.when(home)
    def _():
        own_half().start()

    data_own = pltpu.make_async_copy(data_ref, data_slot(side, n, pl.ds(0, full_cols)), local_sems.at[1])
    data_own.start()
    scores[...] = jnp.zeros_like(scores)
    part[...] = jnp.zeros_like(part)
    data_part[...] = jnp.zeros_like(data_part)

    def round_z(xi):
        for t in (0, 1):
            begin(noise_copy(xi, t, False, z))

    def forward_z(xi):
        for t in (0, 1):
            begin(noise_copy(xi, t, True, noise_wait(xi, t, False)))

    def far_noise(xi, t):
        slot = noise_slot(xi, around(z + 2), pl.ds(t * (rows // 2), rows // 2))
        return remote(slot, slot, far_send.at[xi, t], noise_recv.at[xi, t, 1], device(mate, y, z, core))

    def share_far(xi):
        for t in (0, 1):
            noise_wait(xi, t, True)
            begin(far_noise(xi, t))

    def far_wait(xi):
        for t in (0, 1):
            far_noise(xi, t).wait_recv()

    def far_data(t, block):
        where = along_y(2, core)
        at = pl.ds(t * half_cols, half_cols)
        dst = data_slot(block, where, at)
        return remote(dst, dst, data_send.at[1, 2 + t], data_recv.at[1, 2 + t], device(partner, y, z, core))

    cross_wait(partner)
    slot = noise_slot(partner, z, pl.ds(0, rows))
    begin(remote(slot, slot, cross_send.at[3], cross_recv.at[partner], device(mate, y, z, core)))
    round_z(partner)
    for h in (0, 1):
        begin(cross_data(h, own=True))
    begin(data_copy(0, 4, n, 0, full_cols, sibling, own=True))
    forward_z(x)
    cross_wait(mate)
    round_z(mate)
    for t in (0, 1):
        where = along_y(-HOP[t], core)
        data_wait(0, t, where, 0, full_cols)
        begin(data_copy(0, 2 + t, where, t * half_cols, half_cols, device(x, around(y + HOP[t]), z, core)))
        begin(data_copy(0, 5 + t, where, 0, full_cols, sibling))
    cross_data(0).wait_recv()
    for t in (0, 1):
        begin(data_copy(1, *partner_y(t, 0)))
    forward_z(partner)
    cross_wait(opposite)
    round_z(opposite)
    share_far(x)
    cross_data(1).wait_recv()
    for t in (0, 1):
        begin(data_copy(1, *partner_y(t, 1)))
    begin(data_copy(1, 4, n, 0, full_cols, sibling))
    for t in (0, 1):
        where = along_y(2, core)
        data_wait(0, 2 + t, where, t * half_cols, half_cols)
        begin(far_data(t, side))
        begin(data_copy(0, 7 + t, where, t * half_cols, half_cols, sibling))

    def squares(block):
        value = block.astype(jnp.float32)
        return value * value

    def chunk_product(xi, m):
        cut = pl.ds(pl.multiple_of(m * 256, 256), 256)
        here = pl.ds(pl.multiple_of(lax.rem(m, 4) * 256, 256), 256)
        total = data_part[cut, :]
        for i in range(SIDE):
            total = total + squares(data_all[m // 4, xi, here, lane(i)])
        data_part[cut, :] = total
        return lax.dot_general(
            noise_all[xi], data_all[m // 4, xi, here, :], (((1,), (1,)), ((), ())),
            preferred_element_type=jnp.float32,
        )

    def norms(xi):
        def norm(r, carry):
            cut = pl.ds(pl.multiple_of(r * 64, 64), 64)
            total = part[cut, :]
            for i in range(SIDE):
                total = total + squares(noise_all[xi, cut, lane(i)])
            part[cut, :] = total
            return carry

        lax.fori_loop(0, rows // 64, norm, 0)

    near, other_block = side * 4, 4 - side * 4

    def unit(block, xs, fresh, count=4):
        def column(i, carry):
            m = block + i
            cut = pl.ds(pl.multiple_of(m * 256, 256), 256)
            value = None if fresh else scores[:, cut]
            for xi in xs:
                value = chunk_product(xi, m) if value is None else value + chunk_product(xi, m)
            scores[:, cut] = value
            return carry

        lax.fori_loop(0, count, column, 0)

    def add_unit(block, count, xi):
        unit(block, (xi,), False, count)

    data_own.wait()
    data_wait(0, 4, along_y(0, 1 - core), 0, full_cols)
    for t in (0, 1):
        data_wait(0, 5 + t, along_y(-HOP[t], 1 - core), 0, full_cols)
    for t in (0, 1):
        data_wait(0, 7 + t, along_y(2, 1 - core), t * half_cols, half_cols)

    @pl.when(home)
    def _():
        own_half().wait()

    @pl.when(jnp.logical_not(home))
    def _():
        cross_wait(x)

    unit(near, (x,), True)
    share_far(partner)
    norms(x)
    for t in (0, 1):
        noise_wait(mate, t, False)
    far_wait(mate)
    unit(near, (mate,), False)
    norms(mate)

    def beside(t, h, c):
        return data_copy(1, (5 if h == 0 else 13) + t, along_y(-HOP[t], c), h * half_cols, half_cols, sibling)

    for t in (0, 1):
        partner_wait(t, 0)
        begin(beside(t, 0, core))
    unit(near, (partner,), False)
    norms(partner)
    data_wait(1, 4, along_y(0, 1 - core), 0, full_cols)
    for t in (0, 1):
        beside(t, 0, 1 - core).wait_recv()

    def ahead(i, carry):
        xi = around(y + i + i // 2)
        add_unit(other_block, jnp.where(xi == opposite, 0, jnp.where(i == 0, 4, 2)), xi)
        return carry

    lax.fori_loop(0, 3, ahead, 0)
    for t in (0, 1):
        partner_wait(t, 1)
        begin(beside(t, 1, core))
    for t in (0, 1):
        noise_wait(opposite, t, False)
    far_wait(opposite)
    for t in (0, 1):
        far_data(t, 1 - side).wait_recv()
        begin(data_copy(1, 7 + t, along_y(2, core), t * half_cols, half_cols, sibling))
    norms(opposite)

    factor = 2.0 * kappa / width

    def row_shift(r, carry):
        at = pl.ds(pl.multiple_of(r * 128, 128), 128)
        total = jnp.sum(part[at, :], axis=1, keepdims=True) * (-kappa / width)
        shift[at, :] = jnp.broadcast_to(total, (128, LANES))
        return carry

    lax.fori_loop(0, rows // 128, row_shift, 0)

    def final(block, xi):
        def column(i, carry):
            m = block + i
            cut = pl.ds(pl.multiple_of(m * 256, 256), 256)
            value = (scores[:, cut] + chunk_product(xi, m)) * factor
            scores[:, cut] = value
            for e in (0, 1):
                top = jnp.max(value[:, LANES * e:LANES * (e + 1)] + shift[...], axis=0, keepdims=True)
                colvec[:, pl.ds(pl.multiple_of(m * 256 + e * LANES, LANES), LANES)] = jnp.broadcast_to(top, (8, LANES))
            return carry

        lax.fori_loop(0, 4, column, 0)

    final(near, opposite)
    add_unit(other_block, jnp.where(opposite == y, 4, jnp.where(opposite == around(y + 2), 0, 2)), opposite)
    for t in (0, 1):
        beside(t, 1, 1 - core).wait_recv()
    unit(other_block + 2, (around(y + 1), around(y - 1)), False, 2)
    for t in (0, 1):
        data_wait(1, 7 + t, along_y(2, 1 - core), t * half_cols, half_cols)
    final(other_block, around(y + 2))

    def fold(block, op):
        out = block[0:8]
        for r in range(1, TILE // 8):
            out = op(out, block[8 * r:8 * r + 8])
        return out

    def spread_cols():
        for c in range(chunks):
            colvec[:, lane(c)] = jnp.broadcast_to(colpack[pl.ds(c, 1), :], (8, LANES))

    def tall(ref, c):
        return jnp.concatenate([ref[:, lane(c)]] * (TILE // 8), axis=0)

    def tile_at(t):
        return pl.ds(pl.multiple_of(t * TILE, TILE), TILE)

    def loop(body, init):
        return lax.fori_loop(0, tiles, body, init, unroll=2)

    zeros = tuple(jnp.zeros((8, LANES), jnp.float32) for _ in range(chunks))

    def exp_step(t, accs):
        at = tile_at(t)
        add = shift[at, :]
        return tuple(
            accs[c] + fold(jnp.exp2(scores[at, lane(c)] + add - tall(colvec, c)), jnp.add)
            for c in range(chunks)
        )

    sums = loop(exp_step, zeros)
    for c in range(chunks):
        total = jnp.sum(sums[c], axis=0, keepdims=True)
        col_buf[0, me_col, pl.ds(c, 1), :] = colvec[0:1, lane(c)] + jnp.log(total) * LOG2E
    exchange(col_buf, col_send, col_recv, 0, me_col, col_peers, started)
    col_pot = -log_cols - combine(col_buf, 0, csize)
    colpack[...] = col_pot
    spread_cols()

    def row_step(t, carry):
        at = tile_at(t)
        top = scores[at, lane(0)] + tall(colvec, 0)
        for c in range(1, chunks):
            top = jnp.maximum(top, scores[at, lane(c)] + tall(colvec, c))
        first[at, :] = top
        total = None
        for c in range(chunks):
            value = jnp.exp2(scores[at, lane(c)] + tall(colvec, c) - top)
            scores[at, lane(c)] = value
            total = value if total is None else total + value
        part[at, :] = total
        return carry

    loop(row_step, 0)
    for b in range(row_blocks):
        at = pl.ds(b * LANES, LANES)
        tops = first[at, :].T
        top = jnp.max(tops, axis=0, keepdims=True)
        total = jnp.sum(part[at, :].T * jnp.exp2(tops - top), axis=0, keepdims=True)
        row_buf[0, me_row, pl.ds(b, 1), :] = top + jnp.log(total) * LOG2E
    exchange(row_buf, row_send, row_recv, 0, me_row, row_peers, started)
    row_lse = combine(row_buf, 0, rsize)
    rowpack[...] = row_lse
    for b in range(row_blocks):
        at = pl.ds(b * LANES, LANES)
        base = jnp.exp2(first[at, :] - spread_lanes(rowpack, b))
        first[at, :] = base
        scale[at, :] = base

    def col_step(t, accs):
        at = tile_at(t)
        mul = scale[at, :]
        return tuple(accs[c] + fold(scores[at, lane(c)] * mul, jnp.add) for c in range(chunks))

    def sum_step(keep_values):
        def body(t, carry):
            at = tile_at(t)
            total = None
            for c in range(chunks):
                value = scores[at, lane(c)] * tall(colvec, c)
                if keep_values:
                    scores[at, lane(c)] = value
                total = value if total is None else total + value
            part[at, :] = total * first[at, :]
            return carry

        return body

    for step in range(1, ITERS):
        sums = loop(col_step, zeros)
        for c in range(chunks):
            col_buf[step, me_col, pl.ds(c, 1), :] = jnp.sum(sums[c], axis=0, keepdims=True)
        exchange(col_buf, col_send, col_recv, step, me_col, col_peers, started)
        ratio = 1.0 / add_slots(col_buf, step, csize)
        colpack[...] = ratio
        spread_cols()
        loop(sum_step(step == ITERS - 1), 0)
        for b in range(row_blocks):
            at = pl.ds(b * LANES, LANES)
            row_buf[step, me_row, pl.ds(b, 1), :] = jnp.sum(part[at, :].T, axis=0, keepdims=True)
        exchange(row_buf, row_send, row_recv, step, me_row, row_peers, started)
        total = add_slots(row_buf, step, rsize)
        rowpack[...] = 1.0 / total
        for b in range(row_blocks):
            at = pl.ds(b * LANES, LANES)
            scale[at, :] = first[at, :] * spread_lanes(rowpack, b)

    def weigh(r):
        def body(t, carry):
            at = pl.ds(pl.multiple_of(r * (rows // 2) + t * TILE, TILE), TILE)
            mul = scale[at, :]
            for c in range(chunks):
                weights[at, lane(c)] = (scores[at, lane(c)] * mul).astype(jnp.bfloat16)
            return carry

        lax.fori_loop(0, tiles // 2, body, 0, unroll=2)

    def swap_copy(i, to):
        return remote(swap.at[0], swap.at[i], swap_send.at[i], swap_recv.at[i], to)

    def potentials():
        for c in range(chunks):
            sqy[pl.ds(c, 1), :] = jnp.sum(data_part[pl.ds(c * LANES, LANES), :].T, axis=0, keepdims=True)
        cols_pot = (col_pot + jnp.log(ratio) * LOG2E + (log_rows - log_cols)) / kappa + sqy[...] / width
        colpack[...] = cols_pot
        cols_out[...] = colpack[pl.ds(pl.multiple_of(side * 8, 8), 8), :]
        for b in range(row_blocks):
            sqx[pl.ds(b, 1), :] = shift[pl.ds(b * LANES, LANES), :].T[0:1]
        swap[0] = -(log_rows + row_lse + jnp.log(total) * LOG2E + sqx[...]) / kappa
        begin(swap_copy(1, sibling))
        for i in (0, 1):
            begin(remote(
                swap.at[0], swap.at[2 + core], swap_send.at[2 + i], swap_recv.at[2 + core], device(partner, y, z, i)
            ))

    strip = rows // 2

    def half_rows(r):
        return pl.ds(pl.multiple_of(r * strip, strip), strip)

    def block_x(b):
        return jnp.where(b < 2, jnp.where(b == 0, opposite, mate), jnp.where(b == 2, partner, x))

    def product(p, r, to_z):
        cut = pl.ds(pl.multiple_of(to_z * LANES, LANES), LANES)
        total = None
        for k in (0, 1):
            block = jnp.concatenate(
                [data_all[k, block_x(2 * p + e), :, cut] for e in (0, 1)], axis=1
            )
            value = jnp.dot(
                weights[half_rows(r), k * full_cols:(k + 1) * full_cols], block,
                preferred_element_type=jnp.float32,
            )
            total = value if total is None else total + value
        return total

    def hop(t):
        return 1 - 2 * t

    def sum_copy(b, t, index, src, dst):
        to = device(x, y, around(z + hop(t)), core)
        return remote(src, dst, sum_send.at[b, t, index], sum_recv.at[b, t, index], to)

    def far_copy(b, t):
        return sum_copy(b, t, 0, out_buf.at[b, 2, half_rows(t)], far_buf.at[b - 2, t])

    def direct_copy(b, t):
        at = half_rows(1 - t)
        return sum_copy(b, t, 1, out_buf.at[b, t, at], near_buf.at[b, t, at])

    def added_copy(b, t):
        at = half_rows(t)
        return sum_copy(b, t, 2, out_buf.at[b, t, at], near_buf.at[b, t, at])

    def give_copy(b, r):
        at = half_rows(r)
        return remote(
            out_buf.at[b, 2, at], given.at[b, at], give_send.at[b, r], give_recv.at[b, r], device(mate, y, z, core)
        )

    def relay_copy(r):
        at = half_rows(r)
        return remote(own_buf.at[0, at], relay_in.at[at], in_send.at[r], in_recv.at[4 + r], device(mate, y, z, core))

    def partner_copy(a, r):
        at = half_rows(r)
        return remote(
            own_buf.at[2, at], in_sum.at[a, at], in_send.at[2 + r], part_recv.at[a, r], device(partner, y, z, kind)
        )

    def mate_copy(a):
        return remote(mate_out, mate_in.at[a], in_send.at[4], in_recv.at[2 + a], device(mate, y, z, kind))

    def stay_copy(a):
        return remote(own_buf.at[3], in_sum.at[a], in_send.at[5], in_recv.at[a], sibling)

    def add_far(b):
        for t in (0, 1):
            far_copy(b, t).wait_recv()
            out_buf[b, t, half_rows(t), :] = (
                keep[b - 2, t] + far_buf[b - 2, t].astype(jnp.float32)
            ).astype(jnp.bfloat16)
            added_copy(b, t).start()

    def add_near(b):
        for t in (0, 1):
            direct_copy(b, t).wait_recv()
            added_copy(b, t).wait_recv()
        own_buf[b] = own_buf[b] + near_buf[b, 0].astype(jnp.float32) + near_buf[b, 1].astype(jnp.float32)

    def add_given(b):
        for r in (0, 1):
            at = half_rows(r)
            give_copy(b - 2, r).wait_recv()
            out_buf[b, 2, at, :] = (far_keep[b - 2, at, :] + given[b - 2, at, :].astype(jnp.float32)).astype(jnp.bfloat16)
            far_copy(b, r).start()

    def halves(body):
        def step(r, carry):
            body(r)
            return carry

        lax.fori_loop(0, 2, step, 0)

    def lead(r):
        t = 1 - r
        weigh(r)
        value = product(1, r, around(z + hop(t)))
        for e in (0, 1):
            out_buf[2 + e, t, half_rows(r), :] = value[:, lane(e)].astype(jnp.bfloat16)
        direct_copy(2, t).start()

    def give(r):
        value = product(0, r, around(z + 2))
        for e in (0, 1):
            out_buf[e, 2, half_rows(r), :] = value[:, lane(e)].astype(jnp.bfloat16)
        give_copy(0, r).start()

    def next_products(t):
        def part_of(r):
            value = product(0, r, around(z + hop(t)))
            for e in (0, 1):
                out_buf[e, t, half_rows(r), :] = value[:, lane(e)].astype(jnp.bfloat16)

        halves(part_of)
        direct_copy(0, t).start()
        added_copy(0, t).start()

    def kept_products(t):
        value = product(1, t, around(z + hop(t)))
        for e in (0, 1):
            keep[e, t] = value[:, lane(e)]

    def far_products(r):
        value = product(1, r, around(z + 2))
        for e in (0, 1):
            far_keep[e, half_rows(r), :] = value[:, lane(e)]

    def own_products(p):
        def part_of(r):
            value = product(p, r, z)
            for e in (0, 1):
                own_buf[2 * p + e, half_rows(r), :] = value[:, lane(e)]

        halves(part_of)

    halves(lead)
    halves(give)
    for r in (0, 1):
        give_copy(1, r).start()
    halves(next_products)
    halves(far_products)
    add_given(2)
    for t in (0, 1):
        direct_copy(1, t).start()
        added_copy(1, t).start()
    halves(kept_products)
    halves(own_products)
    add_near(0)
    for r in (0, 1):
        relay_copy(r).start()
    add_far(2)
    add_given(3)
    for t in (0, 1):
        direct_copy(3, t).start()
    add_near(1)
    mate_out[...] = own_buf[1].astype(jnp.bfloat16)
    mate_copy(core).start()
    potentials()
    for copy in started:
        copy.wait_send()

    @pl.when(home)
    def _():
        aside.wait_send()
        for t in (0, 1):
            for a in (0, 1):
                own_round(t, a).wait_send()

    add_near(2)

    def to_partner(r):
        relay_copy(r).wait_recv()
        own_buf[2, half_rows(r), :] = own_buf[2, half_rows(r), :] + relay_in[half_rows(r), :]
        partner_copy(core, r).start()

    to_partner(0)
    add_far(3)
    to_partner(1)

    def settle(b, carry):
        for t in (0, 1):
            direct_copy(b, t).wait_send()
            added_copy(b, t).wait_send()

            @pl.when(b < 2)
            def _():
                give_copy(jnp.minimum(b, 1), t).wait_send()

            @pl.when(b >= 2)
            def _():
                far_copy(jnp.maximum(b, 2), t).wait_send()

        return carry

    lax.fori_loop(0, 3, settle, 0)
    for r in (0, 1):
        relay_copy(r).wait_send()
    swap_copy(1, sibling).wait_recv()
    for i in (0, 1):
        remote(swap.at[0], swap.at[2 + i], swap_send.at[2 + i], swap_recv.at[2 + i], sibling).wait_recv()
    half = rows // LANES
    for a in (0, 1):
        mine_row = jnp.where(core == a, swap[0], swap[1])
        rows_out[pl.ds(a * half, half), :] = jnp.where(home, mine_row, swap[2 + a])

    add_near(3)

    @pl.when(home)
    def _():
        in_sum[core] = own_buf[3]
        stay_copy(1 - core).wait_recv()
        for a in (0, 1):
            mate_copy(a).wait_recv()
            in_sum[a] = in_sum[a] + mate_in[a].astype(jnp.float32)

    @pl.when(jnp.logical_not(home))
    def _():
        stay_copy(core).start()
        for a in (0, 1):
            for r in (0, 1):
                partner_copy(a, r).wait_recv()

    def result_copy(a):
        return pltpu.make_async_copy(in_sum.at[a], targets.at[pl.ds(a * rows, rows)], local_sems.at[a])

    for a in (0, 1):
        result_copy(a).start()

    settle(3, 0)
    for a in (0, 1):
        result_copy(a).wait()
    for r in (0, 1):
        partner_copy(core, r).wait_send()
    mate_copy(core).wait_send()

    @pl.when(jnp.logical_not(home))
    def _():
        stay_copy(core).wait_send()


def hand_on(targets, rows_pot, cols_pot, targets_out, rows_out, cols_out, stage, row_stage, col_stage, sems):
    size = targets.shape[0] // PARTS
    legs = [
        (targets.at[pl.ds(i * size, size)], stage.at[i], targets_out.at[pl.ds(i * size, size)]) for i in range(PARTS)
    ]
    legs += [(rows_pot, row_stage, rows_out), (cols_pot, col_stage, cols_out)]
    first = [pltpu.make_async_copy(src, mid, sems.at[i, 0]) for i, (src, mid, _) in enumerate(legs)]
    second = [pltpu.make_async_copy(mid, dst, sems.at[i, 1]) for i, (_, mid, dst) in enumerate(legs)]
    for copy in first:
        copy.start()
    for before, copy in zip(first, second):
        before.wait()
        copy.start()
    for copy in second:
        copy.wait()


def shards(noise_latents, data_latents):
    nsize = lax.axis_size("noise")
    dsize = lax.axis_size("dp")
    block, piece = noise_latents.shape
    rows, cols = block // 2, 2 * data_latents.shape[0]
    rsize, csize = dsize // 2, nsize * 2
    vmem = pl.BlockSpec(memory_space=pltpu.VMEM)
    f32, bf16 = jnp.float32, jnp.bfloat16
    strip = rows // 2
    row_vec, col_vec = (rows // LANES, LANES), (cols // LANES, LANES)
    sems = pltpu.SemaphoreType.DMA
    targets, rows_pot, cols_pot = pl.pallas_call(
        functools.partial(kernel, rsize, csize, piece * dsize),
        out_shape=(
            jax.ShapeDtypeStruct((block, piece), f32),
            jax.ShapeDtypeStruct((block // LANES, LANES), f32),
            jax.ShapeDtypeStruct((cols // 2 // LANES, LANES), f32),
        ),
        in_specs=[pl.BlockSpec(memory_space=pl.ANY)] * 2,
        out_specs=(pl.BlockSpec(memory_space=pl.ANY), vmem, vmem),
        scratch_shapes=[
            pltpu.VMEM((SIDE, rows, SIDE * piece), bf16),
            pltpu.VMEM((2, SIDE, cols // 2, nsize // SIDE * data_latents.shape[1]), bf16),
            pltpu.VMEM((rows, cols), f32),
            pltpu.VMEM((rows, cols), bf16),
            pltpu.VMEM((rows, LANES), f32),
            pltpu.VMEM((rows, LANES), f32),
            pltpu.VMEM((rows, LANES), f32),
            pltpu.VMEM((rows, LANES), f32),
            pltpu.VMEM((cols, LANES), f32),
            pltpu.VMEM((8, cols), f32),
            pltpu.VMEM(row_vec, f32),
            pltpu.VMEM(col_vec, f32),
            pltpu.VMEM(row_vec, f32),
            pltpu.VMEM(col_vec, f32),
            pltpu.VMEM((4,) + row_vec, f32),
            pltpu.VMEM((ITERS, csize) + col_vec, f32),
            pltpu.VMEM((ITERS, rsize) + row_vec, f32),
            pltpu.VMEM((SIDE, 3, rows, LANES), bf16),
            pltpu.VMEM((SIDE, rows, LANES), f32),
            pltpu.VMEM((2, 2, strip, LANES), bf16),
            pltpu.VMEM((SIDE, 2, rows, LANES), bf16),
            pltpu.VMEM((2, rows, LANES), f32),
            sems((ITERS,)),
            sems((ITERS,)),
            sems((ITERS,)),
            sems((ITERS,)),
            sems((4,)),
            sems((4,)),
            sems((4,)),
            sems((4,)),
            sems((SIDE, 2, 2)),
            sems((SIDE, 2, 2)),
            sems((2, 15)),
            sems((2, 15)),
            sems((SIDE, 2, 3)),
            sems((SIDE, 2, 3)),
            sems((6,)),
            sems((6,)),
            pltpu.VMEM((2, 2, strip, LANES), f32),
            pltpu.VMEM((2, rows, LANES), f32),
            pltpu.VMEM((2, rows, LANES), bf16),
            sems((2, 2)),
            sems((2, 2)),
            sems((2, 2)),
            sems((2,)),
            sems((2, 2)),
            sems((SIDE, 2)),
            pltpu.VMEM((rows, LANES), f32),
            pltpu.VMEM((rows, LANES), bf16),
            pltpu.VMEM((2, rows, LANES), bf16),
        ],
        compiler_params=pltpu.CompilerParams(
            collective_id=0, has_side_effects=True, vmem_limit_bytes=60 * 2**20
        ),
    )(noise_latents, data_latents)
    results = (targets, rows_pot, cols_pot)
    targets, rows_pot, cols_pot = pl.pallas_call(
        hand_on,
        out_shape=tuple(jax.ShapeDtypeStruct(a.shape, a.dtype) for a in results),
        in_specs=[pl.BlockSpec(memory_space=pl.ANY)] * 3,
        out_specs=(pl.BlockSpec(memory_space=pl.ANY),) * 3,
        scratch_shapes=[
            pltpu.VMEM((PARTS, block // PARTS, piece), f32),
            pltpu.VMEM(rows_pot.shape, f32),
            pltpu.VMEM(cols_pot.shape, f32),
            sems((PARTS + 2, 2)),
        ],
        compiler_params=pltpu.CompilerParams(vmem_limit_bytes=60 * 2**20),
    )(*results)
    return targets, rows_pot.reshape(block), cols_pot.reshape(cols // 2)


def solution(mesh):
    return jax.shard_map(
        shards,
        mesh=mesh,
        in_specs=(P("noise", "dp"), P("dp", "noise")),
        out_specs=(P("noise", "dp"), P("noise"), P("dp")),
        check_vma=False,
    )
```

```python
import functools
import math

import jax
import jax.numpy as jnp
from jax import lax
from jax.experimental import pallas as pl
from jax.experimental.pallas import tpu as pltpu
from jax.sharding import PartitionSpec as P

ITERS = 3
EPSILON = 0.04
LOG2E = 1.0 / math.log(2.0)
MESH = pl.DeviceIdType.MESH
LANES = 128
TILE = 32
SIDE = 4
PARTS = 4


def spread_lanes(ref, row):
    return jnp.broadcast_to(ref[pl.ds(row, 1), :], (LANES, LANES)).T


def exchange(buf, send, recv, step, me, peers, started):
    for peer in peers:
        pltpu.make_async_remote_copy(
            src_ref=buf.at[step, me],
            dst_ref=buf.at[step, me],
            send_sem=send.at[step],
            recv_sem=recv.at[step],
            device_id=peer,
            device_id_type=MESH,
        ).start()
    slots = buf.at[step, pl.ds(0, len(peers))]
    every = pltpu.make_async_remote_copy(
        src_ref=slots,
        dst_ref=slots,
        send_sem=send.at[step],
        recv_sem=recv.at[step],
        device_id=peers[0],
        device_id_type=MESH,
    )
    every.wait_recv()
    started.append(every)


def combine(buf, step, size):
    top = buf[step, 0]
    for s in range(1, size):
        top = jnp.maximum(top, buf[step, s])
    total = jnp.exp2(buf[step, 0] - top)
    for s in range(1, size):
        total = total + jnp.exp2(buf[step, s] - top)
    return top + jnp.log(total) * LOG2E


def add_slots(buf, step, size):
    total = buf[step, 0]
    for s in range(1, size):
        total = total + buf[step, s]
    return total


def kernel(
    rsize, csize, width,
    noise_ref, data_ref,
    targets, rows_out, cols_out,
    noise_all, data_all, scores, weights,
    shift, first, scale, part, data_part, colvec, rowpack, colpack, sqx, sqy, swap,
    col_buf, row_buf, out_buf, own_buf, far_buf, near_buf, in_sum,
    col_send, col_recv, row_send, row_recv, swap_send, swap_recv,
    cross_send, cross_recv, noise_send, noise_recv, data_send, data_recv,
    sum_send, sum_recv, in_send, in_recv, keep, far_keep, given, give_send, give_recv, part_recv, local_sems, own_send, far_send, relay_in, mate_out, mate_in,
):
    rows, cols = scores.shape
    n = lax.axis_index("noise")
    d = lax.axis_index("dp")
    x, z = d // SIDE, lax.rem(d, SIDE)
    y, core = n // 2, lax.rem(n, 2)
    kind = lax.rem((x + 1) // 2, 2)
    pair = x // 2
    side = lax.rem(x, 2)
    home = core == kind
    kappa = LOG2E / EPSILON
    log_rows = math.log2(rows * csize)
    log_cols = math.log2(cols * rsize)
    chunks = cols // LANES
    row_blocks = rows // LANES
    tiles = rows // TILE
    started = []

    def around(value):
        return lax.rem(value + SIDE, SIDE)

    def device(xi, yi, zi, ci):
        return (yi * 2 + ci, xi * SIDE + zi)

    me_row = pair * SIDE + z
    me_col = y * 4 + kind * 2 + core

    sibling = device(x, y, z, 1 - core)
    partner = x + 1 - 2 * side
    mate = SIDE - 1 - x
    opposite = around(x + 2)

    barrier = pltpu.get_barrier_semaphore()
    ys, zs = [around(y + k) for k in range(SIDE)], [around(z + k) for k in range(SIDE)]
    rings = [yi * 2 + ci for yi in (ys[2], ys[1], ys[3], ys[0]) for ci in (1 - core, core)]
    col_peers = [(r, di) for di in (partner * SIDE + z, d) for r in rings][:-1]
    row_peers = [(n, xi * SIDE + zi) for xi in (mate, x) for zi in (zs[2], zs[1], zs[3], zs[0])][:-1]
    greeted = [sibling]
    for ci in (0, 1):
        greeted += [device(partner, y, z, ci), device(mate, y, z, ci), device(x, y, zs[1], ci), device(x, y, zs[3], ci)]
    greeted += [device(x, ys[1], z, core), device(x, ys[3], z, core)]
    for to in greeted:
        pl.semaphore_signal(barrier, inc=1, device_id=to, device_id_type=MESH)
    pl.semaphore_wait(barrier, len(greeted))

    def remote(src, dst, send, recv, to):
        return pltpu.make_async_remote_copy(
            src_ref=src, dst_ref=dst, send_sem=send, recv_sem=recv, device_id=to, device_id_type=MESH
        )

    def begin(copy):
        copy.start()
        started.append(copy)

    def lane(c):
        return slice(LANES * c, LANES * (c + 1))

    HOP = (1, -1)

    def noise_slot(xi, zi, at):
        return noise_all.at[xi, at, pl.ds(pl.multiple_of(zi * LANES, LANES), LANES)]

    own = noise_slot(x, z, pl.ds(0, rows))

    def cross_copy(i, half, to):
        return remote(
            noise_ref.at[pl.ds(half * rows, rows)], own, cross_send.at[i], cross_recv.at[x], to
        )

    def cross_wait(xi):
        remote(
            noise_ref.at[pl.ds(0, rows)], noise_slot(xi, z, pl.ds(0, rows)), cross_send.at[0], cross_recv.at[xi], sibling
        ).wait_recv()

    there = jnp.where(home, mate, partner)
    aside = cross_copy(2, 1 - core, sibling)

    def noise_copy(xi, t, forward, zi):
        at = pl.ds(t * (rows // 2), rows // 2) if forward else pl.ds(0, rows)
        f = int(forward)
        slot = noise_slot(xi, zi, at)
        return remote(
            slot, slot, noise_send.at[xi, t, f], noise_recv.at[xi, t, f], device(x, y, around(z + HOP[t]), core)
        )

    def noise_wait(xi, t, forward):
        zi = around(z - HOP[t] * (2 if forward else 1))
        noise_copy(xi, t, forward, zi).wait_recv()
        return zi

    def data_slot(block, where, at):
        width_at = pl.ds(pl.multiple_of(lax.rem(where, 2) * 256, 256), 256)
        return data_all.at[block, where // 2, at, width_at]

    def data_copy(r, index, where, lo, size, to, own=False):
        at = pl.ds(lo, size)
        block = side if r == 0 else 1 - side
        dst = data_slot(block, where, at)
        return remote(data_ref.at[at] if own else dst, dst, data_send.at[r, index], data_recv.at[r, index], to)

    half_cols = cols // 4
    full_cols = cols // 2

    def along_y(step, c):
        return around(y + step) * 2 + c

    def data_wait(r, index, where, lo, size):
        data_copy(r, index, where, lo, size, sibling).wait_recv()

    HALF = 9

    def cross_data(h, own=False):
        at = pl.ds(h * half_cols, half_cols)
        dst = data_slot(side if own else 1 - side, n, at)
        return remote(
            data_ref.at[at], dst, data_send.at[1, 11 + h], data_recv.at[1, 11 + h], device(partner, y, z, core)
        )

    def partner_y(t, h, back=0):
        where = around(y + back) * 2 + core
        to = device(x, around(y + HOP[t]), z, core)
        return t if h == 0 else HALF + t, where, h * half_cols, half_cols, to

    def partner_wait(t, h):
        data_copy(1, *partner_y(t, h, -HOP[t])).wait_recv()

    def own_round(t, a):
        return remote(
            noise_ref.at[pl.ds(a * rows, rows)], own,
            own_send.at[t, a], noise_recv.at[x, t, 0], device(x, y, around(z + HOP[t]), a),
        )

    def own_half():
        return pltpu.make_async_copy(
            noise_ref.at[pl.ds(pl.multiple_of(core * rows, rows), rows)], own, local_sems.at[0]
        )

    @pl.when(home)
    def _():
        for t in (0, 1):
            for a in (0, 1):
                own_round(t, a).start()
        aside.start()

    begin(cross_copy(0, 0, device(there, y, z, 0)))
    begin(cross_copy(1, 1, device(there, y, z, 1)))
    for t in (0, 1):
        begin(data_copy(0, t, n, 0, full_cols, device(x, around(y + HOP[t]), z, core), own=True))
    @pl.when(home)
    def _():
        own_half().start()

    data_own = pltpu.make_async_copy(data_ref, data_slot(side, n, pl.ds(0, full_cols)), local_sems.at[1])
    data_own.start()
    scores[...] = jnp.zeros_like(scores)
    part[...] = jnp.zeros_like(part)
    shift[...] = jnp.zeros_like(shift)
    colvec[...] = jnp.zeros_like(colvec)
    data_part[...] = jnp.zeros_like(data_part)

    def round_z(xi):
        for t in (0, 1):
            begin(noise_copy(xi, t, False, z))

    def forward_z(xi):
        for t in (0, 1):
            begin(noise_copy(xi, t, True, noise_wait(xi, t, False)))

    def far_noise(xi, t):
        slot = noise_slot(xi, around(z + 2), pl.ds(t * (rows // 2), rows // 2))
        return remote(slot, slot, far_send.at[xi, t], noise_recv.at[xi, t, 1], device(mate, y, z, core))

    def share_far(xi):
        for t in (0, 1):
            noise_wait(xi, t, True)
            begin(far_noise(xi, t))

    def far_wait(xi):
        for t in (0, 1):
            far_noise(xi, t).wait_recv()

    def far_data(t, block):
        where = along_y(2, core)
        at = pl.ds(t * half_cols, half_cols)
        dst = data_slot(block, where, at)
        return remote(dst, dst, data_send.at[1, 2 + t], data_recv.at[1, 2 + t], device(partner, y, z, core))

    cross_wait(partner)
    slot = noise_slot(partner, z, pl.ds(0, rows))
    begin(remote(slot, slot, cross_send.at[3], cross_recv.at[partner], device(mate, y, z, core)))
    round_z(partner)
    for h in (0, 1):
        begin(cross_data(h, own=True))
    begin(data_copy(0, 4, n, 0, full_cols, sibling, own=True))
    forward_z(x)
    cross_wait(mate)
    round_z(mate)
    for t in (0, 1):
        where = along_y(-HOP[t], core)
        data_wait(0, t, where, 0, full_cols)
        begin(data_copy(0, 2 + t, where, t * half_cols, half_cols, device(x, around(y + HOP[t]), z, core)))
        begin(data_copy(0, 5 + t, where, 0, full_cols, sibling))
    cross_data(0).wait_recv()
    for t in (0, 1):
        begin(data_copy(1, *partner_y(t, 0)))
    forward_z(partner)
    cross_wait(opposite)
    round_z(opposite)
    share_far(x)
    cross_data(1).wait_recv()
    for t in (0, 1):
        begin(data_copy(1, *partner_y(t, 1)))
    begin(data_copy(1, 4, n, 0, full_cols, sibling))
    for t in (0, 1):
        where = along_y(2, core)
        data_wait(0, 2 + t, where, t * half_cols, half_cols)
        begin(far_data(t, side))
        begin(data_copy(0, 7 + t, where, t * half_cols, half_cols, sibling))

    def squares(block):
        value = block.astype(jnp.float32)
        return value * value

    def chunk_product(xi, m):
        cut = pl.ds(pl.multiple_of(m * 256, 256), 256)
        here = pl.ds(pl.multiple_of(lax.rem(m, 4) * 256, 256), 256)
        total = data_part[cut, :]
        for i in range(SIDE):
            total = total + squares(data_all[m // 4, xi, here, lane(i)])
        data_part[cut, :] = total
        return lax.dot_general(
            noise_all[xi], data_all[m // 4, xi, here, :], (((1,), (1,)), ((), ())),
            preferred_element_type=jnp.float32,
        )

    def norms(xi):
        def norm(r, carry):
            cut = pl.ds(pl.multiple_of(r * 64, 64), 64)
            total = part[cut, :]
            for i in range(SIDE):
                total = total + squares(noise_all[xi, cut, lane(i)])
            part[cut, :] = total
            return carry

        lax.fori_loop(0, rows // 64, norm, 0)

    near, other_block = side * 4, 4 - side * 4

    def unit(block, xs, fresh, count=4):
        def column(i, carry):
            m = block + i
            cut = pl.ds(pl.multiple_of(m * 256, 256), 256)
            value = None if fresh else scores[:, cut]
            for xi in xs:
                value = chunk_product(xi, m) if value is None else value + chunk_product(xi, m)
            scores[:, cut] = value
            return carry

        lax.fori_loop(0, count, column, 0)

    def add_unit(block, count, xi):
        unit(block, (xi,), False, count)

    data_own.wait()
    data_wait(0, 4, along_y(0, 1 - core), 0, full_cols)
    for t in (0, 1):
        data_wait(0, 5 + t, along_y(-HOP[t], 1 - core), 0, full_cols)
    for t in (0, 1):
        data_wait(0, 7 + t, along_y(2, 1 - core), t * half_cols, half_cols)

    @pl.when(home)
    def _():
        own_half().wait()

    @pl.when(jnp.logical_not(home))
    def _():
        cross_wait(x)

    unit(near, (x,), True)
    share_far(partner)
    norms(x)
    for t in (0, 1):
        noise_wait(mate, t, False)
    far_wait(mate)
    unit(near, (mate,), False)
    norms(mate)

    def beside(t, h, c):
        return data_copy(1, (5 if h == 0 else 13) + t, along_y(-HOP[t], c), h * half_cols, half_cols, sibling)

    for t in (0, 1):
        partner_wait(t, 0)
        begin(beside(t, 0, core))
    unit(near, (partner,), False)
    norms(partner)
    data_wait(1, 4, along_y(0, 1 - core), 0, full_cols)
    for t in (0, 1):
        beside(t, 0, 1 - core).wait_recv()

    def ahead(i, carry):
        xi = around(y + i + i // 2)
        add_unit(other_block, jnp.where(xi == opposite, 0, jnp.where(i == 0, 4, 2)), xi)
        return carry

    lax.fori_loop(0, 3, ahead, 0)
    for t in (0, 1):
        partner_wait(t, 1)
        begin(beside(t, 1, core))
    for t in (0, 1):
        noise_wait(opposite, t, False)
    far_wait(opposite)
    for t in (0, 1):
        far_data(t, 1 - side).wait_recv()
        begin(data_copy(1, 7 + t, along_y(2, core), t * half_cols, half_cols, sibling))
    norms(opposite)

    factor = 2.0 * kappa / width

    def row_shift(r, carry):
        at = pl.ds(pl.multiple_of(r * 128, 128), 128)
        total = jnp.sum(part[at, :], axis=1, keepdims=True) * (-kappa / width)
        shift[at, :] = jnp.broadcast_to(total, (128, LANES))
        return carry

    lax.fori_loop(0, rows // 128, row_shift, 0)

    def exp_sums(m):
        for e in (0, 1):
            at = pl.ds(pl.multiple_of(m * 256 + e * LANES, LANES), LANES)
            top = colvec[0:1, at]
            total = jnp.sum(jnp.exp2(scores[:, at] + shift[...] - top), axis=0, keepdims=True)
            col_buf[0, me_col, pl.ds(2 * m + e, 1), :] = top + jnp.log(total) * LOG2E

    def final(block, xi):
        def column(i, carry):
            m = block + i
            exp_sums(block + jnp.maximum(i - 1, 0))
            cut = pl.ds(pl.multiple_of(m * 256, 256), 256)
            value = (scores[:, cut] + chunk_product(xi, m)) * factor
            scores[:, cut] = value
            for e in (0, 1):
                top = jnp.max(value[:, LANES * e:LANES * (e + 1)] + shift[...], axis=0, keepdims=True)
                colvec[:, pl.ds(pl.multiple_of(m * 256 + e * LANES, LANES), LANES)] = jnp.broadcast_to(top, (8, LANES))
            return carry

        lax.fori_loop(0, 4, column, 0)
        exp_sums(block + 3)

    final(near, opposite)
    add_unit(other_block, jnp.where(opposite == y, 4, jnp.where(opposite == around(y + 2), 0, 2)), opposite)
    for t in (0, 1):
        beside(t, 1, 1 - core).wait_recv()
    unit(other_block + 2, (around(y + 1), around(y - 1)), False, 2)
    for t in (0, 1):
        data_wait(1, 7 + t, along_y(2, 1 - core), t * half_cols, half_cols)
    final(other_block, around(y + 2))

    def fold(block, op):
        out = block[0:8]
        for r in range(1, TILE // 8):
            out = op(out, block[8 * r:8 * r + 8])
        return out

    def spread_cols():
        for c in range(chunks):
            colvec[:, lane(c)] = jnp.broadcast_to(colpack[pl.ds(c, 1), :], (8, LANES))

    def tall(ref, c):
        return jnp.concatenate([ref[:, lane(c)]] * (TILE // 8), axis=0)

    def tile_at(t):
        return pl.ds(pl.multiple_of(t * TILE, TILE), TILE)

    def loop(body, init):
        return lax.fori_loop(0, tiles, body, init, unroll=2)

    zeros = tuple(jnp.zeros((8, LANES), jnp.float32) for _ in range(chunks))

    exchange(col_buf, col_send, col_recv, 0, me_col, col_peers, started)
    col_pot = -log_cols - combine(col_buf, 0, csize)
    colpack[...] = col_pot
    spread_cols()

    def row_step(t, carry):
        at = tile_at(t)
        top = scores[at, lane(0)] + tall(colvec, 0)
        for c in range(1, chunks):
            top = jnp.maximum(top, scores[at, lane(c)] + tall(colvec, c))
        first[at, :] = top
        total = None
        for c in range(chunks):
            value = jnp.exp2(scores[at, lane(c)] + tall(colvec, c) - top)
            scores[at, lane(c)] = value
            total = value if total is None else total + value
        part[at, :] = total
        return carry

    loop(row_step, 0)
    for b in range(row_blocks):
        at = pl.ds(b * LANES, LANES)
        tops = first[at, :].T
        top = jnp.max(tops, axis=0, keepdims=True)
        total = jnp.sum(part[at, :].T * jnp.exp2(tops - top), axis=0, keepdims=True)
        row_buf[0, me_row, pl.ds(b, 1), :] = top + jnp.log(total) * LOG2E
    exchange(row_buf, row_send, row_recv, 0, me_row, row_peers, started)
    row_lse = combine(row_buf, 0, rsize)
    rowpack[...] = row_lse
    for b in range(row_blocks):
        at = pl.ds(b * LANES, LANES)
        base = jnp.exp2(first[at, :] - spread_lanes(rowpack, b))
        first[at, :] = base
        scale[at, :] = base

    def col_step(t, accs):
        at = tile_at(t)
        mul = scale[at, :]
        return tuple(accs[c] + fold(scores[at, lane(c)] * mul, jnp.add) for c in range(chunks))

    def sum_step(keep_values):
        def body(t, carry):
            at = tile_at(t)
            total = None
            for c in range(chunks):
                value = scores[at, lane(c)] * tall(colvec, c)
                if keep_values:
                    scores[at, lane(c)] = value
                total = value if total is None else total + value
            part[at, :] = total * first[at, :]
            return carry

        return body

    for step in range(1, ITERS):
        sums = loop(col_step, zeros)
        for c in range(chunks):
            col_buf[step, me_col, pl.ds(c, 1), :] = jnp.sum(sums[c], axis=0, keepdims=True)
        exchange(col_buf, col_send, col_recv, step, me_col, col_peers, started)
        ratio = 1.0 / add_slots(col_buf, step, csize)
        colpack[...] = ratio
        spread_cols()
        loop(sum_step(step == ITERS - 1), 0)
        for b in range(row_blocks):
            at = pl.ds(b * LANES, LANES)
            row_buf[step, me_row, pl.ds(b, 1), :] = jnp.sum(part[at, :].T, axis=0, keepdims=True)
        exchange(row_buf, row_send, row_recv, step, me_row, row_peers, started)
        total = add_slots(row_buf, step, rsize)
        rowpack[...] = 1.0 / total
        for b in range(row_blocks):
            at = pl.ds(b * LANES, LANES)
            scale[at, :] = first[at, :] * spread_lanes(rowpack, b)

    def weigh(r):
        def body(t, carry):
            at = pl.ds(pl.multiple_of(r * (rows // 2) + t * TILE, TILE), TILE)
            mul = scale[at, :]
            for c in range(chunks):
                weights[at, lane(c)] = (scores[at, lane(c)] * mul).astype(jnp.bfloat16)
            return carry

        lax.fori_loop(0, tiles // 2, body, 0, unroll=2)

    def swap_copy(i, to):
        return remote(swap.at[0], swap.at[i], swap_send.at[i], swap_recv.at[i], to)

    def potentials():
        for c in range(chunks):
            sqy[pl.ds(c, 1), :] = jnp.sum(data_part[pl.ds(c * LANES, LANES), :].T, axis=0, keepdims=True)
        cols_pot = (col_pot + jnp.log(ratio) * LOG2E + (log_rows - log_cols)) / kappa + sqy[...] / width
        colpack[...] = cols_pot
        cols_out[...] = colpack[pl.ds(pl.multiple_of(side * 8, 8), 8), :]
        for b in range(row_blocks):
            sqx[pl.ds(b, 1), :] = shift[pl.ds(b * LANES, LANES), :].T[0:1]
        swap[0] = -(log_rows + row_lse + jnp.log(total) * LOG2E + sqx[...]) / kappa
        begin(swap_copy(1, sibling))
        for i in (0, 1):
            begin(remote(
                swap.at[0], swap.at[2 + core], swap_send.at[2 + i], swap_recv.at[2 + core], device(partner, y, z, i)
            ))

    strip = rows // 2

    def half_rows(r):
        return pl.ds(pl.multiple_of(r * strip, strip), strip)

    def block_x(b):
        return jnp.where(b < 2, jnp.where(b == 0, opposite, mate), jnp.where(b == 2, partner, x))

    def product(p, r, to_z):
        cut = pl.ds(pl.multiple_of(to_z * LANES, LANES), LANES)
        total = None
        for k in (0, 1):
            block = jnp.concatenate(
                [data_all[k, block_x(2 * p + e), :, cut] for e in (0, 1)], axis=1
            )
            value = jnp.dot(
                weights[half_rows(r), k * full_cols:(k + 1) * full_cols], block,
                preferred_element_type=jnp.float32,
            )
            total = value if total is None else total + value
        return total

    def hop(t):
        return 1 - 2 * t

    def sum_copy(b, t, index, src, dst):
        to = device(x, y, around(z + hop(t)), core)
        return remote(src, dst, sum_send.at[b, t, index], sum_recv.at[b, t, index], to)

    def far_copy(b, t):
        return sum_copy(b, t, 0, out_buf.at[b, 2, half_rows(t)], far_buf.at[b - 2, t])

    def direct_copy(b, t):
        at = half_rows(1 - t)
        return sum_copy(b, t, 1, out_buf.at[b, t, at], near_buf.at[b, t, at])

    def added_copy(b, t):
        at = half_rows(t)
        return sum_copy(b, t, 2, out_buf.at[b, t, at], near_buf.at[b, t, at])

    def give_copy(b, r):
        at = half_rows(r)
        return remote(
            out_buf.at[b, 2, at], given.at[b, at], give_send.at[b, r], give_recv.at[b, r], device(mate, y, z, core)
        )

    def relay_copy(r):
        at = half_rows(r)
        return remote(own_buf.at[0, at], relay_in.at[at], in_send.at[r], in_recv.at[4 + r], device(mate, y, z, core))

    def partner_copy(a, r):
        at = half_rows(r)
        return remote(
            own_buf.at[2, at], in_sum.at[a, at], in_send.at[2 + r], part_recv.at[a, r], device(partner, y, z, kind)
        )

    def mate_copy(a):
        return remote(mate_out, mate_in.at[a], in_send.at[4], in_recv.at[2 + a], device(mate, y, z, kind))

    def stay_copy(a):
        return remote(own_buf.at[3], in_sum.at[a], in_send.at[5], in_recv.at[a], sibling)

    def add_far(b):
        for t in (0, 1):
            far_copy(b, t).wait_recv()
            out_buf[b, t, half_rows(t), :] = (
                keep[b - 2, t] + far_buf[b - 2, t].astype(jnp.float32)
            ).astype(jnp.bfloat16)
            added_copy(b, t).start()

    def add_near(b):
        for t in (0, 1):
            direct_copy(b, t).wait_recv()
            added_copy(b, t).wait_recv()
        own_buf[b] = own_buf[b] + near_buf[b, 0].astype(jnp.float32) + near_buf[b, 1].astype(jnp.float32)

    def add_given(b):
        for r in (0, 1):
            at = half_rows(r)
            give_copy(b - 2, r).wait_recv()
            out_buf[b, 2, at, :] = (far_keep[b - 2, at, :] + given[b - 2, at, :].astype(jnp.float32)).astype(jnp.bfloat16)
            far_copy(b, r).start()

    def halves(body):
        def step(r, carry):
            body(r)
            return carry

        lax.fori_loop(0, 2, step, 0)

    def lead(r):
        t = 1 - r
        weigh(r)
        value = product(1, r, around(z + hop(t)))
        for e in (0, 1):
            out_buf[2 + e, t, half_rows(r), :] = value[:, lane(e)].astype(jnp.bfloat16)
        direct_copy(2, t).start()

    def give(r):
        value = product(0, r, around(z + 2))
        for e in (0, 1):
            out_buf[e, 2, half_rows(r), :] = value[:, lane(e)].astype(jnp.bfloat16)
        give_copy(0, r).start()

    def next_products(t):
        def part_of(r):
            value = product(0, r, around(z + hop(t)))
            for e in (0, 1):
                out_buf[e, t, half_rows(r), :] = value[:, lane(e)].astype(jnp.bfloat16)

        halves(part_of)
        direct_copy(0, t).start()
        added_copy(0, t).start()

    def kept_products(t):
        value = product(1, t, around(z + hop(t)))
        for e in (0, 1):
            keep[e, t] = value[:, lane(e)]

    def far_products(r):
        value = product(1, r, around(z + 2))
        for e in (0, 1):
            far_keep[e, half_rows(r), :] = value[:, lane(e)]

    def own_products(p):
        def part_of(r):
            value = product(p, r, z)
            for e in (0, 1):
                own_buf[2 * p + e, half_rows(r), :] = value[:, lane(e)]

        halves(part_of)

    halves(lead)
    halves(give)
    for r in (0, 1):
        give_copy(1, r).start()
    halves(next_products)
    halves(far_products)
    add_given(2)
    for t in (0, 1):
        direct_copy(1, t).start()
    halves(kept_products)
    halves(own_products)
    add_near(0)
    for r in (0, 1):
        relay_copy(r).start()
    add_far(2)
    for t in (0, 1):
        added_copy(1, t).start()
    add_given(3)
    for t in (0, 1):
        direct_copy(3, t).start()
    add_near(2)

    def to_partner(r):
        relay_copy(r).wait_recv()
        own_buf[2, half_rows(r), :] = own_buf[2, half_rows(r), :] + relay_in[half_rows(r), :]
        partner_copy(core, r).start()

    to_partner(0)
    add_near(1)
    mate_out[...] = own_buf[1].astype(jnp.bfloat16)
    mate_copy(core).start()
    potentials()
    for copy in started:
        copy.wait_send()

    @pl.when(home)
    def _():
        aside.wait_send()
        for t in (0, 1):
            for a in (0, 1):
                own_round(t, a).wait_send()

    add_far(3)
    to_partner(1)

    def settle(b, carry):
        for t in (0, 1):
            direct_copy(b, t).wait_send()
            added_copy(b, t).wait_send()

            @pl.when(b < 2)
            def _():
                give_copy(jnp.minimum(b, 1), t).wait_send()

            @pl.when(b >= 2)
            def _():
                far_copy(jnp.maximum(b, 2), t).wait_send()

        return carry

    lax.fori_loop(0, 3, settle, 0)
    for r in (0, 1):
        relay_copy(r).wait_send()
    swap_copy(1, sibling).wait_recv()
    for i in (0, 1):
        remote(swap.at[0], swap.at[2 + i], swap_send.at[2 + i], swap_recv.at[2 + i], sibling).wait_recv()
    half = rows // LANES
    for a in (0, 1):
        mine_row = jnp.where(core == a, swap[0], swap[1])
        rows_out[pl.ds(a * half, half), :] = jnp.where(home, mine_row, swap[2 + a])

    add_near(3)

    @pl.when(home)
    def _():
        in_sum[core] = own_buf[3]
        stay_copy(1 - core).wait_recv()
        for a in (0, 1):
            mate_copy(a).wait_recv()
            in_sum[a] = in_sum[a] + mate_in[a].astype(jnp.float32)

    @pl.when(jnp.logical_not(home))
    def _():
        stay_copy(core).start()
        for a in (0, 1):
            for r in (0, 1):
                partner_copy(a, r).wait_recv()

    def result_copy(a):
        return pltpu.make_async_copy(in_sum.at[a], targets.at[pl.ds(a * rows, rows)], local_sems.at[a])

    for a in (0, 1):
        result_copy(a).start()

    settle(3, 0)
    for a in (0, 1):
        result_copy(a).wait()
    for r in (0, 1):
        partner_copy(core, r).wait_send()
    mate_copy(core).wait_send()

    @pl.when(jnp.logical_not(home))
    def _():
        stay_copy(core).wait_send()


def hand_on(targets, rows_pot, cols_pot, targets_out, rows_out, cols_out, stage, row_stage, col_stage, sems):
    size = targets.shape[0] // PARTS
    legs = [
        (targets.at[pl.ds(i * size, size)], stage.at[i], targets_out.at[pl.ds(i * size, size)]) for i in range(PARTS)
    ]
    legs += [(rows_pot, row_stage, rows_out), (cols_pot, col_stage, cols_out)]
    first = [pltpu.make_async_copy(src, mid, sems.at[i, 0]) for i, (src, mid, _) in enumerate(legs)]
    second = [pltpu.make_async_copy(mid, dst, sems.at[i, 1]) for i, (_, mid, dst) in enumerate(legs)]
    for copy in first:
        copy.start()
    for before, copy in zip(first, second):
        before.wait()
        copy.start()
    for copy in second:
        copy.wait()


def shards(noise_latents, data_latents):
    nsize = lax.axis_size("noise")
    dsize = lax.axis_size("dp")
    block, piece = noise_latents.shape
    rows, cols = block // 2, 2 * data_latents.shape[0]
    rsize, csize = dsize // 2, nsize * 2
    vmem = pl.BlockSpec(memory_space=pltpu.VMEM)
    f32, bf16 = jnp.float32, jnp.bfloat16
    strip = rows // 2
    row_vec, col_vec = (rows // LANES, LANES), (cols // LANES, LANES)
    sems = pltpu.SemaphoreType.DMA
    targets, rows_pot, cols_pot = pl.pallas_call(
        functools.partial(kernel, rsize, csize, piece * dsize),
        out_shape=(
            jax.ShapeDtypeStruct((block, piece), f32),
            jax.ShapeDtypeStruct((block // LANES, LANES), f32),
            jax.ShapeDtypeStruct((cols // 2 // LANES, LANES), f32),
        ),
        in_specs=[pl.BlockSpec(memory_space=pl.ANY)] * 2,
        out_specs=(pl.BlockSpec(memory_space=pl.ANY), vmem, vmem),
        scratch_shapes=[
            pltpu.VMEM((SIDE, rows, SIDE * piece), bf16),
            pltpu.VMEM((2, SIDE, cols // 2, nsize // SIDE * data_latents.shape[1]), bf16),
            pltpu.VMEM((rows, cols), f32),
            pltpu.VMEM((rows, cols), bf16),
            pltpu.VMEM((rows, LANES), f32),
            pltpu.VMEM((rows, LANES), f32),
            pltpu.VMEM((rows, LANES), f32),
            pltpu.VMEM((rows, LANES), f32),
            pltpu.VMEM((cols, LANES), f32),
            pltpu.VMEM((8, cols), f32),
            pltpu.VMEM(row_vec, f32),
            pltpu.VMEM(col_vec, f32),
            pltpu.VMEM(row_vec, f32),
            pltpu.VMEM(col_vec, f32),
            pltpu.VMEM((4,) + row_vec, f32),
            pltpu.VMEM((ITERS, csize) + col_vec, f32),
            pltpu.VMEM((ITERS, rsize) + row_vec, f32),
            pltpu.VMEM((SIDE, 3, rows, LANES), bf16),
            pltpu.VMEM((SIDE, rows, LANES), f32),
            pltpu.VMEM((2, 2, strip, LANES), bf16),
            pltpu.VMEM((SIDE, 2, rows, LANES), bf16),
            pltpu.VMEM((2, rows, LANES), f32),
            sems((ITERS,)),
            sems((ITERS,)),
            sems((ITERS,)),
            sems((ITERS,)),
            sems((4,)),
            sems((4,)),
            sems((4,)),
            sems((4,)),
            sems((SIDE, 2, 2)),
            sems((SIDE, 2, 2)),
            sems((2, 15)),
            sems((2, 15)),
            sems((SIDE, 2, 3)),
            sems((SIDE, 2, 3)),
            sems((6,)),
            sems((6,)),
            pltpu.VMEM((2, 2, strip, LANES), f32),
            pltpu.VMEM((2, rows, LANES), f32),
            pltpu.VMEM((2, rows, LANES), bf16),
            sems((2, 2)),
            sems((2, 2)),
            sems((2, 2)),
            sems((2,)),
            sems((2, 2)),
            sems((SIDE, 2)),
            pltpu.VMEM((rows, LANES), f32),
            pltpu.VMEM((rows, LANES), bf16),
            pltpu.VMEM((2, rows, LANES), bf16),
        ],
        compiler_params=pltpu.CompilerParams(
            collective_id=0, has_side_effects=True, vmem_limit_bytes=60 * 2**20
        ),
    )(noise_latents, data_latents)
    results = (targets, rows_pot, cols_pot)
    targets, rows_pot, cols_pot = pl.pallas_call(
        hand_on,
        out_shape=tuple(jax.ShapeDtypeStruct(a.shape, a.dtype) for a in results),
        in_specs=[pl.BlockSpec(memory_space=pl.ANY)] * 3,
        out_specs=(pl.BlockSpec(memory_space=pl.ANY),) * 3,
        scratch_shapes=[
            pltpu.VMEM((PARTS, block // PARTS, piece), f32),
            pltpu.VMEM(rows_pot.shape, f32),
            pltpu.VMEM(cols_pot.shape, f32),
            sems((PARTS + 2, 2)),
        ],
        compiler_params=pltpu.CompilerParams(vmem_limit_bytes=60 * 2**20),
    )(*results)
    return targets, rows_pot.reshape(block), cols_pot.reshape(cols // 2)


def solution(mesh):
    return jax.shard_map(
        shards,
        mesh=mesh,
        in_specs=(P("noise", "dp"), P("dp", "noise")),
        out_specs=(P("noise", "dp"), P("noise"), P("dp")),
        check_vma=False,
    )
```

```python
import functools
import math

import jax
import jax.numpy as jnp
from jax import lax
from jax.experimental import pallas as pl
from jax.experimental.pallas import tpu as pltpu
from jax.sharding import PartitionSpec as P

ITERS = 3
EPSILON = 0.04
LOG2E = 1.0 / math.log(2.0)
MESH = pl.DeviceIdType.MESH
LANES = 128
TILE = 32
SIDE = 4
PARTS = 4


def spread_lanes(ref, row):
    return jnp.broadcast_to(ref[pl.ds(row, 1), :], (LANES, LANES)).T


def exchange(buf, send, recv, step, me, peers, started):
    for peer in peers:
        pltpu.make_async_remote_copy(
            src_ref=buf.at[step, me],
            dst_ref=buf.at[step, me],
            send_sem=send.at[step],
            recv_sem=recv.at[step],
            device_id=peer,
            device_id_type=MESH,
        ).start()
    slots = buf.at[step, pl.ds(0, len(peers))]
    every = pltpu.make_async_remote_copy(
        src_ref=slots,
        dst_ref=slots,
        send_sem=send.at[step],
        recv_sem=recv.at[step],
        device_id=peers[0],
        device_id_type=MESH,
    )
    every.wait_recv()
    started.append(every)


def combine(buf, step, size):
    top = buf[step, 0]
    for s in range(1, size):
        top = jnp.maximum(top, buf[step, s])
    total = jnp.exp2(buf[step, 0] - top)
    for s in range(1, size):
        total = total + jnp.exp2(buf[step, s] - top)
    return top + jnp.log(total) * LOG2E


def add_slots(buf, step, size):
    total = buf[step, 0]
    for s in range(1, size):
        total = total + buf[step, s]
    return total


def kernel(
    rsize, csize, width,
    noise_ref, data_ref,
    targets, rows_out, cols_out,
    noise_all, data_all, scores, weights,
    shift, first, scale, part, data_part, colvec, rowpack, colpack, sqx, sqy, swap,
    col_buf, row_buf, out_buf, own_buf, far_buf, near_buf, in_sum,
    col_send, col_recv, row_send, row_recv, swap_send, swap_recv,
    cross_send, cross_recv, noise_send, noise_recv, data_send, data_recv,
    sum_send, sum_recv, in_send, in_recv, keep, far_keep, given, give_send, give_recv, part_recv, local_sems, own_send, far_send, relay_in, mate_out, mate_in,
):
    rows, cols = scores.shape
    n = lax.axis_index("noise")
    d = lax.axis_index("dp")
    x, z = d // SIDE, lax.rem(d, SIDE)
    y, core = n // 2, lax.rem(n, 2)
    kind = lax.rem((x + 1) // 2, 2)
    pair = x // 2
    side = lax.rem(x, 2)
    home = core == kind
    kappa = LOG2E / EPSILON
    log_rows = math.log2(rows * csize)
    log_cols = math.log2(cols * rsize)
    chunks = cols // LANES
    row_blocks = rows // LANES
    tiles = rows // TILE
    started = []

    def around(value):
        return lax.rem(value + SIDE, SIDE)

    def device(xi, yi, zi, ci):
        return (yi * 2 + ci, xi * SIDE + zi)

    me_row = pair * SIDE + z
    me_col = y * 4 + kind * 2 + core

    sibling = device(x, y, z, 1 - core)
    partner = x + 1 - 2 * side
    mate = SIDE - 1 - x
    opposite = around(x + 2)

    barrier = pltpu.get_barrier_semaphore()
    ys, zs = [around(y + k) for k in range(SIDE)], [around(z + k) for k in range(SIDE)]
    rings = [yi * 2 + ci for yi in (ys[2], ys[1], ys[3], ys[0]) for ci in (1 - core, core)]
    col_peers = [(r, di) for di in (partner * SIDE + z, d) for r in rings][:-1]
    row_peers = [(n, xi * SIDE + zi) for xi in (mate, x) for zi in (zs[2], zs[1], zs[3], zs[0])][:-1]
    greeted = [sibling]
    for ci in (0, 1):
        greeted += [device(partner, y, z, ci), device(mate, y, z, ci), device(x, y, zs[1], ci), device(x, y, zs[3], ci)]
    greeted += [device(x, ys[1], z, core), device(x, ys[3], z, core)]
    for to in greeted:
        pl.semaphore_signal(barrier, inc=1, device_id=to, device_id_type=MESH)
    pl.semaphore_wait(barrier, len(greeted))

    def remote(src, dst, send, recv, to):
        return pltpu.make_async_remote_copy(
            src_ref=src, dst_ref=dst, send_sem=send, recv_sem=recv, device_id=to, device_id_type=MESH
        )

    def begin(copy):
        copy.start()
        started.append(copy)

    def lane(c):
        return slice(LANES * c, LANES * (c + 1))

    HOP = (1, -1)

    def noise_slot(xi, zi, at):
        return noise_all.at[xi, at, pl.ds(pl.multiple_of(zi * LANES, LANES), LANES)]

    own = noise_slot(x, z, pl.ds(0, rows))

    def cross_copy(i, half, to):
        return remote(
            noise_ref.at[pl.ds(half * rows, rows)], own, cross_send.at[i], cross_recv.at[x], to
        )

    def cross_wait(xi):
        remote(
            noise_ref.at[pl.ds(0, rows)], noise_slot(xi, z, pl.ds(0, rows)), cross_send.at[0], cross_recv.at[xi], sibling
        ).wait_recv()

    there = jnp.where(home, mate, partner)
    aside = cross_copy(2, 1 - core, sibling)

    def noise_copy(xi, t, forward, zi):
        at = pl.ds(t * (rows // 2), rows // 2) if forward else pl.ds(0, rows)
        f = int(forward)
        slot = noise_slot(xi, zi, at)
        return remote(
            slot, slot, noise_send.at[xi, t, f], noise_recv.at[xi, t, f], device(x, y, around(z + HOP[t]), core)
        )

    def noise_wait(xi, t, forward):
        zi = around(z - HOP[t] * (2 if forward else 1))
        noise_copy(xi, t, forward, zi).wait_recv()
        return zi

    def data_slot(block, where, at):
        width_at = pl.ds(pl.multiple_of(lax.rem(where, 2) * 256, 256), 256)
        return data_all.at[block, where // 2, at, width_at]

    def data_copy(r, index, where, lo, size, to, own=False):
        at = pl.ds(lo, size)
        block = side if r == 0 else 1 - side
        dst = data_slot(block, where, at)
        return remote(data_ref.at[at] if own else dst, dst, data_send.at[r, index], data_recv.at[r, index], to)

    half_cols = cols // 4
    full_cols = cols // 2

    def along_y(step, c):
        return around(y + step) * 2 + c

    def data_wait(r, index, where, lo, size):
        data_copy(r, index, where, lo, size, sibling).wait_recv()

    HALF = 9

    def cross_data(h, own=False):
        at = pl.ds(h * half_cols, half_cols)
        dst = data_slot(side if own else 1 - side, n, at)
        return remote(
            data_ref.at[at], dst, data_send.at[1, 11 + h], data_recv.at[1, 11 + h], device(partner, y, z, core)
        )

    def partner_y(t, h, back=0):
        where = around(y + back) * 2 + core
        to = device(x, around(y + HOP[t]), z, core)
        return t if h == 0 else HALF + t, where, h * half_cols, half_cols, to

    def partner_wait(t, h):
        data_copy(1, *partner_y(t, h, -HOP[t])).wait_recv()

    def own_round(t, a):
        return remote(
            noise_ref.at[pl.ds(a * rows, rows)], own,
            own_send.at[t, a], noise_recv.at[x, t, 0], device(x, y, around(z + HOP[t]), a),
        )

    def own_half():
        return pltpu.make_async_copy(
            noise_ref.at[pl.ds(pl.multiple_of(core * rows, rows), rows)], own, local_sems.at[0]
        )

    @pl.when(home)
    def _():
        for t in (0, 1):
            for a in (0, 1):
                own_round(t, a).start()
        aside.start()

    begin(cross_copy(0, 0, device(there, y, z, 0)))
    begin(cross_copy(1, 1, device(there, y, z, 1)))
    for t in (0, 1):
        begin(data_copy(0, t, n, 0, full_cols, device(x, around(y + HOP[t]), z, core), own=True))
    @pl.when(home)
    def _():
        own_half().start()

    data_own = pltpu.make_async_copy(data_ref, data_slot(side, n, pl.ds(0, full_cols)), local_sems.at[1])
    data_own.start()
    scores[...] = jnp.zeros_like(scores)
    part[...] = jnp.zeros_like(part)
    data_part[...] = jnp.zeros_like(data_part)

    def round_z(xi):
        for t in (0, 1):
            begin(noise_copy(xi, t, False, z))

    def forward_z(xi):
        for t in (0, 1):
            begin(noise_copy(xi, t, True, noise_wait(xi, t, False)))

    def far_noise(xi, t):
        slot = noise_slot(xi, around(z + 2), pl.ds(t * (rows // 2), rows // 2))
        return remote(slot, slot, far_send.at[xi, t], noise_recv.at[xi, t, 1], device(mate, y, z, core))

    def share_far(xi):
        for t in (0, 1):
            noise_wait(xi, t, True)
            begin(far_noise(xi, t))

    def far_wait(xi):
        for t in (0, 1):
            far_noise(xi, t).wait_recv()

    def far_data(t, block):
        where = along_y(2, core)
        at = pl.ds(t * half_cols, half_cols)
        dst = data_slot(block, where, at)
        return remote(dst, dst, data_send.at[1, 2 + t], data_recv.at[1, 2 + t], device(partner, y, z, core))

    cross_wait(partner)
    slot = noise_slot(partner, z, pl.ds(0, rows))
    begin(remote(slot, slot, cross_send.at[3], cross_recv.at[partner], device(mate, y, z, core)))
    round_z(partner)
    for h in (0, 1):
        begin(cross_data(h, own=True))
    begin(data_copy(0, 4, n, 0, full_cols, sibling, own=True))
    forward_z(x)
    cross_wait(mate)
    round_z(mate)
    for t in (0, 1):
        where = along_y(-HOP[t], core)
        data_wait(0, t, where, 0, full_cols)
        begin(data_copy(0, 2 + t, where, t * half_cols, half_cols, device(x, around(y + HOP[t]), z, core)))
        begin(data_copy(0, 5 + t, where, 0, full_cols, sibling))
    cross_data(0).wait_recv()
    for t in (0, 1):
        begin(data_copy(1, *partner_y(t, 0)))
    forward_z(partner)
    cross_wait(opposite)
    round_z(opposite)
    share_far(x)
    cross_data(1).wait_recv()
    for t in (0, 1):
        begin(data_copy(1, *partner_y(t, 1)))
    begin(data_copy(1, 4, n, 0, full_cols, sibling))
    for t in (0, 1):
        where = along_y(2, core)
        data_wait(0, 2 + t, where, t * half_cols, half_cols)
        begin(far_data(t, side))
        begin(data_copy(0, 7 + t, where, t * half_cols, half_cols, sibling))

    def squares(block):
        value = block.astype(jnp.float32)
        return value * value

    def chunk_product(xi, m):
        cut = pl.ds(pl.multiple_of(m * 256, 256), 256)
        here = pl.ds(pl.multiple_of(lax.rem(m, 4) * 256, 256), 256)
        total = data_part[cut, :]
        for i in range(SIDE):
            total = total + squares(data_all[m // 4, xi, here, lane(i)])
        data_part[cut, :] = total
        return lax.dot_general(
            noise_all[xi], data_all[m // 4, xi, here, :], (((1,), (1,)), ((), ())),
            preferred_element_type=jnp.float32,
        )

    def norms(xi):
        def norm(r, carry):
            cut = pl.ds(pl.multiple_of(r * 64, 64), 64)
            total = part[cut, :]
            for i in range(SIDE):
                total = total + squares(noise_all[xi, cut, lane(i)])
            part[cut, :] = total
            return carry

        lax.fori_loop(0, rows // 64, norm, 0)

    near, other_block = side * 4, 4 - side * 4

    def unit(block, xs, fresh, count=4):
        def column(i, carry):
            m = block + i
            cut = pl.ds(pl.multiple_of(m * 256, 256), 256)
            value = None if fresh else scores[:, cut]
            for xi in xs:
                value = chunk_product(xi, m) if value is None else value + chunk_product(xi, m)
            scores[:, cut] = value
            return carry

        lax.fori_loop(0, count, column, 0)

    def add_unit(block, count, xi):
        unit(block, (xi,), False, count)

    data_own.wait()
    data_wait(0, 4, along_y(0, 1 - core), 0, full_cols)
    for t in (0, 1):
        data_wait(0, 5 + t, along_y(-HOP[t], 1 - core), 0, full_cols)
    for t in (0, 1):
        data_wait(0, 7 + t, along_y(2, 1 - core), t * half_cols, half_cols)

    @pl.when(home)
    def _():
        own_half().wait()

    @pl.when(jnp.logical_not(home))
    def _():
        cross_wait(x)

    unit(near, (x,), True)
    share_far(partner)
    norms(x)
    for t in (0, 1):
        noise_wait(mate, t, False)
    far_wait(mate)
    unit(near, (mate,), False)
    norms(mate)

    def beside(t, h, c):
        return data_copy(1, (5 if h == 0 else 13) + t, along_y(-HOP[t], c), h * half_cols, half_cols, sibling)

    for t in (0, 1):
        partner_wait(t, 0)
        begin(beside(t, 0, core))
    unit(near, (partner,), False)
    norms(partner)
    data_wait(1, 4, along_y(0, 1 - core), 0, full_cols)
    for t in (0, 1):
        beside(t, 0, 1 - core).wait_recv()

    def ahead(i, carry):
        xi = around(y + i + i // 2)
        add_unit(other_block, jnp.where(xi == opposite, 0, jnp.where(i == 0, 4, 2)), xi)
        return carry

    lax.fori_loop(0, 3, ahead, 0)
    for t in (0, 1):
        partner_wait(t, 1)
        begin(beside(t, 1, core))
    for t in (0, 1):
        noise_wait(opposite, t, False)
    far_wait(opposite)
    for t in (0, 1):
        far_data(t, 1 - side).wait_recv()
        begin(data_copy(1, 7 + t, along_y(2, core), t * half_cols, half_cols, sibling))
    norms(opposite)

    factor = 2.0 * kappa / width

    def row_shift(r, carry):
        at = pl.ds(pl.multiple_of(r * 128, 128), 128)
        total = jnp.sum(part[at, :], axis=1, keepdims=True) * (-kappa / width)
        shift[at, :] = jnp.broadcast_to(total, (128, LANES))
        return carry

    lax.fori_loop(0, rows // 128, row_shift, 0)

    def final(block, xi):
        def column(i, carry):
            m = block + i
            cut = pl.ds(pl.multiple_of(m * 256, 256), 256)
            value = (scores[:, cut] + chunk_product(xi, m)) * factor
            scores[:, cut] = value
            for e in (0, 1):
                top = jnp.max(value[:, LANES * e:LANES * (e + 1)] + shift[...], axis=0, keepdims=True)
                colvec[:, pl.ds(pl.multiple_of(m * 256 + e * LANES, LANES), LANES)] = jnp.broadcast_to(top, (8, LANES))
            return carry

        lax.fori_loop(0, 4, column, 0)

    final(near, opposite)
    add_unit(other_block, jnp.where(opposite == y, 4, jnp.where(opposite == around(y + 2), 0, 2)), opposite)
    for t in (0, 1):
        beside(t, 1, 1 - core).wait_recv()
    unit(other_block + 2, (around(y + 1), around(y - 1)), False, 2)
    for t in (0, 1):
        data_wait(1, 7 + t, along_y(2, 1 - core), t * half_cols, half_cols)
    final(other_block, around(y + 2))

    def fold(block, op):
        out = block[0:8]
        for r in range(1, TILE // 8):
            out = op(out, block[8 * r:8 * r + 8])
        return out

    def spread_cols():
        for c in range(chunks):
            colvec[:, lane(c)] = jnp.broadcast_to(colpack[pl.ds(c, 1), :], (8, LANES))

    def tall(ref, c):
        return jnp.concatenate([ref[:, lane(c)]] * (TILE // 8), axis=0)

    def tile_at(t):
        return pl.ds(pl.multiple_of(t * TILE, TILE), TILE)

    def loop(body, init):
        return lax.fori_loop(0, tiles, body, init, unroll=2)

    zeros = tuple(jnp.zeros((8, LANES), jnp.float32) for _ in range(chunks))

    def exp_step(t, accs):
        at = tile_at(t)
        add = shift[at, :]
        return tuple(
            accs[c] + fold(jnp.exp2(scores[at, lane(c)] + add - tall(colvec, c)), jnp.add)
            for c in range(chunks)
        )

    sums = loop(exp_step, zeros)
    for c in range(chunks):
        total = jnp.sum(sums[c], axis=0, keepdims=True)
        col_buf[0, me_col, pl.ds(c, 1), :] = colvec[0:1, lane(c)] + jnp.log(total) * LOG2E
    exchange(col_buf, col_send, col_recv, 0, me_col, col_peers, started)
    col_pot = -log_cols - combine(col_buf, 0, csize)
    colpack[...] = col_pot
    spread_cols()

    def row_step(t, carry):
        at = tile_at(t)
        top = scores[at, lane(0)] + tall(colvec, 0)
        for c in range(1, chunks):
            top = jnp.maximum(top, scores[at, lane(c)] + tall(colvec, c))
        first[at, :] = top
        total = None
        for c in range(chunks):
            value = jnp.exp2(scores[at, lane(c)] + tall(colvec, c) - top)
            scores[at, lane(c)] = value
            total = value if total is None else total + value
        part[at, :] = total
        return carry

    loop(row_step, 0)
    for b in range(row_blocks):
        at = pl.ds(b * LANES, LANES)
        tops = first[at, :].T
        top = jnp.max(tops, axis=0, keepdims=True)
        total = jnp.sum(part[at, :].T * jnp.exp2(tops - top), axis=0, keepdims=True)
        row_buf[0, me_row, pl.ds(b, 1), :] = top + jnp.log(total) * LOG2E
    exchange(row_buf, row_send, row_recv, 0, me_row, row_peers, started)
    row_lse = combine(row_buf, 0, rsize)
    rowpack[...] = row_lse
    for b in range(row_blocks):
        at = pl.ds(b * LANES, LANES)
        base = jnp.exp2(first[at, :] - spread_lanes(rowpack, b))
        first[at, :] = base
        scale[at, :] = base

    def col_step(t, accs):
        at = tile_at(t)
        mul = scale[at, :]
        return tuple(accs[c] + fold(scores[at, lane(c)] * mul, jnp.add) for c in range(chunks))

    def sum_step(keep_values):
        def body(t, carry):
            at = tile_at(t)
            total = None
            for c in range(chunks):
                value = scores[at, lane(c)] * tall(colvec, c)
                if keep_values:
                    scores[at, lane(c)] = value
                total = value if total is None else total + value
            part[at, :] = total * first[at, :]
            return carry

        return body

    for step in range(1, ITERS):
        sums = loop(col_step, zeros)
        for c in range(chunks):
            col_buf[step, me_col, pl.ds(c, 1), :] = jnp.sum(sums[c], axis=0, keepdims=True)
        exchange(col_buf, col_send, col_recv, step, me_col, col_peers, started)
        ratio = 1.0 / add_slots(col_buf, step, csize)
        colpack[...] = ratio
        spread_cols()
        loop(sum_step(step == ITERS - 1), 0)
        for b in range(row_blocks):
            at = pl.ds(b * LANES, LANES)
            row_buf[step, me_row, pl.ds(b, 1), :] = jnp.sum(part[at, :].T, axis=0, keepdims=True)
        exchange(row_buf, row_send, row_recv, step, me_row, row_peers, started)
        total = add_slots(row_buf, step, rsize)
        rowpack[...] = 1.0 / total
        for b in range(row_blocks):
            at = pl.ds(b * LANES, LANES)
            scale[at, :] = first[at, :] * spread_lanes(rowpack, b)

    def weigh(r):
        def body(t, carry):
            at = pl.ds(pl.multiple_of(r * (rows // 2) + t * TILE, TILE), TILE)
            mul = scale[at, :]
            for c in range(chunks):
                weights[at, lane(c)] = (scores[at, lane(c)] * mul).astype(jnp.bfloat16)
            return carry

        lax.fori_loop(0, tiles // 2, body, 0, unroll=2)

    def swap_copy(i, to):
        return remote(swap.at[0], swap.at[i], swap_send.at[i], swap_recv.at[i], to)

    def potentials():
        for c in range(chunks):
            sqy[pl.ds(c, 1), :] = jnp.sum(data_part[pl.ds(c * LANES, LANES), :].T, axis=0, keepdims=True)
        cols_pot = (col_pot + jnp.log(ratio) * LOG2E + (log_rows - log_cols)) / kappa + sqy[...] / width
        colpack[...] = cols_pot
        cols_out[...] = colpack[pl.ds(pl.multiple_of(side * 8, 8), 8), :]
        for b in range(row_blocks):
            sqx[pl.ds(b, 1), :] = shift[pl.ds(b * LANES, LANES), :].T[0:1]
        swap[0] = -(log_rows + row_lse + jnp.log(total) * LOG2E + sqx[...]) / kappa
        begin(swap_copy(1, sibling))
        for i in (0, 1):
            begin(remote(
                swap.at[0], swap.at[2 + core], swap_send.at[2 + i], swap_recv.at[2 + core], device(partner, y, z, i)
            ))

    strip = rows // 2

    def half_rows(r):
        return pl.ds(pl.multiple_of(r * strip, strip), strip)

    def block_x(b):
        return jnp.where(b < 2, jnp.where(b == 0, opposite, mate), jnp.where(b == 2, partner, x))

    def product(p, r, to_z):
        cut = pl.ds(pl.multiple_of(to_z * LANES, LANES), LANES)
        total = None
        for k in (0, 1):
            block = jnp.concatenate(
                [data_all[k, block_x(2 * p + e), :, cut] for e in (0, 1)], axis=1
            )
            value = jnp.dot(
                weights[half_rows(r), k * full_cols:(k + 1) * full_cols], block,
                preferred_element_type=jnp.float32,
            )
            total = value if total is None else total + value
        return total

    def hop(t):
        return 1 - 2 * t

    def sum_copy(b, t, index, src, dst):
        to = device(x, y, around(z + hop(t)), core)
        return remote(src, dst, sum_send.at[b, t, index], sum_recv.at[b, t, index], to)

    def far_copy(b, t):
        return sum_copy(b, t, 0, out_buf.at[b, 2, half_rows(t)], far_buf.at[b - 2, t])

    def direct_copy(b, t):
        at = half_rows(1 - t)
        return sum_copy(b, t, 1, out_buf.at[b, t, at], near_buf.at[b, t, at])

    def added_copy(b, t):
        at = half_rows(t)
        return sum_copy(b, t, 2, out_buf.at[b, t, at], near_buf.at[b, t, at])

    def give_copy(b, r):
        at = half_rows(r)
        return remote(
            out_buf.at[b, 2, at], given.at[b, at], give_send.at[b, r], give_recv.at[b, r], device(mate, y, z, core)
        )

    def relay_copy(r):
        at = half_rows(r)
        return remote(own_buf.at[0, at], relay_in.at[at], in_send.at[r], in_recv.at[4 + r], device(mate, y, z, core))

    def partner_copy(a, r):
        at = half_rows(r)
        return remote(
            own_buf.at[2, at], in_sum.at[a, at], in_send.at[2 + r], part_recv.at[a, r], device(partner, y, z, kind)
        )

    def mate_copy(a):
        return remote(mate_out, mate_in.at[a], in_send.at[4], in_recv.at[2 + a], device(mate, y, z, kind))

    def stay_copy(a):
        return remote(own_buf.at[3], in_sum.at[a], in_send.at[5], in_recv.at[a], sibling)

    def add_far(b):
        for t in (0, 1):
            far_copy(b, t).wait_recv()
            out_buf[b, t, half_rows(t), :] = (
                keep[b - 2, t] + far_buf[b - 2, t].astype(jnp.float32)
            ).astype(jnp.bfloat16)
            added_copy(b, t).start()

    def add_near(b):
        for t in (0, 1):
            direct_copy(b, t).wait_recv()
            added_copy(b, t).wait_recv()
        own_buf[b] = own_buf[b] + near_buf[b, 0].astype(jnp.float32) + near_buf[b, 1].astype(jnp.float32)

    def add_given(b):
        for r in (0, 1):
            at = half_rows(r)
            give_copy(b - 2, r).wait_recv()
            out_buf[b, 2, at, :] = (far_keep[b - 2, at, :] + given[b - 2, at, :].astype(jnp.float32)).astype(jnp.bfloat16)
            far_copy(b, r).start()

    def halves(body):
        def step(r, carry):
            body(r)
            return carry

        lax.fori_loop(0, 2, step, 0)

    def lead(r):
        t = 1 - r
        weigh(r)
        value = product(1, r, around(z + hop(t)))
        for e in (0, 1):
            out_buf[2 + e, t, half_rows(r), :] = value[:, lane(e)].astype(jnp.bfloat16)
        direct_copy(2, t).start()

    def give(r):
        value = product(0, r, around(z + 2))
        for e in (0, 1):
            out_buf[e, 2, half_rows(r), :] = value[:, lane(e)].astype(jnp.bfloat16)
        give_copy(0, r).start()

    def next_products(t):
        def part_of(r):
            value = product(0, r, around(z + hop(t)))
            for e in (0, 1):
                out_buf[e, t, half_rows(r), :] = value[:, lane(e)].astype(jnp.bfloat16)

        halves(part_of)
        direct_copy(0, t).start()
        added_copy(0, t).start()

    def kept_products(t):
        value = product(1, t, around(z + hop(t)))
        for e in (0, 1):
            keep[e, t] = value[:, lane(e)]

    def far_products(r):
        value = product(1, r, around(z + 2))
        for e in (0, 1):
            far_keep[e, half_rows(r), :] = value[:, lane(e)]

    def own_products(p):
        def part_of(r):
            value = product(p, r, z)
            for e in (0, 1):
                own_buf[2 * p + e, half_rows(r), :] = value[:, lane(e)]

        halves(part_of)

    halves(lead)
    halves(give)
    for r in (0, 1):
        give_copy(1, r).start()
    halves(next_products)
    halves(far_products)
    add_given(2)
    for t in (0, 1):
        direct_copy(1, t).start()
    halves(kept_products)
    halves(own_products)
    add_near(0)
    for r in (0, 1):
        relay_copy(r).start()
    add_far(2)
    for t in (0, 1):
        added_copy(1, t).start()
    add_given(3)
    for t in (0, 1):
        direct_copy(3, t).start()
    add_near(2)

    def to_partner(r):
        relay_copy(r).wait_recv()
        own_buf[2, half_rows(r), :] = own_buf[2, half_rows(r), :] + relay_in[half_rows(r), :]
        partner_copy(core, r).start()

    to_partner(0)
    add_near(1)
    mate_out[...] = own_buf[1].astype(jnp.bfloat16)
    mate_copy(core).start()
    potentials()
    for copy in started:
        copy.wait_send()

    @pl.when(home)
    def _():
        aside.wait_send()
        for t in (0, 1):
            for a in (0, 1):
                own_round(t, a).wait_send()

    add_far(3)
    to_partner(1)

    def settle(b, carry):
        for t in (0, 1):
            direct_copy(b, t).wait_send()
            added_copy(b, t).wait_send()

            @pl.when(b < 2)
            def _():
                give_copy(jnp.minimum(b, 1), t).wait_send()

            @pl.when(b >= 2)
            def _():
                far_copy(jnp.maximum(b, 2), t).wait_send()

        return carry

    lax.fori_loop(0, 3, settle, 0)
    for r in (0, 1):
        relay_copy(r).wait_send()
    swap_copy(1, sibling).wait_recv()
    for i in (0, 1):
        remote(swap.at[0], swap.at[2 + i], swap_send.at[2 + i], swap_recv.at[2 + i], sibling).wait_recv()
    half = rows // LANES
    for a in (0, 1):
        mine_row = jnp.where(core == a, swap[0], swap[1])
        rows_out[pl.ds(a * half, half), :] = jnp.where(home, mine_row, swap[2 + a])

    add_near(3)

    @pl.when(home)
    def _():
        in_sum[core] = own_buf[3]
        stay_copy(1 - core).wait_recv()
        for a in (0, 1):
            mate_copy(a).wait_recv()
            in_sum[a] = in_sum[a] + mate_in[a].astype(jnp.float32)

    @pl.when(jnp.logical_not(home))
    def _():
        stay_copy(core).start()
        for a in (0, 1):
            for r in (0, 1):
                partner_copy(a, r).wait_recv()

    def result_copy(a):
        return pltpu.make_async_copy(in_sum.at[a], targets.at[pl.ds(a * rows, rows)], local_sems.at[a])

    for a in (0, 1):
        result_copy(a).start()

    settle(3, 0)
    for a in (0, 1):
        result_copy(a).wait()
    for r in (0, 1):
        partner_copy(core, r).wait_send()
    mate_copy(core).wait_send()

    @pl.when(jnp.logical_not(home))
    def _():
        stay_copy(core).wait_send()


def hand_on(targets, rows_pot, cols_pot, targets_out, rows_out, cols_out, stage, row_stage, col_stage, sems):
    size = targets.shape[0] // PARTS
    legs = [
        (targets.at[pl.ds(i * size, size)], stage.at[i], targets_out.at[pl.ds(i * size, size)]) for i in range(PARTS)
    ]
    legs += [(rows_pot, row_stage, rows_out), (cols_pot, col_stage, cols_out)]
    first = [pltpu.make_async_copy(src, mid, sems.at[i, 0]) for i, (src, mid, _) in enumerate(legs)]
    second = [pltpu.make_async_copy(mid, dst, sems.at[i, 1]) for i, (_, mid, dst) in enumerate(legs)]
    for copy in first:
        copy.start()
    for before, copy in zip(first, second):
        before.wait()
        copy.start()
    for copy in second:
        copy.wait()


def shards(noise_latents, data_latents):
    nsize = lax.axis_size("noise")
    dsize = lax.axis_size("dp")
    block, piece = noise_latents.shape
    rows, cols = block // 2, 2 * data_latents.shape[0]
    rsize, csize = dsize // 2, nsize * 2
    vmem = pl.BlockSpec(memory_space=pltpu.VMEM)
    f32, bf16 = jnp.float32, jnp.bfloat16
    strip = rows // 2
    row_vec, col_vec = (rows // LANES, LANES), (cols // LANES, LANES)
    sems = pltpu.SemaphoreType.DMA
    targets, rows_pot, cols_pot = pl.pallas_call(
        functools.partial(kernel, rsize, csize, piece * dsize),
        out_shape=(
            jax.ShapeDtypeStruct((block, piece), f32),
            jax.ShapeDtypeStruct((block // LANES, LANES), f32),
            jax.ShapeDtypeStruct((cols // 2 // LANES, LANES), f32),
        ),
        in_specs=[pl.BlockSpec(memory_space=pl.ANY)] * 2,
        out_specs=(pl.BlockSpec(memory_space=pl.ANY), vmem, vmem),
        scratch_shapes=[
            pltpu.VMEM((SIDE, rows, SIDE * piece), bf16),
            pltpu.VMEM((2, SIDE, cols // 2, nsize // SIDE * data_latents.shape[1]), bf16),
            pltpu.VMEM((rows, cols), f32),
            pltpu.VMEM((rows, cols), bf16),
            pltpu.VMEM((rows, LANES), f32),
            pltpu.VMEM((rows, LANES), f32),
            pltpu.VMEM((rows, LANES), f32),
            pltpu.VMEM((rows, LANES), f32),
            pltpu.VMEM((cols, LANES), f32),
            pltpu.VMEM((8, cols), f32),
            pltpu.VMEM(row_vec, f32),
            pltpu.VMEM(col_vec, f32),
            pltpu.VMEM(row_vec, f32),
            pltpu.VMEM(col_vec, f32),
            pltpu.VMEM((4,) + row_vec, f32),
            pltpu.VMEM((ITERS, csize) + col_vec, f32),
            pltpu.VMEM((ITERS, rsize) + row_vec, f32),
            pltpu.VMEM((SIDE, 3, rows, LANES), bf16),
            pltpu.VMEM((SIDE, rows, LANES), f32),
            pltpu.VMEM((2, 2, strip, LANES), bf16),
            pltpu.VMEM((SIDE, 2, rows, LANES), bf16),
            pltpu.VMEM((2, rows, LANES), f32),
            sems((ITERS,)),
            sems((ITERS,)),
            sems((ITERS,)),
            sems((ITERS,)),
            sems((4,)),
            sems((4,)),
            sems((4,)),
            sems((4,)),
            sems((SIDE, 2, 2)),
            sems((SIDE, 2, 2)),
            sems((2, 15)),
            sems((2, 15)),
            sems((SIDE, 2, 3)),
            sems((SIDE, 2, 3)),
            sems((6,)),
            sems((6,)),
            pltpu.VMEM((2, 2, strip, LANES), f32),
            pltpu.VMEM((2, rows, LANES), f32),
            pltpu.VMEM((2, rows, LANES), bf16),
            sems((2, 2)),
            sems((2, 2)),
            sems((2, 2)),
            sems((2,)),
            sems((2, 2)),
            sems((SIDE, 2)),
            pltpu.VMEM((rows, LANES), f32),
            pltpu.VMEM((rows, LANES), bf16),
            pltpu.VMEM((2, rows, LANES), bf16),
        ],
        compiler_params=pltpu.CompilerParams(
            collective_id=0, has_side_effects=True, vmem_limit_bytes=60 * 2**20
        ),
    )(noise_latents, data_latents)
    results = (targets, rows_pot, cols_pot)
    targets, rows_pot, cols_pot = pl.pallas_call(
        hand_on,
        out_shape=tuple(jax.ShapeDtypeStruct(a.shape, a.dtype) for a in results),
        in_specs=[pl.BlockSpec(memory_space=pl.ANY)] * 3,
        out_specs=(pl.BlockSpec(memory_space=pl.ANY),) * 3,
        scratch_shapes=[
            pltpu.VMEM((PARTS, block // PARTS, piece), f32),
            pltpu.VMEM(rows_pot.shape, f32),
            pltpu.VMEM(cols_pot.shape, f32),
            sems((PARTS + 2, 2)),
        ],
        compiler_params=pltpu.CompilerParams(vmem_limit_bytes=60 * 2**20),
    )(*results)
    return targets, rows_pot.reshape(block), cols_pot.reshape(cols // 2)


def solution(mesh):
    return jax.shard_map(
        shards,
        mesh=mesh,
        in_specs=(P("noise", "dp"), P("dp", "noise")),
        out_specs=(P("noise", "dp"), P("noise"), P("dp")),
        check_vma=False,
    )
```

```python
import functools
import math

import jax
import jax.numpy as jnp
from jax import lax
from jax.experimental import pallas as pl
from jax.experimental.pallas import tpu as pltpu
from jax.sharding import PartitionSpec as P

ITERS = 3
EPSILON = 0.04
LOG2E = 1.0 / math.log(2.0)
MESH = pl.DeviceIdType.MESH
LANES = 128
TILE = 32
SIDE = 4
PARTS = 4


def spread_lanes(ref, row):
    return jnp.broadcast_to(ref[pl.ds(row, 1), :], (LANES, LANES)).T


def exchange(buf, send, recv, step, me, peers, started):
    for peer in peers:
        pltpu.make_async_remote_copy(
            src_ref=buf.at[step, me],
            dst_ref=buf.at[step, me],
            send_sem=send.at[step],
            recv_sem=recv.at[step],
            device_id=peer,
            device_id_type=MESH,
        ).start()
    slots = buf.at[step, pl.ds(0, len(peers))]
    every = pltpu.make_async_remote_copy(
        src_ref=slots,
        dst_ref=slots,
        send_sem=send.at[step],
        recv_sem=recv.at[step],
        device_id=peers[0],
        device_id_type=MESH,
    )
    every.wait_recv()
    started.append(every)


def combine(buf, step, size):
    top = buf[step, 0]
    for s in range(1, size):
        top = jnp.maximum(top, buf[step, s])
    total = jnp.exp2(buf[step, 0] - top)
    for s in range(1, size):
        total = total + jnp.exp2(buf[step, s] - top)
    return top + jnp.log(total) * LOG2E


def add_slots(buf, step, size):
    total = buf[step, 0]
    for s in range(1, size):
        total = total + buf[step, s]
    return total


def kernel(
    rsize, csize, width,
    noise_ref, data_ref,
    targets, rows_out, cols_out,
    noise_all, data_all, scores, weights,
    shift, first, scale, part, data_part, colvec, rowpack, colpack, sqx, sqy, swap,
    col_buf, row_buf, out_buf, own_buf, far_buf, near_buf, in_sum,
    col_send, col_recv, row_send, row_recv, swap_send, swap_recv,
    cross_send, cross_recv, noise_send, noise_recv, data_send, data_recv,
    sum_send, sum_recv, in_send, in_recv, keep, far_keep, given, give_send, give_recv, part_recv, local_sems, own_send, far_send, relay_in, mate_out, mate_in,
):
    rows, cols = scores.shape
    n = lax.axis_index("noise")
    d = lax.axis_index("dp")
    x, z = d // SIDE, lax.rem(d, SIDE)
    y, core = n // 2, lax.rem(n, 2)
    kind = lax.rem((x + 1) // 2, 2)
    pair = x // 2
    side = lax.rem(x, 2)
    home = core == kind
    kappa = LOG2E / EPSILON
    log_rows = math.log2(rows * csize)
    log_cols = math.log2(cols * rsize)
    chunks = cols // LANES
    row_blocks = rows // LANES
    tiles = rows // TILE
    started = []

    def around(value):
        return lax.rem(value + SIDE, SIDE)

    def device(xi, yi, zi, ci):
        return (yi * 2 + ci, xi * SIDE + zi)

    me_row = pair * SIDE + z
    me_col = y * 4 + kind * 2 + core

    sibling = device(x, y, z, 1 - core)
    partner = x + 1 - 2 * side
    mate = SIDE - 1 - x
    opposite = around(x + 2)

    barrier = pltpu.get_barrier_semaphore()
    ys, zs = [around(y + k) for k in range(SIDE)], [around(z + k) for k in range(SIDE)]
    rings = [yi * 2 + ci for yi in (ys[2], ys[1], ys[3], ys[0]) for ci in (1 - core, core)]
    col_peers = [(r, di) for di in (partner * SIDE + z, d) for r in rings][:-1]
    row_peers = [(n, xi * SIDE + zi) for xi in (mate, x) for zi in (zs[2], zs[1], zs[3], zs[0])][:-1]
    greeted = [sibling]
    for ci in (0, 1):
        greeted += [device(partner, y, z, ci), device(mate, y, z, ci), device(x, y, zs[1], ci), device(x, y, zs[3], ci)]
    greeted += [device(x, ys[1], z, core), device(x, ys[3], z, core)]
    for to in greeted:
        pl.semaphore_signal(barrier, inc=1, device_id=to, device_id_type=MESH)
    pl.semaphore_wait(barrier, len(greeted))

    def remote(src, dst, send, recv, to):
        return pltpu.make_async_remote_copy(
            src_ref=src, dst_ref=dst, send_sem=send, recv_sem=recv, device_id=to, device_id_type=MESH
        )

    def begin(copy):
        copy.start()
        started.append(copy)

    def lane(c):
        return slice(LANES * c, LANES * (c + 1))

    HOP = (1, -1)

    def noise_slot(xi, zi, at):
        return noise_all.at[xi, at, pl.ds(pl.multiple_of(zi * LANES, LANES), LANES)]

    own = noise_slot(x, z, pl.ds(0, rows))

    def cross_copy(i, half, to):
        return remote(
            noise_ref.at[pl.ds(half * rows, rows)], own, cross_send.at[i], cross_recv.at[x], to
        )

    def cross_wait(xi):
        remote(
            noise_ref.at[pl.ds(0, rows)], noise_slot(xi, z, pl.ds(0, rows)), cross_send.at[0], cross_recv.at[xi], sibling
        ).wait_recv()

    there = jnp.where(home, mate, partner)
    aside = cross_copy(2, 1 - core, sibling)

    def noise_copy(xi, t, forward, zi):
        at = pl.ds(t * (rows // 2), rows // 2) if forward else pl.ds(0, rows)
        f = int(forward)
        slot = noise_slot(xi, zi, at)
        return remote(
            slot, slot, noise_send.at[xi, t, f], noise_recv.at[xi, t, f], device(x, y, around(z + HOP[t]), core)
        )

    def noise_wait(xi, t, forward):
        zi = around(z - HOP[t] * (2 if forward else 1))
        noise_copy(xi, t, forward, zi).wait_recv()
        return zi

    def data_slot(block, where, at):
        width_at = pl.ds(pl.multiple_of(lax.rem(where, 2) * 256, 256), 256)
        return data_all.at[block, where // 2, at, width_at]

    def data_copy(r, index, where, lo, size, to, own=False):
        at = pl.ds(lo, size)
        block = side if r == 0 else 1 - side
        dst = data_slot(block, where, at)
        return remote(data_ref.at[at] if own else dst, dst, data_send.at[r, index], data_recv.at[r, index], to)

    half_cols = cols // 4
    full_cols = cols // 2

    def along_y(step, c):
        return around(y + step) * 2 + c

    def data_wait(r, index, where, lo, size):
        data_copy(r, index, where, lo, size, sibling).wait_recv()

    HALF = 9

    def cross_data(h, own=False):
        at = pl.ds(h * half_cols, half_cols)
        dst = data_slot(side if own else 1 - side, n, at)
        return remote(
            data_ref.at[at], dst, data_send.at[1, 11 + h], data_recv.at[1, 11 + h], device(partner, y, z, core)
        )

    def partner_y(t, h, back=0):
        where = around(y + back) * 2 + core
        to = device(x, around(y + HOP[t]), z, core)
        return t if h == 0 else HALF + t, where, h * half_cols, half_cols, to

    def partner_wait(t, h):
        data_copy(1, *partner_y(t, h, -HOP[t])).wait_recv()

    def own_round(t, a):
        return remote(
            noise_ref.at[pl.ds(a * rows, rows)], own,
            own_send.at[t, a], noise_recv.at[x, t, 0], device(x, y, around(z + HOP[t]), a),
        )

    def own_half():
        return pltpu.make_async_copy(
            noise_ref.at[pl.ds(pl.multiple_of(core * rows, rows), rows)], own, local_sems.at[0]
        )

    @pl.when(home)
    def _():
        for t in (0, 1):
            for a in (0, 1):
                own_round(t, a).start()
        aside.start()

    begin(cross_copy(0, 0, device(there, y, z, 0)))
    begin(cross_copy(1, 1, device(there, y, z, 1)))
    for t in (0, 1):
        begin(data_copy(0, t, n, 0, full_cols, device(x, around(y + HOP[t]), z, core), own=True))
    @pl.when(home)
    def _():
        own_half().start()

    data_own = pltpu.make_async_copy(data_ref, data_slot(side, n, pl.ds(0, full_cols)), local_sems.at[1])
    data_own.start()
    scores[...] = jnp.zeros_like(scores)
    part[...] = jnp.zeros_like(part)
    data_part[...] = jnp.zeros_like(data_part)

    def round_z(xi):
        for t in (0, 1):
            begin(noise_copy(xi, t, False, z))

    def forward_z(xi):
        for t in (0, 1):
            begin(noise_copy(xi, t, True, noise_wait(xi, t, False)))

    def far_noise(xi, t):
        slot = noise_slot(xi, around(z + 2), pl.ds(t * (rows // 2), rows // 2))
        return remote(slot, slot, far_send.at[xi, t], noise_recv.at[xi, t, 1], device(mate, y, z, core))

    def share_far(xi):
        for t in (0, 1):
            noise_wait(xi, t, True)
            begin(far_noise(xi, t))

    def far_wait(xi):
        for t in (0, 1):
            far_noise(xi, t).wait_recv()

    def far_data(t, block):
        where = along_y(2, core)
        at = pl.ds(t * half_cols, half_cols)
        dst = data_slot(block, where, at)
        return remote(dst, dst, data_send.at[1, 2 + t], data_recv.at[1, 2 + t], device(partner, y, z, core))

    cross_wait(partner)
    slot = noise_slot(partner, z, pl.ds(0, rows))
    begin(remote(slot, slot, cross_send.at[3], cross_recv.at[partner], device(mate, y, z, core)))
    round_z(partner)
    for h in (0, 1):
        begin(cross_data(h, own=True))
    begin(data_copy(0, 4, n, 0, full_cols, sibling, own=True))
    forward_z(x)
    cross_wait(mate)
    round_z(mate)
    for t in (0, 1):
        where = along_y(-HOP[t], core)
        data_wait(0, t, where, 0, full_cols)
        begin(data_copy(0, 2 + t, where, t * half_cols, half_cols, device(x, around(y + HOP[t]), z, core)))
        begin(data_copy(0, 5 + t, where, 0, full_cols, sibling))
    cross_data(0).wait_recv()
    for t in (0, 1):
        begin(data_copy(1, *partner_y(t, 0)))
    forward_z(partner)
    cross_wait(opposite)
    round_z(opposite)
    share_far(x)
    cross_data(1).wait_recv()
    for t in (0, 1):
        begin(data_copy(1, *partner_y(t, 1)))
    begin(data_copy(1, 4, n, 0, full_cols, sibling))
    for t in (0, 1):
        where = along_y(2, core)
        data_wait(0, 2 + t, where, t * half_cols, half_cols)
        begin(far_data(t, side))
        begin(data_copy(0, 7 + t, where, t * half_cols, half_cols, sibling))

    def squares(block):
        value = block.astype(jnp.float32)
        return value * value

    def chunk_product(xi, m):
        cut = pl.ds(pl.multiple_of(m * 256, 256), 256)
        here = pl.ds(pl.multiple_of(lax.rem(m, 4) * 256, 256), 256)
        total = data_part[cut, :]
        for i in range(SIDE):
            total = total + squares(data_all[m // 4, xi, here, lane(i)])
        data_part[cut, :] = total
        return lax.dot_general(
            noise_all[xi], data_all[m // 4, xi, here, :], (((1,), (1,)), ((), ())),
            preferred_element_type=jnp.float32,
        )

    def norms(xi):
        def norm(r, carry):
            cut = pl.ds(pl.multiple_of(r * 64, 64), 64)
            total = part[cut, :]
            for i in range(SIDE):
                total = total + squares(noise_all[xi, cut, lane(i)])
            part[cut, :] = total
            return carry

        lax.fori_loop(0, rows // 64, norm, 0)

    near, other_block = side * 4, 4 - side * 4

    def unit(block, xs, fresh, count=4):
        def column(i, carry):
            m = block + i
            cut = pl.ds(pl.multiple_of(m * 256, 256), 256)
            value = None if fresh else scores[:, cut]
            for xi in xs:
                value = chunk_product(xi, m) if value is None else value + chunk_product(xi, m)
            scores[:, cut] = value
            return carry

        lax.fori_loop(0, count, column, 0)

    def add_unit(block, count, xi):
        unit(block, (xi,), False, count)

    data_own.wait()
    data_wait(0, 4, along_y(0, 1 - core), 0, full_cols)
    for t in (0, 1):
        data_wait(0, 5 + t, along_y(-HOP[t], 1 - core), 0, full_cols)
    for t in (0, 1):
        data_wait(0, 7 + t, along_y(2, 1 - core), t * half_cols, half_cols)

    @pl.when(home)
    def _():
        own_half().wait()

    @pl.when(jnp.logical_not(home))
    def _():
        cross_wait(x)

    unit(near, (x,), True)
    share_far(partner)
    norms(x)
    for t in (0, 1):
        noise_wait(mate, t, False)
    far_wait(mate)
    unit(near, (mate,), False)
    norms(mate)

    def beside(t, h, c):
        return data_copy(1, (5 if h == 0 else 13) + t, along_y(-HOP[t], c), h * half_cols, half_cols, sibling)

    for t in (0, 1):
        partner_wait(t, 0)
        begin(beside(t, 0, core))
    unit(near, (partner,), False)
    norms(partner)
    data_wait(1, 4, along_y(0, 1 - core), 0, full_cols)
    for t in (0, 1):
        beside(t, 0, 1 - core).wait_recv()

    def ahead(i, carry):
        xi = around(y + i + i // 2)
        add_unit(other_block, jnp.where(xi == opposite, 0, jnp.where(i == 0, 4, 2)), xi)
        return carry

    lax.fori_loop(0, 3, ahead, 0)
    for t in (0, 1):
        partner_wait(t, 1)
        begin(beside(t, 1, core))
    for t in (0, 1):
        noise_wait(opposite, t, False)
    far_wait(opposite)
    for t in (0, 1):
        far_data(t, 1 - side).wait_recv()
        begin(data_copy(1, 7 + t, along_y(2, core), t * half_cols, half_cols, sibling))
    norms(opposite)

    factor = 2.0 * kappa / width

    def row_shift(r, carry):
        at = pl.ds(pl.multiple_of(r * 128, 128), 128)
        total = jnp.sum(part[at, :], axis=1, keepdims=True) * (-kappa / width)
        shift[at, :] = jnp.broadcast_to(total, (128, LANES))
        return carry

    lax.fori_loop(0, rows // 128, row_shift, 0)

    def fold(block, op):
        out = block[0:8]
        for r in range(1, TILE // 8):
            out = op(out, block[8 * r:8 * r + 8])
        return out

    def spread_cols():
        for c in range(chunks):
            colvec[:, lane(c)] = jnp.broadcast_to(colpack[pl.ds(c, 1), :], (8, LANES))

    def tall(ref, c):
        return jnp.concatenate([ref[:, lane(c)]] * (TILE // 8), axis=0)

    def tile_at(t):
        return pl.ds(pl.multiple_of(t * TILE, TILE), TILE)

    def loop(body, init):
        return lax.fori_loop(0, tiles, body, init, unroll=2)

    def first_sums(block):
        count = chunks // 2
        cuts = [pl.ds(pl.multiple_of(block * 256 + c * LANES, LANES), LANES) for c in range(count)]

        def top_step(t, accs):
            at = tile_at(t)
            add = shift[at, :]
            out = []
            for c in range(count):
                value = scores[at, cuts[c]] * factor
                scores[at, cuts[c]] = value
                out.append(jnp.maximum(accs[c], fold(value + add, jnp.maximum)))
            return tuple(out)

        tops = loop(top_step, tuple(jnp.full((8, LANES), -jnp.inf, jnp.float32) for _ in range(count)))
        for c in range(count):
            colvec[:, cuts[c]] = jnp.broadcast_to(jnp.max(tops[c], axis=0, keepdims=True), (8, LANES))

        def exp_step(t, accs):
            at = tile_at(t)
            add = shift[at, :]
            return tuple(
                accs[c] + fold(
                    jnp.exp2(scores[at, cuts[c]] + add - jnp.concatenate([colvec[:, cuts[c]]] * (TILE // 8), axis=0)),
                    jnp.add,
                )
                for c in range(count)
            )

        sums = loop(exp_step, tuple(jnp.zeros((8, LANES), jnp.float32) for _ in range(count)))
        for c in range(count):
            total = jnp.sum(sums[c], axis=0, keepdims=True)
            col_buf[0, me_col, pl.ds(2 * block + c, 1), :] = colvec[0:1, cuts[c]] + jnp.log(total) * LOG2E

    add_unit(near, 4, opposite)
    add_unit(other_block, jnp.where(opposite == y, 4, jnp.where(opposite == around(y + 2), 0, 2)), opposite)
    for t in (0, 1):
        beside(t, 1, 1 - core).wait_recv()
    unit(other_block + 2, (around(y + 1), around(y - 1)), False, 2)
    first_sums(near)
    for t in (0, 1):
        data_wait(1, 7 + t, along_y(2, 1 - core), t * half_cols, half_cols)
    add_unit(other_block, 4, around(y + 2))
    first_sums(other_block)

    zeros = tuple(jnp.zeros((8, LANES), jnp.float32) for _ in range(chunks))

    exchange(col_buf, col_send, col_recv, 0, me_col, col_peers, started)
    col_pot = -log_cols - combine(col_buf, 0, csize)
    colpack[...] = col_pot
    spread_cols()

    def row_step(t, carry):
        at = tile_at(t)
        top = scores[at, lane(0)] + tall(colvec, 0)
        for c in range(1, chunks):
            top = jnp.maximum(top, scores[at, lane(c)] + tall(colvec, c))
        first[at, :] = top
        total = None
        for c in range(chunks):
            value = jnp.exp2(scores[at, lane(c)] + tall(colvec, c) - top)
            scores[at, lane(c)] = value
            total = value if total is None else total + value
        part[at, :] = total
        return carry

    loop(row_step, 0)
    for b in range(row_blocks):
        at = pl.ds(b * LANES, LANES)
        tops = first[at, :].T
        top = jnp.max(tops, axis=0, keepdims=True)
        total = jnp.sum(part[at, :].T * jnp.exp2(tops - top), axis=0, keepdims=True)
        row_buf[0, me_row, pl.ds(b, 1), :] = top + jnp.log(total) * LOG2E
    exchange(row_buf, row_send, row_recv, 0, me_row, row_peers, started)
    row_lse = combine(row_buf, 0, rsize)
    rowpack[...] = row_lse
    for b in range(row_blocks):
        at = pl.ds(b * LANES, LANES)
        base = jnp.exp2(first[at, :] - spread_lanes(rowpack, b))
        first[at, :] = base
        scale[at, :] = base

    def col_step(t, accs):
        at = tile_at(t)
        mul = scale[at, :]
        return tuple(accs[c] + fold(scores[at, lane(c)] * mul, jnp.add) for c in range(chunks))

    def sum_step(keep_values):
        def body(t, carry):
            at = tile_at(t)
            total = None
            for c in range(chunks):
                value = scores[at, lane(c)] * tall(colvec, c)
                if keep_values:
                    scores[at, lane(c)] = value
                total = value if total is None else total + value
            part[at, :] = total * first[at, :]
            return carry

        return body

    for step in range(1, ITERS):
        sums = loop(col_step, zeros)
        for c in range(chunks):
            col_buf[step, me_col, pl.ds(c, 1), :] = jnp.sum(sums[c], axis=0, keepdims=True)
        exchange(col_buf, col_send, col_recv, step, me_col, col_peers, started)
        ratio = 1.0 / add_slots(col_buf, step, csize)
        colpack[...] = ratio
        spread_cols()
        loop(sum_step(step == ITERS - 1), 0)
        for b in range(row_blocks):
            at = pl.ds(b * LANES, LANES)
            row_buf[step, me_row, pl.ds(b, 1), :] = jnp.sum(part[at, :].T, axis=0, keepdims=True)
        exchange(row_buf, row_send, row_recv, step, me_row, row_peers, started)
        total = add_slots(row_buf, step, rsize)
        rowpack[...] = 1.0 / total
        for b in range(row_blocks):
            at = pl.ds(b * LANES, LANES)
            scale[at, :] = first[at, :] * spread_lanes(rowpack, b)

    def weigh(r):
        def body(t, carry):
            at = pl.ds(pl.multiple_of(r * (rows // 2) + t * TILE, TILE), TILE)
            mul = scale[at, :]
            for c in range(chunks):
                weights[at, lane(c)] = (scores[at, lane(c)] * mul).astype(jnp.bfloat16)
            return carry

        lax.fori_loop(0, tiles // 2, body, 0, unroll=2)

    def swap_copy(i, to):
        return remote(swap.at[0], swap.at[i], swap_send.at[i], swap_recv.at[i], to)

    def potentials():
        for c in range(chunks):
            sqy[pl.ds(c, 1), :] = jnp.sum(data_part[pl.ds(c * LANES, LANES), :].T, axis=0, keepdims=True)
        cols_pot = (col_pot + jnp.log(ratio) * LOG2E + (log_rows - log_cols)) / kappa + sqy[...] / width
        colpack[...] = cols_pot
        cols_out[...] = colpack[pl.ds(pl.multiple_of(side * 8, 8), 8), :]
        for b in range(row_blocks):
            sqx[pl.ds(b, 1), :] = shift[pl.ds(b * LANES, LANES), :].T[0:1]
        swap[0] = -(log_rows + row_lse + jnp.log(total) * LOG2E + sqx[...]) / kappa
        begin(swap_copy(1, sibling))
        for i in (0, 1):
            begin(remote(
                swap.at[0], swap.at[2 + core], swap_send.at[2 + i], swap_recv.at[2 + core], device(partner, y, z, i)
            ))

    strip = rows // 2

    def half_rows(r):
        return pl.ds(pl.multiple_of(r * strip, strip), strip)

    def block_x(b):
        return jnp.where(b < 2, jnp.where(b == 0, opposite, mate), jnp.where(b == 2, partner, x))

    def product(p, r, to_z):
        cut = pl.ds(pl.multiple_of(to_z * LANES, LANES), LANES)
        total = None
        for k in (0, 1):
            block = jnp.concatenate(
                [data_all[k, block_x(2 * p + e), :, cut] for e in (0, 1)], axis=1
            )
            value = jnp.dot(
                weights[half_rows(r), k * full_cols:(k + 1) * full_cols], block,
                preferred_element_type=jnp.float32,
            )
            total = value if total is None else total + value
        return total

    def hop(t):
        return 1 - 2 * t

    def sum_copy(b, t, index, src, dst):
        to = device(x, y, around(z + hop(t)), core)
        return remote(src, dst, sum_send.at[b, t, index], sum_recv.at[b, t, index], to)

    def far_copy(b, t):
        return sum_copy(b, t, 0, out_buf.at[b, 2, half_rows(t)], far_buf.at[b - 2, t])

    def direct_copy(b, t):
        at = half_rows(1 - t)
        return sum_copy(b, t, 1, out_buf.at[b, t, at], near_buf.at[b, t, at])

    def added_copy(b, t):
        at = half_rows(t)
        return sum_copy(b, t, 2, out_buf.at[b, t, at], near_buf.at[b, t, at])

    def give_copy(b, r):
        at = half_rows(r)
        return remote(
            out_buf.at[b, 2, at], given.at[b, at], give_send.at[b, r], give_recv.at[b, r], device(mate, y, z, core)
        )

    def relay_copy(r):
        at = half_rows(r)
        return remote(own_buf.at[0, at], relay_in.at[at], in_send.at[r], in_recv.at[4 + r], device(mate, y, z, core))

    def partner_copy(a, r):
        at = half_rows(r)
        return remote(
            own_buf.at[2, at], in_sum.at[a, at], in_send.at[2 + r], part_recv.at[a, r], device(partner, y, z, kind)
        )

    def mate_copy(a):
        return remote(mate_out, mate_in.at[a], in_send.at[4], in_recv.at[2 + a], device(mate, y, z, kind))

    def stay_copy(a):
        return remote(own_buf.at[3], in_sum.at[a], in_send.at[5], in_recv.at[a], sibling)

    def add_far(b):
        for t in (0, 1):
            far_copy(b, t).wait_recv()
            out_buf[b, t, half_rows(t), :] = (
                keep[b - 2, t] + far_buf[b - 2, t].astype(jnp.float32)
            ).astype(jnp.bfloat16)
            added_copy(b, t).start()

    def add_near(b):
        for t in (0, 1):
            direct_copy(b, t).wait_recv()
            added_copy(b, t).wait_recv()
        own_buf[b] = own_buf[b] + near_buf[b, 0].astype(jnp.float32) + near_buf[b, 1].astype(jnp.float32)

    def add_given(b):
        for r in (0, 1):
            at = half_rows(r)
            give_copy(b - 2, r).wait_recv()
            out_buf[b, 2, at, :] = (far_keep[b - 2, at, :] + given[b - 2, at, :].astype(jnp.float32)).astype(jnp.bfloat16)
            far_copy(b, r).start()

    def halves(body):
        def step(r, carry):
            body(r)
            return carry

        lax.fori_loop(0, 2, step, 0)

    def lead(r):
        t = 1 - r
        weigh(r)
        value = product(1, r, around(z + hop(t)))
        for e in (0, 1):
            out_buf[2 + e, t, half_rows(r), :] = value[:, lane(e)].astype(jnp.bfloat16)
        direct_copy(2, t).start()

    def give(r):
        value = product(0, r, around(z + 2))
        for e in (0, 1):
            out_buf[e, 2, half_rows(r), :] = value[:, lane(e)].astype(jnp.bfloat16)
        give_copy(0, r).start()

    def next_products(t):
        def part_of(r):
            value = product(0, r, around(z + hop(t)))
            for e in (0, 1):
                out_buf[e, t, half_rows(r), :] = value[:, lane(e)].astype(jnp.bfloat16)

        halves(part_of)
        direct_copy(0, t).start()
        added_copy(0, t).start()

    def kept_products(t):
        value = product(1, t, around(z + hop(t)))
        for e in (0, 1):
            keep[e, t] = value[:, lane(e)]

    def far_products(r):
        value = product(1, r, around(z + 2))
        for e in (0, 1):
            far_keep[e, half_rows(r), :] = value[:, lane(e)]

    def own_products(p):
        def part_of(r):
            value = product(p, r, z)
            for e in (0, 1):
                own_buf[2 * p + e, half_rows(r), :] = value[:, lane(e)]

        halves(part_of)

    halves(lead)
    halves(give)
    for r in (0, 1):
        give_copy(1, r).start()
    halves(next_products)
    halves(far_products)
    add_given(2)
    for t in (0, 1):
        direct_copy(1, t).start()
    halves(kept_products)
    halves(own_products)
    add_near(0)
    for r in (0, 1):
        relay_copy(r).start()
    add_far(2)
    for t in (0, 1):
        added_copy(1, t).start()
    add_given(3)
    for t in (0, 1):
        direct_copy(3, t).start()
    add_near(2)

    def to_partner(r):
        relay_copy(r).wait_recv()
        own_buf[2, half_rows(r), :] = own_buf[2, half_rows(r), :] + relay_in[half_rows(r), :]
        partner_copy(core, r).start()

    to_partner(0)
    add_near(1)
    mate_out[...] = own_buf[1].astype(jnp.bfloat16)
    mate_copy(core).start()
    potentials()
    for copy in started:
        copy.wait_send()

    @pl.when(home)
    def _():
        aside.wait_send()
        for t in (0, 1):
            for a in (0, 1):
                own_round(t, a).wait_send()

    add_far(3)
    to_partner(1)

    def settle(b, carry):
        for t in (0, 1):
            direct_copy(b, t).wait_send()
            added_copy(b, t).wait_send()

            @pl.when(b < 2)
            def _():
                give_copy(jnp.minimum(b, 1), t).wait_send()

            @pl.when(b >= 2)
            def _():
                far_copy(jnp.maximum(b, 2), t).wait_send()

        return carry

    lax.fori_loop(0, 3, settle, 0)
    for r in (0, 1):
        relay_copy(r).wait_send()
    swap_copy(1, sibling).wait_recv()
    for i in (0, 1):
        remote(swap.at[0], swap.at[2 + i], swap_send.at[2 + i], swap_recv.at[2 + i], sibling).wait_recv()
    half = rows // LANES
    for a in (0, 1):
        mine_row = jnp.where(core == a, swap[0], swap[1])
        rows_out[pl.ds(a * half, half), :] = jnp.where(home, mine_row, swap[2 + a])

    add_near(3)

    @pl.when(home)
    def _():
        in_sum[core] = own_buf[3]
        stay_copy(1 - core).wait_recv()
        for a in (0, 1):
            mate_copy(a).wait_recv()
            in_sum[a] = in_sum[a] + mate_in[a].astype(jnp.float32)

    @pl.when(jnp.logical_not(home))
    def _():
        stay_copy(core).start()
        for a in (0, 1):
            for r in (0, 1):
                partner_copy(a, r).wait_recv()

    def result_copy(a):
        return pltpu.make_async_copy(in_sum.at[a], targets.at[pl.ds(a * rows, rows)], local_sems.at[a])

    for a in (0, 1):
        result_copy(a).start()

    settle(3, 0)
    for a in (0, 1):
        result_copy(a).wait()
    for r in (0, 1):
        partner_copy(core, r).wait_send()
    mate_copy(core).wait_send()

    @pl.when(jnp.logical_not(home))
    def _():
        stay_copy(core).wait_send()


def hand_on(targets, rows_pot, cols_pot, targets_out, rows_out, cols_out, stage, row_stage, col_stage, sems):
    size = targets.shape[0] // PARTS
    legs = [
        (targets.at[pl.ds(i * size, size)], stage.at[i], targets_out.at[pl.ds(i * size, size)]) for i in range(PARTS)
    ]
    legs += [(rows_pot, row_stage, rows_out), (cols_pot, col_stage, cols_out)]
    first = [pltpu.make_async_copy(src, mid, sems.at[i, 0]) for i, (src, mid, _) in enumerate(legs)]
    second = [pltpu.make_async_copy(mid, dst, sems.at[i, 1]) for i, (_, mid, dst) in enumerate(legs)]
    for copy in first:
        copy.start()
    for before, copy in zip(first, second):
        before.wait()
        copy.start()
    for copy in second:
        copy.wait()


def shards(noise_latents, data_latents):
    nsize = lax.axis_size("noise")
    dsize = lax.axis_size("dp")
    block, piece = noise_latents.shape
    rows, cols = block // 2, 2 * data_latents.shape[0]
    rsize, csize = dsize // 2, nsize * 2
    vmem = pl.BlockSpec(memory_space=pltpu.VMEM)
    f32, bf16 = jnp.float32, jnp.bfloat16
    strip = rows // 2
    row_vec, col_vec = (rows // LANES, LANES), (cols // LANES, LANES)
    sems = pltpu.SemaphoreType.DMA
    targets, rows_pot, cols_pot = pl.pallas_call(
        functools.partial(kernel, rsize, csize, piece * dsize),
        out_shape=(
            jax.ShapeDtypeStruct((block, piece), f32),
            jax.ShapeDtypeStruct((block // LANES, LANES), f32),
            jax.ShapeDtypeStruct((cols // 2 // LANES, LANES), f32),
        ),
        in_specs=[pl.BlockSpec(memory_space=pl.ANY)] * 2,
        out_specs=(pl.BlockSpec(memory_space=pl.ANY), vmem, vmem),
        scratch_shapes=[
            pltpu.VMEM((SIDE, rows, SIDE * piece), bf16),
            pltpu.VMEM((2, SIDE, cols // 2, nsize // SIDE * data_latents.shape[1]), bf16),
            pltpu.VMEM((rows, cols), f32),
            pltpu.VMEM((rows, cols), bf16),
            pltpu.VMEM((rows, LANES), f32),
            pltpu.VMEM((rows, LANES), f32),
            pltpu.VMEM((rows, LANES), f32),
            pltpu.VMEM((rows, LANES), f32),
            pltpu.VMEM((cols, LANES), f32),
            pltpu.VMEM((8, cols), f32),
            pltpu.VMEM(row_vec, f32),
            pltpu.VMEM(col_vec, f32),
            pltpu.VMEM(row_vec, f32),
            pltpu.VMEM(col_vec, f32),
            pltpu.VMEM((4,) + row_vec, f32),
            pltpu.VMEM((ITERS, csize) + col_vec, f32),
            pltpu.VMEM((ITERS, rsize) + row_vec, f32),
            pltpu.VMEM((SIDE, 3, rows, LANES), bf16),
            pltpu.VMEM((SIDE, rows, LANES), f32),
            pltpu.VMEM((2, 2, strip, LANES), bf16),
            pltpu.VMEM((SIDE, 2, rows, LANES), bf16),
            pltpu.VMEM((2, rows, LANES), f32),
            sems((ITERS,)),
            sems((ITERS,)),
            sems((ITERS,)),
            sems((ITERS,)),
            sems((4,)),
            sems((4,)),
            sems((4,)),
            sems((4,)),
            sems((SIDE, 2, 2)),
            sems((SIDE, 2, 2)),
            sems((2, 15)),
            sems((2, 15)),
            sems((SIDE, 2, 3)),
            sems((SIDE, 2, 3)),
            sems((6,)),
            sems((6,)),
            pltpu.VMEM((2, 2, strip, LANES), f32),
            pltpu.VMEM((2, rows, LANES), f32),
            pltpu.VMEM((2, rows, LANES), bf16),
            sems((2, 2)),
            sems((2, 2)),
            sems((2, 2)),
            sems((2,)),
            sems((2, 2)),
            sems((SIDE, 2)),
            pltpu.VMEM((rows, LANES), f32),
            pltpu.VMEM((rows, LANES), bf16),
            pltpu.VMEM((2, rows, LANES), bf16),
        ],
        compiler_params=pltpu.CompilerParams(
            collective_id=0, has_side_effects=True, vmem_limit_bytes=60 * 2**20
        ),
    )(noise_latents, data_latents)
    results = (targets, rows_pot, cols_pot)
    targets, rows_pot, cols_pot = pl.pallas_call(
        hand_on,
        out_shape=tuple(jax.ShapeDtypeStruct(a.shape, a.dtype) for a in results),
        in_specs=[pl.BlockSpec(memory_space=pl.ANY)] * 3,
        out_specs=(pl.BlockSpec(memory_space=pl.ANY),) * 3,
        scratch_shapes=[
            pltpu.VMEM((PARTS, block // PARTS, piece), f32),
            pltpu.VMEM(rows_pot.shape, f32),
            pltpu.VMEM(cols_pot.shape, f32),
            sems((PARTS + 2, 2)),
        ],
        compiler_params=pltpu.CompilerParams(vmem_limit_bytes=60 * 2**20),
    )(*results)
    return targets, rows_pot.reshape(block), cols_pot.reshape(cols // 2)


def solution(mesh):
    return jax.shard_map(
        shards,
        mesh=mesh,
        in_specs=(P("noise", "dp"), P("dp", "noise")),
        out_specs=(P("noise", "dp"), P("noise"), P("dp")),
        check_vma=False,
    )
```

```python
import functools
import math

import jax
import jax.numpy as jnp
from jax import lax
from jax.experimental import pallas as pl
from jax.experimental.pallas import tpu as pltpu
from jax.sharding import PartitionSpec as P

ITERS = 3
EPSILON = 0.04
LOG2E = 1.0 / math.log(2.0)
MESH = pl.DeviceIdType.MESH
LANES = 128
TILE = 32
SHORT = 16
TALL = 64
SIDE = 4
PARTS = 4


def spread_lanes(ref, row):
    return jnp.broadcast_to(ref[pl.ds(row, 1), :], (LANES, LANES)).T


def exchange(buf, send, recv, step, me, peers, started):
    for peer in peers:
        pltpu.make_async_remote_copy(
            src_ref=buf.at[step, me],
            dst_ref=buf.at[step, me],
            send_sem=send.at[step],
            recv_sem=recv.at[step],
            device_id=peer,
            device_id_type=MESH,
        ).start()
    slots = buf.at[step, pl.ds(0, len(peers))]
    every = pltpu.make_async_remote_copy(
        src_ref=slots,
        dst_ref=slots,
        send_sem=send.at[step],
        recv_sem=recv.at[step],
        device_id=peers[0],
        device_id_type=MESH,
    )
    every.wait_recv()
    started.append(every)


def combine(buf, step, size):
    top = buf[step, 0]
    for s in range(1, size):
        top = jnp.maximum(top, buf[step, s])
    total = jnp.exp2(buf[step, 0] - top)
    for s in range(1, size):
        total = total + jnp.exp2(buf[step, s] - top)
    return top + jnp.log(total) * LOG2E


def add_slots(buf, step, size):
    total = buf[step, 0]
    for s in range(1, size):
        total = total + buf[step, s]
    return total


def kernel(
    rsize, csize, width,
    noise_ref, data_ref,
    targets, rows_out, cols_out,
    noise_all, data_all, scores, weights,
    shift, first, scale, part, data_part, colvec, rowpack, colpack, sqx, sqy, swap,
    col_buf, row_buf, out_buf, own_buf, far_buf, near_buf, in_sum,
    col_send, col_recv, row_send, row_recv, swap_send, swap_recv,
    cross_send, cross_recv, noise_send, noise_recv, data_send, data_recv,
    sum_send, sum_recv, in_send, in_recv, keep, far_keep, given, give_send, give_recv, part_recv, local_sems, own_send, far_send, relay_in, mate_out, mate_in,
):
    rows, cols = scores.shape
    n = lax.axis_index("noise")
    d = lax.axis_index("dp")
    x, z = d // SIDE, lax.rem(d, SIDE)
    y, core = n // 2, lax.rem(n, 2)
    kind = lax.rem((x + 1) // 2, 2)
    pair = x // 2
    side = lax.rem(x, 2)
    home = core == kind
    kappa = LOG2E / EPSILON
    log_rows = math.log2(rows * csize)
    log_cols = math.log2(cols * rsize)
    chunks = cols // LANES
    row_blocks = rows // LANES
    tiles = rows // TILE
    started = []

    def around(value):
        return lax.rem(value + SIDE, SIDE)

    def device(xi, yi, zi, ci):
        return (yi * 2 + ci, xi * SIDE + zi)

    me_row = pair * SIDE + z
    me_col = y * 4 + kind * 2 + core

    sibling = device(x, y, z, 1 - core)
    partner = x + 1 - 2 * side
    mate = SIDE - 1 - x
    opposite = around(x + 2)

    barrier = pltpu.get_barrier_semaphore()
    ys, zs = [around(y + k) for k in range(SIDE)], [around(z + k) for k in range(SIDE)]
    rings = [yi * 2 + ci for yi in (ys[2], ys[1], ys[3], ys[0]) for ci in (1 - core, core)]
    col_peers = [(r, di) for di in (partner * SIDE + z, d) for r in rings][:-1]
    row_peers = [(n, xi * SIDE + zi) for xi in (mate, x) for zi in (zs[2], zs[1], zs[3], zs[0])][:-1]
    greeted = [sibling]
    for ci in (0, 1):
        greeted += [device(partner, y, z, ci), device(mate, y, z, ci), device(x, y, zs[1], ci), device(x, y, zs[3], ci)]
    greeted += [device(x, ys[1], z, core), device(x, ys[3], z, core)]
    for to in greeted:
        pl.semaphore_signal(barrier, inc=1, device_id=to, device_id_type=MESH)
    pl.semaphore_wait(barrier, len(greeted))

    def remote(src, dst, send, recv, to):
        return pltpu.make_async_remote_copy(
            src_ref=src, dst_ref=dst, send_sem=send, recv_sem=recv, device_id=to, device_id_type=MESH
        )

    def begin(copy):
        copy.start()
        started.append(copy)

    def lane(c):
        return slice(LANES * c, LANES * (c + 1))

    HOP = (1, -1)

    def noise_slot(xi, zi, at):
        return noise_all.at[xi, at, pl.ds(pl.multiple_of(zi * LANES, LANES), LANES)]

    own = noise_slot(x, z, pl.ds(0, rows))

    def cross_copy(i, half, to):
        return remote(
            noise_ref.at[pl.ds(half * rows, rows)], own, cross_send.at[i], cross_recv.at[x], to
        )

    def cross_wait(xi):
        remote(
            noise_ref.at[pl.ds(0, rows)], noise_slot(xi, z, pl.ds(0, rows)), cross_send.at[0], cross_recv.at[xi], sibling
        ).wait_recv()

    there = jnp.where(home, mate, partner)
    aside = cross_copy(2, 1 - core, sibling)

    def noise_copy(xi, t, forward, zi):
        at = pl.ds(t * (rows // 2), rows // 2) if forward else pl.ds(0, rows)
        f = int(forward)
        slot = noise_slot(xi, zi, at)
        return remote(
            slot, slot, noise_send.at[xi, t, f], noise_recv.at[xi, t, f], device(x, y, around(z + HOP[t]), core)
        )

    def noise_wait(xi, t, forward):
        zi = around(z - HOP[t] * (2 if forward else 1))
        noise_copy(xi, t, forward, zi).wait_recv()
        return zi

    def data_slot(block, where, at):
        width_at = pl.ds(pl.multiple_of(lax.rem(where, 2) * 256, 256), 256)
        return data_all.at[block, where // 2, at, width_at]

    def data_copy(r, index, where, lo, size, to, own=False):
        at = pl.ds(lo, size)
        block = side if r == 0 else 1 - side
        dst = data_slot(block, where, at)
        return remote(data_ref.at[at] if own else dst, dst, data_send.at[r, index], data_recv.at[r, index], to)

    half_cols = cols // 4
    full_cols = cols // 2

    def along_y(step, c):
        return around(y + step) * 2 + c

    def data_wait(r, index, where, lo, size):
        data_copy(r, index, where, lo, size, sibling).wait_recv()

    HALF = 9

    def cross_data(h, own=False):
        at = pl.ds(h * half_cols, half_cols)
        dst = data_slot(side if own else 1 - side, n, at)
        return remote(
            data_ref.at[at], dst, data_send.at[1, 11 + h], data_recv.at[1, 11 + h], device(partner, y, z, core)
        )

    def partner_y(t, h, back=0):
        where = around(y + back) * 2 + core
        to = device(x, around(y + HOP[t]), z, core)
        return t if h == 0 else HALF + t, where, h * half_cols, half_cols, to

    def partner_wait(t, h):
        data_copy(1, *partner_y(t, h, -HOP[t])).wait_recv()

    def own_round(t, a):
        return remote(
            noise_ref.at[pl.ds(a * rows, rows)], own,
            own_send.at[t, a], noise_recv.at[x, t, 0], device(x, y, around(z + HOP[t]), a),
        )

    def own_half():
        return pltpu.make_async_copy(
            noise_ref.at[pl.ds(pl.multiple_of(core * rows, rows), rows)], own, local_sems.at[0]
        )

    @pl.when(home)
    def _():
        for t in (0, 1):
            for a in (0, 1):
                own_round(t, a).start()
        aside.start()

    begin(cross_copy(0, 0, device(there, y, z, 0)))
    begin(cross_copy(1, 1, device(there, y, z, 1)))
    for t in (0, 1):
        begin(data_copy(0, t, n, 0, full_cols, device(x, around(y + HOP[t]), z, core), own=True))
    @pl.when(home)
    def _():
        own_half().start()

    data_own = pltpu.make_async_copy(data_ref, data_slot(side, n, pl.ds(0, full_cols)), local_sems.at[1])
    data_own.start()
    scores[...] = jnp.zeros_like(scores)
    part[...] = jnp.zeros_like(part)
    data_part[...] = jnp.zeros_like(data_part)

    def round_z(xi):
        for t in (0, 1):
            begin(noise_copy(xi, t, False, z))

    def forward_z(xi):
        for t in (0, 1):
            begin(noise_copy(xi, t, True, noise_wait(xi, t, False)))

    def far_noise(xi, t):
        slot = noise_slot(xi, around(z + 2), pl.ds(t * (rows // 2), rows // 2))
        return remote(slot, slot, far_send.at[xi, t], noise_recv.at[xi, t, 1], device(mate, y, z, core))

    def share_far(xi):
        for t in (0, 1):
            noise_wait(xi, t, True)
            begin(far_noise(xi, t))

    def far_wait(xi):
        for t in (0, 1):
            far_noise(xi, t).wait_recv()

    def far_data(t, block):
        where = along_y(2, core)
        at = pl.ds(t * half_cols, half_cols)
        dst = data_slot(block, where, at)
        return remote(dst, dst, data_send.at[1, 2 + t], data_recv.at[1, 2 + t], device(partner, y, z, core))

    cross_wait(partner)
    slot = noise_slot(partner, z, pl.ds(0, rows))
    begin(remote(slot, slot, cross_send.at[3], cross_recv.at[partner], device(mate, y, z, core)))
    round_z(partner)
    for h in (0, 1):
        begin(cross_data(h, own=True))
    begin(data_copy(0, 4, n, 0, full_cols, sibling, own=True))
    forward_z(x)
    cross_wait(mate)
    round_z(mate)
    for t in (0, 1):
        where = along_y(-HOP[t], core)
        data_wait(0, t, where, 0, full_cols)
        begin(data_copy(0, 2 + t, where, t * half_cols, half_cols, device(x, around(y + HOP[t]), z, core)))
        begin(data_copy(0, 5 + t, where, 0, full_cols, sibling))
    cross_data(0).wait_recv()
    for t in (0, 1):
        begin(data_copy(1, *partner_y(t, 0)))
    forward_z(partner)
    cross_wait(opposite)
    round_z(opposite)
    share_far(x)
    cross_data(1).wait_recv()
    for t in (0, 1):
        begin(data_copy(1, *partner_y(t, 1)))
    begin(data_copy(1, 4, n, 0, full_cols, sibling))
    for t in (0, 1):
        where = along_y(2, core)
        data_wait(0, 2 + t, where, t * half_cols, half_cols)
        begin(far_data(t, side))
        begin(data_copy(0, 7 + t, where, t * half_cols, half_cols, sibling))

    def squares(block):
        value = block.astype(jnp.float32)
        return value * value

    def chunk_product(xi, m):
        cut = pl.ds(pl.multiple_of(m * 256, 256), 256)
        here = pl.ds(pl.multiple_of(lax.rem(m, 4) * 256, 256), 256)
        total = data_part[cut, :]
        for i in range(SIDE):
            total = total + squares(data_all[m // 4, xi, here, lane(i)])
        data_part[cut, :] = total
        return lax.dot_general(
            noise_all[xi], data_all[m // 4, xi, here, :], (((1,), (1,)), ((), ())),
            preferred_element_type=jnp.float32,
        )

    def norms(xi):
        def norm(r, carry):
            cut = pl.ds(pl.multiple_of(r * 64, 64), 64)
            total = part[cut, :]
            for i in range(SIDE):
                total = total + squares(noise_all[xi, cut, lane(i)])
            part[cut, :] = total
            return carry

        lax.fori_loop(0, rows // 64, norm, 0)

    near, other_block = side * 4, 4 - side * 4

    def unit(block, xs, fresh, count=4):
        def column(i, carry):
            m = block + i
            cut = pl.ds(pl.multiple_of(m * 256, 256), 256)
            value = None if fresh else scores[:, cut]
            for xi in xs:
                value = chunk_product(xi, m) if value is None else value + chunk_product(xi, m)
            scores[:, cut] = value
            return carry

        lax.fori_loop(0, count, column, 0)

    def add_unit(block, count, xi):
        unit(block, (xi,), False, count)

    data_own.wait()
    data_wait(0, 4, along_y(0, 1 - core), 0, full_cols)
    for t in (0, 1):
        data_wait(0, 5 + t, along_y(-HOP[t], 1 - core), 0, full_cols)
    for t in (0, 1):
        data_wait(0, 7 + t, along_y(2, 1 - core), t * half_cols, half_cols)

    @pl.when(home)
    def _():
        own_half().wait()

    @pl.when(jnp.logical_not(home))
    def _():
        cross_wait(x)

    unit(near, (x,), True)
    share_far(partner)
    norms(x)
    for t in (0, 1):
        noise_wait(mate, t, False)
    far_wait(mate)
    unit(near, (mate,), False)
    norms(mate)

    def beside(t, h, c):
        return data_copy(1, (5 if h == 0 else 13) + t, along_y(-HOP[t], c), h * half_cols, half_cols, sibling)

    for t in (0, 1):
        partner_wait(t, 0)
        begin(beside(t, 0, core))
    unit(near, (partner,), False)
    norms(partner)
    data_wait(1, 4, along_y(0, 1 - core), 0, full_cols)
    for t in (0, 1):
        beside(t, 0, 1 - core).wait_recv()

    def ahead(i, carry):
        xi = around(y + i + i // 2)
        add_unit(other_block, jnp.where(xi == opposite, 0, jnp.where(i == 0, 4, 2)), xi)
        return carry

    lax.fori_loop(0, 3, ahead, 0)
    for t in (0, 1):
        partner_wait(t, 1)
        begin(beside(t, 1, core))
    for t in (0, 1):
        noise_wait(opposite, t, False)
    far_wait(opposite)
    for t in (0, 1):
        far_data(t, 1 - side).wait_recv()
        begin(data_copy(1, 7 + t, along_y(2, core), t * half_cols, half_cols, sibling))
    norms(opposite)

    factor = 2.0 * kappa / width

    def row_shift(r, carry):
        at = pl.ds(pl.multiple_of(r * 128, 128), 128)
        total = jnp.sum(part[at, :], axis=1, keepdims=True) * (-kappa / width)
        shift[at, :] = jnp.broadcast_to(total, (128, LANES))
        return carry

    lax.fori_loop(0, rows // 128, row_shift, 0)

    def final(block, xi):
        def column(i, carry):
            m = block + i
            cut = pl.ds(pl.multiple_of(m * 256, 256), 256)
            value = (scores[:, cut] + chunk_product(xi, m)) * factor
            scores[:, cut] = value
            for e in (0, 1):
                top = jnp.max(value[:, LANES * e:LANES * (e + 1)] + shift[...], axis=0, keepdims=True)
                colvec[:, pl.ds(pl.multiple_of(m * 256 + e * LANES, LANES), LANES)] = jnp.broadcast_to(top, (8, LANES))
            return carry

        lax.fori_loop(0, 4, column, 0)

    final(near, opposite)
    add_unit(other_block, jnp.where(opposite == y, 4, jnp.where(opposite == around(y + 2), 0, 2)), opposite)
    for t in (0, 1):
        beside(t, 1, 1 - core).wait_recv()
    unit(other_block + 2, (around(y + 1), around(y - 1)), False, 2)
    for t in (0, 1):
        data_wait(1, 7 + t, along_y(2, 1 - core), t * half_cols, half_cols)
    final(other_block, around(y + 2))

    def fold(block, op):
        out = block[0:8]
        for r in range(1, block.shape[0] // 8):
            out = op(out, block[8 * r:8 * r + 8])
        return out

    def spread_cols():
        for c in range(chunks):
            colvec[:, lane(c)] = jnp.broadcast_to(colpack[pl.ds(c, 1), :], (8, LANES))

    def tall(ref, c, size=TILE):
        return jnp.concatenate([ref[:, lane(c)]] * (size // 8), axis=0)

    def tile_at(t):
        return pl.ds(pl.multiple_of(t * TILE, TILE), TILE)

    def loop(body, init):
        return lax.fori_loop(0, tiles, body, init, unroll=2)

    zeros = tuple(jnp.zeros((8, LANES), jnp.float32) for _ in range(chunks))

    def exp_step(t, accs):
        at = pl.ds(pl.multiple_of(t * TALL, TALL), TALL)
        add = shift[at, :]
        return tuple(
            accs[c] + fold(jnp.exp2(scores[at, lane(c)] + add - tall(colvec, c, TALL)), jnp.add)
            for c in range(chunks)
        )

    sums = lax.fori_loop(0, rows // TALL, exp_step, zeros)
    for c in range(chunks):
        total = jnp.sum(sums[c], axis=0, keepdims=True)
        col_buf[0, me_col, pl.ds(c, 1), :] = colvec[0:1, lane(c)] + jnp.log(total) * LOG2E
    exchange(col_buf, col_send, col_recv, 0, me_col, col_peers, started)
    col_pot = -log_cols - combine(col_buf, 0, csize)
    colpack[...] = col_pot
    spread_cols()

    def row_step(t, carry):
        at = pl.ds(pl.multiple_of(t * SHORT, SHORT), SHORT)
        values = [
            scores[at, lane(c)] + jnp.concatenate([colvec[:, lane(c)]] * (SHORT // 8), axis=0) for c in range(chunks)
        ]
        top = values[0]
        for c in range(1, chunks):
            top = jnp.maximum(top, values[c])
        first[at, :] = top
        total = None
        for c in range(chunks):
            value = jnp.exp2(values[c] - top)
            scores[at, lane(c)] = value
            total = value if total is None else total + value
        part[at, :] = total
        return carry

    lax.fori_loop(0, rows // SHORT, row_step, 0, unroll=2)
    for b in range(row_blocks):
        at = pl.ds(b * LANES, LANES)
        tops = first[at, :].T
        top = jnp.max(tops, axis=0, keepdims=True)
        total = jnp.sum(part[at, :].T * jnp.exp2(tops - top), axis=0, keepdims=True)
        row_buf[0, me_row, pl.ds(b, 1), :] = top + jnp.log(total) * LOG2E
    exchange(row_buf, row_send, row_recv, 0, me_row, row_peers, started)
    row_lse = combine(row_buf, 0, rsize)
    rowpack[...] = row_lse
    for b in range(row_blocks):
        at = pl.ds(b * LANES, LANES)
        base = jnp.exp2(first[at, :] - spread_lanes(rowpack, b))
        first[at, :] = base
        scale[at, :] = base

    def col_step(t, accs):
        at = tile_at(t)
        mul = scale[at, :]
        return tuple(accs[c] + fold(scores[at, lane(c)] * mul, jnp.add) for c in range(chunks))

    def sum_step(keep_values):
        def body(t, carry):
            at = pl.ds(pl.multiple_of(t * TALL, TALL), TALL)
            total = None
            for c in range(chunks):
                value = scores[at, lane(c)] * tall(colvec, c, TALL)
                if keep_values:
                    scores[at, lane(c)] = value
                total = value if total is None else total + value
            part[at, :] = total * first[at, :]
            return carry

        return body

    for step in range(1, ITERS):
        sums = loop(col_step, zeros)
        for c in range(chunks):
            col_buf[step, me_col, pl.ds(c, 1), :] = jnp.sum(sums[c], axis=0, keepdims=True)
        exchange(col_buf, col_send, col_recv, step, me_col, col_peers, started)
        ratio = 1.0 / add_slots(col_buf, step, csize)
        colpack[...] = ratio
        spread_cols()
        lax.fori_loop(0, rows // TALL, sum_step(step == ITERS - 1), 0)
        for b in range(row_blocks):
            at = pl.ds(b * LANES, LANES)
            row_buf[step, me_row, pl.ds(b, 1), :] = jnp.sum(part[at, :].T, axis=0, keepdims=True)
        exchange(row_buf, row_send, row_recv, step, me_row, row_peers, started)
        total = add_slots(row_buf, step, rsize)
        rowpack[...] = 1.0 / total
        for b in range(row_blocks):
            at = pl.ds(b * LANES, LANES)
            scale[at, :] = first[at, :] * spread_lanes(rowpack, b)

    def weigh(r):
        def body(t, carry):
            at = pl.ds(pl.multiple_of(r * (rows // 2) + t * TILE, TILE), TILE)
            mul = scale[at, :]
            for c in range(chunks):
                weights[at, lane(c)] = (scores[at, lane(c)] * mul).astype(jnp.bfloat16)
            return carry

        lax.fori_loop(0, tiles // 2, body, 0, unroll=2)

    def swap_copy(i, to):
        return remote(swap.at[0], swap.at[i], swap_send.at[i], swap_recv.at[i], to)

    def potentials():
        for c in range(chunks):
            sqy[pl.ds(c, 1), :] = jnp.sum(data_part[pl.ds(c * LANES, LANES), :].T, axis=0, keepdims=True)
        cols_pot = (col_pot + jnp.log(ratio) * LOG2E + (log_rows - log_cols)) / kappa + sqy[...] / width
        colpack[...] = cols_pot
        cols_out[...] = colpack[pl.ds(pl.multiple_of(side * 8, 8), 8), :]
        for b in range(row_blocks):
            sqx[pl.ds(b, 1), :] = shift[pl.ds(b * LANES, LANES), :].T[0:1]
        swap[0] = -(log_rows + row_lse + jnp.log(total) * LOG2E + sqx[...]) / kappa
        begin(swap_copy(1, sibling))
        for i in (0, 1):
            begin(remote(
                swap.at[0], swap.at[2 + core], swap_send.at[2 + i], swap_recv.at[2 + core], device(partner, y, z, i)
            ))

    strip = rows // 2

    def half_rows(r):
        return pl.ds(pl.multiple_of(r * strip, strip), strip)

    def block_x(b):
        return jnp.where(b < 2, jnp.where(b == 0, opposite, mate), jnp.where(b == 2, partner, x))

    def product(p, r, to_z):
        cut = pl.ds(pl.multiple_of(to_z * LANES, LANES), LANES)
        total = None
        for k in (0, 1):
            block = jnp.concatenate(
                [data_all[k, block_x(2 * p + e), :, cut] for e in (0, 1)], axis=1
            )
            value = jnp.dot(
                weights[half_rows(r), k * full_cols:(k + 1) * full_cols], block,
                preferred_element_type=jnp.float32,
            )
            total = value if total is None else total + value
        return total

    def hop(t):
        return 1 - 2 * t

    def sum_copy(b, t, index, src, dst):
        to = device(x, y, around(z + hop(t)), core)
        return remote(src, dst, sum_send.at[b, t, index], sum_recv.at[b, t, index], to)

    def far_copy(b, t):
        return sum_copy(b, t, 0, out_buf.at[b, 2, half_rows(t)], far_buf.at[b - 2, t])

    def direct_copy(b, t):
        at = half_rows(1 - t)
        return sum_copy(b, t, 1, out_buf.at[b, t, at], near_buf.at[b, t, at])

    def added_copy(b, t):
        at = half_rows(t)
        return sum_copy(b, t, 2, out_buf.at[b, t, at], near_buf.at[b, t, at])

    def give_copy(b, r):
        at = half_rows(r)
        return remote(
            out_buf.at[b, 2, at], given.at[b, at], give_send.at[b, r], give_recv.at[b, r], device(mate, y, z, core)
        )

    def relay_copy(r):
        at = half_rows(r)
        return remote(own_buf.at[0, at], relay_in.at[at], in_send.at[r], in_recv.at[4 + r], device(mate, y, z, core))

    def partner_copy(a, r):
        at = half_rows(r)
        return remote(
            own_buf.at[2, at], in_sum.at[a, at], in_send.at[2 + r], part_recv.at[a, r], device(partner, y, z, kind)
        )

    def mate_copy(a):
        return remote(mate_out, mate_in.at[a], in_send.at[4], in_recv.at[2 + a], device(mate, y, z, kind))

    def stay_copy(a):
        return remote(own_buf.at[3], in_sum.at[a], in_send.at[5], in_recv.at[a], sibling)

    def add_far(b):
        for t in (0, 1):
            far_copy(b, t).wait_recv()
            out_buf[b, t, half_rows(t), :] = (
                keep[b - 2, t] + far_buf[b - 2, t].astype(jnp.float32)
            ).astype(jnp.bfloat16)
            added_copy(b, t).start()

    def add_near(b):
        for t in (0, 1):
            direct_copy(b, t).wait_recv()
            added_copy(b, t).wait_recv()
        own_buf[b] = own_buf[b] + near_buf[b, 0].astype(jnp.float32) + near_buf[b, 1].astype(jnp.float32)

    def add_given(b):
        for r in (0, 1):
            at = half_rows(r)
            give_copy(b - 2, r).wait_recv()
            out_buf[b, 2, at, :] = (far_keep[b - 2, at, :] + given[b - 2, at, :].astype(jnp.float32)).astype(jnp.bfloat16)
            far_copy(b, r).start()

    def halves(body):
        def step(r, carry):
            body(r)
            return carry

        lax.fori_loop(0, 2, step, 0)

    def lead(r):
        t = 1 - r
        weigh(r)
        value = product(1, r, around(z + hop(t)))
        for e in (0, 1):
            out_buf[2 + e, t, half_rows(r), :] = value[:, lane(e)].astype(jnp.bfloat16)
        direct_copy(2, t).start()

    def give(r):
        value = product(0, r, around(z + 2))
        for e in (0, 1):
            out_buf[e, 2, half_rows(r), :] = value[:, lane(e)].astype(jnp.bfloat16)
        give_copy(0, r).start()

    def next_products(t):
        def part_of(r):
            value = product(0, r, around(z + hop(t)))
            for e in (0, 1):
                out_buf[e, t, half_rows(r), :] = value[:, lane(e)].astype(jnp.bfloat16)

        halves(part_of)
        direct_copy(0, t).start()
        added_copy(0, t).start()

    def kept_products(t):
        value = product(1, t, around(z + hop(t)))
        for e in (0, 1):
            keep[e, t] = value[:, lane(e)]

    def far_products(r):
        value = product(1, r, around(z + 2))
        for e in (0, 1):
            far_keep[e, half_rows(r), :] = value[:, lane(e)]

    def own_products(p):
        def part_of(r):
            value = product(p, r, z)
            for e in (0, 1):
                own_buf[2 * p + e, half_rows(r), :] = value[:, lane(e)]

        halves(part_of)

    halves(lead)
    halves(give)
    for r in (0, 1):
        give_copy(1, r).start()
    halves(next_products)
    halves(far_products)
    add_given(2)
    for t in (0, 1):
        direct_copy(1, t).start()
    halves(kept_products)
    halves(own_products)
    add_near(0)
    for r in (0, 1):
        relay_copy(r).start()
    add_far(2)
    for t in (0, 1):
        added_copy(1, t).start()
    add_given(3)
    for t in (0, 1):
        direct_copy(3, t).start()
    add_near(2)

    def to_partner(r):
        relay_copy(r).wait_recv()
        own_buf[2, half_rows(r), :] = own_buf[2, half_rows(r), :] + relay_in[half_rows(r), :]
        partner_copy(core, r).start()

    to_partner(0)
    add_near(1)
    mate_out[...] = own_buf[1].astype(jnp.bfloat16)
    mate_copy(core).start()
    potentials()
    for copy in started:
        copy.wait_send()

    @pl.when(home)
    def _():
        aside.wait_send()
        for t in (0, 1):
            for a in (0, 1):
                own_round(t, a).wait_send()

    add_far(3)
    to_partner(1)

    def settle(b, carry):
        for t in (0, 1):
            direct_copy(b, t).wait_send()
            added_copy(b, t).wait_send()

            @pl.when(b < 2)
            def _():
                give_copy(jnp.minimum(b, 1), t).wait_send()

            @pl.when(b >= 2)
            def _():
                far_copy(jnp.maximum(b, 2), t).wait_send()

        return carry

    lax.fori_loop(0, 3, settle, 0)
    for r in (0, 1):
        relay_copy(r).wait_send()
    swap_copy(1, sibling).wait_recv()
    for i in (0, 1):
        remote(swap.at[0], swap.at[2 + i], swap_send.at[2 + i], swap_recv.at[2 + i], sibling).wait_recv()
    half = rows // LANES
    for a in (0, 1):
        mine_row = jnp.where(core == a, swap[0], swap[1])
        rows_out[pl.ds(a * half, half), :] = jnp.where(home, mine_row, swap[2 + a])

    add_near(3)

    @pl.when(home)
    def _():
        in_sum[core] = own_buf[3]
        stay_copy(1 - core).wait_recv()
        for a in (0, 1):
            mate_copy(a).wait_recv()
            in_sum[a] = in_sum[a] + mate_in[a].astype(jnp.float32)

    @pl.when(jnp.logical_not(home))
    def _():
        stay_copy(core).start()
        for a in (0, 1):
            for r in (0, 1):
                partner_copy(a, r).wait_recv()

    def result_copy(a):
        return pltpu.make_async_copy(in_sum.at[a], targets.at[pl.ds(a * rows, rows)], local_sems.at[a])

    for a in (0, 1):
        result_copy(a).start()

    settle(3, 0)
    for a in (0, 1):
        result_copy(a).wait()
    for r in (0, 1):
        partner_copy(core, r).wait_send()
    mate_copy(core).wait_send()

    @pl.when(jnp.logical_not(home))
    def _():
        stay_copy(core).wait_send()


def hand_on(targets, rows_pot, cols_pot, targets_out, rows_out, cols_out, stage, row_stage, col_stage, sems):
    size = targets.shape[0] // PARTS
    legs = [
        (targets.at[pl.ds(i * size, size)], stage.at[i], targets_out.at[pl.ds(i * size, size)]) for i in range(PARTS)
    ]
    legs += [(rows_pot, row_stage, rows_out), (cols_pot, col_stage, cols_out)]
    first = [pltpu.make_async_copy(src, mid, sems.at[i, 0]) for i, (src, mid, _) in enumerate(legs)]
    second = [pltpu.make_async_copy(mid, dst, sems.at[i, 1]) for i, (_, mid, dst) in enumerate(legs)]
    for copy in first:
        copy.start()
    for before, copy in zip(first, second):
        before.wait()
        copy.start()
    for copy in second:
        copy.wait()


def shards(noise_latents, data_latents):
    nsize = lax.axis_size("noise")
    dsize = lax.axis_size("dp")
    block, piece = noise_latents.shape
    rows, cols = block // 2, 2 * data_latents.shape[0]
    rsize, csize = dsize // 2, nsize * 2
    vmem = pl.BlockSpec(memory_space=pltpu.VMEM)
    f32, bf16 = jnp.float32, jnp.bfloat16
    strip = rows // 2
    row_vec, col_vec = (rows // LANES, LANES), (cols // LANES, LANES)
    sems = pltpu.SemaphoreType.DMA
    targets, rows_pot, cols_pot = pl.pallas_call(
        functools.partial(kernel, rsize, csize, piece * dsize),
        out_shape=(
            jax.ShapeDtypeStruct((block, piece), f32),
            jax.ShapeDtypeStruct((block // LANES, LANES), f32),
            jax.ShapeDtypeStruct((cols // 2 // LANES, LANES), f32),
        ),
        in_specs=[pl.BlockSpec(memory_space=pl.ANY)] * 2,
        out_specs=(pl.BlockSpec(memory_space=pl.ANY), vmem, vmem),
        scratch_shapes=[
            pltpu.VMEM((SIDE, rows, SIDE * piece), bf16),
            pltpu.VMEM((2, SIDE, cols // 2, nsize // SIDE * data_latents.shape[1]), bf16),
            pltpu.VMEM((rows, cols), f32),
            pltpu.VMEM((rows, cols), bf16),
            pltpu.VMEM((rows, LANES), f32),
            pltpu.VMEM((rows, LANES), f32),
            pltpu.VMEM((rows, LANES), f32),
            pltpu.VMEM((rows, LANES), f32),
            pltpu.VMEM((cols, LANES), f32),
            pltpu.VMEM((8, cols), f32),
            pltpu.VMEM(row_vec, f32),
            pltpu.VMEM(col_vec, f32),
            pltpu.VMEM(row_vec, f32),
            pltpu.VMEM(col_vec, f32),
            pltpu.VMEM((4,) + row_vec, f32),
            pltpu.VMEM((ITERS, csize) + col_vec, f32),
            pltpu.VMEM((ITERS, rsize) + row_vec, f32),
            pltpu.VMEM((SIDE, 3, rows, LANES), bf16),
            pltpu.VMEM((SIDE, rows, LANES), f32),
            pltpu.VMEM((2, 2, strip, LANES), bf16),
            pltpu.VMEM((SIDE, 2, rows, LANES), bf16),
            pltpu.VMEM((2, rows, LANES), f32),
            sems((ITERS,)),
            sems((ITERS,)),
            sems((ITERS,)),
            sems((ITERS,)),
            sems((4,)),
            sems((4,)),
            sems((4,)),
            sems((4,)),
            sems((SIDE, 2, 2)),
            sems((SIDE, 2, 2)),
            sems((2, 15)),
            sems((2, 15)),
            sems((SIDE, 2, 3)),
            sems((SIDE, 2, 3)),
            sems((6,)),
            sems((6,)),
            pltpu.VMEM((2, 2, strip, LANES), f32),
            pltpu.VMEM((2, rows, LANES), f32),
            pltpu.VMEM((2, rows, LANES), bf16),
            sems((2, 2)),
            sems((2, 2)),
            sems((2, 2)),
            sems((2,)),
            sems((2, 2)),
            sems((SIDE, 2)),
            pltpu.VMEM((rows, LANES), f32),
            pltpu.VMEM((rows, LANES), bf16),
            pltpu.VMEM((2, rows, LANES), bf16),
        ],
        compiler_params=pltpu.CompilerParams(
            collective_id=0, has_side_effects=True, vmem_limit_bytes=60 * 2**20
        ),
    )(noise_latents, data_latents)
    results = (targets, rows_pot, cols_pot)
    targets, rows_pot, cols_pot = pl.pallas_call(
        hand_on,
        out_shape=tuple(jax.ShapeDtypeStruct(a.shape, a.dtype) for a in results),
        in_specs=[pl.BlockSpec(memory_space=pl.ANY)] * 3,
        out_specs=(pl.BlockSpec(memory_space=pl.ANY),) * 3,
        scratch_shapes=[
            pltpu.VMEM((PARTS, block // PARTS, piece), f32),
            pltpu.VMEM(rows_pot.shape, f32),
            pltpu.VMEM(cols_pot.shape, f32),
            sems((PARTS + 2, 2)),
        ],
        compiler_params=pltpu.CompilerParams(vmem_limit_bytes=60 * 2**20),
    )(*results)
    return targets, rows_pot.reshape(block), cols_pot.reshape(cols // 2)


def solution(mesh):
    return jax.shard_map(
        shards,
        mesh=mesh,
        in_specs=(P("noise", "dp"), P("dp", "noise")),
        out_specs=(P("noise", "dp"), P("noise"), P("dp")),
        check_vma=False,
    )
```

```python
import functools
import math

import jax
import jax.numpy as jnp
from jax import lax
from jax.experimental import pallas as pl
from jax.experimental.pallas import tpu as pltpu
from jax.sharding import PartitionSpec as P

ITERS = 3
EPSILON = 0.04
LOG2E = 1.0 / math.log(2.0)
MESH = pl.DeviceIdType.MESH
LANES = 128
TILE = 32
SHORT = 16
TALL = 64
SIDE = 4
PARTS = 4


def spread_lanes(ref, row):
    return jnp.broadcast_to(ref[pl.ds(row, 1), :], (LANES, LANES)).T


def exchange(buf, send, recv, step, me, peers, started):
    for peer in peers:
        pltpu.make_async_remote_copy(
            src_ref=buf.at[step, me],
            dst_ref=buf.at[step, me],
            send_sem=send.at[step],
            recv_sem=recv.at[step],
            device_id=peer,
            device_id_type=MESH,
        ).start()
    slots = buf.at[step, pl.ds(0, len(peers))]
    every = pltpu.make_async_remote_copy(
        src_ref=slots,
        dst_ref=slots,
        send_sem=send.at[step],
        recv_sem=recv.at[step],
        device_id=peers[0],
        device_id_type=MESH,
    )
    every.wait_recv()
    started.append(every)


def combine(buf, step, size):
    top = buf[step, 0]
    for s in range(1, size):
        top = jnp.maximum(top, buf[step, s])
    total = jnp.exp2(buf[step, 0] - top)
    for s in range(1, size):
        total = total + jnp.exp2(buf[step, s] - top)
    return top + jnp.log(total) * LOG2E


def add_slots(buf, step, size):
    total = buf[step, 0]
    for s in range(1, size):
        total = total + buf[step, s]
    return total


def kernel(
    rsize, csize, width,
    noise_ref, data_ref,
    targets, rows_out, cols_out,
    noise_all, data_all, scores, weights,
    shift, first, scale, part, data_part, colvec, rowpack, colpack, sqx, sqy, swap,
    col_buf, row_buf, out_buf, own_buf, far_buf, near_buf, in_sum,
    col_send, col_recv, row_send, row_recv, swap_send, swap_recv,
    cross_send, cross_recv, noise_send, noise_recv, data_send, data_recv,
    sum_send, sum_recv, in_send, in_recv, keep, far_keep, given, give_send, give_recv, part_recv, local_sems, own_send, far_send, relay_in, mate_out, mate_in,
):
    rows, cols = scores.shape
    n = lax.axis_index("noise")
    d = lax.axis_index("dp")
    x, z = d // SIDE, lax.rem(d, SIDE)
    y, core = n // 2, lax.rem(n, 2)
    kind = lax.rem((x + 1) // 2, 2)
    pair = x // 2
    side = lax.rem(x, 2)
    home = core == kind
    kappa = LOG2E / EPSILON
    log_rows = math.log2(rows * csize)
    log_cols = math.log2(cols * rsize)
    chunks = cols // LANES
    row_blocks = rows // LANES
    tiles = rows // TILE
    started = []

    def around(value):
        return lax.rem(value + SIDE, SIDE)

    def device(xi, yi, zi, ci):
        return (yi * 2 + ci, xi * SIDE + zi)

    me_row = pair * SIDE + z
    me_col = y * 4 + kind * 2 + core

    sibling = device(x, y, z, 1 - core)
    partner = x + 1 - 2 * side
    mate = SIDE - 1 - x
    opposite = around(x + 2)

    barrier = pltpu.get_barrier_semaphore()
    ys, zs = [around(y + k) for k in range(SIDE)], [around(z + k) for k in range(SIDE)]
    rings = [yi * 2 + ci for yi in (ys[2], ys[1], ys[3], ys[0]) for ci in (1 - core, core)]
    col_peers = [(r, di) for di in (partner * SIDE + z, d) for r in rings][:-1]
    row_peers = [(n, xi * SIDE + zi) for xi in (mate, x) for zi in (zs[2], zs[1], zs[3], zs[0])][:-1]
    greeted = [sibling]
    for ci in (0, 1):
        greeted += [device(partner, y, z, ci), device(mate, y, z, ci), device(x, y, zs[1], ci), device(x, y, zs[3], ci)]
    greeted += [device(x, ys[1], z, core), device(x, ys[3], z, core)]
    for to in greeted:
        pl.semaphore_signal(barrier, inc=1, device_id=to, device_id_type=MESH)
    pl.semaphore_wait(barrier, len(greeted))

    def remote(src, dst, send, recv, to):
        return pltpu.make_async_remote_copy(
            src_ref=src, dst_ref=dst, send_sem=send, recv_sem=recv, device_id=to, device_id_type=MESH
        )

    def begin(copy):
        copy.start()
        started.append(copy)

    def lane(c):
        return slice(LANES * c, LANES * (c + 1))

    HOP = (1, -1)

    def noise_slot(xi, zi, at):
        return noise_all.at[xi, at, pl.ds(pl.multiple_of(zi * LANES, LANES), LANES)]

    own = noise_slot(x, z, pl.ds(0, rows))

    def cross_copy(i, half, to):
        return remote(
            noise_ref.at[pl.ds(half * rows, rows)], own, cross_send.at[i], cross_recv.at[x], to
        )

    def cross_wait(xi):
        remote(
            noise_ref.at[pl.ds(0, rows)], noise_slot(xi, z, pl.ds(0, rows)), cross_send.at[0], cross_recv.at[xi], sibling
        ).wait_recv()

    there = jnp.where(home, mate, partner)
    aside = cross_copy(2, 1 - core, sibling)

    def noise_copy(xi, t, forward, zi):
        at = pl.ds(t * (rows // 2), rows // 2) if forward else pl.ds(0, rows)
        f = int(forward)
        slot = noise_slot(xi, zi, at)
        return remote(
            slot, slot, noise_send.at[xi, t, f], noise_recv.at[xi, t, f], device(x, y, around(z + HOP[t]), core)
        )

    def noise_wait(xi, t, forward):
        zi = around(z - HOP[t] * (2 if forward else 1))
        noise_copy(xi, t, forward, zi).wait_recv()
        return zi

    def data_slot(block, where, at):
        width_at = pl.ds(pl.multiple_of(lax.rem(where, 2) * 256, 256), 256)
        return data_all.at[block, where // 2, at, width_at]

    def data_copy(r, index, where, lo, size, to, own=False):
        at = pl.ds(lo, size)
        block = side if r == 0 else 1 - side
        dst = data_slot(block, where, at)
        return remote(data_ref.at[at] if own else dst, dst, data_send.at[r, index], data_recv.at[r, index], to)

    half_cols = cols // 4
    full_cols = cols // 2

    def along_y(step, c):
        return around(y + step) * 2 + c

    def data_wait(r, index, where, lo, size):
        data_copy(r, index, where, lo, size, sibling).wait_recv()

    HALF = 9

    def cross_data(h, own=False):
        at = pl.ds(h * half_cols, half_cols)
        dst = data_slot(side if own else 1 - side, n, at)
        return remote(
            data_ref.at[at], dst, data_send.at[1, 11 + h], data_recv.at[1, 11 + h], device(partner, y, z, core)
        )

    def partner_y(t, h, back=0):
        where = around(y + back) * 2 + core
        to = device(x, around(y + HOP[t]), z, core)
        return t if h == 0 else HALF + t, where, h * half_cols, half_cols, to

    def partner_wait(t, h):
        data_copy(1, *partner_y(t, h, -HOP[t])).wait_recv()

    def own_round(t, a):
        return remote(
            noise_ref.at[pl.ds(a * rows, rows)], own,
            own_send.at[t, a], noise_recv.at[x, t, 0], device(x, y, around(z + HOP[t]), a),
        )

    def own_half():
        return pltpu.make_async_copy(
            noise_ref.at[pl.ds(pl.multiple_of(core * rows, rows), rows)], own, local_sems.at[0]
        )

    @pl.when(home)
    def _():
        for t in (0, 1):
            for a in (0, 1):
                own_round(t, a).start()
        aside.start()

    begin(cross_copy(0, 0, device(there, y, z, 0)))
    begin(cross_copy(1, 1, device(there, y, z, 1)))
    for t in (0, 1):
        begin(data_copy(0, t, n, 0, full_cols, device(x, around(y + HOP[t]), z, core), own=True))
    @pl.when(home)
    def _():
        own_half().start()

    data_own = pltpu.make_async_copy(data_ref, data_slot(side, n, pl.ds(0, full_cols)), local_sems.at[1])
    data_own.start()
    scores[...] = jnp.zeros_like(scores)
    part[...] = jnp.zeros_like(part)

    def round_z(xi):
        for t in (0, 1):
            begin(noise_copy(xi, t, False, z))

    def forward_z(xi):
        for t in (0, 1):
            begin(noise_copy(xi, t, True, noise_wait(xi, t, False)))

    def far_noise(xi, t):
        slot = noise_slot(xi, around(z + 2), pl.ds(t * (rows // 2), rows // 2))
        return remote(slot, slot, far_send.at[xi, t], noise_recv.at[xi, t, 1], device(mate, y, z, core))

    def share_far(xi):
        for t in (0, 1):
            noise_wait(xi, t, True)
            begin(far_noise(xi, t))

    def far_wait(xi):
        for t in (0, 1):
            far_noise(xi, t).wait_recv()

    def far_data(t, block):
        where = along_y(2, core)
        at = pl.ds(t * half_cols, half_cols)
        dst = data_slot(block, where, at)
        return remote(dst, dst, data_send.at[1, 2 + t], data_recv.at[1, 2 + t], device(partner, y, z, core))

    cross_wait(partner)
    slot = noise_slot(partner, z, pl.ds(0, rows))
    begin(remote(slot, slot, cross_send.at[3], cross_recv.at[partner], device(mate, y, z, core)))
    round_z(partner)
    for h in (0, 1):
        begin(cross_data(h, own=True))
    begin(data_copy(0, 4, n, 0, full_cols, sibling, own=True))
    forward_z(x)
    cross_wait(mate)
    round_z(mate)
    for t in (0, 1):
        where = along_y(-HOP[t], core)
        data_wait(0, t, where, 0, full_cols)
        begin(data_copy(0, 2 + t, where, t * half_cols, half_cols, device(x, around(y + HOP[t]), z, core)))
        begin(data_copy(0, 5 + t, where, 0, full_cols, sibling))
    cross_data(0).wait_recv()
    for t in (0, 1):
        begin(data_copy(1, *partner_y(t, 0)))
    forward_z(partner)
    cross_wait(opposite)
    round_z(opposite)
    share_far(x)
    cross_data(1).wait_recv()
    for t in (0, 1):
        begin(data_copy(1, *partner_y(t, 1)))
    begin(data_copy(1, 4, n, 0, full_cols, sibling))
    for t in (0, 1):
        where = along_y(2, core)
        data_wait(0, 2 + t, where, t * half_cols, half_cols)
        begin(far_data(t, side))
        begin(data_copy(0, 7 + t, where, t * half_cols, half_cols, sibling))

    def squares(block):
        value = block.astype(jnp.float32)
        return value * value

    def chunk_product(xi, m):
        here = pl.ds(pl.multiple_of(lax.rem(m, 4) * 256, 256), 256)
        return lax.dot_general(
            noise_all[xi], data_all[m // 4, xi, here, :], (((1,), (1,)), ((), ())),
            preferred_element_type=jnp.float32,
        )

    def norms(xi):
        def norm(r, carry):
            cut = pl.ds(pl.multiple_of(r * 64, 64), 64)
            total = part[cut, :]
            for i in range(SIDE):
                total = total + squares(noise_all[xi, cut, lane(i)])
            part[cut, :] = total
            return carry

        lax.fori_loop(0, rows // 64, norm, 0)

    near, other_block = side * 4, 4 - side * 4

    def unit(block, xs, fresh, count=4):
        def column(i, carry):
            m = block + i
            cut = pl.ds(pl.multiple_of(m * 256, 256), 256)
            value = None if fresh else scores[:, cut]
            for xi in xs:
                value = chunk_product(xi, m) if value is None else value + chunk_product(xi, m)
            scores[:, cut] = value
            return carry

        lax.fori_loop(0, count, column, 0)

    def add_unit(block, count, xi):
        unit(block, (xi,), False, count)

    data_own.wait()
    data_wait(0, 4, along_y(0, 1 - core), 0, full_cols)
    for t in (0, 1):
        data_wait(0, 5 + t, along_y(-HOP[t], 1 - core), 0, full_cols)
    for t in (0, 1):
        data_wait(0, 7 + t, along_y(2, 1 - core), t * half_cols, half_cols)

    @pl.when(home)
    def _():
        own_half().wait()

    @pl.when(jnp.logical_not(home))
    def _():
        cross_wait(x)

    unit(near, (x,), True)
    share_far(partner)
    norms(x)
    for t in (0, 1):
        noise_wait(mate, t, False)
    far_wait(mate)
    unit(near, (mate,), False)
    norms(mate)

    def beside(t, h, c):
        return data_copy(1, (5 if h == 0 else 13) + t, along_y(-HOP[t], c), h * half_cols, half_cols, sibling)

    for t in (0, 1):
        partner_wait(t, 0)
        begin(beside(t, 0, core))
    unit(near, (partner,), False)
    norms(partner)
    data_wait(1, 4, along_y(0, 1 - core), 0, full_cols)
    for t in (0, 1):
        beside(t, 0, 1 - core).wait_recv()

    def ahead(i, carry):
        xi = around(y + i + i // 2)
        add_unit(other_block, jnp.where(xi == opposite, 0, jnp.where(i == 0, 4, 2)), xi)
        return carry

    lax.fori_loop(0, 3, ahead, 0)
    for t in (0, 1):
        partner_wait(t, 1)
        begin(beside(t, 1, core))
    for t in (0, 1):
        noise_wait(opposite, t, False)
    far_wait(opposite)
    for t in (0, 1):
        far_data(t, 1 - side).wait_recv()
        begin(data_copy(1, 7 + t, along_y(2, core), t * half_cols, half_cols, sibling))
    norms(opposite)

    factor = 2.0 * kappa / width

    def row_shift(r, carry):
        at = pl.ds(pl.multiple_of(r * 128, 128), 128)
        total = jnp.sum(part[at, :], axis=1, keepdims=True) * (-kappa / width)
        shift[at, :] = jnp.broadcast_to(total, (128, LANES))
        return carry

    lax.fori_loop(0, rows // 128, row_shift, 0)

    def final(block, xi):
        def column(i, carry):
            m = block + i
            cut = pl.ds(pl.multiple_of(m * 256, 256), 256)
            value = (scores[:, cut] + chunk_product(xi, m)) * factor
            scores[:, cut] = value
            for e in (0, 1):
                top = jnp.max(value[:, LANES * e:LANES * (e + 1)] + shift[...], axis=0, keepdims=True)
                colvec[:, pl.ds(pl.multiple_of(m * 256 + e * LANES, LANES), LANES)] = jnp.broadcast_to(top, (8, LANES))
            return carry

        lax.fori_loop(0, 4, column, 0)

    final(near, opposite)
    add_unit(other_block, jnp.where(opposite == y, 4, jnp.where(opposite == around(y + 2), 0, 2)), opposite)
    for t in (0, 1):
        beside(t, 1, 1 - core).wait_recv()
    unit(other_block + 2, (around(y + 1), around(y - 1)), False, 2)
    for t in (0, 1):
        data_wait(1, 7 + t, along_y(2, 1 - core), t * half_cols, half_cols)
    final(other_block, around(y + 2))

    def fold(block, op):
        out = block[0:8]
        for r in range(1, block.shape[0] // 8):
            out = op(out, block[8 * r:8 * r + 8])
        return out

    def spread_cols():
        for c in range(chunks):
            colvec[:, lane(c)] = jnp.broadcast_to(colpack[pl.ds(c, 1), :], (8, LANES))

    def tall(ref, c, size=TILE):
        return jnp.concatenate([ref[:, lane(c)]] * (size // 8), axis=0)

    def tile_at(t):
        return pl.ds(pl.multiple_of(t * TILE, TILE), TILE)

    def loop(body, init):
        return lax.fori_loop(0, tiles, body, init, unroll=2)

    zeros = tuple(jnp.zeros((8, LANES), jnp.float32) for _ in range(chunks))

    def exp_step(t, accs):
        at = pl.ds(pl.multiple_of(t * TALL, TALL), TALL)
        add = shift[at, :]
        return tuple(
            accs[c] + fold(jnp.exp2(scores[at, lane(c)] + add - tall(colvec, c, TALL)), jnp.add)
            for c in range(chunks)
        )

    sums = lax.fori_loop(0, rows // TALL, exp_step, zeros)
    for c in range(chunks):
        total = jnp.sum(sums[c], axis=0, keepdims=True)
        col_buf[0, me_col, pl.ds(c, 1), :] = colvec[0:1, lane(c)] + jnp.log(total) * LOG2E
    exchange(col_buf, col_send, col_recv, 0, me_col, col_peers, started)
    col_pot = -log_cols - combine(col_buf, 0, csize)
    colpack[...] = col_pot
    spread_cols()

    def row_step(t, carry):
        at = pl.ds(pl.multiple_of(t * SHORT, SHORT), SHORT)
        values = [
            scores[at, lane(c)] + jnp.concatenate([colvec[:, lane(c)]] * (SHORT // 8), axis=0) for c in range(chunks)
        ]
        top = values[0]
        for c in range(1, chunks):
            top = jnp.maximum(top, values[c])
        first[at, :] = top
        total = None
        for c in range(chunks):
            value = jnp.exp2(values[c] - top)
            scores[at, lane(c)] = value
            total = value if total is None else total + value
        part[at, :] = total
        return carry

    lax.fori_loop(0, rows // SHORT, row_step, 0, unroll=2)
    for b in range(row_blocks):
        at = pl.ds(b * LANES, LANES)
        tops = first[at, :].T
        top = jnp.max(tops, axis=0, keepdims=True)
        total = jnp.sum(part[at, :].T * jnp.exp2(tops - top), axis=0, keepdims=True)
        row_buf[0, me_row, pl.ds(b, 1), :] = top + jnp.log(total) * LOG2E
    exchange(row_buf, row_send, row_recv, 0, me_row, row_peers, started)
    row_lse = combine(row_buf, 0, rsize)
    rowpack[...] = row_lse
    for b in range(row_blocks):
        at = pl.ds(b * LANES, LANES)
        base = jnp.exp2(first[at, :] - spread_lanes(rowpack, b))
        first[at, :] = base
        scale[at, :] = base

    def col_step(t, accs):
        at = tile_at(t)
        mul = scale[at, :]
        return tuple(accs[c] + fold(scores[at, lane(c)] * mul, jnp.add) for c in range(chunks))

    def sum_step(keep_values):
        def body(t, carry):
            at = pl.ds(pl.multiple_of(t * TALL, TALL), TALL)
            total = None
            for c in range(chunks):
                value = scores[at, lane(c)] * tall(colvec, c, TALL)
                if keep_values:
                    scores[at, lane(c)] = value
                total = value if total is None else total + value
            part[at, :] = total * first[at, :]
            return carry

        return body

    for step in range(1, ITERS):
        sums = loop(col_step, zeros)
        for c in range(chunks):
            col_buf[step, me_col, pl.ds(c, 1), :] = jnp.sum(sums[c], axis=0, keepdims=True)
        exchange(col_buf, col_send, col_recv, step, me_col, col_peers, started)
        ratio = 1.0 / add_slots(col_buf, step, csize)
        colpack[...] = ratio
        spread_cols()
        lax.fori_loop(0, rows // TALL, sum_step(step == ITERS - 1), 0)
        for b in range(row_blocks):
            at = pl.ds(b * LANES, LANES)
            row_buf[step, me_row, pl.ds(b, 1), :] = jnp.sum(part[at, :].T, axis=0, keepdims=True)
        exchange(row_buf, row_send, row_recv, step, me_row, row_peers, started)
        total = add_slots(row_buf, step, rsize)
        rowpack[...] = 1.0 / total
        for b in range(row_blocks):
            at = pl.ds(b * LANES, LANES)
            scale[at, :] = first[at, :] * spread_lanes(rowpack, b)

    def weigh(r):
        def body(t, carry):
            at = pl.ds(pl.multiple_of(r * (rows // 2) + t * TILE, TILE), TILE)
            mul = scale[at, :]
            for c in range(chunks):
                weights[at, lane(c)] = (scores[at, lane(c)] * mul).astype(jnp.bfloat16)
            return carry

        lax.fori_loop(0, tiles // 2, body, 0, unroll=2)

    def swap_copy(i, to):
        return remote(swap.at[0], swap.at[i], swap_send.at[i], swap_recv.at[i], to)

    def potentials():
        for c in range(chunks):
            sqy[pl.ds(c, 1), :] = jnp.sum(data_part[pl.ds(c * LANES, LANES), :].T, axis=0, keepdims=True)
        cols_pot = (col_pot + jnp.log(ratio) * LOG2E + (log_rows - log_cols)) / kappa + sqy[...] / width
        colpack[...] = cols_pot
        cols_out[...] = colpack[pl.ds(pl.multiple_of(side * 8, 8), 8), :]
        for b in range(row_blocks):
            sqx[pl.ds(b, 1), :] = shift[pl.ds(b * LANES, LANES), :].T[0:1]
        swap[0] = -(log_rows + row_lse + jnp.log(total) * LOG2E + sqx[...]) / kappa
        begin(swap_copy(1, sibling))
        for i in (0, 1):
            begin(remote(
                swap.at[0], swap.at[2 + core], swap_send.at[2 + i], swap_recv.at[2 + core], device(partner, y, z, i)
            ))

    strip = rows // 2

    def half_rows(r):
        return pl.ds(pl.multiple_of(r * strip, strip), strip)

    def block_x(b):
        return jnp.where(b < 2, jnp.where(b == 0, opposite, mate), jnp.where(b == 2, partner, x))

    def product(p, r, to_z):
        cut = pl.ds(pl.multiple_of(to_z * LANES, LANES), LANES)
        total = None
        for k in (0, 1):
            block = jnp.concatenate(
                [data_all[k, block_x(2 * p + e), :, cut] for e in (0, 1)], axis=1
            )
            value = jnp.dot(
                weights[half_rows(r), k * full_cols:(k + 1) * full_cols], block,
                preferred_element_type=jnp.float32,
            )
            total = value if total is None else total + value
        return total

    def hop(t):
        return 1 - 2 * t

    def sum_copy(b, t, index, src, dst):
        to = device(x, y, around(z + hop(t)), core)
        return remote(src, dst, sum_send.at[b, t, index], sum_recv.at[b, t, index], to)

    def far_copy(b, t):
        return sum_copy(b, t, 0, out_buf.at[b, 2, half_rows(t)], far_buf.at[b - 2, t])

    def direct_copy(b, t):
        at = half_rows(1 - t)
        return sum_copy(b, t, 1, out_buf.at[b, t, at], near_buf.at[b, t, at])

    def added_copy(b, t):
        at = half_rows(t)
        return sum_copy(b, t, 2, out_buf.at[b, t, at], near_buf.at[b, t, at])

    def give_copy(b, r):
        at = half_rows(r)
        return remote(
            out_buf.at[b, 2, at], given.at[b, at], give_send.at[b, r], give_recv.at[b, r], device(mate, y, z, core)
        )

    def relay_copy(r):
        at = half_rows(r)
        return remote(own_buf.at[0, at], relay_in.at[at], in_send.at[r], in_recv.at[4 + r], device(mate, y, z, core))

    def partner_copy(a, r):
        at = half_rows(r)
        return remote(
            own_buf.at[2, at], in_sum.at[a, at], in_send.at[2 + r], part_recv.at[a, r], device(partner, y, z, kind)
        )

    def mate_copy(a):
        return remote(mate_out, mate_in.at[a], in_send.at[4], in_recv.at[2 + a], device(mate, y, z, kind))

    def stay_copy(a):
        return remote(own_buf.at[3], in_sum.at[a], in_send.at[5], in_recv.at[a], sibling)

    def add_far(b):
        for t in (0, 1):
            far_copy(b, t).wait_recv()
            out_buf[b, t, half_rows(t), :] = (
                keep[b - 2, t] + far_buf[b - 2, t].astype(jnp.float32)
            ).astype(jnp.bfloat16)
            added_copy(b, t).start()

    def add_near(b):
        for t in (0, 1):
            direct_copy(b, t).wait_recv()
            added_copy(b, t).wait_recv()
        own_buf[b] = own_buf[b] + near_buf[b, 0].astype(jnp.float32) + near_buf[b, 1].astype(jnp.float32)

    def add_given(b):
        for r in (0, 1):
            at = half_rows(r)
            give_copy(b - 2, r).wait_recv()
            out_buf[b, 2, at, :] = (far_keep[b - 2, at, :] + given[b - 2, at, :].astype(jnp.float32)).astype(jnp.bfloat16)
            far_copy(b, r).start()

    def halves(body):
        def step(r, carry):
            body(r)
            return carry

        lax.fori_loop(0, 2, step, 0)

    def lead(r):
        t = 1 - r
        weigh(r)
        value = product(1, r, around(z + hop(t)))
        for e in (0, 1):
            out_buf[2 + e, t, half_rows(r), :] = value[:, lane(e)].astype(jnp.bfloat16)
        direct_copy(2, t).start()

    def give(r):
        value = product(0, r, around(z + 2))
        for e in (0, 1):
            out_buf[e, 2, half_rows(r), :] = value[:, lane(e)].astype(jnp.bfloat16)
        give_copy(0, r).start()

    def next_products(t):
        def part_of(r):
            value = product(0, r, around(z + hop(t)))
            for e in (0, 1):
                out_buf[e, t, half_rows(r), :] = value[:, lane(e)].astype(jnp.bfloat16)

        halves(part_of)
        direct_copy(0, t).start()
        added_copy(0, t).start()

    def kept_products(t):
        value = product(1, t, around(z + hop(t)))
        for e in (0, 1):
            keep[e, t] = value[:, lane(e)]

    def far_products(r):
        value = product(1, r, around(z + 2))
        for e in (0, 1):
            far_keep[e, half_rows(r), :] = value[:, lane(e)]

    def own_products(p):
        def part_of(r):
            value = product(p, r, z)
            for e in (0, 1):
                own_buf[2 * p + e, half_rows(r), :] = value[:, lane(e)]

        halves(part_of)

    halves(lead)
    halves(give)
    for r in (0, 1):
        give_copy(1, r).start()
    halves(next_products)
    halves(far_products)
    add_given(2)
    for t in (0, 1):
        direct_copy(1, t).start()
    halves(kept_products)
    halves(own_products)
    add_near(0)
    for r in (0, 1):
        relay_copy(r).start()
    add_far(2)
    for t in (0, 1):
        added_copy(1, t).start()
    add_given(3)
    for t in (0, 1):
        direct_copy(3, t).start()
    def data_norms(r, carry):
        per = full_cols // 64
        here = pl.ds(pl.multiple_of(lax.rem(r, per) * 64, 64), 64)
        total = None
        for xi in range(SIDE):
            for i in range(SIDE):
                value = squares(data_all[r // per, xi, here, lane(i)])
                total = value if total is None else total + value
        data_part[pl.ds(pl.multiple_of(r * 64, 64), 64), :] = total
        return carry

    lax.fori_loop(0, cols // 64, data_norms, 0)
    add_near(2)

    def to_partner(r):
        relay_copy(r).wait_recv()
        own_buf[2, half_rows(r), :] = own_buf[2, half_rows(r), :] + relay_in[half_rows(r), :]
        partner_copy(core, r).start()

    to_partner(0)
    add_near(1)
    mate_out[...] = own_buf[1].astype(jnp.bfloat16)
    mate_copy(core).start()
    potentials()
    for copy in started:
        copy.wait_send()

    @pl.when(home)
    def _():
        aside.wait_send()
        for t in (0, 1):
            for a in (0, 1):
                own_round(t, a).wait_send()

    add_far(3)
    to_partner(1)

    def settle(b, carry):
        for t in (0, 1):
            direct_copy(b, t).wait_send()
            added_copy(b, t).wait_send()

            @pl.when(b < 2)
            def _():
                give_copy(jnp.minimum(b, 1), t).wait_send()

            @pl.when(b >= 2)
            def _():
                far_copy(jnp.maximum(b, 2), t).wait_send()

        return carry

    lax.fori_loop(0, 3, settle, 0)
    for r in (0, 1):
        relay_copy(r).wait_send()
    swap_copy(1, sibling).wait_recv()
    for i in (0, 1):
        remote(swap.at[0], swap.at[2 + i], swap_send.at[2 + i], swap_recv.at[2 + i], sibling).wait_recv()
    half = rows // LANES
    for a in (0, 1):
        mine_row = jnp.where(core == a, swap[0], swap[1])
        rows_out[pl.ds(a * half, half), :] = jnp.where(home, mine_row, swap[2 + a])

    add_near(3)

    @pl.when(home)
    def _():
        in_sum[core] = own_buf[3]
        stay_copy(1 - core).wait_recv()
        for a in (0, 1):
            mate_copy(a).wait_recv()
            in_sum[a] = in_sum[a] + mate_in[a].astype(jnp.float32)

    @pl.when(jnp.logical_not(home))
    def _():
        stay_copy(core).start()
        for a in (0, 1):
            for r in (0, 1):
                partner_copy(a, r).wait_recv()

    def result_copy(a):
        return pltpu.make_async_copy(in_sum.at[a], targets.at[pl.ds(a * rows, rows)], local_sems.at[a])

    for a in (0, 1):
        result_copy(a).start()

    settle(3, 0)
    for a in (0, 1):
        result_copy(a).wait()
    for r in (0, 1):
        partner_copy(core, r).wait_send()
    mate_copy(core).wait_send()

    @pl.when(jnp.logical_not(home))
    def _():
        stay_copy(core).wait_send()


def hand_on(targets, rows_pot, cols_pot, targets_out, rows_out, cols_out, stage, row_stage, col_stage, sems):
    size = targets.shape[0] // PARTS
    legs = [
        (targets.at[pl.ds(i * size, size)], stage.at[i], targets_out.at[pl.ds(i * size, size)]) for i in range(PARTS)
    ]
    legs += [(rows_pot, row_stage, rows_out), (cols_pot, col_stage, cols_out)]
    first = [pltpu.make_async_copy(src, mid, sems.at[i, 0]) for i, (src, mid, _) in enumerate(legs)]
    second = [pltpu.make_async_copy(mid, dst, sems.at[i, 1]) for i, (_, mid, dst) in enumerate(legs)]
    for copy in first:
        copy.start()
    for before, copy in zip(first, second):
        before.wait()
        copy.start()
    for copy in second:
        copy.wait()


def shards(noise_latents, data_latents):
    nsize = lax.axis_size("noise")
    dsize = lax.axis_size("dp")
    block, piece = noise_latents.shape
    rows, cols = block // 2, 2 * data_latents.shape[0]
    rsize, csize = dsize // 2, nsize * 2
    vmem = pl.BlockSpec(memory_space=pltpu.VMEM)
    f32, bf16 = jnp.float32, jnp.bfloat16
    strip = rows // 2
    row_vec, col_vec = (rows // LANES, LANES), (cols // LANES, LANES)
    sems = pltpu.SemaphoreType.DMA
    targets, rows_pot, cols_pot = pl.pallas_call(
        functools.partial(kernel, rsize, csize, piece * dsize),
        out_shape=(
            jax.ShapeDtypeStruct((block, piece), f32),
            jax.ShapeDtypeStruct((block // LANES, LANES), f32),
            jax.ShapeDtypeStruct((cols // 2 // LANES, LANES), f32),
        ),
        in_specs=[pl.BlockSpec(memory_space=pl.ANY)] * 2,
        out_specs=(pl.BlockSpec(memory_space=pl.ANY), vmem, vmem),
        scratch_shapes=[
            pltpu.VMEM((SIDE, rows, SIDE * piece), bf16),
            pltpu.VMEM((2, SIDE, cols // 2, nsize // SIDE * data_latents.shape[1]), bf16),
            pltpu.VMEM((rows, cols), f32),
            pltpu.VMEM((rows, cols), bf16),
            pltpu.VMEM((rows, LANES), f32),
            pltpu.VMEM((rows, LANES), f32),
            pltpu.VMEM((rows, LANES), f32),
            pltpu.VMEM((rows, LANES), f32),
            pltpu.VMEM((cols, LANES), f32),
            pltpu.VMEM((8, cols), f32),
            pltpu.VMEM(row_vec, f32),
            pltpu.VMEM(col_vec, f32),
            pltpu.VMEM(row_vec, f32),
            pltpu.VMEM(col_vec, f32),
            pltpu.VMEM((4,) + row_vec, f32),
            pltpu.VMEM((ITERS, csize) + col_vec, f32),
            pltpu.VMEM((ITERS, rsize) + row_vec, f32),
            pltpu.VMEM((SIDE, 3, rows, LANES), bf16),
            pltpu.VMEM((SIDE, rows, LANES), f32),
            pltpu.VMEM((2, 2, strip, LANES), bf16),
            pltpu.VMEM((SIDE, 2, rows, LANES), bf16),
            pltpu.VMEM((2, rows, LANES), f32),
            sems((ITERS,)),
            sems((ITERS,)),
            sems((ITERS,)),
            sems((ITERS,)),
            sems((4,)),
            sems((4,)),
            sems((4,)),
            sems((4,)),
            sems((SIDE, 2, 2)),
            sems((SIDE, 2, 2)),
            sems((2, 15)),
            sems((2, 15)),
            sems((SIDE, 2, 3)),
            sems((SIDE, 2, 3)),
            sems((6,)),
            sems((6,)),
            pltpu.VMEM((2, 2, strip, LANES), f32),
            pltpu.VMEM((2, rows, LANES), f32),
            pltpu.VMEM((2, rows, LANES), bf16),
            sems((2, 2)),
            sems((2, 2)),
            sems((2, 2)),
            sems((2,)),
            sems((2, 2)),
            sems((SIDE, 2)),
            pltpu.VMEM((rows, LANES), f32),
            pltpu.VMEM((rows, LANES), bf16),
            pltpu.VMEM((2, rows, LANES), bf16),
        ],
        compiler_params=pltpu.CompilerParams(
            collective_id=0, has_side_effects=True, vmem_limit_bytes=60 * 2**20
        ),
    )(noise_latents, data_latents)
    results = (targets, rows_pot, cols_pot)
    targets, rows_pot, cols_pot = pl.pallas_call(
        hand_on,
        out_shape=tuple(jax.ShapeDtypeStruct(a.shape, a.dtype) for a in results),
        in_specs=[pl.BlockSpec(memory_space=pl.ANY)] * 3,
        out_specs=(pl.BlockSpec(memory_space=pl.ANY),) * 3,
        scratch_shapes=[
            pltpu.VMEM((PARTS, block // PARTS, piece), f32),
            pltpu.VMEM(rows_pot.shape, f32),
            pltpu.VMEM(cols_pot.shape, f32),
            sems((PARTS + 2, 2)),
        ],
        compiler_params=pltpu.CompilerParams(vmem_limit_bytes=60 * 2**20),
    )(*results)
    return targets, rows_pot.reshape(block), cols_pot.reshape(cols // 2)


def solution(mesh):
    return jax.shard_map(
        shards,
        mesh=mesh,
        in_specs=(P("noise", "dp"), P("dp", "noise")),
        out_specs=(P("noise", "dp"), P("noise"), P("dp")),
        check_vma=False,
    )
```

```python
import functools
import math

import jax
import jax.numpy as jnp
from jax import lax
from jax.experimental import pallas as pl
from jax.experimental.pallas import tpu as pltpu
from jax.sharding import PartitionSpec as P

ITERS = 3
EPSILON = 0.04
LOG2E = 1.0 / math.log(2.0)
MESH = pl.DeviceIdType.MESH
LANES = 128
TILE = 32
SHORT = 16
TALL = 64
SIDE = 4
PARTS = 4


def spread_lanes(ref, row):
    return jnp.broadcast_to(ref[pl.ds(row, 1), :], (LANES, LANES)).T


def exchange(buf, send, recv, step, me, peers, started):
    for peer in peers:
        pltpu.make_async_remote_copy(
            src_ref=buf.at[step, me],
            dst_ref=buf.at[step, me],
            send_sem=send.at[step],
            recv_sem=recv.at[step],
            device_id=peer,
            device_id_type=MESH,
        ).start()
    slots = buf.at[step, pl.ds(0, len(peers))]
    every = pltpu.make_async_remote_copy(
        src_ref=slots,
        dst_ref=slots,
        send_sem=send.at[step],
        recv_sem=recv.at[step],
        device_id=peers[0],
        device_id_type=MESH,
    )
    every.wait_recv()
    started.append(every)


def combine(buf, step, size):
    top = buf[step, 0]
    for s in range(1, size):
        top = jnp.maximum(top, buf[step, s])
    total = jnp.exp2(buf[step, 0] - top)
    for s in range(1, size):
        total = total + jnp.exp2(buf[step, s] - top)
    return top + jnp.log(total) * LOG2E


def add_slots(buf, step, size):
    total = buf[step, 0]
    for s in range(1, size):
        total = total + buf[step, s]
    return total


def kernel(
    rsize, csize, width,
    noise_ref, data_ref,
    targets, rows_out, cols_out,
    noise_all, data_all, scores, weights,
    shift, first, scale, part, data_part, colvec, rowpack, colpack, sqx, sqy, swap,
    col_buf, row_buf, out_buf, own_buf, far_buf, near_buf, in_sum,
    col_send, col_recv, row_send, row_recv, swap_send, swap_recv,
    cross_send, cross_recv, noise_send, noise_recv, data_send, data_recv,
    sum_send, sum_recv, in_send, in_recv, keep, far_keep, given, give_send, give_recv, part_recv, local_sems, own_send, far_send, relay_in, mate_out, mate_in,
):
    rows, cols = scores.shape
    n = lax.axis_index("noise")
    d = lax.axis_index("dp")
    x, z = d // SIDE, lax.rem(d, SIDE)
    y, core = n // 2, lax.rem(n, 2)
    kind = lax.rem((x + 1) // 2, 2)
    pair = x // 2
    side = lax.rem(x, 2)
    home = core == kind
    kappa = LOG2E / EPSILON
    log_rows = math.log2(rows * csize)
    log_cols = math.log2(cols * rsize)
    chunks = cols // LANES
    row_blocks = rows // LANES
    tiles = rows // TILE
    started = []

    def around(value):
        return lax.rem(value + SIDE, SIDE)

    def device(xi, yi, zi, ci):
        return (yi * 2 + ci, xi * SIDE + zi)

    me_row = pair * SIDE + z
    me_col = y * 4 + kind * 2 + core

    sibling = device(x, y, z, 1 - core)
    partner = x + 1 - 2 * side
    mate = SIDE - 1 - x
    opposite = around(x + 2)

    barrier = pltpu.get_barrier_semaphore()
    ys, zs = [around(y + k) for k in range(SIDE)], [around(z + k) for k in range(SIDE)]
    rings = [yi * 2 + ci for yi in (ys[2], ys[1], ys[3], ys[0]) for ci in (1 - core, core)]
    col_peers = [(r, di) for di in (partner * SIDE + z, d) for r in rings][:-1]
    row_peers = [(n, xi * SIDE + zi) for xi in (mate, x) for zi in (zs[2], zs[1], zs[3], zs[0])][:-1]
    greeted = [sibling]
    for ci in (0, 1):
        greeted += [device(partner, y, z, ci), device(mate, y, z, ci), device(x, y, zs[1], ci), device(x, y, zs[3], ci)]
    greeted += [device(x, ys[1], z, core), device(x, ys[3], z, core)]
    for to in greeted:
        pl.semaphore_signal(barrier, inc=1, device_id=to, device_id_type=MESH)
    pl.semaphore_wait(barrier, len(greeted))

    def remote(src, dst, send, recv, to):
        return pltpu.make_async_remote_copy(
            src_ref=src, dst_ref=dst, send_sem=send, recv_sem=recv, device_id=to, device_id_type=MESH
        )

    def begin(copy):
        copy.start()
        started.append(copy)

    def lane(c):
        return slice(LANES * c, LANES * (c + 1))

    HOP = (1, -1)

    def noise_slot(xi, zi, at):
        return noise_all.at[xi, at, pl.ds(pl.multiple_of(zi * LANES, LANES), LANES)]

    own = noise_slot(x, z, pl.ds(0, rows))

    def cross_copy(i, half, to):
        return remote(
            noise_ref.at[pl.ds(half * rows, rows)], own, cross_send.at[i], cross_recv.at[x], to
        )

    def cross_wait(xi):
        remote(
            noise_ref.at[pl.ds(0, rows)], noise_slot(xi, z, pl.ds(0, rows)), cross_send.at[0], cross_recv.at[xi], sibling
        ).wait_recv()

    there = jnp.where(home, mate, partner)
    aside = cross_copy(2, 1 - core, sibling)

    def noise_copy(xi, t, forward, zi):
        at = pl.ds(t * (rows // 2), rows // 2) if forward else pl.ds(0, rows)
        f = int(forward)
        slot = noise_slot(xi, zi, at)
        return remote(
            slot, slot, noise_send.at[xi, t, f], noise_recv.at[xi, t, f], device(x, y, around(z + HOP[t]), core)
        )

    def noise_wait(xi, t, forward):
        zi = around(z - HOP[t] * (2 if forward else 1))
        noise_copy(xi, t, forward, zi).wait_recv()
        return zi

    def data_slot(block, where, at):
        width_at = pl.ds(pl.multiple_of(lax.rem(where, 2) * 256, 256), 256)
        return data_all.at[block, where // 2, at, width_at]

    def data_copy(r, index, where, lo, size, to, own=False):
        at = pl.ds(lo, size)
        block = side if r == 0 else 1 - side
        dst = data_slot(block, where, at)
        return remote(data_ref.at[at] if own else dst, dst, data_send.at[r, index], data_recv.at[r, index], to)

    half_cols = cols // 4
    full_cols = cols // 2

    def along_y(step, c):
        return around(y + step) * 2 + c

    def data_wait(r, index, where, lo, size):
        data_copy(r, index, where, lo, size, sibling).wait_recv()

    HALF = 9

    def cross_data(h, own=False):
        at = pl.ds(h * half_cols, half_cols)
        dst = data_slot(side if own else 1 - side, n, at)
        return remote(
            data_ref.at[at], dst, data_send.at[1, 11 + h], data_recv.at[1, 11 + h], device(partner, y, z, core)
        )

    def partner_y(t, h, back=0):
        where = around(y + back) * 2 + core
        to = device(x, around(y + HOP[t]), z, core)
        return t if h == 0 else HALF + t, where, h * half_cols, half_cols, to

    def partner_wait(t, h):
        data_copy(1, *partner_y(t, h, -HOP[t])).wait_recv()

    def own_round(t, a):
        return remote(
            noise_ref.at[pl.ds(a * rows, rows)], own,
            own_send.at[t, a], noise_recv.at[x, t, 0], device(x, y, around(z + HOP[t]), a),
        )

    def own_half():
        return pltpu.make_async_copy(
            noise_ref.at[pl.ds(pl.multiple_of(core * rows, rows), rows)], own, local_sems.at[0]
        )

    @pl.when(home)
    def _():
        for t in (0, 1):
            for a in (0, 1):
                own_round(t, a).start()
        aside.start()

    begin(cross_copy(0, 0, device(there, y, z, 0)))
    begin(cross_copy(1, 1, device(there, y, z, 1)))
    for t in (0, 1):
        begin(data_copy(0, t, n, 0, full_cols, device(x, around(y + HOP[t]), z, core), own=True))
    @pl.when(home)
    def _():
        own_half().start()

    data_own = pltpu.make_async_copy(data_ref, data_slot(side, n, pl.ds(0, full_cols)), local_sems.at[1])
    data_own.start()
    scores[...] = jnp.zeros_like(scores)
    part[...] = jnp.zeros_like(part)

    def round_z(xi):
        for t in (0, 1):
            begin(noise_copy(xi, t, False, z))

    def forward_z(xi):
        for t in (0, 1):
            begin(noise_copy(xi, t, True, noise_wait(xi, t, False)))

    def far_noise(xi, t):
        slot = noise_slot(xi, around(z + 2), pl.ds(t * (rows // 2), rows // 2))
        return remote(slot, slot, far_send.at[xi, t], noise_recv.at[xi, t, 1], device(mate, y, z, core))

    def share_far(xi):
        for t in (0, 1):
            noise_wait(xi, t, True)
            begin(far_noise(xi, t))

    def far_wait(xi):
        for t in (0, 1):
            far_noise(xi, t).wait_recv()

    def far_data(t, block):
        where = along_y(2, core)
        at = pl.ds(t * half_cols, half_cols)
        dst = data_slot(block, where, at)
        return remote(dst, dst, data_send.at[1, 2 + t], data_recv.at[1, 2 + t], device(partner, y, z, core))

    cross_wait(partner)
    slot = noise_slot(partner, z, pl.ds(0, rows))
    begin(remote(slot, slot, cross_send.at[3], cross_recv.at[partner], device(mate, y, z, core)))
    round_z(partner)
    for h in (0, 1):
        begin(cross_data(h, own=True))
    begin(data_copy(0, 4, n, 0, full_cols, sibling, own=True))
    forward_z(x)
    cross_wait(mate)
    round_z(mate)
    for t in (0, 1):
        where = along_y(-HOP[t], core)
        data_wait(0, t, where, 0, full_cols)
        begin(data_copy(0, 2 + t, where, t * half_cols, half_cols, device(x, around(y + HOP[t]), z, core)))
        begin(data_copy(0, 5 + t, where, 0, full_cols, sibling))
    cross_data(0).wait_recv()
    for t in (0, 1):
        begin(data_copy(1, *partner_y(t, 0)))
    forward_z(partner)
    cross_wait(opposite)
    round_z(opposite)
    share_far(x)
    cross_data(1).wait_recv()
    for t in (0, 1):
        begin(data_copy(1, *partner_y(t, 1)))
    begin(data_copy(1, 4, n, 0, full_cols, sibling))
    for t in (0, 1):
        where = along_y(2, core)
        data_wait(0, 2 + t, where, t * half_cols, half_cols)
        begin(far_data(t, side))
        begin(data_copy(0, 7 + t, where, t * half_cols, half_cols, sibling))

    def squares(block):
        value = block.astype(jnp.float32)
        return value * value

    def chunk_product(xi, m, size=256):
        per = full_cols // size
        here = pl.ds(pl.multiple_of(lax.rem(m, per) * size, size), size)
        return lax.dot_general(
            noise_all[xi], data_all[m // per, xi, here, :], (((1,), (1,)), ((), ())),
            preferred_element_type=jnp.float32,
        )

    def norms(xi):
        def norm(r, carry):
            cut = pl.ds(pl.multiple_of(r * 64, 64), 64)
            total = part[cut, :]
            for i in range(SIDE):
                total = total + squares(noise_all[xi, cut, lane(i)])
            part[cut, :] = total
            return carry

        lax.fori_loop(0, rows // 64, norm, 0)

    near, other_block = side * 4, 4 - side * 4

    def unit(block, xs, fresh, count=2):
        def column(i, carry):
            m = block + i
            cut = pl.ds(pl.multiple_of(m * 512, 512), 512)
            value = None if fresh else scores[:, cut]
            for xi in xs:
                product = chunk_product(xi, m, 512)
                value = product if value is None else value + product
            scores[:, cut] = value
            return carry

        lax.fori_loop(0, count, column, 0)

    def add_unit(block, count, xi):
        unit(block, (xi,), False, count)

    data_own.wait()
    data_wait(0, 4, along_y(0, 1 - core), 0, full_cols)
    for t in (0, 1):
        data_wait(0, 5 + t, along_y(-HOP[t], 1 - core), 0, full_cols)
    for t in (0, 1):
        data_wait(0, 7 + t, along_y(2, 1 - core), t * half_cols, half_cols)

    @pl.when(home)
    def _():
        own_half().wait()

    @pl.when(jnp.logical_not(home))
    def _():
        cross_wait(x)

    unit(near // 2, (x,), True)
    share_far(partner)
    norms(x)
    for t in (0, 1):
        noise_wait(mate, t, False)
    far_wait(mate)
    unit(near // 2, (mate,), False)
    norms(mate)

    def beside(t, h, c):
        return data_copy(1, (5 if h == 0 else 13) + t, along_y(-HOP[t], c), h * half_cols, half_cols, sibling)

    for t in (0, 1):
        partner_wait(t, 0)
        begin(beside(t, 0, core))
    unit(near // 2, (partner,), False)
    norms(partner)
    data_wait(1, 4, along_y(0, 1 - core), 0, full_cols)
    for t in (0, 1):
        beside(t, 0, 1 - core).wait_recv()

    def ahead(i, carry):
        xi = around(y + i + i // 2)
        add_unit(other_block // 2, jnp.where(xi == opposite, 0, jnp.where(i == 0, 2, 1)), xi)
        return carry

    lax.fori_loop(0, 3, ahead, 0)
    for t in (0, 1):
        partner_wait(t, 1)
        begin(beside(t, 1, core))
    for t in (0, 1):
        noise_wait(opposite, t, False)
    far_wait(opposite)
    for t in (0, 1):
        far_data(t, 1 - side).wait_recv()
        begin(data_copy(1, 7 + t, along_y(2, core), t * half_cols, half_cols, sibling))
    norms(opposite)

    factor = 2.0 * kappa / width

    def row_shift(r, carry):
        at = pl.ds(pl.multiple_of(r * 128, 128), 128)
        total = jnp.sum(part[at, :], axis=1, keepdims=True) * (-kappa / width)
        shift[at, :] = jnp.broadcast_to(total, (128, LANES))
        return carry

    lax.fori_loop(0, rows // 128, row_shift, 0)

    def final(block, xi):
        def column(i, carry):
            m = block + i
            cut = pl.ds(pl.multiple_of(m * 256, 256), 256)
            value = (scores[:, cut] + chunk_product(xi, m)) * factor
            scores[:, cut] = value
            for e in (0, 1):
                top = jnp.max(value[:, LANES * e:LANES * (e + 1)] + shift[...], axis=0, keepdims=True)
                colvec[:, pl.ds(pl.multiple_of(m * 256 + e * LANES, LANES), LANES)] = jnp.broadcast_to(top, (8, LANES))
            return carry

        lax.fori_loop(0, 4, column, 0)

    final(near, opposite)
    add_unit(other_block // 2, jnp.where(opposite == y, 2, jnp.where(opposite == around(y + 2), 0, 1)), opposite)
    for t in (0, 1):
        beside(t, 1, 1 - core).wait_recv()
    unit(other_block // 2 + 1, (around(y + 1), around(y - 1)), False, 1)
    for t in (0, 1):
        data_wait(1, 7 + t, along_y(2, 1 - core), t * half_cols, half_cols)
    final(other_block, around(y + 2))

    def fold(block, op):
        out = block[0:8]
        for r in range(1, block.shape[0] // 8):
            out = op(out, block[8 * r:8 * r + 8])
        return out

    def spread_cols():
        for c in range(chunks):
            colvec[:, lane(c)] = jnp.broadcast_to(colpack[pl.ds(c, 1), :], (8, LANES))

    def tall(ref, c, size=TILE):
        return jnp.concatenate([ref[:, lane(c)]] * (size // 8), axis=0)

    def tile_at(t):
        return pl.ds(pl.multiple_of(t * TILE, TILE), TILE)

    def loop(body, init):
        return lax.fori_loop(0, tiles, body, init, unroll=2)

    zeros = tuple(jnp.zeros((8, LANES), jnp.float32) for _ in range(chunks))

    def exp_step(t, accs):
        at = pl.ds(pl.multiple_of(t * TALL, TALL), TALL)
        add = shift[at, :]
        return tuple(
            accs[c] + fold(jnp.exp2(scores[at, lane(c)] + add - tall(colvec, c, TALL)), jnp.add)
            for c in range(chunks)
        )

    sums = lax.fori_loop(0, rows // TALL, exp_step, zeros)
    for c in range(chunks):
        total = jnp.sum(sums[c], axis=0, keepdims=True)
        col_buf[0, me_col, pl.ds(c, 1), :] = colvec[0:1, lane(c)] + jnp.log(total) * LOG2E
    exchange(col_buf, col_send, col_recv, 0, me_col, col_peers, started)
    col_pot = -log_cols - combine(col_buf, 0, csize)
    colpack[...] = col_pot
    spread_cols()

    def row_step(t, carry):
        at = pl.ds(pl.multiple_of(t * SHORT, SHORT), SHORT)
        values = [
            scores[at, lane(c)] + jnp.concatenate([colvec[:, lane(c)]] * (SHORT // 8), axis=0) for c in range(chunks)
        ]
        top = values[0]
        for c in range(1, chunks):
            top = jnp.maximum(top, values[c])
        first[at, :] = top
        total = None
        for c in range(chunks):
            value = jnp.exp2(values[c] - top)
            scores[at, lane(c)] = value
            total = value if total is None else total + value
        part[at, :] = total
        return carry

    lax.fori_loop(0, rows // SHORT, row_step, 0, unroll=2)
    for b in range(row_blocks):
        at = pl.ds(b * LANES, LANES)
        tops = first[at, :].T
        top = jnp.max(tops, axis=0, keepdims=True)
        total = jnp.sum(part[at, :].T * jnp.exp2(tops - top), axis=0, keepdims=True)
        row_buf[0, me_row, pl.ds(b, 1), :] = top + jnp.log(total) * LOG2E
    exchange(row_buf, row_send, row_recv, 0, me_row, row_peers, started)
    row_lse = combine(row_buf, 0, rsize)
    rowpack[...] = row_lse
    for b in range(row_blocks):
        at = pl.ds(b * LANES, LANES)
        base = jnp.exp2(first[at, :] - spread_lanes(rowpack, b))
        first[at, :] = base
        scale[at, :] = base

    def col_step(t, accs):
        at = tile_at(t)
        mul = scale[at, :]
        return tuple(accs[c] + fold(scores[at, lane(c)] * mul, jnp.add) for c in range(chunks))

    def sum_step(keep_values):
        def body(t, carry):
            at = pl.ds(pl.multiple_of(t * TALL, TALL), TALL)
            total = None
            for c in range(chunks):
                value = scores[at, lane(c)] * tall(colvec, c, TALL)
                if keep_values:
                    scores[at, lane(c)] = value
                total = value if total is None else total + value
            part[at, :] = total * first[at, :]
            return carry

        return body

    for step in range(1, ITERS):
        sums = loop(col_step, zeros)
        for c in range(chunks):
            col_buf[step, me_col, pl.ds(c, 1), :] = jnp.sum(sums[c], axis=0, keepdims=True)
        exchange(col_buf, col_send, col_recv, step, me_col, col_peers, started)
        ratio = 1.0 / add_slots(col_buf, step, csize)
        colpack[...] = ratio
        spread_cols()
        lax.fori_loop(0, rows // TALL, sum_step(step == ITERS - 1), 0)
        for b in range(row_blocks):
            at = pl.ds(b * LANES, LANES)
            row_buf[step, me_row, pl.ds(b, 1), :] = jnp.sum(part[at, :].T, axis=0, keepdims=True)
        exchange(row_buf, row_send, row_recv, step, me_row, row_peers, started)
        total = add_slots(row_buf, step, rsize)
        rowpack[...] = 1.0 / total
        for b in range(row_blocks):
            at = pl.ds(b * LANES, LANES)
            scale[at, :] = first[at, :] * spread_lanes(rowpack, b)

    def weigh(r):
        def body(t, carry):
            at = pl.ds(pl.multiple_of(r * (rows // 2) + t * TILE, TILE), TILE)
            mul = scale[at, :]
            for c in range(chunks):
                weights[at, lane(c)] = (scores[at, lane(c)] * mul).astype(jnp.bfloat16)
            return carry

        lax.fori_loop(0, tiles // 2, body, 0, unroll=2)

    def swap_copy(i, to):
        return remote(swap.at[0], swap.at[i], swap_send.at[i], swap_recv.at[i], to)

    def potentials():
        for c in range(chunks):
            sqy[pl.ds(c, 1), :] = jnp.sum(data_part[pl.ds(c * LANES, LANES), :].T, axis=0, keepdims=True)
        cols_pot = (col_pot + jnp.log(ratio) * LOG2E + (log_rows - log_cols)) / kappa + sqy[...] / width
        colpack[...] = cols_pot
        cols_out[...] = colpack[pl.ds(pl.multiple_of(side * 8, 8), 8), :]
        for b in range(row_blocks):
            sqx[pl.ds(b, 1), :] = shift[pl.ds(b * LANES, LANES), :].T[0:1]
        swap[0] = -(log_rows + row_lse + jnp.log(total) * LOG2E + sqx[...]) / kappa
        begin(swap_copy(1, sibling))
        for i in (0, 1):
            begin(remote(
                swap.at[0], swap.at[2 + core], swap_send.at[2 + i], swap_recv.at[2 + core], device(partner, y, z, i)
            ))

    strip = rows // 2

    def half_rows(r):
        return pl.ds(pl.multiple_of(r * strip, strip), strip)

    def block_x(b):
        return jnp.where(b < 2, jnp.where(b == 0, opposite, mate), jnp.where(b == 2, partner, x))

    def product(p, r, to_z):
        cut = pl.ds(pl.multiple_of(to_z * LANES, LANES), LANES)
        total = None
        for k in (0, 1):
            block = jnp.concatenate(
                [data_all[k, block_x(2 * p + e), :, cut] for e in (0, 1)], axis=1
            )
            value = jnp.dot(
                weights[half_rows(r), k * full_cols:(k + 1) * full_cols], block,
                preferred_element_type=jnp.float32,
            )
            total = value if total is None else total + value
        return total

    def hop(t):
        return 1 - 2 * t

    def sum_copy(b, t, index, src, dst):
        to = device(x, y, around(z + hop(t)), core)
        return remote(src, dst, sum_send.at[b, t, index], sum_recv.at[b, t, index], to)

    def far_copy(b, t):
        return sum_copy(b, t, 0, out_buf.at[b, 2, half_rows(t)], far_buf.at[b - 2, t])

    def direct_copy(b, t):
        at = half_rows(1 - t)
        return sum_copy(b, t, 1, out_buf.at[b, t, at], near_buf.at[b, t, at])

    def added_copy(b, t):
        at = half_rows(t)
        return sum_copy(b, t, 2, out_buf.at[b, t, at], near_buf.at[b, t, at])

    def give_copy(b, r):
        at = half_rows(r)
        return remote(
            out_buf.at[b, 2, at], given.at[b, at], give_send.at[b, r], give_recv.at[b, r], device(mate, y, z, core)
        )

    def relay_copy(r):
        at = half_rows(r)
        return remote(own_buf.at[0, at], relay_in.at[at], in_send.at[r], in_recv.at[4 + r], device(mate, y, z, core))

    def partner_copy(a, r):
        at = half_rows(r)
        return remote(
            own_buf.at[2, at], in_sum.at[a, at], in_send.at[2 + r], part_recv.at[a, r], device(partner, y, z, kind)
        )

    def mate_copy(a):
        return remote(mate_out, mate_in.at[a], in_send.at[4], in_recv.at[2 + a], device(mate, y, z, kind))

    def stay_copy(a):
        return remote(own_buf.at[3], in_sum.at[a], in_send.at[5], in_recv.at[a], sibling)

    def add_far(b):
        for t in (0, 1):
            far_copy(b, t).wait_recv()
            out_buf[b, t, half_rows(t), :] = (
                keep[b - 2, t] + far_buf[b - 2, t].astype(jnp.float32)
            ).astype(jnp.bfloat16)
            added_copy(b, t).start()

    def add_near(b):
        for t in (0, 1):
            direct_copy(b, t).wait_recv()
            added_copy(b, t).wait_recv()
        own_buf[b] = own_buf[b] + near_buf[b, 0].astype(jnp.float32) + near_buf[b, 1].astype(jnp.float32)

    def add_given(b):
        for r in (0, 1):
            at = half_rows(r)
            give_copy(b - 2, r).wait_recv()
            out_buf[b, 2, at, :] = (far_keep[b - 2, at, :] + given[b - 2, at, :].astype(jnp.float32)).astype(jnp.bfloat16)
            far_copy(b, r).start()

    def halves(body):
        def step(r, carry):
            body(r)
            return carry

        lax.fori_loop(0, 2, step, 0)

    def lead(r):
        t = 1 - r
        weigh(r)
        value = product(1, r, around(z + hop(t)))
        for e in (0, 1):
            out_buf[2 + e, t, half_rows(r), :] = value[:, lane(e)].astype(jnp.bfloat16)
        direct_copy(2, t).start()

    def give(r):
        value = product(0, r, around(z + 2))
        for e in (0, 1):
            out_buf[e, 2, half_rows(r), :] = value[:, lane(e)].astype(jnp.bfloat16)
        give_copy(0, r).start()

    def next_products(t):
        def part_of(r):
            value = product(0, r, around(z + hop(t)))
            for e in (0, 1):
                out_buf[e, t, half_rows(r), :] = value[:, lane(e)].astype(jnp.bfloat16)

        halves(part_of)
        direct_copy(0, t).start()
        added_copy(0, t).start()

    def kept_products(t):
        value = product(1, t, around(z + hop(t)))
        for e in (0, 1):
            keep[e, t] = value[:, lane(e)]

    def far_products(r):
        value = product(1, r, around(z + 2))
        for e in (0, 1):
            far_keep[e, half_rows(r), :] = value[:, lane(e)]

    def own_products(p):
        def part_of(r):
            value = product(p, r, z)
            for e in (0, 1):
                own_buf[2 * p + e, half_rows(r), :] = value[:, lane(e)]

        halves(part_of)

    halves(lead)
    halves(give)
    for r in (0, 1):
        give_copy(1, r).start()
    halves(next_products)
    halves(far_products)
    add_given(2)
    for t in (0, 1):
        direct_copy(1, t).start()
    halves(kept_products)
    halves(own_products)
    add_near(0)
    for r in (0, 1):
        relay_copy(r).start()
    add_far(2)
    for t in (0, 1):
        added_copy(1, t).start()
    add_given(3)
    for t in (0, 1):
        direct_copy(3, t).start()
    def data_norms(r, carry):
        per = full_cols // 64
        here = pl.ds(pl.multiple_of(lax.rem(r, per) * 64, 64), 64)
        total = None
        for xi in range(SIDE):
            for i in range(SIDE):
                value = squares(data_all[r // per, xi, here, lane(i)])
                total = value if total is None else total + value
        data_part[pl.ds(pl.multiple_of(r * 64, 64), 64), :] = total
        return carry

    lax.fori_loop(0, cols // 64, data_norms, 0)
    add_near(2)

    def to_partner(r):
        relay_copy(r).wait_recv()
        own_buf[2, half_rows(r), :] = own_buf[2, half_rows(r), :] + relay_in[half_rows(r), :]
        partner_copy(core, r).start()

    to_partner(0)
    add_near(1)
    mate_out[...] = own_buf[1].astype(jnp.bfloat16)
    mate_copy(core).start()
    potentials()
    for copy in started:
        copy.wait_send()

    @pl.when(home)
    def _():
        aside.wait_send()
        for t in (0, 1):
            for a in (0, 1):
                own_round(t, a).wait_send()

    add_far(3)
    to_partner(1)

    def settle(b, carry):
        for t in (0, 1):
            direct_copy(b, t).wait_send()
            added_copy(b, t).wait_send()

            @pl.when(b < 2)
            def _():
                give_copy(jnp.minimum(b, 1), t).wait_send()

            @pl.when(b >= 2)
            def _():
                far_copy(jnp.maximum(b, 2), t).wait_send()

        return carry

    lax.fori_loop(0, 3, settle, 0)
    for r in (0, 1):
        relay_copy(r).wait_send()
    swap_copy(1, sibling).wait_recv()
    for i in (0, 1):
        remote(swap.at[0], swap.at[2 + i], swap_send.at[2 + i], swap_recv.at[2 + i], sibling).wait_recv()
    half = rows // LANES
    for a in (0, 1):
        mine_row = jnp.where(core == a, swap[0], swap[1])
        rows_out[pl.ds(a * half, half), :] = jnp.where(home, mine_row, swap[2 + a])

    add_near(3)

    @pl.when(home)
    def _():
        in_sum[core] = own_buf[3]
        stay_copy(1 - core).wait_recv()
        for a in (0, 1):
            mate_copy(a).wait_recv()
            in_sum[a] = in_sum[a] + mate_in[a].astype(jnp.float32)

    @pl.when(jnp.logical_not(home))
    def _():
        stay_copy(core).start()
        for a in (0, 1):
            for r in (0, 1):
                partner_copy(a, r).wait_recv()

    def result_copy(a):
        return pltpu.make_async_copy(in_sum.at[a], targets.at[pl.ds(a * rows, rows)], local_sems.at[a])

    for a in (0, 1):
        result_copy(a).start()

    settle(3, 0)
    for a in (0, 1):
        result_copy(a).wait()
    for r in (0, 1):
        partner_copy(core, r).wait_send()
    mate_copy(core).wait_send()

    @pl.when(jnp.logical_not(home))
    def _():
        stay_copy(core).wait_send()


def hand_on(targets, rows_pot, cols_pot, targets_out, rows_out, cols_out, stage, row_stage, col_stage, sems):
    size = targets.shape[0] // PARTS
    legs = [
        (targets.at[pl.ds(i * size, size)], stage.at[i], targets_out.at[pl.ds(i * size, size)]) for i in range(PARTS)
    ]
    legs += [(rows_pot, row_stage, rows_out), (cols_pot, col_stage, cols_out)]
    first = [pltpu.make_async_copy(src, mid, sems.at[i, 0]) for i, (src, mid, _) in enumerate(legs)]
    second = [pltpu.make_async_copy(mid, dst, sems.at[i, 1]) for i, (_, mid, dst) in enumerate(legs)]
    for copy in first:
        copy.start()
    for before, copy in zip(first, second):
        before.wait()
        copy.start()
    for copy in second:
        copy.wait()


def shards(noise_latents, data_latents):
    nsize = lax.axis_size("noise")
    dsize = lax.axis_size("dp")
    block, piece = noise_latents.shape
    rows, cols = block // 2, 2 * data_latents.shape[0]
    rsize, csize = dsize // 2, nsize * 2
    vmem = pl.BlockSpec(memory_space=pltpu.VMEM)
    f32, bf16 = jnp.float32, jnp.bfloat16
    strip = rows // 2
    row_vec, col_vec = (rows // LANES, LANES), (cols // LANES, LANES)
    sems = pltpu.SemaphoreType.DMA
    targets, rows_pot, cols_pot = pl.pallas_call(
        functools.partial(kernel, rsize, csize, piece * dsize),
        out_shape=(
            jax.ShapeDtypeStruct((block, piece), f32),
            jax.ShapeDtypeStruct((block // LANES, LANES), f32),
            jax.ShapeDtypeStruct((cols // 2 // LANES, LANES), f32),
        ),
        in_specs=[pl.BlockSpec(memory_space=pl.ANY)] * 2,
        out_specs=(pl.BlockSpec(memory_space=pl.ANY), vmem, vmem),
        scratch_shapes=[
            pltpu.VMEM((SIDE, rows, SIDE * piece), bf16),
            pltpu.VMEM((2, SIDE, cols // 2, nsize // SIDE * data_latents.shape[1]), bf16),
            pltpu.VMEM((rows, cols), f32),
            pltpu.VMEM((rows, cols), bf16),
            pltpu.VMEM((rows, LANES), f32),
            pltpu.VMEM((rows, LANES), f32),
            pltpu.VMEM((rows, LANES), f32),
            pltpu.VMEM((rows, LANES), f32),
            pltpu.VMEM((cols, LANES), f32),
            pltpu.VMEM((8, cols), f32),
            pltpu.VMEM(row_vec, f32),
            pltpu.VMEM(col_vec, f32),
            pltpu.VMEM(row_vec, f32),
            pltpu.VMEM(col_vec, f32),
            pltpu.VMEM((4,) + row_vec, f32),
            pltpu.VMEM((ITERS, csize) + col_vec, f32),
            pltpu.VMEM((ITERS, rsize) + row_vec, f32),
            pltpu.VMEM((SIDE, 3, rows, LANES), bf16),
            pltpu.VMEM((SIDE, rows, LANES), f32),
            pltpu.VMEM((2, 2, strip, LANES), bf16),
            pltpu.VMEM((SIDE, 2, rows, LANES), bf16),
            pltpu.VMEM((2, rows, LANES), f32),
            sems((ITERS,)),
            sems((ITERS,)),
            sems((ITERS,)),
            sems((ITERS,)),
            sems((4,)),
            sems((4,)),
            sems((4,)),
            sems((4,)),
            sems((SIDE, 2, 2)),
            sems((SIDE, 2, 2)),
            sems((2, 15)),
            sems((2, 15)),
            sems((SIDE, 2, 3)),
            sems((SIDE, 2, 3)),
            sems((6,)),
            sems((6,)),
            pltpu.VMEM((2, 2, strip, LANES), f32),
            pltpu.VMEM((2, rows, LANES), f32),
            pltpu.VMEM((2, rows, LANES), bf16),
            sems((2, 2)),
            sems((2, 2)),
            sems((2, 2)),
            sems((2,)),
            sems((2, 2)),
            sems((SIDE, 2)),
            pltpu.VMEM((rows, LANES), f32),
            pltpu.VMEM((rows, LANES), bf16),
            pltpu.VMEM((2, rows, LANES), bf16),
        ],
        compiler_params=pltpu.CompilerParams(
            collective_id=0, has_side_effects=True, vmem_limit_bytes=60 * 2**20
        ),
    )(noise_latents, data_latents)
    results = (targets, rows_pot, cols_pot)
    targets, rows_pot, cols_pot = pl.pallas_call(
        hand_on,
        out_shape=tuple(jax.ShapeDtypeStruct(a.shape, a.dtype) for a in results),
        in_specs=[pl.BlockSpec(memory_space=pl.ANY)] * 3,
        out_specs=(pl.BlockSpec(memory_space=pl.ANY),) * 3,
        scratch_shapes=[
            pltpu.VMEM((PARTS, block // PARTS, piece), f32),
            pltpu.VMEM(rows_pot.shape, f32),
            pltpu.VMEM(cols_pot.shape, f32),
            sems((PARTS + 2, 2)),
        ],
        compiler_params=pltpu.CompilerParams(vmem_limit_bytes=60 * 2**20),
    )(*results)
    return targets, rows_pot.reshape(block), cols_pot.reshape(cols // 2)


def solution(mesh):
    return jax.shard_map(
        shards,
        mesh=mesh,
        in_specs=(P("noise", "dp"), P("dp", "noise")),
        out_specs=(P("noise", "dp"), P("noise"), P("dp")),
        check_vma=False,
    )
```

```python
import functools
import math

import jax
import jax.numpy as jnp
from jax import lax
from jax.experimental import pallas as pl
from jax.experimental.pallas import tpu as pltpu
from jax.sharding import PartitionSpec as P

ITERS = 3
EPSILON = 0.04
LOG2E = 1.0 / math.log(2.0)
MESH = pl.DeviceIdType.MESH
LANES = 128
TILE = 32
SHORT = 16
TALL = 64
SIDE = 4
PARTS = 4


def spread_lanes(ref, row):
    return jnp.broadcast_to(ref[pl.ds(row, 1), :], (LANES, LANES)).T


def exchange(buf, send, recv, step, me, peers, started):
    for peer in peers:
        pltpu.make_async_remote_copy(
            src_ref=buf.at[step, me],
            dst_ref=buf.at[step, me],
            send_sem=send.at[step],
            recv_sem=recv.at[step],
            device_id=peer,
            device_id_type=MESH,
        ).start()
    slots = buf.at[step, pl.ds(0, len(peers))]
    every = pltpu.make_async_remote_copy(
        src_ref=slots,
        dst_ref=slots,
        send_sem=send.at[step],
        recv_sem=recv.at[step],
        device_id=peers[0],
        device_id_type=MESH,
    )
    every.wait_recv()
    started.append(every)


def combine(buf, step, size):
    top = buf[step, 0]
    for s in range(1, size):
        top = jnp.maximum(top, buf[step, s])
    total = jnp.exp2(buf[step, 0] - top)
    for s in range(1, size):
        total = total + jnp.exp2(buf[step, s] - top)
    return top + jnp.log(total) * LOG2E


def add_slots(buf, step, size):
    total = buf[step, 0]
    for s in range(1, size):
        total = total + buf[step, s]
    return total


def kernel(
    rsize, csize, width,
    noise_ref, data_ref,
    targets, rows_out, cols_out,
    noise_all, data_all, scores, weights,
    shift, first, scale, part, data_part, colvec, rowpack, colpack, sqx, sqy, swap,
    col_buf, row_buf, out_buf, own_buf, far_buf, near_buf, in_sum,
    col_send, col_recv, row_send, row_recv, swap_send, swap_recv,
    cross_send, cross_recv, noise_send, noise_recv, data_send, data_recv,
    sum_send, sum_recv, in_send, in_recv, keep, far_keep, given, give_send, give_recv, part_recv, local_sems, own_send, far_send, relay_in, mate_out, mate_in,
):
    rows, cols = scores.shape
    n = lax.axis_index("noise")
    d = lax.axis_index("dp")
    x, z = d // SIDE, lax.rem(d, SIDE)
    y, core = n // 2, lax.rem(n, 2)
    kind = lax.rem((x + 1) // 2, 2)
    pair = x // 2
    side = lax.rem(x, 2)
    home = core == kind
    kappa = LOG2E / EPSILON
    log_rows = math.log2(rows * csize)
    log_cols = math.log2(cols * rsize)
    chunks = cols // LANES
    row_blocks = rows // LANES
    tiles = rows // TILE
    started = []

    def around(value):
        return lax.rem(value + SIDE, SIDE)

    def device(xi, yi, zi, ci):
        return (yi * 2 + ci, xi * SIDE + zi)

    me_row = pair * SIDE + z
    me_col = y * 4 + kind * 2 + core

    sibling = device(x, y, z, 1 - core)
    partner = x + 1 - 2 * side
    mate = SIDE - 1 - x
    opposite = around(x + 2)

    barrier = pltpu.get_barrier_semaphore()
    ys, zs = [around(y + k) for k in range(SIDE)], [around(z + k) for k in range(SIDE)]
    rings = [yi * 2 + ci for yi in (ys[2], ys[1], ys[3], ys[0]) for ci in (1 - core, core)]
    col_peers = [(r, di) for di in (partner * SIDE + z, d) for r in rings][:-1]
    row_peers = [(n, xi * SIDE + zi) for xi in (mate, x) for zi in (zs[2], zs[1], zs[3], zs[0])][:-1]
    greeted = [sibling]
    for ci in (0, 1):
        greeted += [device(partner, y, z, ci), device(mate, y, z, ci), device(x, y, zs[1], ci), device(x, y, zs[3], ci)]
    greeted += [device(x, ys[1], z, core), device(x, ys[3], z, core)]
    for to in greeted:
        pl.semaphore_signal(barrier, inc=1, device_id=to, device_id_type=MESH)
    pl.semaphore_wait(barrier, len(greeted))

    def remote(src, dst, send, recv, to):
        return pltpu.make_async_remote_copy(
            src_ref=src, dst_ref=dst, send_sem=send, recv_sem=recv, device_id=to, device_id_type=MESH
        )

    def begin(copy):
        copy.start()
        started.append(copy)

    def lane(c):
        return slice(LANES * c, LANES * (c + 1))

    HOP = (1, -1)

    def noise_slot(xi, zi, at):
        return noise_all.at[xi, at, pl.ds(pl.multiple_of(zi * LANES, LANES), LANES)]

    own = noise_slot(x, z, pl.ds(0, rows))

    def cross_copy(i, half, to):
        return remote(
            noise_ref.at[pl.ds(half * rows, rows)], own, cross_send.at[i], cross_recv.at[x], to
        )

    def cross_wait(xi):
        remote(
            noise_ref.at[pl.ds(0, rows)], noise_slot(xi, z, pl.ds(0, rows)), cross_send.at[0], cross_recv.at[xi], sibling
        ).wait_recv()

    there = jnp.where(home, mate, partner)
    aside = cross_copy(2, 1 - core, sibling)

    def noise_copy(xi, t, forward, zi):
        at = pl.ds(t * (rows // 2), rows // 2) if forward else pl.ds(0, rows)
        f = int(forward)
        slot = noise_slot(xi, zi, at)
        return remote(
            slot, slot, noise_send.at[xi, t, f], noise_recv.at[xi, t, f], device(x, y, around(z + HOP[t]), core)
        )

    def noise_wait(xi, t, forward):
        zi = around(z - HOP[t] * (2 if forward else 1))
        noise_copy(xi, t, forward, zi).wait_recv()
        return zi

    def data_slot(block, where, at):
        width_at = pl.ds(pl.multiple_of(lax.rem(where, 2) * 256, 256), 256)
        return data_all.at[block, where // 2, at, width_at]

    def data_copy(r, index, where, lo, size, to, own=False):
        at = pl.ds(lo, size)
        block = side if r == 0 else 1 - side
        dst = data_slot(block, where, at)
        return remote(data_ref.at[at] if own else dst, dst, data_send.at[r, index], data_recv.at[r, index], to)

    half_cols = cols // 4
    full_cols = cols // 2

    def along_y(step, c):
        return around(y + step) * 2 + c

    def data_wait(r, index, where, lo, size):
        data_copy(r, index, where, lo, size, sibling).wait_recv()

    HALF = 9

    def cross_data(h, own=False):
        at = pl.ds(h * half_cols, half_cols)
        dst = data_slot(side if own else 1 - side, n, at)
        return remote(
            data_ref.at[at], dst, data_send.at[1, 11 + h], data_recv.at[1, 11 + h], device(partner, y, z, core)
        )

    def partner_y(t, h, back=0):
        where = around(y + back) * 2 + core
        to = device(x, around(y + HOP[t]), z, core)
        return t if h == 0 else HALF + t, where, h * half_cols, half_cols, to

    def partner_wait(t, h):
        data_copy(1, *partner_y(t, h, -HOP[t])).wait_recv()

    def own_round(t, a):
        return remote(
            noise_ref.at[pl.ds(a * rows, rows)], own,
            own_send.at[t, a], noise_recv.at[x, t, 0], device(x, y, around(z + HOP[t]), a),
        )

    def own_half():
        return pltpu.make_async_copy(
            noise_ref.at[pl.ds(pl.multiple_of(core * rows, rows), rows)], own, local_sems.at[0]
        )

    @pl.when(home)
    def _():
        for t in (0, 1):
            for a in (0, 1):
                own_round(t, a).start()
        aside.start()

    begin(cross_copy(0, 0, device(there, y, z, 0)))
    begin(cross_copy(1, 1, device(there, y, z, 1)))
    for t in (0, 1):
        begin(data_copy(0, t, n, 0, full_cols, device(x, around(y + HOP[t]), z, core), own=True))
    @pl.when(home)
    def _():
        own_half().start()

    data_own = pltpu.make_async_copy(data_ref, data_slot(side, n, pl.ds(0, full_cols)), local_sems.at[1])
    data_own.start()
    scores[...] = jnp.zeros_like(scores)
    part[...] = jnp.zeros_like(part)

    def round_z(xi):
        for t in (0, 1):
            begin(noise_copy(xi, t, False, z))

    def forward_z(xi):
        for t in (0, 1):
            begin(noise_copy(xi, t, True, noise_wait(xi, t, False)))

    def far_noise(xi, t):
        slot = noise_slot(xi, around(z + 2), pl.ds(t * (rows // 2), rows // 2))
        return remote(slot, slot, far_send.at[xi, t], noise_recv.at[xi, t, 1], device(mate, y, z, core))

    def share_far(xi):
        for t in (0, 1):
            noise_wait(xi, t, True)
            begin(far_noise(xi, t))

    def far_wait(xi):
        for t in (0, 1):
            far_noise(xi, t).wait_recv()

    def far_data(t, block):
        where = along_y(2, core)
        at = pl.ds(t * half_cols, half_cols)
        dst = data_slot(block, where, at)
        return remote(dst, dst, data_send.at[1, 2 + t], data_recv.at[1, 2 + t], device(partner, y, z, core))

    cross_wait(partner)
    slot = noise_slot(partner, z, pl.ds(0, rows))
    begin(remote(slot, slot, cross_send.at[3], cross_recv.at[partner], device(mate, y, z, core)))
    round_z(partner)
    for h in (0, 1):
        begin(cross_data(h, own=True))
    begin(data_copy(0, 4, n, 0, full_cols, sibling, own=True))
    forward_z(x)
    cross_wait(mate)
    round_z(mate)
    for t in (0, 1):
        where = along_y(-HOP[t], core)
        data_wait(0, t, where, 0, full_cols)
        begin(data_copy(0, 2 + t, where, t * half_cols, half_cols, device(x, around(y + HOP[t]), z, core)))
        begin(data_copy(0, 5 + t, where, 0, full_cols, sibling))
    cross_data(0).wait_recv()
    for t in (0, 1):
        begin(data_copy(1, *partner_y(t, 0)))
    forward_z(partner)
    cross_wait(opposite)
    round_z(opposite)
    share_far(x)
    cross_data(1).wait_recv()
    for t in (0, 1):
        begin(data_copy(1, *partner_y(t, 1)))
    begin(data_copy(1, 4, n, 0, full_cols, sibling))
    for t in (0, 1):
        where = along_y(2, core)
        data_wait(0, 2 + t, where, t * half_cols, half_cols)
        begin(far_data(t, side))
        begin(data_copy(0, 7 + t, where, t * half_cols, half_cols, sibling))

    def squares(block):
        value = block.astype(jnp.float32)
        return value * value

    def chunk_product(xi, m, size=256):
        per = full_cols // size
        here = pl.ds(pl.multiple_of(lax.rem(m, per) * size, size), size)
        return lax.dot_general(
            noise_all[xi], data_all[m // per, xi, here, :], (((1,), (1,)), ((), ())),
            preferred_element_type=jnp.float32,
        )

    def norms(xi):
        def norm(r, carry):
            cut = pl.ds(pl.multiple_of(r * 64, 64), 64)
            total = part[cut, :]
            for i in range(SIDE):
                total = total + squares(noise_all[xi, cut, lane(i)])
            part[cut, :] = total
            return carry

        lax.fori_loop(0, rows // 64, norm, 0)

    near, other_block = side * 4, 4 - side * 4

    def unit(block, xs, fresh, count=2):
        def column(i, carry):
            m = block + i
            cut = pl.ds(pl.multiple_of(m * 512, 512), 512)
            value = None if fresh else scores[:, cut]
            for xi in xs:
                product = chunk_product(xi, m, 512)
                value = product if value is None else value + product
            scores[:, cut] = value
            return carry

        lax.fori_loop(0, count, column, 0)

    def add_unit(block, count, xi):
        unit(block, (xi,), False, count)

    data_own.wait()
    data_wait(0, 4, along_y(0, 1 - core), 0, full_cols)
    for t in (0, 1):
        data_wait(0, 5 + t, along_y(-HOP[t], 1 - core), 0, full_cols)
    for t in (0, 1):
        data_wait(0, 7 + t, along_y(2, 1 - core), t * half_cols, half_cols)

    @pl.when(home)
    def _():
        own_half().wait()

    @pl.when(jnp.logical_not(home))
    def _():
        cross_wait(x)

    unit(near // 2, (x,), True)
    share_far(partner)
    norms(x)
    for t in (0, 1):
        noise_wait(mate, t, False)
    far_wait(mate)
    unit(near // 2, (mate,), False)
    norms(mate)

    def beside(t, h, c):
        return data_copy(1, (5 if h == 0 else 13) + t, along_y(-HOP[t], c), h * half_cols, half_cols, sibling)

    for t in (0, 1):
        partner_wait(t, 0)
        begin(beside(t, 0, core))
    unit(near // 2, (partner,), False)
    norms(partner)
    data_wait(1, 4, along_y(0, 1 - core), 0, full_cols)
    for t in (0, 1):
        beside(t, 0, 1 - core).wait_recv()

    def ahead(i, carry):
        xi = around(y + i + i // 2)
        add_unit(other_block // 2, jnp.where(xi == opposite, 0, jnp.where(i == 0, 2, 1)), xi)
        return carry

    lax.fori_loop(0, 3, ahead, 0)
    for t in (0, 1):
        partner_wait(t, 1)
        begin(beside(t, 1, core))
    for t in (0, 1):
        noise_wait(opposite, t, False)
    far_wait(opposite)
    for t in (0, 1):
        far_data(t, 1 - side).wait_recv()
        begin(data_copy(1, 7 + t, along_y(2, core), t * half_cols, half_cols, sibling))
    norms(opposite)

    factor = 2.0 * kappa / width

    def row_shift(r, carry):
        at = pl.ds(pl.multiple_of(r * 128, 128), 128)
        total = jnp.sum(part[at, :], axis=1, keepdims=True) * (-kappa / width)
        shift[at, :] = jnp.broadcast_to(total, (128, LANES))
        return carry

    lax.fori_loop(0, rows // 128, row_shift, 0)

    def final(block, xi):
        def column(i, carry):
            m = block + i
            cut = pl.ds(pl.multiple_of(m * 512, 512), 512)
            value = (scores[:, cut] + chunk_product(xi, m, 512)) * factor
            scores[:, cut] = value
            for e in range(SIDE):
                top = jnp.max(value[:, lane(e)] + shift[...], axis=0, keepdims=True)
                colvec[:, pl.ds(pl.multiple_of(m * 512 + e * LANES, LANES), LANES)] = jnp.broadcast_to(top, (8, LANES))
            return carry

        lax.fori_loop(0, 2, column, 0)

    final(near // 2, opposite)
    add_unit(other_block // 2, jnp.where(opposite == y, 2, jnp.where(opposite == around(y + 2), 0, 1)), opposite)
    for t in (0, 1):
        beside(t, 1, 1 - core).wait_recv()
    unit(other_block // 2 + 1, (around(y + 1), around(y - 1)), False, 1)
    for t in (0, 1):
        data_wait(1, 7 + t, along_y(2, 1 - core), t * half_cols, half_cols)
    final(other_block // 2, around(y + 2))

    def fold(block, op):
        out = block[0:8]
        for r in range(1, block.shape[0] // 8):
            out = op(out, block[8 * r:8 * r + 8])
        return out

    def spread_cols():
        for c in range(chunks):
            colvec[:, lane(c)] = jnp.broadcast_to(colpack[pl.ds(c, 1), :], (8, LANES))

    def tall(ref, c, size=TILE):
        return jnp.concatenate([ref[:, lane(c)]] * (size // 8), axis=0)

    def tile_at(t):
        return pl.ds(pl.multiple_of(t * TILE, TILE), TILE)

    def loop(body, init):
        return lax.fori_loop(0, tiles, body, init, unroll=2)

    zeros = tuple(jnp.zeros((8, LANES), jnp.float32) for _ in range(chunks))

    def exp_step(t, accs):
        at = pl.ds(pl.multiple_of(t * TALL, TALL), TALL)
        add = shift[at, :]
        return tuple(
            accs[c] + fold(jnp.exp2(scores[at, lane(c)] + add - tall(colvec, c, TALL)), jnp.add)
            for c in range(chunks)
        )

    sums = lax.fori_loop(0, rows // TALL, exp_step, zeros)
    for c in range(chunks):
        total = jnp.sum(sums[c], axis=0, keepdims=True)
        col_buf[0, me_col, pl.ds(c, 1), :] = colvec[0:1, lane(c)] + jnp.log(total) * LOG2E
    exchange(col_buf, col_send, col_recv, 0, me_col, col_peers, started)
    col_pot = -log_cols - combine(col_buf, 0, csize)
    colpack[...] = col_pot
    spread_cols()

    def row_step(t, carry):
        at = pl.ds(pl.multiple_of(t * SHORT, SHORT), SHORT)
        values = [
            scores[at, lane(c)] + jnp.concatenate([colvec[:, lane(c)]] * (SHORT // 8), axis=0) for c in range(chunks)
        ]
        top = values[0]
        for c in range(1, chunks):
            top = jnp.maximum(top, values[c])
        first[at, :] = top
        total = None
        for c in range(chunks):
            value = jnp.exp2(values[c] - top)
            scores[at, lane(c)] = value
            total = value if total is None else total + value
        part[at, :] = total
        return carry

    lax.fori_loop(0, rows // SHORT, row_step, 0, unroll=2)
    for b in range(row_blocks):
        at = pl.ds(b * LANES, LANES)
        tops = first[at, :].T
        top = jnp.max(tops, axis=0, keepdims=True)
        total = jnp.sum(part[at, :].T * jnp.exp2(tops - top), axis=0, keepdims=True)
        row_buf[0, me_row, pl.ds(b, 1), :] = top + jnp.log(total) * LOG2E
    exchange(row_buf, row_send, row_recv, 0, me_row, row_peers, started)
    row_lse = combine(row_buf, 0, rsize)
    rowpack[...] = row_lse
    for b in range(row_blocks):
        at = pl.ds(b * LANES, LANES)
        base = jnp.exp2(first[at, :] - spread_lanes(rowpack, b))
        first[at, :] = base
        scale[at, :] = base

    def col_step(t, accs):
        at = tile_at(t)
        mul = scale[at, :]
        return tuple(accs[c] + fold(scores[at, lane(c)] * mul, jnp.add) for c in range(chunks))

    def sum_step(keep_values):
        def body(t, carry):
            at = pl.ds(pl.multiple_of(t * TALL, TALL), TALL)
            total = None
            for c in range(chunks):
                value = scores[at, lane(c)] * tall(colvec, c, TALL)
                if keep_values:
                    scores[at, lane(c)] = value
                total = value if total is None else total + value
            part[at, :] = total * first[at, :]
            return carry

        return body

    for step in range(1, ITERS):
        sums = loop(col_step, zeros)
        for c in range(chunks):
            col_buf[step, me_col, pl.ds(c, 1), :] = jnp.sum(sums[c], axis=0, keepdims=True)
        exchange(col_buf, col_send, col_recv, step, me_col, col_peers, started)
        ratio = 1.0 / add_slots(col_buf, step, csize)
        colpack[...] = ratio
        spread_cols()
        lax.fori_loop(0, rows // TALL, sum_step(step == ITERS - 1), 0)
        for b in range(row_blocks):
            at = pl.ds(b * LANES, LANES)
            row_buf[step, me_row, pl.ds(b, 1), :] = jnp.sum(part[at, :].T, axis=0, keepdims=True)
        exchange(row_buf, row_send, row_recv, step, me_row, row_peers, started)
        total = add_slots(row_buf, step, rsize)
        rowpack[...] = 1.0 / total
        for b in range(row_blocks):
            at = pl.ds(b * LANES, LANES)
            scale[at, :] = first[at, :] * spread_lanes(rowpack, b)

    def weigh(r):
        def body(t, carry):
            at = pl.ds(pl.multiple_of(r * (rows // 2) + t * TILE, TILE), TILE)
            mul = scale[at, :]
            for c in range(chunks):
                weights[at, lane(c)] = (scores[at, lane(c)] * mul).astype(jnp.bfloat16)
            return carry

        lax.fori_loop(0, tiles // 2, body, 0, unroll=2)

    def swap_copy(i, to):
        return remote(swap.at[0], swap.at[i], swap_send.at[i], swap_recv.at[i], to)

    def potentials():
        for c in range(chunks):
            sqy[pl.ds(c, 1), :] = jnp.sum(data_part[pl.ds(c * LANES, LANES), :].T, axis=0, keepdims=True)
        cols_pot = (col_pot + jnp.log(ratio) * LOG2E + (log_rows - log_cols)) / kappa + sqy[...] / width
        colpack[...] = cols_pot
        cols_out[...] = colpack[pl.ds(pl.multiple_of(side * 8, 8), 8), :]
        for b in range(row_blocks):
            sqx[pl.ds(b, 1), :] = shift[pl.ds(b * LANES, LANES), :].T[0:1]
        swap[0] = -(log_rows + row_lse + jnp.log(total) * LOG2E + sqx[...]) / kappa
        begin(swap_copy(1, sibling))
        for i in (0, 1):
            begin(remote(
                swap.at[0], swap.at[2 + core], swap_send.at[2 + i], swap_recv.at[2 + core], device(partner, y, z, i)
            ))

    strip = rows // 2

    def half_rows(r):
        return pl.ds(pl.multiple_of(r * strip, strip), strip)

    def block_x(b):
        return jnp.where(b < 2, jnp.where(b == 0, opposite, mate), jnp.where(b == 2, partner, x))

    def product(p, r, to_z):
        cut = pl.ds(pl.multiple_of(to_z * LANES, LANES), LANES)
        total = None
        for k in (0, 1):
            block = jnp.concatenate(
                [data_all[k, block_x(2 * p + e), :, cut] for e in (0, 1)], axis=1
            )
            value = jnp.dot(
                weights[half_rows(r), k * full_cols:(k + 1) * full_cols], block,
                preferred_element_type=jnp.float32,
            )
            total = value if total is None else total + value
        return total

    def hop(t):
        return 1 - 2 * t

    def sum_copy(b, t, index, src, dst):
        to = device(x, y, around(z + hop(t)), core)
        return remote(src, dst, sum_send.at[b, t, index], sum_recv.at[b, t, index], to)

    def far_copy(b, t):
        return sum_copy(b, t, 0, out_buf.at[b, 2, half_rows(t)], far_buf.at[b - 2, t])

    def direct_copy(b, t):
        at = half_rows(1 - t)
        return sum_copy(b, t, 1, out_buf.at[b, t, at], near_buf.at[b, t, at])

    def added_copy(b, t):
        at = half_rows(t)
        return sum_copy(b, t, 2, out_buf.at[b, t, at], near_buf.at[b, t, at])

    def give_copy(b, r):
        at = half_rows(r)
        return remote(
            out_buf.at[b, 2, at], given.at[b, at], give_send.at[b, r], give_recv.at[b, r], device(mate, y, z, core)
        )

    def relay_copy(r):
        at = half_rows(r)
        return remote(own_buf.at[0, at], relay_in.at[at], in_send.at[r], in_recv.at[4 + r], device(mate, y, z, core))

    def partner_copy(a, r):
        at = half_rows(r)
        return remote(
            own_buf.at[2, at], in_sum.at[a, at], in_send.at[2 + r], part_recv.at[a, r], device(partner, y, z, kind)
        )

    def mate_copy(a):
        return remote(mate_out, mate_in.at[a], in_send.at[4], in_recv.at[2 + a], device(mate, y, z, kind))

    def stay_copy(a):
        return remote(own_buf.at[3], in_sum.at[a], in_send.at[5], in_recv.at[a], sibling)

    def add_far(b):
        for t in (0, 1):
            far_copy(b, t).wait_recv()
            out_buf[b, t, half_rows(t), :] = (
                keep[b - 2, t] + far_buf[b - 2, t].astype(jnp.float32)
            ).astype(jnp.bfloat16)
            added_copy(b, t).start()

    def add_near(b):
        for t in (0, 1):
            direct_copy(b, t).wait_recv()
            added_copy(b, t).wait_recv()
        own_buf[b] = own_buf[b] + near_buf[b, 0].astype(jnp.float32) + near_buf[b, 1].astype(jnp.float32)

    def add_given(b):
        for r in (0, 1):
            at = half_rows(r)
            give_copy(b - 2, r).wait_recv()
            out_buf[b, 2, at, :] = (far_keep[b - 2, at, :] + given[b - 2, at, :].astype(jnp.float32)).astype(jnp.bfloat16)
            far_copy(b, r).start()

    def halves(body):
        def step(r, carry):
            body(r)
            return carry

        lax.fori_loop(0, 2, step, 0)

    def lead(r):
        t = 1 - r
        weigh(r)
        value = product(1, r, around(z + hop(t)))
        for e in (0, 1):
            out_buf[2 + e, t, half_rows(r), :] = value[:, lane(e)].astype(jnp.bfloat16)
        direct_copy(2, t).start()

    def give(r):
        value = product(0, r, around(z + 2))
        for e in (0, 1):
            out_buf[e, 2, half_rows(r), :] = value[:, lane(e)].astype(jnp.bfloat16)
        give_copy(0, r).start()

    def next_products(t):
        def part_of(r):
            value = product(0, r, around(z + hop(t)))
            for e in (0, 1):
                out_buf[e, t, half_rows(r), :] = value[:, lane(e)].astype(jnp.bfloat16)

        halves(part_of)
        direct_copy(0, t).start()
        added_copy(0, t).start()

    def kept_products(t):
        value = product(1, t, around(z + hop(t)))
        for e in (0, 1):
            keep[e, t] = value[:, lane(e)]

    def far_products(r):
        value = product(1, r, around(z + 2))
        for e in (0, 1):
            far_keep[e, half_rows(r), :] = value[:, lane(e)]

    def own_products(p):
        def part_of(r):
            value = product(p, r, z)
            for e in (0, 1):
                own_buf[2 * p + e, half_rows(r), :] = value[:, lane(e)]

        halves(part_of)

    halves(lead)
    halves(give)
    for r in (0, 1):
        give_copy(1, r).start()
    halves(next_products)
    halves(far_products)
    add_given(2)
    for t in (0, 1):
        direct_copy(1, t).start()
    halves(kept_products)
    halves(own_products)
    add_near(0)
    for r in (0, 1):
        relay_copy(r).start()
    add_far(2)
    for t in (0, 1):
        added_copy(1, t).start()
    add_given(3)
    for t in (0, 1):
        direct_copy(3, t).start()
    def data_norms(r, carry):
        per = full_cols // 64
        here = pl.ds(pl.multiple_of(lax.rem(r, per) * 64, 64), 64)
        total = None
        for xi in range(SIDE):
            for i in range(SIDE):
                value = squares(data_all[r // per, xi, here, lane(i)])
                total = value if total is None else total + value
        data_part[pl.ds(pl.multiple_of(r * 64, 64), 64), :] = total
        return carry

    lax.fori_loop(0, cols // 64, data_norms, 0)
    add_near(2)

    def to_partner(r):
        relay_copy(r).wait_recv()
        own_buf[2, half_rows(r), :] = own_buf[2, half_rows(r), :] + relay_in[half_rows(r), :]
        partner_copy(core, r).start()

    to_partner(0)
    add_near(1)
    mate_out[...] = own_buf[1].astype(jnp.bfloat16)
    mate_copy(core).start()
    potentials()
    for copy in started:
        copy.wait_send()

    @pl.when(home)
    def _():
        aside.wait_send()
        for t in (0, 1):
            for a in (0, 1):
                own_round(t, a).wait_send()

    add_far(3)
    to_partner(1)

    def settle(b, carry):
        for t in (0, 1):
            direct_copy(b, t).wait_send()
            added_copy(b, t).wait_send()

            @pl.when(b < 2)
            def _():
                give_copy(jnp.minimum(b, 1), t).wait_send()

            @pl.when(b >= 2)
            def _():
                far_copy(jnp.maximum(b, 2), t).wait_send()

        return carry

    lax.fori_loop(0, 3, settle, 0)
    for r in (0, 1):
        relay_copy(r).wait_send()
    swap_copy(1, sibling).wait_recv()
    for i in (0, 1):
        remote(swap.at[0], swap.at[2 + i], swap_send.at[2 + i], swap_recv.at[2 + i], sibling).wait_recv()
    half = rows // LANES
    for a in (0, 1):
        mine_row = jnp.where(core == a, swap[0], swap[1])
        rows_out[pl.ds(a * half, half), :] = jnp.where(home, mine_row, swap[2 + a])

    add_near(3)

    @pl.when(home)
    def _():
        in_sum[core] = own_buf[3]
        stay_copy(1 - core).wait_recv()
        for a in (0, 1):
            mate_copy(a).wait_recv()
            in_sum[a] = in_sum[a] + mate_in[a].astype(jnp.float32)

    @pl.when(jnp.logical_not(home))
    def _():
        stay_copy(core).start()
        for a in (0, 1):
            for r in (0, 1):
                partner_copy(a, r).wait_recv()

    def result_copy(a):
        return pltpu.make_async_copy(in_sum.at[a], targets.at[pl.ds(a * rows, rows)], local_sems.at[a])

    for a in (0, 1):
        result_copy(a).start()

    settle(3, 0)
    for a in (0, 1):
        result_copy(a).wait()
    for r in (0, 1):
        partner_copy(core, r).wait_send()
    mate_copy(core).wait_send()

    @pl.when(jnp.logical_not(home))
    def _():
        stay_copy(core).wait_send()


def hand_on(targets, rows_pot, cols_pot, targets_out, rows_out, cols_out, stage, row_stage, col_stage, sems):
    size = targets.shape[0] // PARTS
    legs = [
        (targets.at[pl.ds(i * size, size)], stage.at[i], targets_out.at[pl.ds(i * size, size)]) for i in range(PARTS)
    ]
    legs += [(rows_pot, row_stage, rows_out), (cols_pot, col_stage, cols_out)]
    first = [pltpu.make_async_copy(src, mid, sems.at[i, 0]) for i, (src, mid, _) in enumerate(legs)]
    second = [pltpu.make_async_copy(mid, dst, sems.at[i, 1]) for i, (_, mid, dst) in enumerate(legs)]
    for copy in first:
        copy.start()
    for before, copy in zip(first, second):
        before.wait()
        copy.start()
    for copy in second:
        copy.wait()


def shards(noise_latents, data_latents):
    nsize = lax.axis_size("noise")
    dsize = lax.axis_size("dp")
    block, piece = noise_latents.shape
    rows, cols = block // 2, 2 * data_latents.shape[0]
    rsize, csize = dsize // 2, nsize * 2
    vmem = pl.BlockSpec(memory_space=pltpu.VMEM)
    f32, bf16 = jnp.float32, jnp.bfloat16
    strip = rows // 2
    row_vec, col_vec = (rows // LANES, LANES), (cols // LANES, LANES)
    sems = pltpu.SemaphoreType.DMA
    targets, rows_pot, cols_pot = pl.pallas_call(
        functools.partial(kernel, rsize, csize, piece * dsize),
        out_shape=(
            jax.ShapeDtypeStruct((block, piece), f32),
            jax.ShapeDtypeStruct((block // LANES, LANES), f32),
            jax.ShapeDtypeStruct((cols // 2 // LANES, LANES), f32),
        ),
        in_specs=[pl.BlockSpec(memory_space=pl.ANY)] * 2,
        out_specs=(pl.BlockSpec(memory_space=pl.ANY), vmem, vmem),
        scratch_shapes=[
            pltpu.VMEM((SIDE, rows, SIDE * piece), bf16),
            pltpu.VMEM((2, SIDE, cols // 2, nsize // SIDE * data_latents.shape[1]), bf16),
            pltpu.VMEM((rows, cols), f32),
            pltpu.VMEM((rows, cols), bf16),
            pltpu.VMEM((rows, LANES), f32),
            pltpu.VMEM((rows, LANES), f32),
            pltpu.VMEM((rows, LANES), f32),
            pltpu.VMEM((rows, LANES), f32),
            pltpu.VMEM((cols, LANES), f32),
            pltpu.VMEM((8, cols), f32),
            pltpu.VMEM(row_vec, f32),
            pltpu.VMEM(col_vec, f32),
            pltpu.VMEM(row_vec, f32),
            pltpu.VMEM(col_vec, f32),
            pltpu.VMEM((4,) + row_vec, f32),
            pltpu.VMEM((ITERS, csize) + col_vec, f32),
            pltpu.VMEM((ITERS, rsize) + row_vec, f32),
            pltpu.VMEM((SIDE, 3, rows, LANES), bf16),
            pltpu.VMEM((SIDE, rows, LANES), f32),
            pltpu.VMEM((2, 2, strip, LANES), bf16),
            pltpu.VMEM((SIDE, 2, rows, LANES), bf16),
            pltpu.VMEM((2, rows, LANES), f32),
            sems((ITERS,)),
            sems((ITERS,)),
            sems((ITERS,)),
            sems((ITERS,)),
            sems((4,)),
            sems((4,)),
            sems((4,)),
            sems((4,)),
            sems((SIDE, 2, 2)),
            sems((SIDE, 2, 2)),
            sems((2, 15)),
            sems((2, 15)),
            sems((SIDE, 2, 3)),
            sems((SIDE, 2, 3)),
            sems((6,)),
            sems((6,)),
            pltpu.VMEM((2, 2, strip, LANES), f32),
            pltpu.VMEM((2, rows, LANES), f32),
            pltpu.VMEM((2, rows, LANES), bf16),
            sems((2, 2)),
            sems((2, 2)),
            sems((2, 2)),
            sems((2,)),
            sems((2, 2)),
            sems((SIDE, 2)),
            pltpu.VMEM((rows, LANES), f32),
            pltpu.VMEM((rows, LANES), bf16),
            pltpu.VMEM((2, rows, LANES), bf16),
        ],
        compiler_params=pltpu.CompilerParams(
            collective_id=0, has_side_effects=True, vmem_limit_bytes=60 * 2**20
        ),
    )(noise_latents, data_latents)
    results = (targets, rows_pot, cols_pot)
    targets, rows_pot, cols_pot = pl.pallas_call(
        hand_on,
        out_shape=tuple(jax.ShapeDtypeStruct(a.shape, a.dtype) for a in results),
        in_specs=[pl.BlockSpec(memory_space=pl.ANY)] * 3,
        out_specs=(pl.BlockSpec(memory_space=pl.ANY),) * 3,
        scratch_shapes=[
            pltpu.VMEM((PARTS, block // PARTS, piece), f32),
            pltpu.VMEM(rows_pot.shape, f32),
            pltpu.VMEM(cols_pot.shape, f32),
            sems((PARTS + 2, 2)),
        ],
        compiler_params=pltpu.CompilerParams(vmem_limit_bytes=60 * 2**20),
    )(*results)
    return targets, rows_pot.reshape(block), cols_pot.reshape(cols // 2)


def solution(mesh):
    return jax.shard_map(
        shards,
        mesh=mesh,
        in_specs=(P("noise", "dp"), P("dp", "noise")),
        out_specs=(P("noise", "dp"), P("noise"), P("dp")),
        check_vma=False,
    )
```
